32 devices in a mesh: wide: 8 (over y, x, core), narrow: 4 (over z).
Axes of the slice: x: 2, y: 2, z: 4, core: 2. Of those that a mesh axis runs over, the one named last changes fastest.
Arguments:
- embeds: bfloat16 [8192, 768], P(('wide', 'narrow')), may hold values from -6 to 6
- skip_tokens: bfloat16 [8192, 768], P(('wide', 'narrow')), may hold values from -6 to 6
- cotangent: bfloat16 [8192, 768], P(('wide', 'narrow')), may hold values from -6 to 6
- lengths: int32 [64], P(('wide', 'narrow')), may hold values from 32 to 128, as said below
- qkv_weight: float32 [2, 768, 2304], P(None, ('wide', 'narrow')), may hold values from -0.21875 to 0.21875
- out_weight: float32 [2, 768, 768], P(None, ('wide', 'narrow')), may hold values from -0.625 to 0.625
- up_weight: float32 [2, 768, 3072], P(None, ('wide', 'narrow')), may hold values from -0.21875 to 0.21875
- down_weight: float32 [2, 3072, 768], P(None, ('wide', 'narrow')), may hold values from -0.109375 to 0.109375
- up_bias: float32 [2, 3072], P(None, ('wide', 'narrow')), may hold values from -2 to 2
- norm_gains: float32 [2, 2, 768], P(None, None, ('wide', 'narrow')), may hold values from 0.5 to 1.5
- biases: float32 [2, 6, 768], P(None, None, ('wide', 'narrow')), may hold values from -2 to 2
- qkv_moments: float32 [2, 2, 768, 2304], P(None, None, ('wide', 'narrow')), as said below
- out_moments: float32 [2, 2, 768, 768], P(None, None, ('wide', 'narrow')), as said below
- up_moments: float32 [2, 2, 768, 3072], P(None, None, ('wide', 'narrow')), as said below
- down_moments: float32 [2, 2, 3072, 768], P(None, None, ('wide', 'narrow')), as said below
- up_bias_moments: float32 [2, 2, 3072], P(None, None, ('wide', 'narrow')), as said below
- gain_moments: float32 [2, 2, 2, 768], P(None, None, None, ('wide', 'narrow')), as said below
- bias_moments: float32 [2, 2, 6, 768], P(None, None, None, ('wide', 'narrow')), as said below
Outputs:
- head_output: bfloat16 [8192, 768], P(('wide', 'narrow'))
- embeds_grad: float32 [8192, 768], P(('wide', 'narrow'))
- skip_grad: float32 [8192, 768], P(('wide', 'narrow'))
- qkv_weight_step: float32 [2, 768, 2304], P(None, ('wide', 'narrow'))
- out_weight_step: float32 [2, 768, 768], P(None, ('wide', 'narrow'))
- up_weight_step: float32 [2, 768, 3072], P(None, ('wide', 'narrow'))
- down_weight_step: float32 [2, 3072, 768], P(None, ('wide', 'narrow'))
- up_bias_step: float32 [2, 3072], P(None, ('wide', 'narrow'))
- norm_gains_step: float32 [2, 2, 768], P(None, None, ('wide', 'narrow'))
- biases_step: float32 [2, 6, 768], P(None, None, ('wide', 'narrow'))
- qkv_moments_new: float32 [2, 2, 768, 2304], P(None, None, ('wide', 'narrow'))
- out_moments_new: float32 [2, 2, 768, 768], P(None, None, ('wide', 'narrow'))
- up_moments_new: float32 [2, 2, 768, 3072], P(None, None, ('wide', 'narrow'))
- down_moments_new: float32 [2, 2, 3072, 768], P(None, None, ('wide', 'narrow'))
- up_bias_moments_new: float32 [2, 2, 3072], P(None, None, ('wide', 'narrow'))
- gain_moments_new: float32 [2, 2, 2, 768], P(None, None, None, ('wide', 'narrow'))
- bias_moments_new: float32 [2, 2, 6, 768], P(None, None, None, ('wide', 'narrow'))
The draws below stay inside these ranges and needn't reach their ends.
Inputs may be any that keep to these rules, and one draw needn't show every extreme that they name: `lengths`: positions at or past a span's length are padding; some span has length exactly 32 and some exactly 128. `qkv_moments`: index 0 of the first dimension holds first moments, index 1 second moments, which are positive. `out_moments`: index 0 of the first dimension holds first moments, index 1 second moments, which are positive. `up_moments`: index 0 of the first dimension holds first moments, index 1 second moments, which are positive. `down_moments`: index 0 of the first dimension holds first moments, index 1 second moments, which are positive. `up_bias_moments`: index 0 of the first dimension holds first moments, index 1 second moments, which are positive. `gain_moments`: index 0 of the first dimension holds first moments, index 1 second moments, which are positive. `bias_moments`: index 0 of the first dimension holds first moments, index 1 second moments, which are positive.
All inputs are finite; a program needn't handle non-finite values.
Results may differ from the reference program's by a relative error of at most 0.02.
Values may be sent and summed in bfloat16 or wider, within the bound.
A program may use at most 256 MiB of HBM per device.

```python
import math
import jax
import jax.numpy as jnp
from jax import lax

D = 768
HEADS = 12
FF = 3072
SPAN = 128
LAYERS = 2
SPANS = 64
TOKENS = 8192


def moment_pair(key, shape):
    first_key, second_key = jax.random.split(key)
    first_moment = jax.random.normal(first_key, shape, jnp.float32) * 0.5
    second_moment = jnp.exp(jax.random.uniform(second_key, shape, jnp.float32, math.log(0.5), math.log(4.0)))
    return jnp.stack([first_moment, second_moment])


def draw_lengths(key, part):
    key = jax.random.fold_in(key, 11)
    base_key, long_key, short_key = jax.random.split(key, 3)
    drawn = jax.random.randint(base_key, (SPANS,), SPAN // 4, SPAN + 1, jnp.int32)
    longest = jax.random.randint(long_key, (), 0, SPANS, jnp.int32)
    shortest = (longest + 1 + jax.random.randint(short_key, (), 0, SPANS - 1, jnp.int32)) % SPANS
    return drawn.at[longest].set(SPAN).at[shortest].set(SPAN // 4).astype(jnp.int32)


def draw_qkv_moments(key, part):
    key = jax.random.fold_in(key, 21)
    return moment_pair(key, (LAYERS, D, 3 * D))


def draw_out_moments(key, part):
    key = jax.random.fold_in(key, 22)
    return moment_pair(key, (LAYERS, D, D))


def draw_up_moments(key, part):
    key = jax.random.fold_in(key, 23)
    return moment_pair(key, (LAYERS, D, FF))


def draw_down_moments(key, part):
    key = jax.random.fold_in(key, 24)
    return moment_pair(key, (LAYERS, FF, D))


def draw_up_bias_moments(key, part):
    key = jax.random.fold_in(key, 25)
    return moment_pair(key, (LAYERS, FF))


def draw_gain_moments(key, part):
    key = jax.random.fold_in(key, 26)
    return moment_pair(key, (LAYERS, 2, D))


def draw_bias_moments(key, part):
    key = jax.random.fold_in(key, 27)
    return moment_pair(key, (LAYERS, 6, D))


def block_levels(stream_key, dims, cuts, least, largest):
    gain = 1.0
    for axis_at, shards_of in cuts:
        draws = jax.random.uniform(jax.random.fold_in(jax.random.fold_in(stream_key, 6), axis_at), (shards_of,), jnp.float32, least / len(cuts), largest / len(cuts))
        gain = gain * jnp.repeat(jnp.exp(draws), dims[axis_at] // shards_of).reshape((-1,) + (1,) * (len(dims) - 1 - axis_at))
    return gain


def scatter_about(own_key, extent, deviation, reach, cuts=(), dtype=jnp.bfloat16):
    loudness = block_levels(own_key, extent, cuts, -0.22, 0.18) if cuts else 1.0
    values = jax.random.normal(own_key, extent, jnp.float32) * deviation * loudness
    return jnp.minimum(jnp.maximum(values, -reach), reach).astype(dtype)


def setup_inputs(seed: int = 0) -> dict:
    splits = jax.random.split(jax.random.key(seed), 19)
    embeds = scatter_about(splits[0], (TOKENS, D), 1.0, 6.0, ((0, 32),))
    skip_tokens = scatter_about(splits[1], (TOKENS, D), 1.0, 6.0, ((0, 32),))
    cotangent = scatter_about(splits[2], (TOKENS, D), 1.0, 6.0, ((0, 32),))
    lengths = draw_lengths(jax.random.fold_in(splits[18], 71), 0)
    qkv_weight = scatter_about(splits[4], (LAYERS, D, 3 * D), D ** -0.5, 0.21875, ((1, 32),), jnp.float32)
    out_weight = scatter_about(splits[5], (LAYERS, D, D), (D // 8) ** -0.5, 0.625, ((1, 32),), jnp.float32)
    up_weight = scatter_about(splits[6], (LAYERS, D, FF), D ** -0.5, 0.21875, ((1, 32),), jnp.float32)
    down_weight = scatter_about(splits[7], (LAYERS, FF, D), FF ** -0.5, 0.109375, ((1, 32),), jnp.float32)
    up_bias = scatter_about(splits[8], (LAYERS, FF), 0.3, 2.0, ((1, 32),), jnp.float32)
    norm_gains = jnp.clip(1.0 + 0.1 * jax.random.normal(splits[9], (LAYERS, 2, D), jnp.float32), 0.5, 1.5)
    biases = scatter_about(splits[10], (LAYERS, 6, D), 0.3, 2.0, ((2, 32),), jnp.float32)
    qkv_moments = draw_qkv_moments(jax.random.fold_in(splits[18], 71), 0)
    out_moments = draw_out_moments(jax.random.fold_in(splits[18], 71), 0)
    up_moments = draw_up_moments(jax.random.fold_in(splits[18], 71), 0)
    down_moments = draw_down_moments(jax.random.fold_in(splits[18], 71), 0)
    up_bias_moments = draw_up_bias_moments(jax.random.fold_in(splits[18], 71), 0)
    gain_moments = draw_gain_moments(jax.random.fold_in(splits[18], 71), 0)
    bias_moments = draw_bias_moments(jax.random.fold_in(splits[18], 71), 0)
    return {"embeds": embeds, "skip_tokens": skip_tokens, "cotangent": cotangent, "lengths": lengths, "qkv_weight": qkv_weight, "out_weight": out_weight, "up_weight": up_weight, "down_weight": down_weight, "up_bias": up_bias, "norm_gains": norm_gains, "biases": biases, "qkv_moments": qkv_moments, "out_moments": out_moments, "up_moments": up_moments, "down_moments": down_moments, "up_bias_moments": up_bias_moments, "gain_moments": gain_moments, "bias_moments": bias_moments}


@jax.custom_vjp
def low(v):
    return lax.optimization_barrier(v.astype(jnp.bfloat16)).astype(jnp.float32)

@jax.custom_vjp
def low_back(v):
    return v

def low_keep(v):
    return (low(v), None)

def low_pass(kept, grad):
    return (grad,)

def back_keep(v):
    return (v, None)

def back_low(kept, grad):
    return (low(grad),)
low.defvjp(low_keep, low_pass)
low_back.defvjp(back_keep, back_low)
norm_epsilon = 1e-12
score_scale = 0.125
masked_score = -1000000000.0
beta_first = 0.9
beta_second = 0.999
adam_epsilon = 1e-08
weight_decay = 0.01
first_fix = 1.0 - 0.9 ** 10
second_fix = 1.0 - 0.999 ** 10
highest = lax.Precision.HIGHEST

def layer_norm(values, gain_row, shift_row):
    centred = values - lax.optimization_barrier(jnp.mean(values, axis=-1, keepdims=True))
    inv_scale = lax.rsqrt(lax.optimization_barrier(jnp.mean(centred * centred, axis=-1, keepdims=True)) + norm_epsilon)
    return centred * inv_scale * gain_row + shift_row

def block(weights, inputs, key_valid):
    qkv_w, out_w, up_w, down_w, up_b, gain_rows, biases = weights
    row_count, model_width = inputs.shape
    span_count = row_count // SPAN

    def head_view(tensor):
        return tensor.reshape(span_count, SPAN, HEADS, model_width // HEADS)
    mixed_in = jnp.dot(inputs, qkv_w, precision=highest)
    queries = low_back(low(mixed_in[:, :model_width] + biases[0]))
    keys_low = low_back(low(mixed_in[:, model_width:2 * model_width]))
    values_low = low_back(low(mixed_in[:, 2 * model_width:] + biases[1]))
    scores = jnp.einsum('bqhe,bkhe->bhqk', head_view(queries), head_view(keys_low), precision=highest) * score_scale
    scores = low_back(scores)
    scores = jnp.where(key_valid[:, None, None, :], scores, masked_score)
    softmax_out = low(jax.nn.softmax(scores, axis=-1))
    context = jnp.einsum('bhqk,bkhe->bqhe', softmax_out, head_view(values_low), precision=highest)
    context = low_back(low(context.reshape(row_count, model_width)))
    attended = low_back(jnp.dot(context, out_w, precision=highest) + biases[2])
    hidden = layer_norm(inputs + attended, gain_rows[0], biases[3])
    pre_gelu = low_back(jnp.dot(low(hidden), up_w, precision=highest) + up_b)
    activated = low(jax.nn.gelu(pre_gelu, approximate=False))
    branch_out = low_back(jnp.dot(activated, down_w, precision=highest) + biases[4])
    return layer_norm(hidden + branch_out, gain_rows[1], biases[5])

def forward(params, embeds, skip_tokens, key_valid):
    rounded = tuple((low(parameter) for parameter in params))
    first_layer = tuple((parameter[0] for parameter in rounded))
    second_layer = tuple((parameter[1] for parameter in rounded))
    per_group = math.gcd(SPANS, 32)
    groups = SPANS // per_group

    def one_group(carried, pieces):
        embed_rows, skip_rows, valid_rows = pieces
        backbone = low(block(first_layer, embed_rows, valid_rows)).reshape(per_group, SPAN, D)
        skip_view = skip_rows.reshape(per_group, SPAN, D)
        head_in = jnp.concatenate([backbone[:, :1], skip_view[:, 1:]], axis=1).reshape(per_group * SPAN, D)
        return (carried, block(second_layer, head_in, valid_rows))
    _, outputs = lax.scan(jax.checkpoint(one_group), jnp.zeros((), jnp.float32), (embeds.reshape(groups, per_group * SPAN, D), skip_tokens.reshape(groups, per_group * SPAN, D), key_valid.reshape(groups, per_group, SPAN)))
    return outputs.reshape(TOKENS, D)

def adam_direction(parameter, moment, gradient, decayed):
    first_moment = beta_first * moment[0] + (1.0 - beta_first) * gradient
    second_moment = beta_second * moment[1] + (1.0 - beta_second) * gradient * gradient
    update = first_moment / first_fix / (jnp.sqrt(second_moment / second_fix) + adam_epsilon)
    update = update + decayed * weight_decay * parameter
    return (update, jnp.stack([first_moment, second_moment]))

def reference(embeds, skip_tokens, cotangent, lengths, qkv_weight, out_weight, up_weight, down_weight, up_bias, norm_gains, biases, qkv_moments, out_moments, up_moments, down_moments, up_bias_moments, gain_moments, bias_moments):
    params = (qkv_weight, out_weight, up_weight, down_weight, up_bias, norm_gains, biases)
    moments = (qkv_moments, out_moments, up_moments, down_moments, up_bias_moments, gain_moments, bias_moments)
    positions = lax.broadcasted_iota(jnp.int32, (SPANS, SPAN), 1)
    key_valid = positions < lengths.astype(jnp.int32)[:, None]
    output, pullback = jax.vjp(lambda p, e, s: forward(p, e, s, key_valid), params, embeds.astype(jnp.float32), skip_tokens.astype(jnp.float32))
    param_grads, embeds_grad, skip_grad = pullback(cotangent.astype(jnp.float32))
    new_steps = []
    new_moments = []
    for index in range(7):
        decayed = 1.0 if index < 4 else 0.0
        direction, moment = adam_direction(params[index], moments[index], param_grads[index], decayed)
        new_steps.append(direction)
        new_moments.append(moment)
    return (output.astype(jnp.bfloat16), embeds_grad, skip_grad, new_steps[0], new_steps[1], new_steps[2], new_steps[3], new_steps[4], new_steps[5], new_steps[6], new_moments[0], new_moments[1], new_moments[2], new_moments[3], new_moments[4], new_moments[5], new_moments[6])
```

```python
import jax
import jax.numpy as jnp
from jax import lax
from jax.experimental import pallas as pl
from jax.experimental.pallas import tpu as pltpu
from jax.sharding import PartitionSpec as P

HEADS = 12
SPAN = 128

norm_epsilon = 1e-12
score_scale = 0.125
masked_score = -1000000000.0
beta_first = 0.9
beta_second = 0.999
adam_epsilon = 1e-08
weight_decay = 0.01
first_fix = 1.0 - 0.9**10
second_fix = 1.0 - 0.999**10


def dot_first(left_side, right_side):
    return lax.dot_general(
        left_side, right_side, (((0,), (0,)), ((), ())), preferred_element_type=jnp.float32
    )


def dot_last(left_side, right_side):
    return lax.dot_general(
        left_side, right_side, (((1,), (1,)), ((), ())), preferred_element_type=jnp.float32
    )


def normalize(values, gain_row, shift_row):
    centred = values - jnp.mean(values, axis=-1, keepdims=True)
    inv_scale = lax.rsqrt(jnp.mean(centred * centred, axis=-1, keepdims=True) + norm_epsilon)
    normed = centred * inv_scale
    return (normed * gain_row + shift_row, normed, inv_scale)


def normalize_back(gradient, normed, inv_scale, gain_row):
    grad_gain = jnp.sum(gradient * normed, axis=0)
    grad_shift = jnp.sum(gradient, axis=0)
    scaled = gradient * gain_row
    grad_in = inv_scale * (
        scaled
        - jnp.mean(scaled, axis=-1, keepdims=True)
        - normed * jnp.mean(scaled * normed, axis=-1, keepdims=True)
    )
    return (grad_in, grad_gain, grad_shift)


def head_view(tensor):
    return tensor.reshape(tensor.shape[0] // SPAN, SPAN, HEADS, tensor.shape[1] // HEADS)


def attend_scores(queries, keys_low, key_valid):
    scores = (
        jnp.einsum(
            "bqhe,bkhe->bhqk",
            head_view(queries),
            head_view(keys_low),
            preferred_element_type=jnp.float32,
        )
        * score_scale
    )
    return jnp.where(key_valid[:, None, None, :], scores, masked_score)


def forward_block(weights, inputs, key_valid):
    qkv_w, out_w, up_w, down_w, up_b, gain_rows, biases = weights
    gains_wide = gain_rows.astype(jnp.float32)
    biases_wide = biases.astype(jnp.float32)
    row_count, model_width = inputs.shape
    mixed_in = jnp.dot(inputs, qkv_w, preferred_element_type=jnp.float32)
    queries = (mixed_in[:, :model_width] + biases_wide[0]).astype(jnp.bfloat16)
    keys_low = mixed_in[:, model_width : 2 * model_width].astype(jnp.bfloat16)
    values_low = (mixed_in[:, 2 * model_width :] + biases_wide[1]).astype(jnp.bfloat16)
    scores = attend_scores(queries, keys_low, key_valid)
    row_max = jnp.max(scores, axis=-1, keepdims=True)
    weights_exp = jnp.exp(scores - row_max)
    row_total = jnp.sum(weights_exp, axis=-1, keepdims=True)
    softmax_out = (weights_exp / row_total).astype(jnp.bfloat16)
    log_total = row_max + jnp.log(row_total)
    context = jnp.einsum(
        "bhqk,bkhe->bqhe", softmax_out, head_view(values_low), preferred_element_type=jnp.float32
    )
    context = context.reshape(row_count, model_width).astype(jnp.bfloat16)
    attended = jnp.dot(context, out_w, preferred_element_type=jnp.float32) + biases_wide[2]
    hidden, normed_one, scale_one = normalize(
        inputs.astype(jnp.float32) + attended, gains_wide[0], biases_wide[3]
    )
    hidden_low = hidden.astype(jnp.bfloat16)
    pre_gelu = jnp.dot(hidden_low, up_w, preferred_element_type=jnp.float32) + up_b.astype(
        jnp.float32
    )
    activated = jax.nn.gelu(pre_gelu, approximate=False).astype(jnp.bfloat16)
    branch_out = jnp.dot(activated, down_w, preferred_element_type=jnp.float32) + biases_wide[4]
    output, normed_two, scale_two = normalize(hidden + branch_out, gains_wide[1], biases_wide[5])
    saved = (
        queries,
        keys_low,
        values_low,
        log_total,
        context,
        normed_one,
        scale_one,
        hidden_low,
        pre_gelu,
        activated,
        normed_two,
        scale_two,
    )
    return (output, saved)


def backward_block(weights, inputs, key_valid, grad_out):
    qkv_w, out_w, up_w, down_w, up_b, gain_rows, biases = weights
    gains_wide = gain_rows.astype(jnp.float32)
    row_count, model_width = inputs.shape
    output, saved = forward_block(weights, inputs, key_valid)
    (
        queries,
        keys_low,
        values_low,
        log_total,
        context,
        normed_one,
        scale_one,
        hidden_low,
        pre_gelu,
        activated,
        normed_two,
        scale_two,
    ) = saved
    grad_pre_two, grad_gain_two, grad_shift_two = normalize_back(
        grad_out, normed_two, scale_two, gains_wide[1]
    )
    grad_branch = grad_pre_two.astype(jnp.bfloat16)
    grad_down_w = dot_first(activated, grad_branch)
    grad_act = dot_last(grad_branch, down_w)
    _, gelu_back = jax.vjp(lambda inner: jax.nn.gelu(inner, approximate=False), pre_gelu)
    grad_pre_gelu = gelu_back(grad_act)[0].astype(jnp.bfloat16)
    grad_up_w = dot_first(hidden_low, grad_pre_gelu)
    grad_hidden = grad_pre_two + dot_last(grad_pre_gelu, up_w)
    grad_pre_one, grad_gain_one, grad_shift_one = normalize_back(
        grad_hidden, normed_one, scale_one, gains_wide[0]
    )
    grad_attended = grad_pre_one.astype(jnp.bfloat16)
    grad_out_w = dot_first(context, grad_attended)
    grad_context = head_view(dot_last(grad_attended, out_w).astype(jnp.bfloat16))
    scores = attend_scores(queries, keys_low, key_valid)
    softmax_full = jnp.exp(scores - log_total)
    grad_probs = jnp.einsum(
        "bqhe,bkhe->bhqk", grad_context, head_view(values_low), preferred_element_type=jnp.float32
    )
    grad_values = jnp.einsum(
        "bhqk,bqhe->bkhe",
        softmax_full.astype(jnp.bfloat16),
        grad_context,
        preferred_element_type=jnp.float32,
    )
    grad_values = grad_values.reshape(row_count, model_width).astype(jnp.bfloat16)
    grad_scores = softmax_full * (
        grad_probs - jnp.sum(softmax_full * grad_probs, axis=-1, keepdims=True)
    )
    grad_scores = grad_scores.astype(jnp.bfloat16)
    grad_queries = (
        jnp.einsum(
            "bhqk,bkhe->bqhe", grad_scores, head_view(keys_low), preferred_element_type=jnp.float32
        )
        * score_scale
    )
    grad_queries = grad_queries.reshape(row_count, model_width).astype(jnp.bfloat16)
    grad_keys = (
        jnp.einsum(
            "bhqk,bqhe->bkhe", grad_scores, head_view(queries), preferred_element_type=jnp.float32
        )
        * score_scale
    )
    grad_keys = grad_keys.reshape(row_count, model_width).astype(jnp.bfloat16)
    grad_mixed = jnp.concatenate([grad_queries, grad_keys, grad_values], axis=1)
    grad_qkv_w = dot_first(inputs, grad_mixed)
    grad_inputs = grad_pre_one + dot_last(grad_mixed, qkv_w)
    grad_gains = jnp.stack([grad_gain_one, grad_gain_two])
    grad_biases = jnp.stack(
        [
            jnp.sum(grad_queries, axis=0, dtype=jnp.float32),
            jnp.sum(grad_values, axis=0, dtype=jnp.float32),
            jnp.sum(grad_attended, axis=0, dtype=jnp.float32),
            grad_shift_one,
            jnp.sum(grad_branch, axis=0, dtype=jnp.float32),
            grad_shift_two,
        ]
    )
    grads = (
        grad_qkv_w,
        grad_out_w,
        grad_up_w,
        grad_down_w,
        jnp.sum(grad_pre_gelu, axis=0, dtype=jnp.float32),
        grad_gains,
        grad_biases,
    )
    return (output, grad_inputs, grads)


MESH = pl.DeviceIdType.MESH


def place():
    wide = lax.axis_index("wide")
    z = lax.axis_index("narrow")
    return wide // 4, (wide // 2) % 2, wide % 2, z


def device(y, x, c, z):
    return ((y * 2 + x) * 2 + c, z)


def flat(y, x, c, z):
    return ((y * 2 + x) * 2 + c) * 4 + z


def near(z, k):
    if k == 0:
        return z
    if k == 1:
        return z + 1 - 2 * (z % 2)
    if k == 2:
        return (z + 2) % 4
    return 3 - z


def greet(y, x, c, z):
    barrier = pltpu.get_barrier_semaphore()
    for there in (device(y, 1 - x, c, z), device(1 - y, x, c, z), device(y, x, 1 - c, z)):
        pl.semaphore_signal(barrier, inc=1, device_id=there, device_id_type=MESH)

    @pl.when(z < 3)
    def _():
        pl.semaphore_signal(barrier, inc=1, device_id=device(y, x, c, z + 1), device_id_type=MESH)

    @pl.when(z > 0)
    def _():
        pl.semaphore_signal(barrier, inc=1, device_id=device(y, x, c, z - 1), device_id_type=MESH)

    pl.semaphore_wait(barrier, 4 + ((z + 1) // 2) % 2)


def run_if(pred, action):
    if pred is None:
        action()
    else:
        pl.when(pred)(action)


class Sender:
    def __init__(self, send_sem):
        self.send_sem = send_sem
        self.count = 0
        self.pending = []

    def send(self, src, dst, recv, there, pred=None):
        copy = pltpu.make_async_remote_copy(
            src_ref=src,
            dst_ref=dst,
            send_sem=self.send_sem.at[self.count],
            recv_sem=recv,
            device_id=there,
            device_id_type=MESH,
        )
        self.count += 1
        run_if(pred, copy.start)
        self.pending.append((pred, copy))

    def local(self, src, dst):
        copy = pltpu.make_async_copy(src, dst, self.send_sem.at[self.count])
        self.count += 1
        copy.start()
        return copy

    def drain(self):
        for pred, copy in self.pending:
            run_if(pred, copy.wait_send)
        self.pending = []


def arrived(dst, recv, me, pred=None):
    def wait():
        pltpu.make_async_remote_copy(
            src_ref=dst, dst_ref=dst, send_sem=recv, recv_sem=recv, device_id=me, device_id_type=MESH
        ).wait_recv()

    run_if(pred, wait)


def gather_steps(sender, subs, recv_sem, base=0):
    y, x, c, z = place()
    sib = device(y, x, 1 - c, z)
    xn = device(y, 1 - x, c, z)
    yn = device(1 - y, x, c, z)

    def there(sub, stage):
        return (xn if stage == 1 else yn) if sub[2] == "x" else (yn if stage == 1 else xn)

    def unit(sub, far1, far2, zz, core):
        fx, fy = (far1, far2) if sub[2] == "x" else (far2, far1)
        return flat(1 - y if fy else y, 1 - x if fx else x, core, zz)

    def push(i, sub, src, slab_at, target, pred=None):
        sender.send(src, sub[1](slab_at), recv_sem.at[base + i, slab_at], target, pred)

    mine = flat(y, x, c, z)
    locals_ = []
    for i, sub in enumerate(subs):
        own = sub[0]
        push(i, sub, own, mine, device(y, x, c, z + 1), z < 3)
        push(i, sub, own, mine, device(y, x, c, z - 1), z > 0)
        push(i, sub, own, mine, there(sub, 1))
        push(i, sub, own, mine, there(sub, 2))
        push(i, sub, own, mine, sib)
        locals_.append(sender.local(own, sub[1](mine)))
    yield

    def from_z(dist):
        for i, sub in enumerate(subs):
            for up in (True, False):
                zz = z - dist if up else z + dist
                have = (z >= dist) if up else (z <= 3 - dist)
                at = flat(y, x, c, zz)

                @pl.when(have)
                def _(i=i, sub=sub, up=up, at=at):
                    arrived(sub[1](at), recv_sem.at[base + i, at], device(y, x, c, z))

                if dist < 3:
                    if up:
                        push(i, sub, sub[1](at), at, device(y, x, c, z + 1), (z >= dist) & (z < 3))
                    else:
                        push(i, sub, sub[1](at), at, device(y, x, c, z - 1), (z <= 3 - dist) & (z > 0))
                push(i, sub, sub[1](at), at, there(sub, 1), have)
                push(i, sub, sub[1](at), at, there(sub, 2), have)
                push(i, sub, sub[1](at), at, sib, have)

    def from_first(k):
        for i, sub in enumerate(subs):
            at = unit(sub, True, False, near(z, k), c)
            arrived(sub[1](at), recv_sem.at[base + i, at], device(y, x, c, z))
            push(i, sub, sub[1](at), at, there(sub, 2))
            push(i, sub, sub[1](at), at, sib)

    def from_second(far, k):
        for i, sub in enumerate(subs):
            at = unit(sub, far, True, near(z, k), c)
            arrived(sub[1](at), recv_sem.at[base + i, at], device(y, x, c, z))
            push(i, sub, sub[1](at), at, sib)

    from_z(1)
    yield
    from_first(0)
    yield
    from_z(2)
    yield
    from_first(1)
    yield
    from_z(3)
    yield
    from_first(2)
    from_first(3)
    yield
    for far in (False, True):
        for k in range(4):
            from_second(far, k)
            yield
    for i, sub in enumerate(subs):
        for a in range(2):
            for b in range(2):
                for k in range(4):
                    at = unit(sub, a == 1, b == 1, near(z, k), 1 - c)
                    arrived(sub[1](at), recv_sem.at[base + i, at], device(y, x, c, z))
    for copy in locals_:
        copy.wait()


SENDS_PER_GATHER = 6 + 2 * 4 + 2 * 4 + 2 * 3 + 4 * 2 + 8

def reduce_steps(sender, subs, recv_sem, base=0):
    y, x, c, z = place()
    me = device(y, x, c, z)
    sib = device(y, x, 1 - c, z)
    xn = device(y, 1 - x, c, z)
    yn = device(1 - y, x, c, z)
    targets = (0, 3, 1, 2)

    def chip(sub, far1, far2):
        fx, fy = (far1, far2) if sub["dim"] == "x" else (far2, far1)
        return (1 - y if fy else y), (1 - x if fx else x)

    def own(sub, far1, far2, zz, core):
        cy, cx = chip(sub, far1, far2)
        return sub["own"](flat(cy, cx, core, zz))

    def sib_slot(sub, far1, far2, zz):
        cy, cx = chip(sub, far1, far2)
        return (cy * 2 + cx) * 4 + zz

    def first_of(sub):
        return xn if sub["dim"] == "x" else yn

    def second_of(sub):
        return yn if sub["dim"] == "x" else xn

    def coord1(sub, far):
        here = x if sub["dim"] == "x" else y
        return 1 - here if far else here

    kinds = ((False, True), (True, True), (True, False), (False, False))

    def start_sib(zz):
        for i, sub in enumerate(subs):
            for far1, far2 in kinds:
                slot = sib_slot(sub, far1, far2, zz)
                sender.send(
                    own(sub, far1, far2, zz, 1 - c),
                    sub["sib"].at[slot],
                    recv_sem.at[base + i, slot],
                    sib,
                )

    def take(sub, i, kind, slot):
        buf = sub[kind].at[slot]
        at = {"sib": 0, "second": 16, "first": 24, "chain": 28}[kind] + slot
        arrived(buf, recv_sem.at[base + i, at], me)
        return buf

    def add_into(sub, dst, parts):
        total = dst[...].astype(jnp.float32)
        for part in parts:
            total = total + part[...].astype(jnp.float32)
        dst[...] = total.astype(dst.dtype)

    def step_a(zz):
        for i, sub in enumerate(subs):
            for far1 in (False, True):
                acc = own(sub, far1, True, zz, c)
                add_into(sub, acc, [take(sub, i, "sib", sib_slot(sub, far1, True, zz))])
                slot = coord1(sub, far1) * 4 + zz
                sender.send(acc, sub["second"].at[slot], recv_sem.at[base + i, 16 + slot], second_of(sub))

    def step_b(zz):
        for i, sub in enumerate(subs):
            acc = own(sub, True, False, zz, c)
            parts = [
                take(sub, i, "sib", sib_slot(sub, True, False, zz)),
                take(sub, i, "second", coord1(sub, True) * 4 + zz),
            ]
            add_into(sub, acc, parts)
            sender.send(acc, sub["first"].at[zz], recv_sem.at[base + i, 24 + zz], first_of(sub))

    def chain_send(sub, i, acc, zz, up, pred):
        slot = zz if up else jnp.where(z - 1 == zz, 4, zz)
        there = device(y, x, c, z + 1) if up else device(y, x, c, z - 1)
        sender.send(acc, sub["chain"].at[slot], recv_sem.at[base + i, 28 + slot], there, pred)

    def step_c(zz):
        for i, sub in enumerate(subs):
            acc = own(sub, False, False, zz, c)
            parts = [
                take(sub, i, "sib", sib_slot(sub, False, False, zz)),
                take(sub, i, "second", coord1(sub, False) * 4 + zz),
                take(sub, i, "first", zz),
            ]
            add_into(sub, acc, parts)
            if zz > 0:
                chain_send(sub, i, acc, zz, True, z == 0)
            if zz < 3:
                chain_send(sub, i, acc, zz, False, z == 3)

    def step_d(zz):
        for i, sub in enumerate(subs):
            acc = own(sub, False, False, zz, c)
            for up in (True, False):
                pred = (z > 0) & (z < zz) if up else (z < 3) & (z > zz)

                @pl.when(pred)
                def _(i=i, sub=sub, acc=acc):
                    add_into(sub, acc, [take(sub, i, "chain", zz)])

                chain_send(sub, i, acc, zz, up, pred)

    def step_f():
        for i, sub in enumerate(subs):
            total = own(sub, False, False, z, c)[...].astype(jnp.float32)
            sub["out"][...] = total

            @pl.when(z > 0)
            def _(i=i, sub=sub):
                sub["out"][...] += take(sub, i, "chain", z)[...].astype(jnp.float32)

            @pl.when(z < 3)
            def _(i=i, sub=sub):
                sub["out"][...] += take(sub, i, "chain", 4)[...].astype(jnp.float32)

    t0, t1, t2, t3 = targets
    for zz in targets:
        start_sib(zz)
    yield
    for action, zz in (
        (step_a, t0), (step_a, t1), (step_b, t0), (step_a, t2), (step_b, t1), (step_c, t0), (step_a, t3),
        (step_b, t2), (step_d, t0), (step_c, t1), (step_b, t3), (step_d, t1), (step_c, t2), (step_d, t2),
        (step_c, t3), (step_d, t3),
    ):
        action(zz)
        yield
    step_f()


SENDS_PER_REDUCE = 16 + 8 + 4 + 12 + 12

def adam_direction(parameter, moment, gradient, decayed):
    first_moment = beta_first * moment[0] + (1.0 - beta_first) * gradient
    second_moment = beta_second * moment[1] + (1.0 - beta_second) * gradient * gradient
    update = first_moment / first_fix / (jnp.sqrt(second_moment / second_fix) + adam_epsilon)
    update = update + decayed * weight_decay * parameter
    return (update, jnp.stack([first_moment, second_moment]))


def first_forward(weights, inputs, key_valid):
    qkv_w, out_w, up_w, down_w, up_b, gain_rows, biases = weights
    row_count, width = inputs.shape
    span_count = row_count // SPAN
    first = inputs.reshape(span_count, SPAN, width)[:, 0]
    mixed = jnp.dot(inputs, qkv_w[:, width:], preferred_element_type=jnp.float32)
    keys = mixed[:, :width].astype(jnp.bfloat16).reshape(span_count, SPAN, HEADS, width // HEADS)
    values = (mixed[:, width:] + biases[1]).astype(jnp.bfloat16)
    values = values.reshape(span_count, SPAN, HEADS, width // HEADS)
    queries = jnp.dot(first, qkv_w[:, :width], preferred_element_type=jnp.float32) + biases[0]
    queries = queries.astype(jnp.bfloat16).reshape(span_count, HEADS, width // HEADS)
    scores = (
        jnp.einsum("bhe,bkhe->bhk", queries, keys, preferred_element_type=jnp.float32) * score_scale
    )
    scores = jnp.where(key_valid[:, None, :], scores, masked_score)
    probs = jax.nn.softmax(scores, axis=-1)
    context = jnp.einsum(
        "bhk,bkhe->bhe", probs.astype(jnp.bfloat16), values, preferred_element_type=jnp.float32
    )
    context = context.reshape(span_count, width).astype(jnp.bfloat16)
    attended = jnp.dot(context, out_w, preferred_element_type=jnp.float32) + biases[2]
    hidden, normed_one, scale_one = normalize(
        first.astype(jnp.float32) + attended, gain_rows[0], biases[3]
    )
    hidden_low = hidden.astype(jnp.bfloat16)
    pre_gelu = jnp.dot(hidden_low, up_w, preferred_element_type=jnp.float32) + up_b
    activated = jax.nn.gelu(pre_gelu, approximate=False).astype(jnp.bfloat16)
    branch_out = jnp.dot(activated, down_w, preferred_element_type=jnp.float32) + biases[4]
    output, normed_two, scale_two = normalize(hidden + branch_out, gain_rows[1], biases[5])
    saved = (
        first, queries, keys, values, probs, context, normed_one, scale_one, hidden_low, pre_gelu,
        activated, normed_two, scale_two,
    )
    return output, saved


def first_backward(weights, inputs, saved, grad_out):
    qkv_w, out_w, up_w, down_w, up_b, gain_rows, biases = weights
    (
        first, queries, keys, values, probs, context, normed_one, scale_one, hidden_low, pre_gelu,
        activated, normed_two, scale_two,
    ) = saved
    row_count, width = inputs.shape
    span_count = row_count // SPAN
    grad_pre_two, grad_gain_two, grad_shift_two = normalize_back(
        grad_out, normed_two, scale_two, gain_rows[1]
    )
    grad_branch = grad_pre_two.astype(jnp.bfloat16)
    grad_act = dot_last(grad_branch, down_w)
    _, gelu_back = jax.vjp(lambda inner: jax.nn.gelu(inner, approximate=False), pre_gelu)
    grad_pre_gelu = gelu_back(grad_act)[0].astype(jnp.bfloat16)
    grad_hidden = grad_pre_two + dot_last(grad_pre_gelu, up_w)
    grad_pre_one, grad_gain_one, grad_shift_one = normalize_back(
        grad_hidden, normed_one, scale_one, gain_rows[0]
    )
    grad_attended = grad_pre_one.astype(jnp.bfloat16)
    grad_context = dot_last(grad_attended, out_w).astype(jnp.bfloat16)
    grad_context = grad_context.reshape(span_count, HEADS, width // HEADS)
    grad_probs = jnp.einsum(
        "bhe,bkhe->bhk", grad_context, values, preferred_element_type=jnp.float32
    )
    grad_values = jnp.einsum("bhk,bhe->bkhe", probs.astype(jnp.bfloat16), grad_context)
    grad_values = grad_values.reshape(row_count, width).astype(jnp.bfloat16)
    grad_scores = probs * (grad_probs - jnp.sum(probs * grad_probs, axis=-1, keepdims=True))
    grad_scores = grad_scores.astype(jnp.bfloat16)
    grad_queries = (
        jnp.einsum("bhk,bkhe->bhe", grad_scores, keys, preferred_element_type=jnp.float32)
        * score_scale
    )
    grad_queries = grad_queries.reshape(span_count, width).astype(jnp.bfloat16)
    grad_keys = (
        jnp.einsum("bhk,bhe->bkhe", grad_scores, queries, preferred_element_type=jnp.float32)
        * score_scale
    )
    grad_keys = grad_keys.reshape(row_count, width).astype(jnp.bfloat16)
    grad_kv = jnp.concatenate([grad_keys, grad_values], axis=1)
    grad_kv_w = dot_first(inputs, grad_kv)
    grad_inputs = dot_last(grad_kv, qkv_w[:, width:])
    grad_first = grad_pre_one + dot_last(grad_queries, qkv_w[:, :width])
    placed = jnp.pad(grad_first[:, None], ((0, 0), (0, SPAN - 1), (0, 0))).reshape(row_count, width)
    grad_inputs = grad_inputs + placed
    rows = jnp.concatenate(
        [context, grad_attended, hidden_low, grad_pre_gelu, activated, grad_branch, first, grad_queries],
        axis=1,
    )

    def total(values):
        return jnp.sum(values, axis=0, dtype=jnp.float32)

    small = (
        total(grad_pre_gelu),
        jnp.stack([grad_gain_one, grad_gain_two]),
        jnp.stack(
            [
                total(grad_queries), total(grad_values), total(grad_attended), grad_shift_one,
                total(grad_branch), grad_shift_two,
            ]
        ),
    )
    return grad_inputs, grad_kv_w, rows, small


def first_weight_grads(rows, kv_owned, at):
    width = rows.shape[1] // 16
    wide = 4 * width
    context, grad_attended = rows[:, :width], rows[:, width : 2 * width]
    hidden_low = rows[:, 2 * width : 3 * width]
    grad_pre_gelu = rows[:, 3 * width : 3 * width + wide]
    activated = rows[:, 7 * width : 11 * width]
    grad_branch = rows[:, 11 * width : 12 * width]
    first = rows[:, 12 * width : 13 * width]
    grad_queries = rows[:, 13 * width : 14 * width]
    count = kv_owned.shape[0]
    own = lambda values, many: lax.dynamic_slice_in_dim(values, at * many, many, 1)
    return (
        jnp.concatenate([dot_first(own(first, count), grad_queries), kv_owned], axis=1),
        dot_first(own(context, count), grad_attended),
        dot_first(own(hidden_low, count), grad_pre_gelu),
        dot_first(own(activated, 4 * count), grad_branch),
    )


def pack_small(up_b, gains, biases, owners):
    parts = [up_b.reshape(owners, -1)]
    for tensor in (gains, biases):
        parts.append(tensor.reshape(tensor.shape[0], owners, -1).transpose(1, 0, 2).reshape(owners, -1))
    return jnp.concatenate(parts, axis=1)


def unpack_small(packed, width):
    owners = packed.shape[0]
    share = width // owners
    up_b = packed[:, : 4 * share].reshape(4 * width)
    gains = packed[:, 4 * share : 6 * share].reshape(owners, 2, share).transpose(1, 0, 2)
    biases = packed[:, 6 * share :].reshape(owners, 6, share).transpose(1, 0, 2)
    return up_b, gains.reshape(2, width), biases.reshape(6, width)


def gather_kernel(p1, p2, small, w1a, w1b, w2a, w2b, small_out, send_sem, recv_sem):
    y, x, c, z = place()
    greet(y, x, c, z)
    sender = Sender(send_sem)
    subs = [(small, lambda u: small_out.at[u], "x")]
    half = p1.shape[2] // 2
    mid = p2.shape[1] // 2
    for layer, (w1, w2) in enumerate(((w1a, w2a), (w1b, w2b))):
        subs += [
            (p1.at[layer, :, :half], lambda u, w1=w1: w1.at[u, :, :half], "x"),
            (p1.at[layer, :, half:], lambda u, w1=w1: w1.at[u, :, half:], "y"),
            (p2.at[layer, :mid], lambda u, w2=w2: w2.at[u, :mid], "x"),
            (p2.at[layer, mid:], lambda u, w2=w2: w2.at[u, mid:], "y"),
        ]
    for _ in gather_steps(sender, subs, recv_sem):
        pass
    sender.drain()


def gather_weights(p1, p2, small):
    many = 9
    hbm = pl.BlockSpec(memory_space=pl.ANY)
    out = lambda a, rows: jax.ShapeDtypeStruct((32,) + rows, a.dtype)
    return pl.pallas_call(
        gather_kernel,
        out_shape=[out(p1, p1.shape[1:])] * 2 + [out(p2, p2.shape[1:])] * 2 + [out(small, small.shape)],
        in_specs=[hbm] * 3,
        out_specs=[hbm] * 5,
        scratch_shapes=[
            pltpu.SemaphoreType.DMA((many * SENDS_PER_GATHER,)),
            pltpu.SemaphoreType.DMA((many, 32)),
        ],
        compiler_params=pltpu.CompilerParams(collective_id=1, has_side_effects=True),
    )(p1, p2, small)


def reduce_kernel(g1, g2, kv, small, rows, o1, o2, okv, osmall, orows, v1, v2, vkv, vsmall, *rest):
    y, x, c, z = place()
    bufs, (send_sem, recv_sem, gather_sem, load_sem) = rest[:-4], rest[-4:]
    loads = [
        pltpu.make_async_copy(src, dst, load_sem.at[k])
        for k, (src, dst) in enumerate(((g1, v1), (g2, v2), (kv, vkv), (small, vsmall)))
    ]
    for load in loads:
        load.start()
    greet(y, x, c, z)
    for load in loads:
        load.wait()
    sender = Sender(send_sem)
    subs = []

    def add(own, out, dim):
        k = 4 * len(subs)
        subs.append(
            dict(own=own, sib=bufs[k], second=bufs[k + 1], first=bufs[k + 2], chain=bufs[k + 3], out=out, dim=dim)
        )

    half, mid, half_kv = v1.shape[2] // 2, v2.shape[1] // 2, vkv.shape[2] // 2
    add(lambda u: vsmall.at[u], osmall, "x")
    add(lambda u: vkv.at[u, :, :half_kv], okv.at[:, :half_kv], "x")
    add(lambda u: vkv.at[u, :, half_kv:], okv.at[:, half_kv:], "y")
    add(lambda u: v1.at[u, :, :half], o1.at[:, :half], "x")
    add(lambda u: v1.at[u, :, half:], o1.at[:, half:], "y")
    add(lambda u: v2.at[u, :mid], o2.at[:mid], "x")
    add(lambda u: v2.at[u, mid:], o2.at[mid:], "y")
    spread = gather_steps(sender, [(rows, lambda u: orows.at[u], "x")], gather_sem)
    for _ in reduce_steps(sender, subs, recv_sem):
        next(spread, None)
    for _ in spread:
        pass
    sender.drain()


def reduce_grads(g1, g2, kv, small, rows):
    hbm = pl.BlockSpec(memory_space=pl.ANY)
    vmem = pl.BlockSpec(memory_space=pltpu.VMEM)
    half = lambda a: (a.shape[1], a.shape[2] // 2)
    blocks = [(small.shape[1:], small.dtype)]
    blocks += [(half(kv), kv.dtype)] * 2 + [(half(g1), g1.dtype)] * 2
    blocks += [((g2.shape[1] // 2, g2.shape[2]), g2.dtype)] * 2
    scratch = [pltpu.VMEM(a.shape, a.dtype) for a in (g1, g2, kv, small)]
    for shape, dtype in blocks:
        scratch += [pltpu.VMEM((many,) + shape, dtype) for many in (16, 8, 4, 5)]
    return pl.pallas_call(
        reduce_kernel,
        out_shape=[jax.ShapeDtypeStruct(a.shape[1:], jnp.float32) for a in (g1, g2, kv, small)]
        + [jax.ShapeDtypeStruct((32,) + rows.shape, rows.dtype)],
        in_specs=[hbm] * 5,
        out_specs=[vmem] * 4 + [hbm],
        scratch_shapes=scratch
        + [
            pltpu.SemaphoreType.DMA((len(blocks) * SENDS_PER_REDUCE + SENDS_PER_GATHER,)),
            pltpu.SemaphoreType.DMA((len(blocks), 33)),
            pltpu.SemaphoreType.DMA((1, 32)),
            pltpu.SemaphoreType.DMA((4,)),
        ],
        compiler_params=pltpu.CompilerParams(
            collective_id=2, has_side_effects=True, vmem_limit_bytes=63 * 2**20
        ),
    )(g1, g2, kv, small, rows)


def exchange_weights(p1, p2, small, fast):
    if fast:
        w1a, w1b, w2a, w2b, small_all = gather_weights(p1, p2, small)
        return (w1a, w1b), (w2a, w2b), small_all
    both = ("wide", "narrow")
    w1 = lax.all_gather(p1, both, axis=0)
    w2 = lax.all_gather(p2, both, axis=0)
    return (w1[:, 0], w1[:, 1]), (w2[:, 0], w2[:, 1]), lax.all_gather(small, both, axis=0)


def exchange_grads(g1, g2, kv, small, rows, fast):
    if fast:
        return reduce_grads(g1, g2, kv, small, rows)
    both = ("wide", "narrow")
    summed = [
        lax.psum_scatter(a, both, scatter_dimension=0).astype(jnp.float32) for a in (g1, g2, kv, small)
    ]
    return summed + [lax.all_gather(rows, both, axis=0)]


def per_device(
    embeds, skip_tokens, cotangent, lengths, qkv_weight, out_weight, up_weight, down_weight, up_bias,
    norm_gains, biases, qkv_moments, out_moments, up_moments, down_moments, up_bias_moments,
    gain_moments, bias_moments,
):
    params = (qkv_weight, out_weight, up_weight, down_weight, up_bias, norm_gains, biases)
    moments = (
        qkv_moments, out_moments, up_moments, down_moments, up_bias_moments, gain_moments, bias_moments,
    )
    wide_size, narrow_size = lax.axis_size("wide"), lax.axis_size("narrow")
    fast = (wide_size, narrow_size) == (8, 4)
    owners = wide_size * narrow_size
    at = lax.axis_index("wide") * narrow_size + lax.axis_index("narrow")
    span_count = lengths.shape[0]
    row_count, width = embeds.shape
    positions = lax.broadcasted_iota(jnp.int32, (span_count, SPAN), 1)
    key_valid = positions < lengths[:, None]
    row_index = lax.broadcasted_iota(jnp.int32, (1, SPAN, 1), 1)

    p1 = jnp.concatenate([qkv_weight, out_weight, up_weight], axis=2).astype(jnp.bfloat16)
    p2 = down_weight.astype(jnp.bfloat16)
    share = 12 * width // owners
    tiles = -(-2 * share // 1024)
    small_own = jnp.concatenate(
        [up_bias, norm_gains.reshape(2, -1), biases.reshape(2, -1)], axis=1
    ).reshape(-1)
    small_own = jnp.pad(small_own, (0, tiles * 1024 - 2 * share)).reshape(tiles * 8, 128)
    w1, w2, small_all = exchange_weights(p1, p2, small_own, fast)
    small_all = small_all.reshape(owners, -1)[:, : 2 * share].astype(jnp.bfloat16).astype(jnp.float32)

    def layer_weights(layer):
        joined = w1[layer].reshape(width, -1)
        return (
            joined[:, : 3 * width], joined[:, 3 * width : 4 * width], joined[:, 4 * width :],
            w2[layer].reshape(-1, width),
        ) + unpack_small(small_all[:, layer * share : (layer + 1) * share], width)

    backbone, head = layer_weights(0), layer_weights(1)
    backbone_out, saved = first_forward(backbone, embeds, key_valid)
    skip_view = skip_tokens.reshape(span_count, SPAN, width)
    head_in = jnp.where(row_index == 0, backbone_out.astype(jnp.bfloat16)[:, None], skip_view)
    head_in = head_in.reshape(row_count, width)
    head_out, grad_head_in, head_grads = backward_block(
        head, head_in, key_valid, cotangent.astype(jnp.float32)
    )
    grad_view = grad_head_in.reshape(span_count, SPAN, width)
    skip_grad = jnp.where(row_index == 0, 0.0, grad_view).reshape(row_count, width)
    embeds_grad, grad_kv_w, rows, small_first = first_backward(
        backbone, embeds, saved, grad_view[:, 0]
    )
    low = lambda a: a.astype(jnp.bfloat16)
    g1 = jnp.concatenate([low(head_grads[0]), low(head_grads[1]), low(head_grads[2])], axis=1)
    g1 = g1.reshape(owners, width // owners, -1)
    g2 = low(head_grads[3]).reshape(owners, -1, width)
    kv = low(grad_kv_w).reshape(owners, width // owners, -1)
    small_grads = jnp.concatenate(
        [pack_small(*small_first, owners), pack_small(*head_grads[4:], owners)], axis=1
    )
    small_grads = jnp.pad(small_grads, ((0, 0), (0, tiles * 1024 - 2 * share)))
    small_grads = small_grads.reshape(owners, tiles * 8, 128)
    rows_wide = jnp.pad(rows, ((0, 0), (0, 2 * width)))
    own_g1, own_g2, own_kv, own_small, all_rows = exchange_grads(
        g1, g2, kv, small_grads, rows_wide.reshape(16 * span_count // 2, -1), fast
    )
    all_rows = all_rows.reshape(owners * span_count, -1)
    first_grads = first_weight_grads(all_rows, own_kv, at)
    own_small = own_small.reshape(-1)[: 2 * share].reshape(2, share)
    sixth = width // owners
    owned = [
        jnp.stack([first_grads[0], own_g1[:, : 3 * width]]),
        jnp.stack([first_grads[1], own_g1[:, 3 * width : 4 * width]]),
        jnp.stack([first_grads[2], own_g1[:, 4 * width :]]),
        jnp.stack([first_grads[3], own_g2]),
        own_small[:, : 4 * sixth],
        own_small[:, 4 * sixth : 6 * sixth].reshape(2, 2, sixth),
        own_small[:, 6 * sixth :].reshape(2, 6, sixth),
    ]
    new_steps = []
    new_moments = []
    for index in range(7):
        decayed = 1.0 if index < 4 else 0.0
        direction, moment = adam_direction(params[index], moments[index], owned[index], decayed)
        new_steps.append(direction)
        new_moments.append(moment)
    return (head_out.astype(jnp.bfloat16), embeds_grad, skip_grad, *new_steps, *new_moments)


def solution(mesh):
    return jax.shard_map(
        per_device,
        mesh=mesh,
        in_specs=(
            P(("wide", "narrow"), None),
            P(("wide", "narrow"), None),
            P(("wide", "narrow"), None),
            P(("wide", "narrow")),
            P(None, ("wide", "narrow"), None),
            P(None, ("wide", "narrow"), None),
            P(None, ("wide", "narrow"), None),
            P(None, ("wide", "narrow"), None),
            P(None, ("wide", "narrow")),
            P(None, None, ("wide", "narrow")),
            P(None, None, ("wide", "narrow")),
            P(None, None, ("wide", "narrow"), None),
            P(None, None, ("wide", "narrow"), None),
            P(None, None, ("wide", "narrow"), None),
            P(None, None, ("wide", "narrow"), None),
            P(None, None, ("wide", "narrow")),
            P(None, None, None, ("wide", "narrow")),
            P(None, None, None, ("wide", "narrow")),
        ),
        out_specs=(
            P(("wide", "narrow"), None),
            P(("wide", "narrow"), None),
            P(("wide", "narrow"), None),
            P(None, ("wide", "narrow"), None),
            P(None, ("wide", "narrow"), None),
            P(None, ("wide", "narrow"), None),
            P(None, ("wide", "narrow"), None),
            P(None, ("wide", "narrow")),
            P(None, None, ("wide", "narrow")),
            P(None, None, ("wide", "narrow")),
            P(None, None, ("wide", "narrow"), None),
            P(None, None, ("wide", "narrow"), None),
            P(None, None, ("wide", "narrow"), None),
            P(None, None, ("wide", "narrow"), None),
            P(None, None, ("wide", "narrow")),
            P(None, None, None, ("wide", "narrow")),
            P(None, None, None, ("wide", "narrow")),
        ),
        check_vma=False,
    )
```

```python
import math

import jax
import jax.numpy as jnp
from jax import lax
from jax.experimental import pallas as pl
from jax.experimental.pallas import tpu as pltpu
from jax.sharding import PartitionSpec as P

HEADS = 12
SPAN = 128

norm_epsilon = 1e-12
score_scale = 0.125
masked_score = -1000000000.0
beta_first = 0.9
beta_second = 0.999
adam_epsilon = 1e-08
weight_decay = 0.01
first_fix = 1.0 - 0.9**10
second_fix = 1.0 - 0.999**10


def dot_first(left_side, right_side):
    return lax.dot_general(
        left_side, right_side, (((0,), (0,)), ((), ())), preferred_element_type=jnp.float32
    )


def dot_last(left_side, right_side):
    return lax.dot_general(
        left_side, right_side, (((1,), (1,)), ((), ())), preferred_element_type=jnp.float32
    )


def normalize(values, gain_row, shift_row):
    centred = values - jnp.mean(values, axis=-1, keepdims=True)
    inv_scale = lax.rsqrt(jnp.mean(centred * centred, axis=-1, keepdims=True) + norm_epsilon)
    normed = centred * inv_scale
    return (normed * gain_row + shift_row, normed, inv_scale)


def normalize_back(gradient, normed, inv_scale, gain_row):
    grad_gain = jnp.sum(gradient * normed, axis=0)
    grad_shift = jnp.sum(gradient, axis=0)
    scaled = gradient * gain_row
    grad_in = inv_scale * (
        scaled
        - jnp.mean(scaled, axis=-1, keepdims=True)
        - normed * jnp.mean(scaled * normed, axis=-1, keepdims=True)
    )
    return (grad_in, grad_gain, grad_shift)


def head_view(tensor):
    return tensor.reshape(tensor.shape[0] // SPAN, SPAN, HEADS, tensor.shape[1] // HEADS)


def attend_scores(queries, keys_low, key_valid):
    scores = (
        jnp.einsum(
            "bqhe,bkhe->bhqk",
            head_view(queries),
            head_view(keys_low),
            preferred_element_type=jnp.float32,
        )
        * score_scale
    )
    return jnp.where(key_valid[:, None, None, :], scores, masked_score)


def forward_block(weights, inputs, key_valid):
    qkv_w, out_w, up_w, down_w, up_b, gain_rows, biases = weights
    gains_wide = gain_rows.astype(jnp.float32)
    biases_wide = biases.astype(jnp.float32)
    row_count, model_width = inputs.shape
    mixed_in = jnp.dot(inputs, qkv_w, preferred_element_type=jnp.float32)
    queries = (mixed_in[:, :model_width] + biases_wide[0]).astype(jnp.bfloat16)
    keys_low = mixed_in[:, model_width : 2 * model_width].astype(jnp.bfloat16)
    values_low = (mixed_in[:, 2 * model_width :] + biases_wide[1]).astype(jnp.bfloat16)
    scores = attend_scores(queries, keys_low, key_valid)
    row_max = jnp.max(scores, axis=-1, keepdims=True)
    weights_exp = jnp.exp(scores - row_max)
    row_total = jnp.sum(weights_exp, axis=-1, keepdims=True)
    softmax_out = (weights_exp / row_total).astype(jnp.bfloat16)
    log_total = row_max + jnp.log(row_total)
    context = jnp.einsum(
        "bhqk,bkhe->bqhe", softmax_out, head_view(values_low), preferred_element_type=jnp.float32
    )
    context = context.reshape(row_count, model_width).astype(jnp.bfloat16)
    attended = jnp.dot(context, out_w, preferred_element_type=jnp.float32) + biases_wide[2]
    hidden, normed_one, scale_one = normalize(
        inputs.astype(jnp.float32) + attended, gains_wide[0], biases_wide[3]
    )
    hidden_low = hidden.astype(jnp.bfloat16)
    pre_gelu = jnp.dot(hidden_low, up_w, preferred_element_type=jnp.float32) + up_b.astype(
        jnp.float32
    )
    activated = jax.nn.gelu(pre_gelu, approximate=False).astype(jnp.bfloat16)
    branch_out = jnp.dot(activated, down_w, preferred_element_type=jnp.float32) + biases_wide[4]
    output, normed_two, scale_two = normalize(hidden + branch_out, gains_wide[1], biases_wide[5])
    saved = (
        queries,
        keys_low,
        values_low,
        log_total,
        context,
        normed_one,
        scale_one,
        hidden_low,
        pre_gelu,
        activated,
        normed_two,
        scale_two,
    )
    return (output, saved)


def backward_block(weights, inputs, key_valid, grad_out):
    qkv_w, out_w, up_w, down_w, up_b, gain_rows, biases = weights
    gains_wide = gain_rows.astype(jnp.float32)
    row_count, model_width = inputs.shape
    output, saved = forward_block(weights, inputs, key_valid)
    (
        queries,
        keys_low,
        values_low,
        log_total,
        context,
        normed_one,
        scale_one,
        hidden_low,
        pre_gelu,
        activated,
        normed_two,
        scale_two,
    ) = saved
    grad_pre_two, grad_gain_two, grad_shift_two = normalize_back(
        grad_out, normed_two, scale_two, gains_wide[1]
    )
    grad_branch = grad_pre_two.astype(jnp.bfloat16)
    grad_down_w = dot_first(activated, grad_branch)
    grad_act = dot_last(grad_branch, down_w)
    _, gelu_back = jax.vjp(lambda inner: jax.nn.gelu(inner, approximate=False), pre_gelu)
    grad_pre_gelu = gelu_back(grad_act)[0].astype(jnp.bfloat16)
    grad_up_w = dot_first(hidden_low, grad_pre_gelu)
    grad_hidden = grad_pre_two + dot_last(grad_pre_gelu, up_w)
    grad_pre_one, grad_gain_one, grad_shift_one = normalize_back(
        grad_hidden, normed_one, scale_one, gains_wide[0]
    )
    grad_attended = grad_pre_one.astype(jnp.bfloat16)
    grad_out_w = dot_first(context, grad_attended)
    grad_context = head_view(dot_last(grad_attended, out_w).astype(jnp.bfloat16))
    scores = attend_scores(queries, keys_low, key_valid)
    softmax_full = jnp.exp(scores - log_total)
    grad_probs = jnp.einsum(
        "bqhe,bkhe->bhqk", grad_context, head_view(values_low), preferred_element_type=jnp.float32
    )
    grad_values = jnp.einsum(
        "bhqk,bqhe->bkhe",
        softmax_full.astype(jnp.bfloat16),
        grad_context,
        preferred_element_type=jnp.float32,
    )
    grad_values = grad_values.reshape(row_count, model_width).astype(jnp.bfloat16)
    grad_scores = softmax_full * (
        grad_probs - jnp.sum(softmax_full * grad_probs, axis=-1, keepdims=True)
    )
    grad_scores = grad_scores.astype(jnp.bfloat16)
    grad_queries = (
        jnp.einsum(
            "bhqk,bkhe->bqhe", grad_scores, head_view(keys_low), preferred_element_type=jnp.float32
        )
        * score_scale
    )
    grad_queries = grad_queries.reshape(row_count, model_width).astype(jnp.bfloat16)
    grad_keys = (
        jnp.einsum(
            "bhqk,bqhe->bkhe", grad_scores, head_view(queries), preferred_element_type=jnp.float32
        )
        * score_scale
    )
    grad_keys = grad_keys.reshape(row_count, model_width).astype(jnp.bfloat16)
    grad_mixed = jnp.concatenate([grad_queries, grad_keys, grad_values], axis=1)
    grad_qkv_w = dot_first(inputs, grad_mixed)
    grad_inputs = grad_pre_one + dot_last(grad_mixed, qkv_w)
    grad_gains = jnp.stack([grad_gain_one, grad_gain_two])
    grad_biases = jnp.stack(
        [
            jnp.sum(grad_queries, axis=0, dtype=jnp.float32),
            jnp.sum(grad_values, axis=0, dtype=jnp.float32),
            jnp.sum(grad_attended, axis=0, dtype=jnp.float32),
            grad_shift_one,
            jnp.sum(grad_branch, axis=0, dtype=jnp.float32),
            grad_shift_two,
        ]
    )
    grads = (
        grad_qkv_w,
        grad_out_w,
        grad_up_w,
        grad_down_w,
        jnp.sum(grad_pre_gelu, axis=0, dtype=jnp.float32),
        grad_gains,
        grad_biases,
    )
    return (output, grad_inputs, grads)


MESH = pl.DeviceIdType.MESH


def place():
    wide = lax.axis_index("wide")
    z = lax.axis_index("narrow")
    return wide // 4, (wide // 2) % 2, wide % 2, z


def device(y, x, c, z):
    return ((y * 2 + x) * 2 + c, z)


def flat(y, x, c, z):
    return ((y * 2 + x) * 2 + c) * 4 + z


def near(z, k):
    if k == 0:
        return z
    if k == 1:
        return z + 1 - 2 * (z % 2)
    if k == 2:
        return (z + 2) % 4
    return 3 - z


def greet(y, x, c, z):
    barrier = pltpu.get_barrier_semaphore()
    for there in (device(y, 1 - x, c, z), device(1 - y, x, c, z), device(y, x, 1 - c, z)):
        pl.semaphore_signal(barrier, inc=1, device_id=there, device_id_type=MESH)

    @pl.when(z < 3)
    def _():
        pl.semaphore_signal(barrier, inc=1, device_id=device(y, x, c, z + 1), device_id_type=MESH)

    @pl.when(z > 0)
    def _():
        pl.semaphore_signal(barrier, inc=1, device_id=device(y, x, c, z - 1), device_id_type=MESH)

    pl.semaphore_wait(barrier, 4 + ((z + 1) // 2) % 2)


def run_if(pred, action):
    if pred is None:
        action()
    else:
        pl.when(pred)(action)


class Sender:
    def __init__(self, send_sem):
        self.send_sem = send_sem
        self.count = 0
        self.pending = []

    def send(self, src, dst, recv, there, pred=None):
        copy = pltpu.make_async_remote_copy(
            src_ref=src,
            dst_ref=dst,
            send_sem=self.send_sem.at[self.count],
            recv_sem=recv,
            device_id=there,
            device_id_type=MESH,
        )
        self.count += 1
        run_if(pred, copy.start)
        self.pending.append((pred, copy))

    def local(self, src, dst):
        copy = pltpu.make_async_copy(src, dst, self.send_sem.at[self.count])
        self.count += 1
        copy.start()
        return copy

    def drain(self):
        for pred, copy in self.pending:
            run_if(pred, copy.wait_send)
        self.pending = []


def arrived(dst, recv, me, pred=None):
    def wait():
        pltpu.make_async_remote_copy(
            src_ref=dst, dst_ref=dst, send_sem=recv, recv_sem=recv, device_id=me, device_id_type=MESH
        ).wait_recv()

    run_if(pred, wait)


def gather_steps(sender, subs, recv_sem, base=0):
    y, x, c, z = place()
    sib = device(y, x, 1 - c, z)
    xn = device(y, 1 - x, c, z)
    yn = device(1 - y, x, c, z)

    def there(sub, stage):
        return (xn if stage == 1 else yn) if sub[2] == "x" else (yn if stage == 1 else xn)

    def unit(sub, far1, far2, zz, core):
        fx, fy = (far1, far2) if sub[2] == "x" else (far2, far1)
        return flat(1 - y if fy else y, 1 - x if fx else x, core, zz)

    def push(i, sub, src, slab_at, target, pred=None):
        sender.send(src, sub[1](slab_at), recv_sem.at[base + i, slab_at], target, pred)

    mine = flat(y, x, c, z)
    locals_ = []
    for i, sub in enumerate(subs):
        own = sub[0]
        push(i, sub, own, mine, device(y, x, c, z + 1), z < 3)
        push(i, sub, own, mine, device(y, x, c, z - 1), z > 0)
        push(i, sub, own, mine, there(sub, 1))
        push(i, sub, own, mine, there(sub, 2))
        push(i, sub, own, mine, sib)
        locals_.append(sender.local(own, sub[1](mine)))
    yield

    def from_z(dist):
        for i, sub in enumerate(subs):
            for up in (True, False):
                zz = z - dist if up else z + dist
                have = (z >= dist) if up else (z <= 3 - dist)
                at = flat(y, x, c, zz)

                @pl.when(have)
                def _(i=i, sub=sub, up=up, at=at):
                    arrived(sub[1](at), recv_sem.at[base + i, at], device(y, x, c, z))

                if dist < 3:
                    if up:
                        push(i, sub, sub[1](at), at, device(y, x, c, z + 1), (z >= dist) & (z < 3))
                    else:
                        push(i, sub, sub[1](at), at, device(y, x, c, z - 1), (z <= 3 - dist) & (z > 0))
                push(i, sub, sub[1](at), at, there(sub, 1), have)
                push(i, sub, sub[1](at), at, there(sub, 2), have)
                push(i, sub, sub[1](at), at, sib, have)

    def from_first(k):
        for i, sub in enumerate(subs):
            at = unit(sub, True, False, near(z, k), c)
            arrived(sub[1](at), recv_sem.at[base + i, at], device(y, x, c, z))
            push(i, sub, sub[1](at), at, there(sub, 2))
            push(i, sub, sub[1](at), at, sib)

    def from_second(far, k):
        for i, sub in enumerate(subs):
            at = unit(sub, far, True, near(z, k), c)
            arrived(sub[1](at), recv_sem.at[base + i, at], device(y, x, c, z))
            push(i, sub, sub[1](at), at, sib)

    from_z(1)
    yield
    from_first(0)
    yield
    from_z(2)
    yield
    from_first(1)
    yield
    from_z(3)
    yield
    from_first(2)
    from_first(3)
    yield
    for far in (False, True):
        for k in range(4):
            from_second(far, k)
            yield
    for i, sub in enumerate(subs):
        for a in range(2):
            for b in range(2):
                for k in range(4):
                    at = unit(sub, a == 1, b == 1, near(z, k), 1 - c)
                    arrived(sub[1](at), recv_sem.at[base + i, at], device(y, x, c, z))
    for copy in locals_:
        copy.wait()


SENDS_PER_GATHER = 6 + 2 * 4 + 2 * 4 + 2 * 3 + 4 * 2 + 8

def reduce_steps(sender, subs, recv_sem, base=0):
    y, x, c, z = place()
    me = device(y, x, c, z)
    sib = device(y, x, 1 - c, z)
    xn = device(y, 1 - x, c, z)
    yn = device(1 - y, x, c, z)
    targets = (0, 3, 1, 2)

    def chip(sub, far1, far2):
        fx, fy = (far1, far2) if sub["dim"] == "x" else (far2, far1)
        return (1 - y if fy else y), (1 - x if fx else x)

    def own(sub, far1, far2, zz, core):
        cy, cx = chip(sub, far1, far2)
        return sub["own"](flat(cy, cx, core, zz))

    def sib_slot(sub, far1, far2, zz):
        cy, cx = chip(sub, far1, far2)
        return (cy * 2 + cx) * 4 + zz

    def first_of(sub):
        return xn if sub["dim"] == "x" else yn

    def second_of(sub):
        return yn if sub["dim"] == "x" else xn

    def coord1(sub, far):
        here = x if sub["dim"] == "x" else y
        return 1 - here if far else here

    kinds = ((False, True), (True, True), (True, False), (False, False))

    def start_sib(zz):
        for i, sub in enumerate(subs):
            for far1, far2 in kinds:
                slot = sib_slot(sub, far1, far2, zz)
                sender.send(
                    own(sub, far1, far2, zz, 1 - c),
                    sub["sib"].at[slot],
                    recv_sem.at[base + i, slot],
                    sib,
                )

    def take(sub, i, kind, slot):
        buf = sub[kind].at[slot]
        at = {"sib": 0, "second": 16, "first": 24, "chain": 28}[kind] + slot
        arrived(buf, recv_sem.at[base + i, at], me)
        return buf

    def add_into(sub, dst, parts):
        total = dst[...].astype(jnp.float32)
        for part in parts:
            total = total + part[...].astype(jnp.float32)
        dst[...] = total.astype(dst.dtype)

    def step_a(zz):
        for i, sub in enumerate(subs):
            for far1 in (False, True):
                acc = own(sub, far1, True, zz, c)
                add_into(sub, acc, [take(sub, i, "sib", sib_slot(sub, far1, True, zz))])
                slot = coord1(sub, far1) * 4 + zz
                sender.send(acc, sub["second"].at[slot], recv_sem.at[base + i, 16 + slot], second_of(sub))

    def step_b(zz):
        for i, sub in enumerate(subs):
            acc = own(sub, True, False, zz, c)
            parts = [
                take(sub, i, "sib", sib_slot(sub, True, False, zz)),
                take(sub, i, "second", coord1(sub, True) * 4 + zz),
            ]
            add_into(sub, acc, parts)
            sender.send(acc, sub["first"].at[zz], recv_sem.at[base + i, 24 + zz], first_of(sub))

    def chain_send(sub, i, acc, zz, up, pred):
        slot = zz if up else jnp.where(z - 1 == zz, 4, zz)
        there = device(y, x, c, z + 1) if up else device(y, x, c, z - 1)
        sender.send(acc, sub["chain"].at[slot], recv_sem.at[base + i, 28 + slot], there, pred)

    def step_c(zz):
        for i, sub in enumerate(subs):
            acc = own(sub, False, False, zz, c)
            parts = [
                take(sub, i, "sib", sib_slot(sub, False, False, zz)),
                take(sub, i, "second", coord1(sub, False) * 4 + zz),
                take(sub, i, "first", zz),
            ]
            add_into(sub, acc, parts)
            if zz > 0:
                chain_send(sub, i, acc, zz, True, z == 0)
            if zz < 3:
                chain_send(sub, i, acc, zz, False, z == 3)

    def step_d(zz):
        for i, sub in enumerate(subs):
            acc = own(sub, False, False, zz, c)
            for up in (True, False):
                pred = (z > 0) & (z < zz) if up else (z < 3) & (z > zz)

                @pl.when(pred)
                def _(i=i, sub=sub, acc=acc):
                    add_into(sub, acc, [take(sub, i, "chain", zz)])

                chain_send(sub, i, acc, zz, up, pred)

    def step_f():
        for i, sub in enumerate(subs):
            total = own(sub, False, False, z, c)[...].astype(jnp.float32)
            sub["out"][...] = total

            @pl.when(z > 0)
            def _(i=i, sub=sub):
                sub["out"][...] += take(sub, i, "chain", z)[...].astype(jnp.float32)

            @pl.when(z < 3)
            def _(i=i, sub=sub):
                sub["out"][...] += take(sub, i, "chain", 4)[...].astype(jnp.float32)

    t0, t1, t2, t3 = targets
    for zz in targets:
        start_sib(zz)
    yield
    for action, zz in (
        (step_a, t0), (step_a, t1), (step_b, t0), (step_a, t2), (step_b, t1), (step_c, t0), (step_a, t3),
        (step_b, t2), (step_d, t0), (step_c, t1), (step_b, t3), (step_d, t1), (step_c, t2), (step_d, t2),
        (step_c, t3), (step_d, t3),
    ):
        action(zz)
        yield
    step_f()


SENDS_PER_REDUCE = 16 + 8 + 4 + 12 + 12

def erf_of(v):
    return lax.erf(v)


def mm(a, b):
    return jnp.dot(a, b, preferred_element_type=jnp.float32)


def mm_nt(a, b):
    return lax.dot_general(a, b, (((1,), (1,)), ((), ())), preferred_element_type=jnp.float32)


def mm_tn(a, b):
    return lax.dot_general(a, b, (((0,), (0,)), ((), ())), preferred_element_type=jnp.float32)


def columns(ref, start, stop):
    block = ref[:, :, start:stop]
    return block.reshape(block.shape[0] * block.shape[1], stop - start)


def rows_of(ref, start, stop):
    block = ref[start:stop]
    return block.reshape(block.shape[0] * block.shape[1], block.shape[2])


def put_columns(ref, start, values):
    owners, share = ref.shape[0], ref.shape[1]
    ref[:, :, start : start + values.shape[1]] = values.astype(ref.dtype).reshape(
        owners, share, values.shape[1]
    )


def norm_rows(values):
    centred = values - jnp.mean(values, axis=-1, keepdims=True)
    inv_scale = lax.rsqrt(jnp.mean(centred * centred, axis=-1, keepdims=True) + norm_epsilon)
    return centred * inv_scale, inv_scale


def norm_rows_back(gradient, normed, inv_scale, gain_row):
    scaled = gradient * gain_row
    return inv_scale * (
        scaled
        - jnp.mean(scaled, axis=-1, keepdims=True)
        - normed * jnp.mean(scaled * normed, axis=-1, keepdims=True)
    )


def column_sum(values):
    return jnp.sum(values.astype(jnp.float32), axis=0, keepdims=True)


def head_forward(s, w1, w2, small, valid):
    width = s["x"].shape[1]
    spans = s["x"].shape[0] // SPAN
    x = s["x"][...]
    s["q"][...] = (mm(x, columns(w1, 0, width)) + small(6)).astype(jnp.bfloat16)
    s["k"][...] = mm(x, columns(w1, width, 2 * width)).astype(jnp.bfloat16)
    s["v"][...] = (mm(x, columns(w1, 2 * width, 3 * width)) + small(7)).astype(jnp.bfloat16)
    yield
    lane = lax.broadcasted_iota(jnp.int32, (SPAN, 128), 1)
    for span in range(spans):
        keep = valid[span : span + 1, :] > 0.5
        for pair in range(width // 128):
            at = (slice(span * SPAN, (span + 1) * SPAN), slice(pair * 128, (pair + 1) * 128))
            q, k, v = s["q"][at], s["k"][at], s["v"][at]
            parts = []
            for side in range(2):
                here = (lane < 64) if side == 0 else (lane >= 64)
                scores = mm_nt(jnp.where(here, q, jnp.zeros_like(q)), k) * score_scale
                scores = jnp.where(keep, scores, masked_score)
                weight = jnp.exp(scores - jnp.max(scores, axis=-1, keepdims=True))
                probs = weight / jnp.sum(weight, axis=-1, keepdims=True)
                s["p"][(span * 6 + pair) * 2 + side] = probs
                parts.append(mm(probs.astype(jnp.bfloat16), v))
            s["ctx"][at] = jnp.where(lane < 64, parts[0], parts[1]).astype(jnp.bfloat16)
        yield
    attended = mm(s["ctx"][...], columns(w1, 3 * width, 4 * width)) + small(8)
    normed, inv_scale = norm_rows(s["x"][...].astype(jnp.float32) + attended)
    s["n1"][...] = normed
    s["r1"][...] = inv_scale
    hidden = normed * small(4) + small(9)
    s["h"][...] = hidden
    s["hl"][...] = hidden.astype(jnp.bfloat16)
    yield
    for part in range(4):
        cut = slice(part * width, (part + 1) * width)
        pre = mm(s["hl"][...], columns(w1, (4 + part) * width, (5 + part) * width)) + small(part)
        half_erf = 0.5 + 0.5 * erf_of(pre * (0.5**0.5))
        s["g"][:, cut] = (pre * half_erf).astype(jnp.bfloat16)
        s["gp"][:, cut] = half_erf + pre * (jnp.exp(-0.5 * pre * pre) * (0.5 / math.pi) ** 0.5)
        yield
    branch = mm(s["g"][...], rows_of(w2, 0, w2.shape[0])) + small(10)
    normed, inv_scale = norm_rows(s["h"][...] + branch)
    s["n2"][...] = normed
    s["r2"][...] = inv_scale
    s["y"][...] = (normed * small(5) + small(11)).astype(jnp.bfloat16)
    yield


def head_backward(s, w1, w2, g1, g2, small, sums, grad_in):
    width = s["x"].shape[1]
    spans = s["x"].shape[0] // SPAN
    grad_out = s["cot"][...].astype(jnp.float32)
    sums[5:6] = column_sum(grad_out * s["n2"][...])
    sums[11:12] = column_sum(grad_out)
    pre_two = norm_rows_back(grad_out, s["n2"][...], s["r2"][...], small(5))
    s["h"][...] = pre_two
    branch = pre_two.astype(jnp.bfloat16)
    s["dz"][...] = branch
    sums[10:11] = column_sum(branch)
    yield
    owners = w2.shape[0]
    share = owners // 4
    for part in range(4):
        cut = slice(part * width, (part + 1) * width)
        own = slice(part * share, (part + 1) * share)
        grad_act = mm_nt(s["dz"][...], rows_of(w2, part * share, (part + 1) * share))
        grad_pre = (grad_act * s["gp"][:, cut]).astype(jnp.bfloat16)
        g2[own] = (
            mm_tn(s["g"][:, cut], s["dz"][...]).astype(jnp.bfloat16).reshape(share, g2.shape[1], width)
        )
        s["g"][:, cut] = grad_pre
        sums[part : part + 1] = column_sum(grad_pre)
        yield
    grad_hidden = s["h"][...]
    for part in range(4):
        cut = slice(part * width, (part + 1) * width)
        at = (4 + part) * width
        grad_pre = s["g"][:, cut]
        grad_hidden = grad_hidden + mm_nt(grad_pre, columns(w1, at, at + width))
        put_columns(g1, at, mm_tn(s["hl"][...], grad_pre))
    sums[4:5] = column_sum(grad_hidden * s["n1"][...])
    sums[9:10] = column_sum(grad_hidden)
    pre_one = norm_rows_back(grad_hidden, s["n1"][...], s["r1"][...], small(4))
    s["h"][...] = pre_one
    attended = pre_one.astype(jnp.bfloat16)
    s["da"][...] = attended
    sums[8:9] = column_sum(attended)
    yield
    s["dc"][...] = mm_nt(attended, columns(w1, 3 * width, 4 * width)).astype(jnp.bfloat16)
    put_columns(g1, 3 * width, mm_tn(s["ctx"][...], attended))
    yield
    lane = lax.broadcasted_iota(jnp.int32, (SPAN, 128), 1)
    for span in range(spans):
        for pair in range(width // 128):
            at = (slice(span * SPAN, (span + 1) * SPAN), slice(pair * 128, (pair + 1) * 128))
            q, k, v, dc = s["q"][at], s["k"][at], s["v"][at], s["dc"][at]
            dq, dk, dv = [], [], []
            for side in range(2):
                here = (lane < 64) if side == 0 else (lane >= 64)
                probs = s["p"][(span * 6 + pair) * 2 + side]
                grad_probs = mm_nt(jnp.where(here, dc, jnp.zeros_like(dc)), v)
                dv.append(mm_tn(probs.astype(jnp.bfloat16), dc))
                grad_scores = probs * (
                    grad_probs - jnp.sum(probs * grad_probs, axis=-1, keepdims=True)
                )
                grad_scores = grad_scores.astype(jnp.bfloat16)
                dq.append(mm(grad_scores, k))
                dk.append(mm_tn(grad_scores, q))
            join = lambda two: jnp.where(lane < 64, two[0], two[1])
            s["q"][at] = (join(dq) * score_scale).astype(jnp.bfloat16)
            s["k"][at] = (join(dk) * score_scale).astype(jnp.bfloat16)
            s["v"][at] = join(dv).astype(jnp.bfloat16)
        yield
    sums[6:7] = column_sum(s["q"][...])
    sums[7:8] = column_sum(s["v"][...])
    total = s["h"][...]
    for k, name in enumerate(("q", "k", "v")):
        total = total + mm_nt(s[name][...], columns(w1, k * width, (k + 1) * width))
    grad_in[...] = total
    yield
    for k, name in enumerate(("q", "k", "v")):
        put_columns(g1, k * width, mm_tn(s["x"][...], s[name][...]))
    yield


HEAD_SCRATCH = (
    ("x", 1, jnp.bfloat16), ("q", 1, jnp.bfloat16), ("k", 1, jnp.bfloat16), ("v", 1, jnp.bfloat16),
    ("ctx", 1, jnp.bfloat16), ("n1", 1, jnp.float32), ("h", 1, jnp.float32), ("hl", 1, jnp.bfloat16),
    ("g", 4, jnp.bfloat16), ("gp", 4, jnp.float32), ("n2", 1, jnp.float32), ("dz", 1, jnp.bfloat16),
    ("da", 1, jnp.bfloat16), ("dc", 1, jnp.bfloat16),
)

def head_kernel(x, cot, valid, small, w1_in, w2_in, y, g1_out, g2_out, sums, grad_in, *scratch):
    names = [name for name, _, _ in HEAD_SCRATCH if name != "x"]
    s = dict(zip(names, scratch))
    s["p"], s["r1"], s["r2"], w1, w2, sem = scratch[len(names) :]
    s["x"], s["cot"], s["y"] = x, cot, y
    copies = [pltpu.make_async_copy(w1_in, w1, sem.at[0]), pltpu.make_async_copy(w2_in, w2, sem.at[1])]
    for copy in copies:
        copy.start()
    for copy in copies:
        copy.wait()
    row = lambda k: small[k : k + 1]
    for _ in head_forward(s, w1, w2, row, valid):
        pass
    for _ in head_backward(s, w1, w2, w1, w2, row, sums, grad_in):
        pass
    copies = [pltpu.make_async_copy(w1, g1_out, sem.at[0]), pltpu.make_async_copy(w2, g2_out, sem.at[1])]
    for copy in copies:
        copy.start()
    for copy in copies:
        copy.wait()


def head_call(x, cot, valid, small, w1, w2):
    vmem, hbm = pl.BlockSpec(memory_space=pltpu.VMEM), pl.BlockSpec(memory_space=pl.ANY)
    rows, width = x.shape
    scratch = [
        pltpu.VMEM((rows, many * width), dtype) for name, many, dtype in HEAD_SCRATCH if name != "x"
    ]
    scratch += [
        pltpu.VMEM((rows // SPAN * HEADS, SPAN, SPAN), jnp.float32),
        pltpu.VMEM((rows, 1), jnp.float32),
        pltpu.VMEM((rows, 1), jnp.float32),
        pltpu.VMEM(w1.shape, w1.dtype),
        pltpu.VMEM(w2.shape, w2.dtype),
        pltpu.SemaphoreType.DMA((2,)),
    ]
    shape = lambda a, dtype: jax.ShapeDtypeStruct(a.shape, dtype)
    return pl.pallas_call(
        head_kernel,
        out_shape=[
            shape(x, jnp.bfloat16), shape(w1, w1.dtype), shape(w2, w2.dtype), shape(small, jnp.float32),
            shape(x, jnp.float32),
        ],
        in_specs=[vmem] * 4 + [hbm] * 2,
        out_specs=[vmem, hbm, hbm, vmem, vmem],
        scratch_shapes=scratch,
        compiler_params=pltpu.CompilerParams(vmem_limit_bytes=60 * 2**20),
    )(x, cot, valid, small, w1, w2)

def adam_parts(parameter, first, second, gradient, decayed):
    first = beta_first * first + (1.0 - beta_first) * gradient
    second = beta_second * second + (1.0 - beta_second) * gradient * gradient
    update = first / first_fix / (jnp.sqrt(second / second_fix) + adam_epsilon)
    if decayed:
        update = update + weight_decay * parameter
    return update, first, second


def adam_kernel(*refs):
    params, moments, grads, steps, news = (refs[7 * k : 7 * k + 7] for k in range(5))

    def update(index):
        step, first, second = adam_parts(
            params[index][...], moments[index][0], moments[index][1], grads[index][...], index < 4
        )
        steps[index][...] = step
        news[index][0] = first
        news[index][1] = second

    for index in range(4):
        update(index)

    @pl.when((pl.program_id(0) == 0) & (pl.program_id(1) == 0))
    def _():
        for index in range(4, 7):
            update(index)


def adam_update(params, moments, joined, down, small):
    cuts = 3 if params[0].shape[1] % 24 == 0 else 1

    def whole(a):
        return pl.BlockSpec(a.shape, lambda l, r, n=a.ndim: (0,) * n)

    def rows(a, columns=None, at=0):
        columns = a.shape[2] if columns is None else columns
        return pl.BlockSpec((1, a.shape[1] // cuts, columns), lambda l, r: (l, r, at))

    def pairs(a):
        return pl.BlockSpec((2, 1, a.shape[2] // cuts, a.shape[3]), lambda l, r: (0, l, r, 0))

    qkv, out, up = (params[k].shape[2] for k in range(3))
    grads = [joined, joined, joined, down, *small]
    grad_specs = [
        rows(joined, qkv, 0), rows(joined, out, qkv // out), rows(joined, up, (qkv + out) // up), rows(down),
        *(whole(a) for a in small),
    ]
    param_specs = [rows(a) for a in params[:4]] + [whole(a) for a in params[4:]]
    moment_specs = [pairs(a) for a in moments[:4]] + [whole(a) for a in moments[4:]]
    shape = lambda a: jax.ShapeDtypeStruct(a.shape, a.dtype)
    out = pl.pallas_call(
        adam_kernel,
        grid=(2, cuts),
        out_shape=[shape(a) for a in params] + [shape(a) for a in moments],
        in_specs=param_specs + moment_specs + grad_specs,
        out_specs=param_specs + moment_specs,
        compiler_params=pltpu.CompilerParams(vmem_limit_bytes=48 * 2**20),
    )(*params, *moments, *grads)
    return out[:7], out[7:]

def first_forward(weights, inputs, key_valid):
    qkv_w, out_w, up_w, down_w, up_b, gain_rows, biases = weights
    row_count, width = inputs.shape
    span_count = row_count // SPAN
    first = inputs.reshape(span_count, SPAN, width)[:, 0]
    mixed = jnp.dot(inputs, qkv_w[:, width:], preferred_element_type=jnp.float32)
    keys = mixed[:, :width].astype(jnp.bfloat16).reshape(span_count, SPAN, HEADS, width // HEADS)
    values = (mixed[:, width:] + biases[1]).astype(jnp.bfloat16)
    values = values.reshape(span_count, SPAN, HEADS, width // HEADS)
    queries = jnp.dot(first, qkv_w[:, :width], preferred_element_type=jnp.float32) + biases[0]
    queries = queries.astype(jnp.bfloat16).reshape(span_count, HEADS, width // HEADS)
    scores = (
        jnp.einsum("bhe,bkhe->bhk", queries, keys, preferred_element_type=jnp.float32) * score_scale
    )
    scores = jnp.where(key_valid[:, None, :], scores, masked_score)
    probs = jax.nn.softmax(scores, axis=-1)
    context = jnp.einsum(
        "bhk,bkhe->bhe", probs.astype(jnp.bfloat16), values, preferred_element_type=jnp.float32
    )
    context = context.reshape(span_count, width).astype(jnp.bfloat16)
    attended = jnp.dot(context, out_w, preferred_element_type=jnp.float32) + biases[2]
    hidden, normed_one, scale_one = normalize(
        first.astype(jnp.float32) + attended, gain_rows[0], biases[3]
    )
    hidden_low = hidden.astype(jnp.bfloat16)
    pre_gelu = jnp.dot(hidden_low, up_w, preferred_element_type=jnp.float32) + up_b
    activated = jax.nn.gelu(pre_gelu, approximate=False).astype(jnp.bfloat16)
    branch_out = jnp.dot(activated, down_w, preferred_element_type=jnp.float32) + biases[4]
    output, normed_two, scale_two = normalize(hidden + branch_out, gain_rows[1], biases[5])
    saved = (
        first, queries, keys, values, probs, context, normed_one, scale_one, hidden_low, pre_gelu,
        activated, normed_two, scale_two,
    )
    return output, saved


def first_backward(weights, inputs, saved, grad_out):
    qkv_w, out_w, up_w, down_w, up_b, gain_rows, biases = weights
    (
        first, queries, keys, values, probs, context, normed_one, scale_one, hidden_low, pre_gelu,
        activated, normed_two, scale_two,
    ) = saved
    row_count, width = inputs.shape
    span_count = row_count // SPAN
    grad_pre_two, grad_gain_two, grad_shift_two = normalize_back(
        grad_out, normed_two, scale_two, gain_rows[1]
    )
    grad_branch = grad_pre_two.astype(jnp.bfloat16)
    grad_act = dot_last(grad_branch, down_w)
    _, gelu_back = jax.vjp(lambda inner: jax.nn.gelu(inner, approximate=False), pre_gelu)
    grad_pre_gelu = gelu_back(grad_act)[0].astype(jnp.bfloat16)
    grad_hidden = grad_pre_two + dot_last(grad_pre_gelu, up_w)
    grad_pre_one, grad_gain_one, grad_shift_one = normalize_back(
        grad_hidden, normed_one, scale_one, gain_rows[0]
    )
    grad_attended = grad_pre_one.astype(jnp.bfloat16)
    grad_context = dot_last(grad_attended, out_w).astype(jnp.bfloat16)
    grad_context = grad_context.reshape(span_count, HEADS, width // HEADS)
    grad_probs = jnp.einsum(
        "bhe,bkhe->bhk", grad_context, values, preferred_element_type=jnp.float32
    )
    grad_values = jnp.einsum("bhk,bhe->bkhe", probs.astype(jnp.bfloat16), grad_context)
    grad_values = grad_values.reshape(row_count, width).astype(jnp.bfloat16)
    grad_scores = probs * (grad_probs - jnp.sum(probs * grad_probs, axis=-1, keepdims=True))
    grad_scores = grad_scores.astype(jnp.bfloat16)
    grad_queries = (
        jnp.einsum("bhk,bkhe->bhe", grad_scores, keys, preferred_element_type=jnp.float32)
        * score_scale
    )
    grad_queries = grad_queries.reshape(span_count, width).astype(jnp.bfloat16)
    grad_keys = (
        jnp.einsum("bhk,bhe->bkhe", grad_scores, queries, preferred_element_type=jnp.float32)
        * score_scale
    )
    grad_keys = grad_keys.reshape(row_count, width).astype(jnp.bfloat16)
    grad_kv = jnp.concatenate([grad_keys, grad_values], axis=1)
    grad_kv_w = dot_first(inputs, grad_kv)
    grad_inputs = dot_last(grad_kv, qkv_w[:, width:])
    grad_first = grad_pre_one + dot_last(grad_queries, qkv_w[:, :width])
    placed = jnp.pad(grad_first[:, None], ((0, 0), (0, SPAN - 1), (0, 0))).reshape(row_count, width)
    grad_inputs = grad_inputs + placed
    rows = jnp.concatenate(
        [context, grad_attended, hidden_low, grad_pre_gelu, activated, grad_branch, first, grad_queries],
        axis=1,
    )

    def total(values):
        return jnp.sum(values, axis=0, dtype=jnp.float32)

    small = (
        total(grad_pre_gelu),
        jnp.stack([grad_gain_one, grad_gain_two]),
        jnp.stack(
            [
                total(grad_queries), total(grad_values), total(grad_attended), grad_shift_one,
                total(grad_branch), grad_shift_two,
            ]
        ),
    )
    return grad_inputs, grad_kv_w, rows, small


def first_weight_grads(rows, kv_owned, at):
    width = rows.shape[1] // 16
    wide = 4 * width
    context, grad_attended = rows[:, :width], rows[:, width : 2 * width]
    hidden_low = rows[:, 2 * width : 3 * width]
    grad_pre_gelu = rows[:, 3 * width : 3 * width + wide]
    activated = rows[:, 7 * width : 11 * width]
    grad_branch = rows[:, 11 * width : 12 * width]
    first = rows[:, 12 * width : 13 * width]
    grad_queries = rows[:, 13 * width : 14 * width]
    count = kv_owned.shape[0]
    own = lambda values, many: lax.dynamic_slice_in_dim(values, at * many, many, 1)
    return (
        jnp.concatenate([dot_first(own(first, count), grad_queries), kv_owned], axis=1),
        dot_first(own(context, count), grad_attended),
        dot_first(own(hidden_low, count), grad_pre_gelu),
        dot_first(own(activated, 4 * count), grad_branch),
    )


def pack_small(up_b, gains, biases, owners):
    parts = [up_b.reshape(owners, -1)]
    for tensor in (gains, biases):
        parts.append(tensor.reshape(tensor.shape[0], owners, -1).transpose(1, 0, 2).reshape(owners, -1))
    return jnp.concatenate(parts, axis=1)


def unpack_small(packed, width):
    owners = packed.shape[0]
    share = width // owners
    up_b = packed[:, : 4 * share].reshape(4 * width)
    gains = packed[:, 4 * share : 6 * share].reshape(owners, 2, share).transpose(1, 0, 2)
    biases = packed[:, 6 * share :].reshape(owners, 6, share).transpose(1, 0, 2)
    return up_b, gains.reshape(2, width), biases.reshape(6, width)


def gather_kernel(p1, p2, small, w1a, w1b, w2a, w2b, small_out, send_sem, recv_sem):
    y, x, c, z = place()
    greet(y, x, c, z)
    sender = Sender(send_sem)
    subs = [(small, lambda u: small_out.at[u], "x")]
    half = p1.shape[2] // 2
    mid = p2.shape[1] // 2
    for layer, (w1, w2) in enumerate(((w1a, w2a), (w1b, w2b))):
        subs += [
            (p1.at[layer, :, :half], lambda u, w1=w1: w1.at[u, :, :half], "x"),
            (p1.at[layer, :, half:], lambda u, w1=w1: w1.at[u, :, half:], "y"),
            (p2.at[layer, :mid], lambda u, w2=w2: w2.at[u, :mid], "x"),
            (p2.at[layer, mid:], lambda u, w2=w2: w2.at[u, mid:], "y"),
        ]
    for _ in gather_steps(sender, subs, recv_sem):
        pass
    sender.drain()


def gather_weights(p1, p2, small):
    many = 9
    hbm = pl.BlockSpec(memory_space=pl.ANY)
    out = lambda a, rows: jax.ShapeDtypeStruct((32,) + rows, a.dtype)
    return pl.pallas_call(
        gather_kernel,
        out_shape=[out(p1, p1.shape[1:])] * 2 + [out(p2, p2.shape[1:])] * 2 + [out(small, small.shape)],
        in_specs=[hbm] * 3,
        out_specs=[hbm] * 5,
        scratch_shapes=[
            pltpu.SemaphoreType.DMA((many * SENDS_PER_GATHER,)),
            pltpu.SemaphoreType.DMA((many, 32)),
        ],
        compiler_params=pltpu.CompilerParams(collective_id=1, has_side_effects=True),
    )(p1, p2, small)


def reduce_kernel(g1, g2, kv, small, rows, o1, o2, okv, osmall, orows, v1, v2, vkv, vsmall, *rest):
    y, x, c, z = place()
    bufs, (send_sem, recv_sem, gather_sem, load_sem) = rest[:-4], rest[-4:]
    loads = [
        pltpu.make_async_copy(src, dst, load_sem.at[k])
        for k, (src, dst) in enumerate(((g1, v1), (g2, v2), (kv, vkv), (small, vsmall)))
    ]
    for load in loads:
        load.start()
    greet(y, x, c, z)
    for load in loads:
        load.wait()
    sender = Sender(send_sem)
    subs = []

    def add(own, out, dim):
        k = 4 * len(subs)
        subs.append(
            dict(own=own, sib=bufs[k], second=bufs[k + 1], first=bufs[k + 2], chain=bufs[k + 3], out=out, dim=dim)
        )

    half, mid, half_kv = v1.shape[2] // 2, v2.shape[1] // 2, vkv.shape[2] // 2
    add(lambda u: vsmall.at[u], osmall, "x")
    add(lambda u: vkv.at[u, :, :half_kv], okv.at[:, :half_kv], "x")
    add(lambda u: vkv.at[u, :, half_kv:], okv.at[:, half_kv:], "y")
    add(lambda u: v1.at[u, :, :half], o1.at[:, :half], "x")
    add(lambda u: v1.at[u, :, half:], o1.at[:, half:], "y")
    add(lambda u: v2.at[u, :mid], o2.at[:mid], "x")
    add(lambda u: v2.at[u, mid:], o2.at[mid:], "y")
    spread = gather_steps(sender, [(rows, lambda u: orows.at[u], "x")], gather_sem)
    for _ in reduce_steps(sender, subs, recv_sem):
        next(spread, None)
    for _ in spread:
        pass
    sender.drain()


def reduce_grads(g1, g2, kv, small, rows):
    hbm = pl.BlockSpec(memory_space=pl.ANY)
    vmem = pl.BlockSpec(memory_space=pltpu.VMEM)
    half = lambda a: (a.shape[1], a.shape[2] // 2)
    blocks = [(small.shape[1:], small.dtype)]
    blocks += [(half(kv), kv.dtype)] * 2 + [(half(g1), g1.dtype)] * 2
    blocks += [((g2.shape[1] // 2, g2.shape[2]), g2.dtype)] * 2
    scratch = [pltpu.VMEM(a.shape, a.dtype) for a in (g1, g2, kv, small)]
    for shape, dtype in blocks:
        scratch += [pltpu.VMEM((many,) + shape, dtype) for many in (16, 8, 4, 5)]
    return pl.pallas_call(
        reduce_kernel,
        out_shape=[jax.ShapeDtypeStruct(a.shape[1:], jnp.float32) for a in (g1, g2, kv, small)]
        + [jax.ShapeDtypeStruct((32,) + rows.shape, rows.dtype)],
        in_specs=[hbm] * 5,
        out_specs=[vmem] * 4 + [hbm],
        scratch_shapes=scratch
        + [
            pltpu.SemaphoreType.DMA((len(blocks) * SENDS_PER_REDUCE + SENDS_PER_GATHER,)),
            pltpu.SemaphoreType.DMA((len(blocks), 33)),
            pltpu.SemaphoreType.DMA((1, 32)),
            pltpu.SemaphoreType.DMA((4,)),
        ],
        compiler_params=pltpu.CompilerParams(
            collective_id=2, has_side_effects=True, vmem_limit_bytes=63 * 2**20
        ),
    )(g1, g2, kv, small, rows)


def exchange_weights(p1, p2, small, fast):
    if fast:
        w1a, w1b, w2a, w2b, small_all = gather_weights(p1, p2, small)
        return (w1a, w1b), (w2a, w2b), small_all
    both = ("wide", "narrow")
    w1 = lax.all_gather(p1, both, axis=0)
    w2 = lax.all_gather(p2, both, axis=0)
    return (w1[:, 0], w1[:, 1]), (w2[:, 0], w2[:, 1]), lax.all_gather(small, both, axis=0)


def exchange_grads(g1, g2, kv, small, rows, fast):
    if fast:
        return reduce_grads(g1, g2, kv, small, rows)
    both = ("wide", "narrow")
    summed = [
        lax.psum_scatter(a, both, scatter_dimension=0).astype(jnp.float32) for a in (g1, g2, kv, small)
    ]
    return summed + [lax.all_gather(rows, both, axis=0)]


def per_device(
    embeds, skip_tokens, cotangent, lengths, qkv_weight, out_weight, up_weight, down_weight, up_bias,
    norm_gains, biases, qkv_moments, out_moments, up_moments, down_moments, up_bias_moments,
    gain_moments, bias_moments,
):
    params = (qkv_weight, out_weight, up_weight, down_weight, up_bias, norm_gains, biases)
    moments = (
        qkv_moments, out_moments, up_moments, down_moments, up_bias_moments, gain_moments, bias_moments,
    )
    wide_size, narrow_size = lax.axis_size("wide"), lax.axis_size("narrow")
    fast = (wide_size, narrow_size) == (8, 4)
    owners = wide_size * narrow_size
    at = lax.axis_index("wide") * narrow_size + lax.axis_index("narrow")
    span_count = lengths.shape[0]
    row_count, width = embeds.shape
    low = lambda a: a.astype(jnp.bfloat16)
    positions = lax.broadcasted_iota(jnp.int32, (span_count, SPAN), 1)
    key_valid = positions < lengths[:, None]
    row_index = lax.broadcasted_iota(jnp.int32, (1, SPAN, 1), 1)

    p1 = jnp.concatenate([qkv_weight, out_weight, up_weight], axis=2).astype(jnp.bfloat16)
    p2 = down_weight.astype(jnp.bfloat16)
    share = 12 * width // owners
    tiles = -(-2 * share // 1024)
    small_own = jnp.concatenate(
        [up_bias, norm_gains.reshape(2, -1), biases.reshape(2, -1)], axis=1
    ).reshape(-1)
    small_own = jnp.pad(small_own, (0, tiles * 1024 - 2 * share)).reshape(tiles * 8, 128)
    w1, w2, small_all = exchange_weights(p1, p2, small_own, fast)
    small_all = small_all.reshape(owners, -1)[:, : 2 * share].astype(jnp.bfloat16).astype(jnp.float32)

    def layer_weights(layer):
        joined = w1[layer].reshape(width, -1)
        return (
            joined[:, : 3 * width], joined[:, 3 * width : 4 * width], joined[:, 4 * width :],
            w2[layer].reshape(-1, width),
        ) + unpack_small(small_all[:, layer * share : (layer + 1) * share], width)

    backbone, head = layer_weights(0), layer_weights(1)
    backbone_out, saved = first_forward(backbone, embeds, key_valid)
    skip_view = skip_tokens.reshape(span_count, SPAN, width)
    head_in = jnp.where(row_index == 0, backbone_out.astype(jnp.bfloat16)[:, None], skip_view)
    head_in = head_in.reshape(row_count, width)
    if fast:
        head_out, g1, g2, head_sums, grad_head_in = head_call(
            head_in, cotangent, key_valid.astype(jnp.float32), jnp.concatenate(
                [head[4].reshape(4, width), head[5], head[6]]
            ), w1[1], w2[1],
        )
        small_head = (head_sums[:4].reshape(4 * width), head_sums[4:6], head_sums[6:])
    else:
        head_out, grad_head_in, head_grads = backward_block(
            head, head_in, key_valid, cotangent.astype(jnp.float32)
        )
        g1 = jnp.concatenate([low(head_grads[0]), low(head_grads[1]), low(head_grads[2])], axis=1)
        g1 = g1.reshape(owners, width // owners, -1)
        g2 = low(head_grads[3]).reshape(owners, -1, width)
        small_head = head_grads[4:]
    grad_view = grad_head_in.reshape(span_count, SPAN, width)
    skip_grad = jnp.where(row_index == 0, 0.0, grad_view).reshape(row_count, width)
    embeds_grad, grad_kv_w, rows, small_first = first_backward(
        backbone, embeds, saved, grad_view[:, 0]
    )
    kv = low(grad_kv_w).reshape(owners, width // owners, -1)
    small_grads = jnp.concatenate(
        [pack_small(*small_first, owners), pack_small(*small_head, owners)], axis=1
    )
    small_grads = jnp.pad(small_grads, ((0, 0), (0, tiles * 1024 - 2 * share)))
    small_grads = small_grads.reshape(owners, tiles * 8, 128)
    rows_wide = jnp.pad(rows, ((0, 0), (0, 2 * width)))
    own_g1, own_g2, own_kv, own_small, all_rows = exchange_grads(
        g1, g2, kv, small_grads, rows_wide.reshape(16 * span_count // 2, -1), fast
    )
    all_rows = all_rows.reshape(owners * span_count, -1)
    first_grads = first_weight_grads(all_rows, own_kv, at)
    own_small = own_small.reshape(-1)[: 2 * share].reshape(2, share)
    sixth = width // owners
    joined = jnp.stack([jnp.concatenate(first_grads[:3], axis=1), own_g1])
    down = jnp.stack([first_grads[3], own_g2])
    small = (
        own_small[:, : 4 * sixth],
        own_small[:, 4 * sixth : 6 * sixth].reshape(2, 2, sixth),
        own_small[:, 6 * sixth :].reshape(2, 6, sixth),
    )
    new_steps, new_moments = adam_update(params, moments, joined, down, small)
    return (head_out.astype(jnp.bfloat16), embeds_grad, skip_grad, *new_steps, *new_moments)


def solution(mesh):
    return jax.shard_map(
        per_device,
        mesh=mesh,
        in_specs=(
            P(("wide", "narrow"), None),
            P(("wide", "narrow"), None),
            P(("wide", "narrow"), None),
            P(("wide", "narrow")),
            P(None, ("wide", "narrow"), None),
            P(None, ("wide", "narrow"), None),
            P(None, ("wide", "narrow"), None),
            P(None, ("wide", "narrow"), None),
            P(None, ("wide", "narrow")),
            P(None, None, ("wide", "narrow")),
            P(None, None, ("wide", "narrow")),
            P(None, None, ("wide", "narrow"), None),
            P(None, None, ("wide", "narrow"), None),
            P(None, None, ("wide", "narrow"), None),
            P(None, None, ("wide", "narrow"), None),
            P(None, None, ("wide", "narrow")),
            P(None, None, None, ("wide", "narrow")),
            P(None, None, None, ("wide", "narrow")),
        ),
        out_specs=(
            P(("wide", "narrow"), None),
            P(("wide", "narrow"), None),
            P(("wide", "narrow"), None),
            P(None, ("wide", "narrow"), None),
            P(None, ("wide", "narrow"), None),
            P(None, ("wide", "narrow"), None),
            P(None, ("wide", "narrow"), None),
            P(None, ("wide", "narrow")),
            P(None, None, ("wide", "narrow")),
            P(None, None, ("wide", "narrow")),
            P(None, None, ("wide", "narrow"), None),
            P(None, None, ("wide", "narrow"), None),
            P(None, None, ("wide", "narrow"), None),
            P(None, None, ("wide", "narrow"), None),
            P(None, None, ("wide", "narrow")),
            P(None, None, None, ("wide", "narrow")),
            P(None, None, None, ("wide", "narrow")),
        ),
        check_vma=False,
    )
```

```python
import math

import jax
import jax.numpy as jnp
from jax import lax
from jax.experimental import pallas as pl
from jax.experimental.pallas import tpu as pltpu
from jax.sharding import PartitionSpec as P

HEADS = 12
SPAN = 128

norm_epsilon = 1e-12
score_scale = 0.125
masked_score = -1000000000.0
beta_first = 0.9
beta_second = 0.999
adam_epsilon = 1e-08
weight_decay = 0.01
first_fix = 1.0 - 0.9**10
second_fix = 1.0 - 0.999**10


def dot_first(left_side, right_side):
    return lax.dot_general(
        left_side, right_side, (((0,), (0,)), ((), ())), preferred_element_type=jnp.float32
    )


def dot_last(left_side, right_side):
    return lax.dot_general(
        left_side, right_side, (((1,), (1,)), ((), ())), preferred_element_type=jnp.float32
    )


def normalize(values, gain_row, shift_row):
    centred = values - jnp.mean(values, axis=-1, keepdims=True)
    inv_scale = lax.rsqrt(jnp.mean(centred * centred, axis=-1, keepdims=True) + norm_epsilon)
    normed = centred * inv_scale
    return (normed * gain_row + shift_row, normed, inv_scale)


def normalize_back(gradient, normed, inv_scale, gain_row):
    grad_gain = jnp.sum(gradient * normed, axis=0)
    grad_shift = jnp.sum(gradient, axis=0)
    scaled = gradient * gain_row
    grad_in = inv_scale * (
        scaled
        - jnp.mean(scaled, axis=-1, keepdims=True)
        - normed * jnp.mean(scaled * normed, axis=-1, keepdims=True)
    )
    return (grad_in, grad_gain, grad_shift)


def head_view(tensor):
    return tensor.reshape(tensor.shape[0] // SPAN, SPAN, HEADS, tensor.shape[1] // HEADS)


def attend_scores(queries, keys_low, key_valid):
    scores = (
        jnp.einsum(
            "bqhe,bkhe->bhqk",
            head_view(queries),
            head_view(keys_low),
            preferred_element_type=jnp.float32,
        )
        * score_scale
    )
    return jnp.where(key_valid[:, None, None, :], scores, masked_score)


def forward_block(weights, inputs, key_valid):
    qkv_w, out_w, up_w, down_w, up_b, gain_rows, biases = weights
    gains_wide = gain_rows.astype(jnp.float32)
    biases_wide = biases.astype(jnp.float32)
    row_count, model_width = inputs.shape
    mixed_in = jnp.dot(inputs, qkv_w, preferred_element_type=jnp.float32)
    queries = (mixed_in[:, :model_width] + biases_wide[0]).astype(jnp.bfloat16)
    keys_low = mixed_in[:, model_width : 2 * model_width].astype(jnp.bfloat16)
    values_low = (mixed_in[:, 2 * model_width :] + biases_wide[1]).astype(jnp.bfloat16)
    scores = attend_scores(queries, keys_low, key_valid)
    row_max = jnp.max(scores, axis=-1, keepdims=True)
    weights_exp = jnp.exp(scores - row_max)
    row_total = jnp.sum(weights_exp, axis=-1, keepdims=True)
    softmax_out = (weights_exp / row_total).astype(jnp.bfloat16)
    log_total = row_max + jnp.log(row_total)
    context = jnp.einsum(
        "bhqk,bkhe->bqhe", softmax_out, head_view(values_low), preferred_element_type=jnp.float32
    )
    context = context.reshape(row_count, model_width).astype(jnp.bfloat16)
    attended = jnp.dot(context, out_w, preferred_element_type=jnp.float32) + biases_wide[2]
    hidden, normed_one, scale_one = normalize(
        inputs.astype(jnp.float32) + attended, gains_wide[0], biases_wide[3]
    )
    hidden_low = hidden.astype(jnp.bfloat16)
    pre_gelu = jnp.dot(hidden_low, up_w, preferred_element_type=jnp.float32) + up_b.astype(
        jnp.float32
    )
    activated = jax.nn.gelu(pre_gelu, approximate=False).astype(jnp.bfloat16)
    branch_out = jnp.dot(activated, down_w, preferred_element_type=jnp.float32) + biases_wide[4]
    output, normed_two, scale_two = normalize(hidden + branch_out, gains_wide[1], biases_wide[5])
    saved = (
        queries,
        keys_low,
        values_low,
        log_total,
        context,
        normed_one,
        scale_one,
        hidden_low,
        pre_gelu,
        activated,
        normed_two,
        scale_two,
    )
    return (output, saved)


def backward_block(weights, inputs, key_valid, grad_out):
    qkv_w, out_w, up_w, down_w, up_b, gain_rows, biases = weights
    gains_wide = gain_rows.astype(jnp.float32)
    row_count, model_width = inputs.shape
    output, saved = forward_block(weights, inputs, key_valid)
    (
        queries,
        keys_low,
        values_low,
        log_total,
        context,
        normed_one,
        scale_one,
        hidden_low,
        pre_gelu,
        activated,
        normed_two,
        scale_two,
    ) = saved
    grad_pre_two, grad_gain_two, grad_shift_two = normalize_back(
        grad_out, normed_two, scale_two, gains_wide[1]
    )
    grad_branch = grad_pre_two.astype(jnp.bfloat16)
    grad_down_w = dot_first(activated, grad_branch)
    grad_act = dot_last(grad_branch, down_w)
    _, gelu_back = jax.vjp(lambda inner: jax.nn.gelu(inner, approximate=False), pre_gelu)
    grad_pre_gelu = gelu_back(grad_act)[0].astype(jnp.bfloat16)
    grad_up_w = dot_first(hidden_low, grad_pre_gelu)
    grad_hidden = grad_pre_two + dot_last(grad_pre_gelu, up_w)
    grad_pre_one, grad_gain_one, grad_shift_one = normalize_back(
        grad_hidden, normed_one, scale_one, gains_wide[0]
    )
    grad_attended = grad_pre_one.astype(jnp.bfloat16)
    grad_out_w = dot_first(context, grad_attended)
    grad_context = head_view(dot_last(grad_attended, out_w).astype(jnp.bfloat16))
    scores = attend_scores(queries, keys_low, key_valid)
    softmax_full = jnp.exp(scores - log_total)
    grad_probs = jnp.einsum(
        "bqhe,bkhe->bhqk", grad_context, head_view(values_low), preferred_element_type=jnp.float32
    )
    grad_values = jnp.einsum(
        "bhqk,bqhe->bkhe",
        softmax_full.astype(jnp.bfloat16),
        grad_context,
        preferred_element_type=jnp.float32,
    )
    grad_values = grad_values.reshape(row_count, model_width).astype(jnp.bfloat16)
    grad_scores = softmax_full * (
        grad_probs - jnp.sum(softmax_full * grad_probs, axis=-1, keepdims=True)
    )
    grad_scores = grad_scores.astype(jnp.bfloat16)
    grad_queries = (
        jnp.einsum(
            "bhqk,bkhe->bqhe", grad_scores, head_view(keys_low), preferred_element_type=jnp.float32
        )
        * score_scale
    )
    grad_queries = grad_queries.reshape(row_count, model_width).astype(jnp.bfloat16)
    grad_keys = (
        jnp.einsum(
            "bhqk,bqhe->bkhe", grad_scores, head_view(queries), preferred_element_type=jnp.float32
        )
        * score_scale
    )
    grad_keys = grad_keys.reshape(row_count, model_width).astype(jnp.bfloat16)
    grad_mixed = jnp.concatenate([grad_queries, grad_keys, grad_values], axis=1)
    grad_qkv_w = dot_first(inputs, grad_mixed)
    grad_inputs = grad_pre_one + dot_last(grad_mixed, qkv_w)
    grad_gains = jnp.stack([grad_gain_one, grad_gain_two])
    grad_biases = jnp.stack(
        [
            jnp.sum(grad_queries, axis=0, dtype=jnp.float32),
            jnp.sum(grad_values, axis=0, dtype=jnp.float32),
            jnp.sum(grad_attended, axis=0, dtype=jnp.float32),
            grad_shift_one,
            jnp.sum(grad_branch, axis=0, dtype=jnp.float32),
            grad_shift_two,
        ]
    )
    grads = (
        grad_qkv_w,
        grad_out_w,
        grad_up_w,
        grad_down_w,
        jnp.sum(grad_pre_gelu, axis=0, dtype=jnp.float32),
        grad_gains,
        grad_biases,
    )
    return (output, grad_inputs, grads)


MESH = pl.DeviceIdType.MESH


class Refs:
    def __init__(self, **refs):
        for name, ref in refs.items():
            setattr(self, name, ref)


def place():
    wide = lax.axis_index("wide")
    z = lax.axis_index("narrow")
    return wide // 4, (wide // 2) % 2, wide % 2, z


def device(y, x, c, z):
    return ((y * 2 + x) * 2 + c, z)


def flat(y, x, c, z):
    return ((y * 2 + x) * 2 + c) * 4 + z


def near(z, k):
    if k == 0:
        return z
    if k == 1:
        return z + 1 - 2 * (z % 2)
    if k == 2:
        return (z + 2) % 4
    return 3 - z


def greet(wide, z):
    barrier = pltpu.get_barrier_semaphore()
    for k in range(1, 8):
        pl.semaphore_signal(barrier, inc=1, device_id=((wide + k) % 8, z), device_id_type=MESH)

    @pl.when(z < 3)
    def _():
        pl.semaphore_signal(barrier, inc=1, device_id=(wide, z + 1), device_id_type=MESH)

    @pl.when(z > 0)
    def _():
        pl.semaphore_signal(barrier, inc=1, device_id=(wide, z - 1), device_id_type=MESH)

    pl.semaphore_wait(barrier, 8 + ((z + 1) // 2) % 2)


def run_if(pred, action):
    if pred is None:
        action()
    else:
        pl.when(pred)(action)


def send(src, dst, send_sem, recv_sem, there, pred=None):
    run_if(
        pred,
        lambda: pltpu.make_async_remote_copy(
            src_ref=src, dst_ref=dst, send_sem=send_sem, recv_sem=recv_sem, device_id=there, device_id_type=MESH
        ).start(),
    )


def bytes_of(ref, sem):
    me = (lax.axis_index("wide"), lax.axis_index("narrow"))
    return pltpu.make_async_remote_copy(
        src_ref=ref, dst_ref=ref, send_sem=sem, recv_sem=sem, device_id=me, device_id_type=MESH
    )


def await_bytes(ref, sem, pred=None):
    run_if(pred, lambda: bytes_of(ref, sem).wait_recv())


def await_sent(ref, sem, pred=None):
    run_if(pred, lambda: bytes_of(ref, sem).wait_send())


def await_column_sends(many, each, sem, z):
    await_sent(many(each), sem, (z == 0) | (z == 3))
    await_sent(many(5 * each), sem, (z == 1) | (z == 2))


def column_steps(slabs, manys, sem):
    y, x, c, z = place()
    up, down = device(y, x, c, z + 1), device(y, x, c, z - 1)

    def push(i, slab, zz, there, pred):
        send(slab(zz), slab(zz), sem.at[i, 4], sem.at[i, zz], there, pred)

    def own():
        for i, slab in enumerate(slabs):
            push(i, slab, z, up, z < 3)
            push(i, slab, z, down, z > 0)

    def take(dist):
        for i, slab in enumerate(slabs):
            low, high = z - dist, z + dist
            await_bytes(slab(low), sem.at[i, low], z >= dist)
            if dist < 3:
                push(i, slab, low, up, (z >= dist) & (z < 3))
            await_bytes(slab(high), sem.at[i, high], z <= 3 - dist)
            if dist < 3:
                push(i, slab, high, down, (z <= 3 - dist) & (z > 0))

    def drain():
        for i, many in enumerate(manys):
            await_column_sends(many, 1, sem.at[i, 4], z)

    return [own] + [lambda dist=dist: take(dist) for dist in (1, 2, 3)], drain


GATHER_SEMS = 21


def gather_steps(subs, many, sem):
    y, x, c, z = place()
    each = len(subs)
    sib = device(y, x, 1 - c, z)
    xn = device(y, 1 - x, c, z)
    yn = device(1 - y, x, c, z)
    mine = flat(y, x, c, z)

    def unit(sub, far1, far2, zz, core):
        fx, fy = (far1, far2) if sub[2] == "x" else (far2, far1)
        return flat(1 - y if fy else y, 1 - x if fx else x, core, zz)

    def push(sub, at, send_at, role, target, pred=None, src=None):
        send(sub[1](at) if src is None else src, sub[1](at), sem.at[send_at], sem.at[role], target, pred)

    def along(sub, at, up, role, pred, src=None):
        push(sub, at, 17, role, device(y, x, c, z + 1 if up else z - 1), pred, src)

    def first(sub, at, zz, pred=None, src=None):
        push(sub, at, 18, 4 + zz, xn if sub[2] == "x" else yn, pred, src)

    def second(sub, at, far, zz, pred=None, src=None):
        push(sub, at, 19, 8 + 4 * far + zz, yn if sub[2] == "x" else xn, pred, src)

    def sibling(sub, at, pred=None, src=None):
        push(sub, at, 20, 16, sib, pred, src)

    def own():
        for sub in subs:
            along(sub, mine, True, z, z < 3, sub[0])
            along(sub, mine, False, z, z > 0, sub[0])
        for sub in subs:
            first(sub, mine, z, None, sub[0])
            second(sub, mine, 0, z, None, sub[0])
        for sub in subs:
            sibling(sub, mine, None, sub[0])

    def from_z(dist):
        for up in (True, False):
            zz = z - dist if up else z + dist
            have = (z >= dist) if up else (z <= 3 - dist)
            at = flat(y, x, c, zz)

            @pl.when(have)
            def _(up=up, zz=zz, at=at):
                await_bytes(many(each), sem.at[zz])
                for sub in subs:
                    if dist < 3:
                        along(sub, at, up, zz, (z < 3) if up else (z > 0))
                for sub in subs:
                    first(sub, at, zz)
                    second(sub, at, 0, zz)
                    sibling(sub, at)

    def from_first(k):
        zz = near(z, k)
        await_bytes(many(each), sem.at[4 + zz])
        for sub in subs:
            at = unit(sub, True, False, zz, c)
            second(sub, at, 1, zz)
            sibling(sub, at)

    def from_second(far, k):
        zz = near(z, k)
        await_bytes(many(each), sem.at[8 + 4 * far + zz])
        for sub in subs:
            sibling(sub, unit(sub, far == 1, True, zz, c))

    def finish():
        await_bytes(many(16 * each), sem.at[16])

    def drain():
        await_column_sends(many, each, sem.at[17], z)
        await_sent(many(4 * each), sem.at[18])
        await_sent(many(8 * each), sem.at[19])
        await_sent(many(16 * each), sem.at[20])

    steps = [own, lambda: from_z(1), lambda: from_first(0), lambda: from_z(2), lambda: from_first(1)]
    steps += [lambda: from_z(3), lambda: (from_first(2), from_first(3))]
    for far in range(2):
        steps += [lambda far=far, k=k: from_second(far, k) for k in range(4)]
    return steps + [finish], drain


REDUCE_SEMS = 33
TARGETS = (0, 3, 1, 2)


class Reduce:
    def __init__(self, subs, sem):
        self.subs, self.sem, self.each = subs, sem, len(subs)
        self.y, self.x, self.c, self.z = place()
        y, x, c, z = self.y, self.x, self.c, self.z
        self.sib = device(y, x, 1 - c, z)
        self.xn, self.yn = device(y, 1 - x, c, z), device(1 - y, x, c, z)

    def own(self, sub, far1, far2, zz, core):
        fx, fy = (far1, far2) if sub.dim == "x" else (far2, far1)
        cy, cx = (1 - self.y if fy else self.y), (1 - self.x if fx else self.x)
        return sub.own(flat(cy, cx, core, zz)), (cy * 2 + cx) * 4 + zz

    def coord(self, sub, far):
        here = self.x if sub.dim == "x" else self.y
        return 1 - here if far else here

    def take(self, at, buffer, count=1):
        await_bytes(buffer.at[pl.ds(0, count * self.each)], self.sem.at[at])

    def add(self, dst, *parts):
        total = dst[...].astype(jnp.float32)
        for part in parts:
            total = total + part[...].astype(jnp.float32)
        dst[...] = total.astype(dst.dtype)

    def start(self, zz):
        for far1, far2 in ((False, True), (True, True), (True, False), (False, False)):
            at = 6 * zz + (0 if far2 else 1 if far1 else 2)
            for sub in self.subs:
                src, slot = self.own(sub, far1, far2, zz, 1 - self.c)
                send(src, sub.sib.at[slot], self.sem.at[29], self.sem.at[at], self.sib)

    def step_a(self, zz):
        self.take(6 * zz, self.subs[0].sib, 2)
        for far1 in (False, True):
            for sub in self.subs:
                acc, slot = self.own(sub, far1, True, zz, self.c)
                self.add(acc, sub.sib.at[slot])
                slot = self.coord(sub, far1) * 4 + zz
                there = self.yn if sub.dim == "x" else self.xn
                send(acc, sub.second.at[slot], self.sem.at[30], self.sem.at[6 * zz + (3 if far1 else 4)], there)

    def step_b(self, zz):
        self.take(6 * zz + 1, self.subs[0].sib)
        self.take(6 * zz + 3, self.subs[0].second)
        for sub in self.subs:
            acc, slot = self.own(sub, True, False, zz, self.c)
            self.add(acc, sub.sib.at[slot], sub.second.at[self.coord(sub, True) * 4 + zz])
            there = self.xn if sub.dim == "x" else self.yn
            send(acc, sub.first.at[zz], self.sem.at[31], self.sem.at[6 * zz + 5], there)

    def chain(self, sub, acc, zz, up, pred):
        z = self.z
        slot = zz if up else jnp.where(z - 1 == zz, 4, zz)
        there = device(self.y, self.x, self.c, z + 1 if up else z - 1)
        send(acc, sub.chain.at[slot], self.sem.at[32], self.sem.at[24 + slot], there, pred)

    def step_c(self, zz):
        self.take(6 * zz + 2, self.subs[0].sib)
        self.take(6 * zz + 4, self.subs[0].second)
        self.take(6 * zz + 5, self.subs[0].first)
        for sub in self.subs:
            acc, slot = self.own(sub, False, False, zz, self.c)
            self.add(acc, sub.sib.at[slot], sub.second.at[self.coord(sub, False) * 4 + zz], sub.first.at[zz])
            if zz > 0:
                self.chain(sub, acc, zz, True, self.z == 0)
            if zz < 3:
                self.chain(sub, acc, zz, False, self.z == 3)

    def relay(self, zz, at, up):
        @pl.when(self.z == at)
        def _():
            self.take(24 + zz, self.subs[0].chain)
            for sub in self.subs:
                acc, _ = self.own(sub, False, False, zz, self.c)
                self.add(acc, sub.chain.at[zz])
                self.chain(sub, acc, zz, up, None)

    def step_d(self, zz):
        if zz >= 2:
            self.relay(zz, 1, True)
        else:
            self.relay(zz, 2, False)

    def step_e(self, zz):
        if zz == 3:
            self.relay(zz, 2, True)
        if zz == 0:
            self.relay(zz, 1, False)

    def finish(self):
        z = self.z
        for sub in self.subs:
            acc, _ = self.own(sub, False, False, z, self.c)
            sub.out[...] = acc[...].astype(jnp.float32)
        for pred, slot in ((z > 0, z), (z < 3, 4)):

            @pl.when(pred)
            def _(slot=slot):
                self.take(24 + slot, self.subs[0].chain)
                for sub in self.subs:
                    sub.out[...] += sub.chain[slot].astype(jnp.float32)

        for at, count in ((29, 16), (30, 8), (31, 4), (32, 3)):
            await_sent(self.subs[0].all.at[pl.ds(0, count * self.each)], self.sem.at[at])


class Waves:
    def __init__(self, groups, lags):
        self.waves = [(made, zz) for made in groups for zz in TARGETS]
        self.lags = lags
        self.at = 0

    def step(self):
        stages = (Reduce.step_a, Reduce.step_b, Reduce.step_c, Reduce.step_d, Reduce.step_e)
        for lag, stage in zip(self.lags, stages):
            k = self.at - lag
            if 0 <= k < len(self.waves):
                group, zz = self.waves[k]
                for made in group:
                    stage(made, zz)
        self.at += 1

    def left(self):
        return len(self.waves) + self.lags[-1] - self.at


def erf_of(v):
    return lax.erf(v)


def mm(a, b):
    return jnp.dot(a, b, preferred_element_type=jnp.float32)


def mm_nt(a, b):
    return lax.dot_general(a, b, (((1,), (1,)), ((), ())), preferred_element_type=jnp.float32)


def mm_tn(a, b):
    return lax.dot_general(a, b, (((0,), (0,)), ((), ())), preferred_element_type=jnp.float32)


def columns(ref, start, stop):
    block = ref[:, :, start:stop]
    return block.reshape(block.shape[0] * block.shape[1], stop - start)


def rows_of(ref, start, stop):
    block = ref[start:stop]
    return block.reshape(block.shape[0] * block.shape[1], block.shape[2])


def put_columns(ref, start, values):
    owners, share = ref.shape[0], ref.shape[1]
    ref[:, :, start : start + values.shape[1]] = values.astype(ref.dtype).reshape(
        owners, share, values.shape[1]
    )


def norm_rows(values):
    centred = values - jnp.mean(values, axis=-1, keepdims=True)
    inv_scale = lax.rsqrt(jnp.mean(centred * centred, axis=-1, keepdims=True) + norm_epsilon)
    return centred * inv_scale, inv_scale


def norm_rows_back(gradient, normed, inv_scale, gain_row):
    scaled = gradient * gain_row
    return inv_scale * (
        scaled
        - jnp.mean(scaled, axis=-1, keepdims=True)
        - normed * jnp.mean(scaled * normed, axis=-1, keepdims=True)
    )


def column_sum(values):
    return jnp.sum(values.astype(jnp.float32), axis=0, keepdims=True)


def head_forward(s, w1, w2, small, lengths):
    width = s.x.shape[1]
    spans = s.x.shape[0] // SPAN
    x = s.x[...]
    s.q[...] = (mm(x, columns(w1, 0, width)) + small(2)).astype(jnp.bfloat16)
    s.k[...] = mm(x, columns(w1, width, 2 * width)).astype(jnp.bfloat16)
    s.v[...] = (mm(x, columns(w1, 2 * width, 3 * width)) + small(3)).astype(jnp.bfloat16)
    yield
    lane = lax.broadcasted_iota(jnp.int32, (SPAN, 128), 1)
    for span in range(spans):
        keep = lax.broadcasted_iota(jnp.int32, (SPAN, 128), 1) < lengths[span]
        for pair in range(width // 128):
            at = (slice(span * SPAN, (span + 1) * SPAN), slice(pair * 128, (pair + 1) * 128))
            q, k, v = s.q[at], s.k[at], s.v[at]
            parts = []
            for side in range(2):
                here = (lane < 64) if side == 0 else (lane >= 64)
                scores = mm_nt(jnp.where(here, q, jnp.zeros_like(q)), k) * score_scale
                scores = jnp.where(keep, scores, masked_score)
                weight = jnp.exp(scores - jnp.max(scores, axis=-1, keepdims=True))
                probs = weight / jnp.sum(weight, axis=-1, keepdims=True)
                s.p[(span * 6 + pair) * 2 + side] = probs
                parts.append(mm(probs.astype(jnp.bfloat16), v))
            s.ctx[at] = jnp.where(lane < 64, parts[0], parts[1]).astype(jnp.bfloat16)
        yield
    attended = mm(s.ctx[...], columns(w1, 3 * width, 4 * width)) + small(4)
    normed, inv_scale = norm_rows(s.x[...].astype(jnp.float32) + attended)
    s.n1[...] = normed
    s.r1[...] = inv_scale
    hidden = normed * small(0) + small(5)
    s.h[...] = hidden
    s.hl[...] = hidden.astype(jnp.bfloat16)
    yield
    for part in range(4):
        pre = mm(s.hl[...], columns(w1, (4 + part) * width, (5 + part) * width)) + small(8 + part)
        half_erf = 0.5 + 0.5 * erf_of(pre * (0.5**0.5))
        s.g[part] = (pre * half_erf).astype(jnp.bfloat16)
        s.gp[part] = half_erf + pre * (jnp.exp(-0.5 * pre * pre) * (0.5 / math.pi) ** 0.5)
        yield
    branch = small(6)
    share = w2.shape[0] // 4
    for part in range(4):
        branch = branch + mm(s.g[part], rows_of(w2, part * share, (part + 1) * share))
    normed, inv_scale = norm_rows(s.h[...] + branch)
    s.n2[...] = normed
    s.r2[...] = inv_scale
    s.y[...] = (normed * small(1) + small(7)).astype(jnp.bfloat16)
    yield


def head_backward(s, w1, w2, g1, g2, small, sums, grad_in):
    width = s.x.shape[1]
    spans = s.x.shape[0] // SPAN
    grad_out = s.cot[...].astype(jnp.float32)
    sums[1:2] = column_sum(grad_out * s.n2[...])
    sums[7:8] = column_sum(grad_out)
    pre_two = norm_rows_back(grad_out, s.n2[...], s.r2[...], small(1))
    s.h[...] = pre_two
    branch = pre_two.astype(jnp.bfloat16)
    s.dz[...] = branch
    sums[6:7] = column_sum(branch)
    yield
    owners = w2.shape[0]
    share = owners // 4
    for part in range(4):
        own = slice(part * share, (part + 1) * share)
        grad_act = mm_nt(s.dz[...], rows_of(w2, part * share, (part + 1) * share))
        grad_pre = (grad_act * s.gp[part]).astype(jnp.bfloat16)
        g2[own] = (
            mm_tn(s.g[part], s.dz[...]).astype(jnp.bfloat16).reshape(share, g2.shape[1], width)
        )
        s.g[part] = grad_pre
        sums[8 + part : 9 + part] = column_sum(grad_pre)
        yield
    for part in range(4):
        at = (4 + part) * width
        grad_pre = s.g[part]
        s.h[...] += mm_nt(grad_pre, columns(w1, at, at + width))
        put_columns(g1, at, mm_tn(s.hl[...], grad_pre))
        yield
    grad_hidden = s.h[...]
    sums[0:1] = column_sum(grad_hidden * s.n1[...])
    sums[5:6] = column_sum(grad_hidden)
    pre_one = norm_rows_back(grad_hidden, s.n1[...], s.r1[...], small(0))
    s.h[...] = pre_one
    attended = pre_one.astype(jnp.bfloat16)
    s.dz[...] = attended
    sums[4:5] = column_sum(attended)
    yield
    s.hl[...] = mm_nt(attended, columns(w1, 3 * width, 4 * width)).astype(jnp.bfloat16)
    put_columns(g1, 3 * width, mm_tn(s.ctx[...], attended))
    yield
    lane = lax.broadcasted_iota(jnp.int32, (SPAN, 128), 1)
    for span in range(spans):
        for pair in range(width // 128):
            at = (slice(span * SPAN, (span + 1) * SPAN), slice(pair * 128, (pair + 1) * 128))
            q, k, v, dc = s.q[at], s.k[at], s.v[at], s.hl[at]
            dq, dk, dv = [], [], []
            for side in range(2):
                here = (lane < 64) if side == 0 else (lane >= 64)
                probs = s.p[(span * 6 + pair) * 2 + side]
                grad_probs = mm_nt(jnp.where(here, dc, jnp.zeros_like(dc)), v)
                dv.append(mm_tn(probs.astype(jnp.bfloat16), dc))
                grad_scores = probs * (
                    grad_probs - jnp.sum(probs * grad_probs, axis=-1, keepdims=True)
                )
                grad_scores = grad_scores.astype(jnp.bfloat16)
                dq.append(mm(grad_scores, k))
                dk.append(mm_tn(grad_scores, q))
            join = lambda two: jnp.where(lane < 64, two[0], two[1])
            s.q[at] = (join(dq) * score_scale).astype(jnp.bfloat16)
            s.k[at] = (join(dk) * score_scale).astype(jnp.bfloat16)
            s.v[at] = join(dv).astype(jnp.bfloat16)
        yield
    sums[2:3] = column_sum(s.q[...])
    sums[3:4] = column_sum(s.v[...])
    total = s.h[...]
    for k, ref in enumerate((s.q, s.k, s.v)):
        total = total + mm_nt(ref[...], columns(w1, k * width, (k + 1) * width))
    grad_in[...] = total
    yield
    for k, ref in enumerate((s.q, s.k, s.v)):
        put_columns(g1, k * width, mm_tn(s.x[...], ref[...]))
    yield


HIGHEST = lax.Precision.HIGHEST
ROWS = 16


def iota(shape, axis):
    return lax.broadcasted_iota(jnp.int32, shape, axis)


def ones_where(condition, dtype):
    return jnp.where(condition, 1.0, 0.0).astype(dtype)


def exact(a, b, dims):
    return lax.dot_general(
        a, b, (dims, ((), ())), precision=HIGHEST, preferred_element_type=jnp.float32
    )


class Plane:
    def __init__(self, sem):
        self.sem = sem
        self.wide, self.z = lax.axis_index("wide"), lax.axis_index("narrow")
        self.sent = []

    def send(self, index, src, recv):
        for k in range(1, 8):
            peer = (self.wide + k) % 8
            send(src(peer), recv.at[self.wide], self.sem.at[index, 0], self.sem.at[index, 1], (peer, self.z))
        self.sent.append((index, recv))

    def arrive(self, index, recv):
        await_bytes(recv.at[pl.ds(0, 7)], self.sem.at[index, 1])

    def drain(self):
        for index, recv in self.sent:
            await_sent(recv.at[pl.ds(0, 7)], self.sem.at[index, 0])

    def total(self, index, recv):
        self.arrive(index, recv)
        total = recv[0].astype(jnp.float32)
        for k in range(1, 8):
            total = total + recv[k].astype(jnp.float32)
        return total

    def place_rows(self, two):
        row = iota((ROWS, two.shape[1]), 0)
        rows = jnp.where(row % 2 == 0, two[0:1], two[1:2])
        return jnp.where(row // 2 == self.wide, rows, 0.0)

    def pick_rows(self, values, first):
        row = iota(values.shape, 0)
        one = lambda k: jnp.sum(jnp.where(row == first + k, values, 0.0), axis=0, keepdims=True)
        return jnp.concatenate([one(0), one(1)], axis=0)

    def share(self, index, two, src, recv):
        placed = self.place_rows(two).astype(src.dtype)
        src[...] = placed
        recv[self.wide] = placed
        self.send(index, lambda peer: src, recv)

    def collect(self, index, values, src, recv):
        for k in range(2):
            src[k] = values[8 * k : 8 * k + 8]
        recv[self.wide] = jnp.where(self.wide // 4 == 0, values[0:8], values[8:16])
        self.send(index, lambda peer: src.at[peer // 4], recv)

    def collected(self, index, recv):
        return self.pick_rows(self.total(index, recv), 2 * (self.wide % 4))


def backbone_forward(s, plane, small, finish):
    x0, w0 = s.x0, s.w0
    width = x0.shape[1]
    spans = x0.shape[0] // SPAN
    wide = plane.wide
    x = x0[...]
    s.k0[...] = mm(x, columns(w0, width, 2 * width)).astype(jnp.bfloat16)
    s.v0[...] = (mm(x, columns(w0, 2 * width, 3 * width)) + small(3)).astype(jnp.bfloat16)
    first = jnp.concatenate(
        [x0[SPAN * span : SPAN * span + 1].astype(jnp.float32) for span in range(spans)], axis=0
    )
    query = mm(first.astype(jnp.bfloat16), columns(w0, 0, width)) + small(2)
    s.keep[0, 0:spans] = first
    s.keep[1, 0:spans] = query.astype(jnp.bfloat16).astype(jnp.float32)
    yield
    heads = ones_where(iota((width, 128), 0) // (width // HEADS) == iota((width, 128), 1), jnp.bfloat16)
    context = []
    for span in range(spans):
        at = slice(span * SPAN, (span + 1) * SPAN)
        product = s.k0[at].astype(jnp.float32) * s.keep[1, span : span + 1]
        scores = exact(product, heads.astype(jnp.float32), ((1,), (0,))) * score_scale
        scores = jnp.where(iota(scores.shape, 0) < s.lengths[span], scores, masked_score)
        weight = jnp.exp(scores - jnp.max(scores, axis=0, keepdims=True))
        probs = weight / jnp.sum(weight, axis=0, keepdims=True)
        s.p0[span] = probs
        spread = mm_nt(probs.astype(jnp.bfloat16), heads)
        context.append(jnp.sum(spread * s.v0[at].astype(jnp.float32), axis=0, keepdims=True))
    context = jnp.concatenate(context, axis=0).astype(jnp.bfloat16)
    s.keep[2, 0:spans] = context.astype(jnp.float32)
    attended = mm(context, columns(w0, 3 * width, 4 * width)) + small(4)
    normed, inv_scale = norm_rows(s.keep[0, 0:spans] + attended)
    hidden = normed * small(0) + small(5)
    s.keep[3, 0:spans] = normed
    s.keep[4, 0:spans] = jnp.broadcast_to(inv_scale, normed.shape)
    s.keep[5, 0:spans] = hidden
    plane.share(0, hidden, s.e0_src, s.e0)
    yield
    hidden_all = plane.total(0, s.e0).astype(jnp.bfloat16)
    share = width // 8
    pick = ones_where(iota((width, share), 0) == share * wide + iota((width, share), 1), jnp.bfloat16)
    own = mm(hidden_all, pick).astype(jnp.bfloat16)
    upz = s.upz
    part = upz.shape[2] // 8
    for k in range(8):
        s.e1_src[k] = mm(own, columns(upz, k * part, (k + 1) * part))
    s.e1[wide] = s.e1_src[wide]
    plane.send(1, lambda peer: s.e1_src.at[peer], s.e1)
    yield
    bias = jnp.where(wide % 2 == 0, small(8 + wide // 2)[:, :part], small(8 + wide // 2)[:, part:])
    pre = plane.total(1, s.e1) + bias
    half_erf = 0.5 + 0.5 * erf_of(pre * (0.5**0.5))
    s.g0[...] = (pre * half_erf).astype(jnp.bfloat16)
    s.gp0[...] = half_erf + pre * (jnp.exp(-0.5 * pre * pre) * (0.5 / math.pi) ** 0.5)
    plane.collect(2, mm(s.g0[...], rows_of(s.downz, 0, 4)), s.e2_src, s.e2)
    yield
    branch = plane.collected(2, s.e2) + small(6)
    normed, inv_scale = norm_rows(s.keep[5, 0:spans] + branch)
    s.keep[6, 0:spans] = normed
    s.keep[7, 0:spans] = jnp.broadcast_to(inv_scale, normed.shape)
    finish(normed * small(1) + small(7))
    yield


def backbone_backward(s, plane, small, grad_rows):
    x0, w0 = s.x0, s.w0
    width = x0.shape[1]
    spans = x0.shape[0] // SPAN
    wide = plane.wide
    keep = lambda k: s.keep[k, 0:spans]
    acts, sums = s.acts, s.sums0

    def put(item, values):
        for span in range(spans):
            row = span * ROWS + item
            acts[row : row + 1] = values[span : span + 1]

    acts[...] = jnp.zeros_like(acts)
    grad_out = grad_rows()
    sums[1:2] = column_sum(grad_out * keep(6))
    sums[7:8] = column_sum(grad_out)
    pre_two = norm_rows_back(grad_out, keep(6), keep(7), small(1))
    s.keep[8, 0:spans] = pre_two
    low = lambda a: a.astype(jnp.bfloat16).astype(jnp.float32)
    put(11, low(pre_two))
    plane.share(3, pre_two, s.e3_src, s.e3)
    yield
    branch = plane.total(3, s.e3).astype(jnp.bfloat16)
    grad_act = mm_nt(branch, rows_of(s.downz, 0, 4))
    part = s.g0.shape[1]
    s.e4_src[:, :part] = (grad_act * s.gp0[...]).astype(jnp.bfloat16)
    s.e4_src[:, part:] = s.g0[...]
    s.e4[wide] = s.e4_src[...]
    plane.send(4, lambda peer: s.e4_src, s.e4)
    yield
    plane.arrive(4, s.e4)
    total = jnp.zeros((ROWS, width // 8), jnp.float32)
    for k in range(8):
        both = s.e4[k]
        total = total + mm_nt(both[:, :part], columns(s.upz, k * part, (k + 1) * part))
        rows = plane.pick_rows(both.astype(jnp.float32), 2 * wide)
        at = slice((k % 2) * part, (k % 2 + 1) * part)
        for span in range(spans):
            row = span * ROWS + 3 + k // 2
            acts[row : row + 1, at] = rows[span : span + 1, :part]
            acts[row + 4 : row + 5, at] = rows[span : span + 1, part:]
    share = width // 8
    pick = ones_where(iota((width, share), 0) == share * wide + iota((width, share), 1), jnp.float32)
    plane.collect(5, exact(total, pick, ((1,), (1,))), s.e5_src, s.e5)
    yield
    grad_hidden = keep(8) + plane.collected(5, s.e5)
    sums[0:1] = column_sum(grad_hidden * keep(3))
    sums[5:6] = column_sum(grad_hidden)
    pre_one = norm_rows_back(grad_hidden, keep(3), keep(4), small(0))
    attended = pre_one.astype(jnp.bfloat16)
    context = low(mm_nt(attended, columns(w0, 3 * width, 4 * width)))
    heads = ones_where(iota((width, 128), 0) // (width // HEADS) == iota((width, 128), 1), jnp.bfloat16)
    queries = []
    for span in range(spans):
        at = slice(span * SPAN, (span + 1) * SPAN)
        probs = s.p0[span]
        grad_context = context[span : span + 1]
        product = s.v0[at].astype(jnp.float32) * grad_context
        grad_probs = exact(product, heads.astype(jnp.float32), ((1,), (0,)))
        grad_scores = probs * (grad_probs - jnp.sum(probs * grad_probs, axis=0, keepdims=True))
        spread = mm_nt(grad_scores.astype(jnp.bfloat16), heads) * score_scale
        queries.append(jnp.sum(spread * s.k0[at].astype(jnp.float32), axis=0, keepdims=True))
        s.k0[at] = (spread * s.keep[1, span : span + 1]).astype(jnp.bfloat16)
        s.v0[at] = (mm_nt(probs.astype(jnp.bfloat16), heads) * grad_context).astype(jnp.bfloat16)
    queries = jnp.concatenate(queries, axis=0).astype(jnp.bfloat16)
    sums[3:4] = column_sum(s.v0[...])
    put(0, keep(2))
    put(1, attended.astype(jnp.float32))
    put(2, low(keep(5)))
    put(12, keep(0))
    put(13, queries.astype(jnp.float32))
    s.acts_low[...] = acts[...].astype(jnp.bfloat16)
    s.keep[9, 0:spans] = pre_one + mm_nt(queries, columns(w0, 0, width))
    yield
    grad_in = s.embeds_grad
    grad_in[...] = mm_nt(s.k0[...], columns(w0, width, 2 * width))
    grad_in[...] += mm_nt(s.v0[...], columns(w0, 2 * width, 3 * width))
    for span in range(spans):
        grad_in[SPAN * span : SPAN * span + 1] += s.keep[9, span : span + 1]
    put_columns(w0, width, mm_tn(x0[...], s.k0[...]))
    put_columns(w0, 2 * width, mm_tn(x0[...], s.v0[...]))
    yield


def backbone_weight_grads(s, at, o1, o2, small_out):
    width = s.x0.shape[1]
    gathered = s.g[...].reshape(-1, width)
    spans = 64

    def item(k):
        shape = (spans, gathered.shape[0])
        row, column = iota(shape, 0), iota(shape, 1)
        pick = column == (row // 2) * 32 + (row % 2) * ROWS + k
        return mm(ones_where(pick, jnp.bfloat16), gathered)

    share = width // 32
    shape = (width, 128)

    def picker(count, offset, dtype):
        row, column = iota(shape, 0), iota(shape, 1)
        return ones_where((row + offset == count * at + column) & (column < count), dtype)

    narrow = picker(share, 0, jnp.bfloat16)
    own = lambda k: mm(item(k).astype(jnp.bfloat16), narrow).astype(jnp.bfloat16)
    grad_query = item(13)
    o1[0, :, 0:width] = mm_tn(own(12), grad_query.astype(jnp.bfloat16))[:share]
    grad_attended = item(1)
    o1[0, :, 3 * width : 4 * width] = mm_tn(own(0), grad_attended.astype(jnp.bfloat16))[:share]
    branch = item(11)
    hidden = own(2)
    wide_sum = jnp.zeros((1, 128), jnp.float32)
    act = jnp.zeros((spans, 128), jnp.float32)
    for part in range(4):
        grad_pre = item(3 + part)
        o1[0, :, (4 + part) * width : (5 + part) * width] = mm_tn(hidden, grad_pre.astype(jnp.bfloat16))[:share]
        act = act + mm(item(7 + part).astype(jnp.bfloat16), picker(4 * share, part * width, jnp.bfloat16))
        wide_sum = wide_sum + exact(
            column_sum(grad_pre), picker(4 * share, part * width, jnp.float32), ((1,), (0,))
        )
    o2[0] = mm_tn(act.astype(jnp.bfloat16), branch.astype(jnp.bfloat16))[: 4 * share]
    exact_narrow = picker(share, 0, jnp.float32)
    for row, values in ((2, grad_query), (4, grad_attended), (6, branch)):
        small_out[row : row + 1] += exact(column_sum(values), exact_narrow, ((1,), (0,)))
    small_out[8:9] = wide_sum


def step_kernel(
    qkv_in, out_in, up_in, down_in, up_bias, gains, biases, x0, skip, cot, lengths, y_out, embeds_grad, skip_grad,
    o1, o2, small_out, acts_all, *scratch,
):
    s = Refs(x0=x0, cot=cot, lengths=lengths, y=y_out, embeds_grad=embeds_grad)
    for (name, _, _), ref in zip(step_scratch(x0.shape[1]), scratch):
        setattr(s, name, ref)
    gather_sem, column_sem, reduce_sem, plane_sem, load_sem = scratch[-5:]
    width = x0.shape[1]
    spans = x0.shape[0] // SPAN
    y, x, c, z = place()
    wide = lax.axis_index("wide")
    me = flat(y, x, c, z)
    w0, w1, w2, upz, downz, pars = s.w0, s.w1, s.w2, s.upz, s.downz, s.pars
    loads = [
        pltpu.make_async_copy(src, dst, load_sem.at[k])
        for k, (src, dst) in enumerate(
            (
                (qkv_in, o1.at[:, :, : 3 * width]), (out_in, o1.at[:, :, 3 * width : 4 * width]),
                (up_in, o1.at[:, :, 4 * width :]), (down_in, o2),
            )
        )
    ]
    for load in loads:
        load.start()
    greet(wide, z)
    for load in loads:
        load.wait()
    w0[me] = o1[0, :, : 4 * width].astype(jnp.bfloat16)
    w1[me] = o1[1].astype(jnp.bfloat16)
    w2[me] = o2[1].astype(jnp.bfloat16)
    upz[z] = o1[0, :, 4 * width :].astype(jnp.bfloat16)
    downz[z] = o2[0].astype(jnp.bfloat16)
    s.small_all[me] = jnp.zeros((2 * ROWS, 128), jnp.float32)
    for layer in range(2):
        r, share = ROWS * layer, width // 32
        s.small_all[me, r : r + 2, :share] = gains[layer]
        s.small_all[me, r + 2 : r + 8, :share] = biases[layer]
        s.small_all[me, r + 8 : r + 9, : 4 * share] = up_bias[layer : layer + 1]

    half, mid = 2 * width, w2.shape[1] // 2

    def column_pair(ref, start):
        cut = lambda at: (lambda u: ref.at[u, :, at : at + half])
        subs = [(None, cut(start), "x"), (None, cut(start + half), "y")]
        return subs, lambda n: ref.at[pl.ds(0, n), :, start : start + half]

    rows_cut = lambda at: (lambda u: w2.at[u, at : at + mid])
    sets = [
        ([(None, lambda u: s.small_all.at[u], "x")], lambda n: s.small_all.at[pl.ds(0, n)]),
        column_pair(w0, 0),
        column_pair(w1, 0),
        column_pair(w1, 2 * half),
        ([(None, rows_cut(0), "x"), (None, rows_cut(mid), "y")], lambda n: w2.at[pl.ds(0, n), :mid]),
    ]
    events = []
    drains = []
    for k, (subs, many) in enumerate(sets):
        steps, drain = gather_steps(subs, many, gather_sem.at[k])
        drains.append(drain)
        for step, action in enumerate(steps):
            events.append((LAG * max(k - 1, 0) + step, action))
    steps, drain = column_steps(
        [lambda zz: upz.at[zz], lambda zz: downz.at[zz]],
        [lambda n: w1.at[pl.ds(0, n), :, : 2 * half], lambda n: w2.at[pl.ds(0, n)]],
        column_sem,
    )
    drains.append(drain)
    events += zip(COLUMN_AT, steps)

    def row_of(layer):
        return lambda k: pars[pl.ds(ROWS * layer + k, 1), :]

    def unpack():
        share = width // 32
        for layer in range(2):
            r = ROWS * layer
            for d in range(32):
                pars[r : r + 8, share * d : share * (d + 1)] = s.small_all[d, r : r + 8, :share]
                at = slice((d % 8) * 4 * share, (d % 8 + 1) * 4 * share)
                pars[r + 8 + d // 8 : r + 9 + d // 8, at] = s.small_all[d, r + 8 : r + 9, : 4 * share]
        pars[...] = pars[...].astype(jnp.bfloat16).astype(jnp.float32)

    def join(rows):
        row = iota(skip.shape, 0)
        joined = skip[...].astype(jnp.float32)
        for span in range(spans):
            joined = jnp.where(row == SPAN * span, rows[span : span + 1], joined)
        s.x[...] = joined.astype(jnp.bfloat16)

    plane = Plane(plane_sem)
    forward0 = backbone_forward(s, plane, row_of(0), join)
    forward1 = head_forward(s, w1, w2, row_of(1), lengths)
    events += [(15.2, unpack)]
    events += [(at, lambda: next(forward0)) for at in FORWARD0_AT]
    events += [(at, lambda: next(forward1)) for at in FORWARD1_AT]
    for _, action in sorted(events, key=lambda event: event[0]):
        action()
    for drain in drains:
        drain()

    back1 = head_backward(s, w1, w2, w1, w2, row_of(1), s.sums, skip_grad)
    back0 = backbone_backward(
        s, plane, row_of(0),
        lambda: jnp.concatenate([skip_grad[SPAN * k : SPAN * k + 1] for k in range(spans)], axis=0),
    )

    def reduced(whole, own, out, name, dim):
        bufs = [getattr(s, name + kind) for kind in KINDS]
        return Refs(all=whole, own=own, out=out, dim=dim, sib=bufs[0], second=bufs[1], first=bufs[2], chain=bufs[3])

    def pair(ref, start, stop, out, name):
        middle = (start + stop) // 2
        cut = lambda a, b: (ref.at[:, :, a:b], lambda u: ref.at[u, :, a:b], out.at[:, a:b])
        return [
            reduced(*cut(start, middle), name + "a", "x"),
            reduced(*cut(middle, stop), name + "b", "y"),
        ]

    made = iter(range(6))
    group = lambda *subs: Reduce(subs, reduce_sem.at[next(made)])
    cut = lambda a, b: (w2.at[:, a:b], lambda u: w2.at[u, a:b], o2.at[1, a:b])
    downs = [group(reduced(*cut(0, mid), "da", "x"), reduced(*cut(mid, 2 * mid), "db", "y"))]
    ups = [group(*pair(w1, 4 * width, 8 * width, o1.at[1], "u"))]
    lefts = [
        group(*pair(w1, 0, 4 * width, o1.at[1], "q")),
        group(reduced(s.block1, lambda u: s.block1.at[u], small_out.at[ROWS : 2 * ROWS], "s1", "x")),
    ]
    kvs = [
        group(*pair(w0, width, 3 * width, o1.at[0], "k")),
        group(reduced(s.block0, lambda u: s.block0.at[u], small_out.at[0:8], "s0", "y")),
    ]
    waves = Waves([downs, ups, lefts, kvs], LAGS)

    def start(groups):
        for zz in TARGETS:
            for each in groups:
                each.start(zz)

    def fill_blocks(block, sums, wide_too):
        share = width // 32
        block[...] = jnp.zeros_like(block)
        for d in range(32):
            block[d, 0:8, :share] = sums[0:8, share * d : share * (d + 1)]
            if wide_too:
                at = slice((d % 8) * 4 * share, (d % 8 + 1) * 4 * share)
                block[d, 8:9, : 4 * share] = sums[8 + d // 8 : 9 + d // 8, at]

    def step(times):
        for _ in range(times):
            waves.step()

    for _ in range(5):
        next(back1)
    start(downs)
    next(back1)
    next(back1)
    step(STEPS[0])
    next(back1)
    next(back1)
    step(STEPS[1])
    next(back1)
    start(ups)
    next(back1)
    step(STEPS[2])
    next(back1)
    step(STEPS[3])
    next(back1)
    step(STEPS[4])
    next(back1)
    next(back0)
    step(STEPS[5])
    next(back1)
    fill_blocks(s.block1, s.sums, True)
    start(lefts)
    next(back0)
    step(STEPS[6])
    next(back0)
    step(STEPS[7])
    next(back0)
    home = lambda u: acts_all.at[u // 8, pl.ds(pl.multiple_of((u % 8) * 32, 32), 32)]
    own_acts = pltpu.make_async_copy(s.acts_low, home(me), load_sem.at[0])
    own_acts.start()
    rows = lambda n: acts_all.at[pl.ds(0, n // 8)] if n >= 8 else acts_all.at[0, pl.ds(0, 32 * n)]
    spread, drain = gather_steps([(s.acts_low, home, "x")], rows, gather_sem.at[5])
    spread[0]()
    next(back0)
    fill_blocks(s.block0, s.sums0, False)
    start(kvs)
    row = iota(skip_grad.shape, 0)
    skip_grad[...] = jnp.where(row % SPAN == 0, 0.0, skip_grad[...])
    left = waves.left()
    for k in range(left):
        waves.step()
        for action in spread[1 + 15 * k // left : 1 + 15 * (k + 1) // left]:
            action()
    own_acts.wait()
    load = pltpu.make_async_copy(acts_all, s.g, load_sem.at[1])
    load.start()
    for groups in (downs, ups, lefts, kvs):
        for each in groups:
            each.finish()
    load.wait()
    backbone_weight_grads(s, me, o1, o2, small_out)
    drain()
    plane.drain()


LAG = 5
COLUMN_AT = (2.5, 4.5, 6.5, 8.5)
FORWARD0_AT = (15.3, 16.5, 18.5, 20.5, 22.5)
FORWARD1_AT = (22.6, 23.6, 24.6, 25.5, 26.5, 27.5, 28.5, 29.5, 30.5)
LAGS = (0, 1, 2, 3, 4)
STEPS = (1, 1, 1, 1, 1, 1, 1, 1)
KINDS = ("sib", "second", "first", "chain")


def step_scratch(width):
    low, full = jnp.bfloat16, jnp.float32
    share = width // 32
    rows = 2 * SPAN
    found = [
        ("w0", (32, share, 4 * width), low), ("upz", (4, share, 4 * width), low),
        ("downz", (4, 4 * share, width), low), ("w1", (32, share, 8 * width), low),
        ("w2", (32, 4 * share, width), low), ("small_all", (32, 2 * ROWS, 128), full),
        ("pars", (2 * ROWS, width), full), ("sums", (ROWS, width), full), ("sums0", (8, width), full),
        ("keep", (ROWS, 8, width), full), ("p0", (2, SPAN, 128), full),
        ("g0", (ROWS, width // 2), low), ("gp0", (ROWS, width // 2), full),
        ("e0_src", (ROWS, width), low), ("e0", (8, ROWS, width), low),
        ("e1_src", (8, ROWS, width // 2), full), ("e1", (8, ROWS, width // 2), full),
        ("e2_src", (2, 8, width), full), ("e2", (8, 8, width), full),
        ("e3_src", (ROWS, width), low), ("e3", (8, ROWS, width), low),
        ("e4_src", (ROWS, width), low), ("e4", (8, ROWS, width), low),
        ("e5_src", (2, 8, width), full), ("e5", (8, 8, width), full),
        ("acts", (2 * ROWS, width), full), ("acts_low", (2 * ROWS, width), low),
        ("block1", (32, ROWS, 128), full), ("block0", (32, 8, 128), full),
        ("g", (4, rows, width), low), ("gp", (4, rows, width), full),
        ("p", (2 * HEADS, SPAN, SPAN), full), ("r1", (rows, 1), full), ("r2", (rows, 1), full),
    ]
    found += [(name, (rows, width), low) for name in ("x", "q", "k", "v", "ctx", "hl", "dz", "k0", "v0")]
    found += [(name, (rows, width), full) for name in ("n1", "h", "n2")]
    shapes = {
        "d": ((2 * share, width), low), "u": ((share, 2 * width), low), "q": ((share, 2 * width), low),
        "k": ((share, width), low),
    }
    blocks = [(name + side, shape) for name, shape in shapes.items() for side in "ab"]
    blocks += [("s1", ((ROWS, 128), full)), ("s0", ((8, 128), full))]
    for name, (shape, dtype) in blocks:
        for kind, many in zip(KINDS, (16, 8, 4, 5)):
            found.append((name + kind, (many,) + shape, dtype))
    return found


def step_call(params, embeds, skip_tokens, cotangent, lengths):
    vmem, hbm = pl.BlockSpec(memory_space=pltpu.VMEM), pl.BlockSpec(memory_space=pl.ANY)
    rows, width = embeds.shape
    share = width // 32
    scratch = [pltpu.VMEM(shape, dtype) for _, shape, dtype in step_scratch(width)]
    scratch += [
        pltpu.SemaphoreType.DMA((6, GATHER_SEMS)),
        pltpu.SemaphoreType.DMA((2, 5)),
        pltpu.SemaphoreType.DMA((6, REDUCE_SEMS)),
        pltpu.SemaphoreType.DMA((6, 2)),
        pltpu.SemaphoreType.DMA((4,)),
    ]
    shape = jax.ShapeDtypeStruct
    return pl.pallas_call(
        step_kernel,
        out_shape=[
            shape((rows, width), jnp.bfloat16), shape((rows, width), jnp.float32),
            shape((rows, width), jnp.float32), shape((2, share, 8 * width), jnp.float32),
            shape((2, 4 * share, width), jnp.float32), shape((2 * ROWS, 128), jnp.float32),
            shape((4, rows, width), jnp.bfloat16),
        ],
        in_specs=[hbm] * 4 + [vmem] * 6 + [pl.BlockSpec(memory_space=pltpu.SMEM)],
        out_specs=[vmem] * 6 + [hbm],
        scratch_shapes=scratch,
        compiler_params=pltpu.CompilerParams(
            collective_id=1, has_side_effects=True, vmem_limit_bytes=64 * 2**20
        ),
    )(*params, embeds, skip_tokens, cotangent, lengths)


def adam_parts(parameter, first, second, gradient, decayed):
    first = beta_first * first + (1.0 - beta_first) * gradient
    second = beta_second * second + (1.0 - beta_second) * gradient * gradient
    update = first / first_fix / (jnp.sqrt(second / second_fix) + adam_epsilon)
    if decayed:
        update = update + weight_decay * parameter
    return update, first, second


def adam_kernel(*refs):
    params, moments = refs[0:7], refs[7:14]
    joined, down, small = refs[14:17]
    passed, steps, news, handed = refs[17:20], refs[20:27], refs[27:34], refs[34:37]

    def update(index, gradient):
        step, first, second = adam_parts(
            params[index][...], moments[index][0], moments[index][1], gradient, index < 4
        )
        steps[index][...] = step
        news[index][0] = first
        news[index][1] = second

    qkv, out = params[0].shape[2], params[1].shape[2]
    update(0, joined[:, :, :qkv])
    update(1, joined[:, :, qkv : qkv + out])
    update(2, joined[:, :, qkv + out :])
    update(3, down[...])

    @pl.when(pl.program_id(1) == 0)
    def _():
        for src, dst in zip(passed, handed):
            dst[...] = src[...]

    @pl.when((pl.program_id(0) == 0) & (pl.program_id(1) == 0))
    def _():
        many = small.shape[0] // 2
        for layer in range(2):
            at = layer * many
            for index, start, stop in ((4, 8, 9), (5, 0, 2), (6, 2, 8)):
                width = params[index].shape[-1]
                here = slice(layer, layer + 1) if index == 4 else layer
                step, first, second = adam_parts(
                    params[index][here], moments[index][0, here], moments[index][1, here],
                    small[at + start : at + stop, :width], False,
                )
                steps[index][here] = step
                news[index][0, here] = first
                news[index][1, here] = second


def adam_update(params, moments, joined, down, small, passed):
    cuts = 3 if params[0].shape[1] % 24 == 0 else 1

    def whole(a):
        return pl.BlockSpec(a.shape, lambda l, r, n=a.ndim: (0,) * n)

    def rows(a):
        return pl.BlockSpec((1, a.shape[1] // cuts, a.shape[2]), lambda l, r: (l, r, 0))

    def pairs(a):
        return pl.BlockSpec((2, 1, a.shape[2] // cuts, a.shape[3]), lambda l, r: (0, l, r, 0))

    halves = [pl.BlockSpec((a.shape[0] // 2, a.shape[1]), lambda l, r: (l, 0)) for a in passed]
    param_specs = [rows(a) for a in params[:4]] + [whole(a) for a in params[4:]]
    moment_specs = [pairs(a) for a in moments[:4]] + [whole(a) for a in moments[4:]]
    shape = lambda a: jax.ShapeDtypeStruct(a.shape, a.dtype)
    out = pl.pallas_call(
        adam_kernel,
        grid=(2, cuts),
        out_shape=[shape(a) for a in (*params, *moments, *passed)],
        in_specs=param_specs + moment_specs + [rows(joined), rows(down), whole(small)] + halves,
        out_specs=param_specs + moment_specs + halves,
        compiler_params=pltpu.CompilerParams(vmem_limit_bytes=63 * 2**20),
    )(*params, *moments, joined, down, small, *passed)
    return out[:7], out[7:14], out[14:]


def first_forward(weights, inputs, key_valid):
    qkv_w, out_w, up_w, down_w, up_b, gain_rows, biases = weights
    row_count, width = inputs.shape
    span_count = row_count // SPAN
    first = inputs.reshape(span_count, SPAN, width)[:, 0]
    mixed = jnp.dot(inputs, qkv_w[:, width:], preferred_element_type=jnp.float32)
    keys = mixed[:, :width].astype(jnp.bfloat16).reshape(span_count, SPAN, HEADS, width // HEADS)
    values = (mixed[:, width:] + biases[1]).astype(jnp.bfloat16)
    values = values.reshape(span_count, SPAN, HEADS, width // HEADS)
    queries = jnp.dot(first, qkv_w[:, :width], preferred_element_type=jnp.float32) + biases[0]
    queries = queries.astype(jnp.bfloat16).reshape(span_count, HEADS, width // HEADS)
    scores = (
        jnp.einsum("bhe,bkhe->bhk", queries, keys, preferred_element_type=jnp.float32) * score_scale
    )
    scores = jnp.where(key_valid[:, None, :], scores, masked_score)
    probs = jax.nn.softmax(scores, axis=-1)
    context = jnp.einsum(
        "bhk,bkhe->bhe", probs.astype(jnp.bfloat16), values, preferred_element_type=jnp.float32
    )
    context = context.reshape(span_count, width).astype(jnp.bfloat16)
    attended = jnp.dot(context, out_w, preferred_element_type=jnp.float32) + biases[2]
    hidden, normed_one, scale_one = normalize(
        first.astype(jnp.float32) + attended, gain_rows[0], biases[3]
    )
    hidden_low = hidden.astype(jnp.bfloat16)
    pre_gelu = jnp.dot(hidden_low, up_w, preferred_element_type=jnp.float32) + up_b
    activated = jax.nn.gelu(pre_gelu, approximate=False).astype(jnp.bfloat16)
    branch_out = jnp.dot(activated, down_w, preferred_element_type=jnp.float32) + biases[4]
    output, normed_two, scale_two = normalize(hidden + branch_out, gain_rows[1], biases[5])
    saved = (
        first, queries, keys, values, probs, context, normed_one, scale_one, hidden_low, pre_gelu,
        activated, normed_two, scale_two,
    )
    return output, saved


def first_backward(weights, inputs, saved, grad_out):
    qkv_w, out_w, up_w, down_w, up_b, gain_rows, biases = weights
    (
        first, queries, keys, values, probs, context, normed_one, scale_one, hidden_low, pre_gelu,
        activated, normed_two, scale_two,
    ) = saved
    row_count, width = inputs.shape
    span_count = row_count // SPAN
    grad_pre_two, grad_gain_two, grad_shift_two = normalize_back(
        grad_out, normed_two, scale_two, gain_rows[1]
    )
    grad_branch = grad_pre_two.astype(jnp.bfloat16)
    grad_act = dot_last(grad_branch, down_w)
    _, gelu_back = jax.vjp(lambda inner: jax.nn.gelu(inner, approximate=False), pre_gelu)
    grad_pre_gelu = gelu_back(grad_act)[0].astype(jnp.bfloat16)
    grad_hidden = grad_pre_two + dot_last(grad_pre_gelu, up_w)
    grad_pre_one, grad_gain_one, grad_shift_one = normalize_back(
        grad_hidden, normed_one, scale_one, gain_rows[0]
    )
    grad_attended = grad_pre_one.astype(jnp.bfloat16)
    grad_context = dot_last(grad_attended, out_w).astype(jnp.bfloat16)
    grad_context = grad_context.reshape(span_count, HEADS, width // HEADS)
    grad_probs = jnp.einsum(
        "bhe,bkhe->bhk", grad_context, values, preferred_element_type=jnp.float32
    )
    grad_values = jnp.einsum("bhk,bhe->bkhe", probs.astype(jnp.bfloat16), grad_context)
    grad_values = grad_values.reshape(row_count, width).astype(jnp.bfloat16)
    grad_scores = probs * (grad_probs - jnp.sum(probs * grad_probs, axis=-1, keepdims=True))
    grad_scores = grad_scores.astype(jnp.bfloat16)
    grad_queries = (
        jnp.einsum("bhk,bkhe->bhe", grad_scores, keys, preferred_element_type=jnp.float32)
        * score_scale
    )
    grad_queries = grad_queries.reshape(span_count, width).astype(jnp.bfloat16)
    grad_keys = (
        jnp.einsum("bhk,bhe->bkhe", grad_scores, queries, preferred_element_type=jnp.float32)
        * score_scale
    )
    grad_keys = grad_keys.reshape(row_count, width).astype(jnp.bfloat16)
    grad_kv = jnp.concatenate([grad_keys, grad_values], axis=1)
    grad_kv_w = dot_first(inputs, grad_kv)
    grad_inputs = dot_last(grad_kv, qkv_w[:, width:])
    grad_first = grad_pre_one + dot_last(grad_queries, qkv_w[:, :width])
    placed = jnp.pad(grad_first[:, None], ((0, 0), (0, SPAN - 1), (0, 0))).reshape(row_count, width)
    grad_inputs = grad_inputs + placed
    rows = jnp.concatenate(
        [context, grad_attended, hidden_low, grad_pre_gelu, activated, grad_branch, first, grad_queries],
        axis=1,
    )

    def total(values):
        return jnp.sum(values, axis=0, dtype=jnp.float32)

    small = (
        total(grad_pre_gelu),
        jnp.stack([grad_gain_one, grad_gain_two]),
        jnp.stack(
            [
                total(grad_queries), total(grad_values), total(grad_attended), grad_shift_one,
                total(grad_branch), grad_shift_two,
            ]
        ),
    )
    return grad_inputs, grad_kv_w, rows, small


def first_weight_grads(rows, kv_owned, at):
    width = rows.shape[1] // 16
    wide = 4 * width
    context, grad_attended = rows[:, :width], rows[:, width : 2 * width]
    hidden_low = rows[:, 2 * width : 3 * width]
    grad_pre_gelu = rows[:, 3 * width : 3 * width + wide]
    activated = rows[:, 7 * width : 11 * width]
    grad_branch = rows[:, 11 * width : 12 * width]
    first = rows[:, 12 * width : 13 * width]
    grad_queries = rows[:, 13 * width : 14 * width]
    count = kv_owned.shape[0]
    own = lambda values, many: lax.dynamic_slice_in_dim(values, at * many, many, 1)
    return (
        jnp.concatenate([dot_first(own(first, count), grad_queries), kv_owned], axis=1),
        dot_first(own(context, count), grad_attended),
        dot_first(own(hidden_low, count), grad_pre_gelu),
        dot_first(own(activated, 4 * count), grad_branch),
    )


def pack_small(up_b, gains, biases, owners):
    parts = [up_b.reshape(owners, -1)]
    for tensor in (gains, biases):
        parts.append(tensor.reshape(tensor.shape[0], owners, -1).transpose(1, 0, 2).reshape(owners, -1))
    return jnp.concatenate(parts, axis=1)


def unpack_small(packed, width):
    owners = packed.shape[0]
    share = width // owners
    up_b = packed[:, : 4 * share].reshape(4 * width)
    gains = packed[:, 4 * share : 6 * share].reshape(owners, 2, share).transpose(1, 0, 2)
    biases = packed[:, 6 * share :].reshape(owners, 6, share).transpose(1, 0, 2)
    return up_b, gains.reshape(2, width), biases.reshape(6, width)


def exchange_weights(p1, p2, small):
    both = ("wide", "narrow")
    w1 = lax.all_gather(p1, both, axis=0)
    w2 = lax.all_gather(p2, both, axis=0)
    return (w1[:, 0], w1[:, 1]), (w2[:, 0], w2[:, 1]), lax.all_gather(small, both, axis=0)


def exchange_grads(g1, g2, kv, small, rows):
    both = ("wide", "narrow")
    summed = [
        lax.psum_scatter(a, both, scatter_dimension=0).astype(jnp.float32) for a in (g1, g2, kv, small)
    ]
    return summed + [lax.all_gather(rows, both, axis=0)]


def fused_step(embeds, skip_tokens, cotangent, lengths, params, moments):
    y, embeds_grad, skip_grad, o1, o2, small, _ = step_call(params, embeds, skip_tokens, cotangent, lengths)
    new_steps, new_moments, passed = adam_update(params, moments, o1, o2, small, (y, embeds_grad, skip_grad))
    return (*passed, *new_steps, *new_moments)


def per_device(
    embeds, skip_tokens, cotangent, lengths, qkv_weight, out_weight, up_weight, down_weight, up_bias,
    norm_gains, biases, qkv_moments, out_moments, up_moments, down_moments, up_bias_moments,
    gain_moments, bias_moments,
):
    params = (qkv_weight, out_weight, up_weight, down_weight, up_bias, norm_gains, biases)
    moments = (
        qkv_moments, out_moments, up_moments, down_moments, up_bias_moments, gain_moments, bias_moments,
    )
    wide_size, narrow_size = lax.axis_size("wide"), lax.axis_size("narrow")
    if (wide_size, narrow_size) == (8, 4):
        return fused_step(embeds, skip_tokens, cotangent, lengths, params, moments)
    owners = wide_size * narrow_size
    at = lax.axis_index("wide") * narrow_size + lax.axis_index("narrow")
    span_count = lengths.shape[0]
    row_count, width = embeds.shape
    positions = lax.broadcasted_iota(jnp.int32, (span_count, SPAN), 1)
    key_valid = positions < lengths[:, None]
    row_index = lax.broadcasted_iota(jnp.int32, (1, SPAN, 1), 1)

    p1 = jnp.concatenate([qkv_weight, out_weight, up_weight], axis=2).astype(jnp.bfloat16)
    p2 = down_weight.astype(jnp.bfloat16)
    share = 12 * width // owners
    tiles = -(-2 * share // 1024)
    small_own = jnp.concatenate(
        [up_bias, norm_gains.reshape(2, -1), biases.reshape(2, -1)], axis=1
    ).reshape(-1)
    small_own = jnp.pad(small_own, (0, tiles * 1024 - 2 * share)).reshape(tiles * 8, 128)
    w1, w2, small_all = exchange_weights(p1, p2, small_own)
    small_all = small_all.reshape(owners, -1)[:, : 2 * share].astype(jnp.bfloat16).astype(jnp.float32)

    def layer_weights(layer):
        joined = w1[layer].reshape(width, -1)
        return (
            joined[:, : 3 * width], joined[:, 3 * width : 4 * width], joined[:, 4 * width :],
            w2[layer].reshape(-1, width),
        ) + unpack_small(small_all[:, layer * share : (layer + 1) * share], width)

    backbone, head = layer_weights(0), layer_weights(1)
    backbone_out, saved = first_forward(backbone, embeds, key_valid)
    skip_view = skip_tokens.reshape(span_count, SPAN, width)
    head_in = jnp.where(row_index == 0, backbone_out.astype(jnp.bfloat16)[:, None], skip_view)
    head_in = head_in.reshape(row_count, width)
    head_out, grad_head_in, head_grads = backward_block(
        head, head_in, key_valid, cotangent.astype(jnp.float32)
    )
    grad_view = grad_head_in.reshape(span_count, SPAN, width)
    skip_grad = jnp.where(row_index == 0, 0.0, grad_view).reshape(row_count, width)
    embeds_grad, grad_kv_w, rows, small_first = first_backward(
        backbone, embeds, saved, grad_view[:, 0]
    )
    low = lambda a: a.astype(jnp.bfloat16)
    g1 = jnp.concatenate([low(head_grads[0]), low(head_grads[1]), low(head_grads[2])], axis=1)
    g1 = g1.reshape(owners, width // owners, -1)
    g2 = low(head_grads[3]).reshape(owners, -1, width)
    kv = low(grad_kv_w).reshape(owners, width // owners, -1)
    small_grads = jnp.concatenate(
        [pack_small(*small_first, owners), pack_small(*head_grads[4:], owners)], axis=1
    )
    small_grads = jnp.pad(small_grads, ((0, 0), (0, tiles * 1024 - 2 * share)))
    small_grads = small_grads.reshape(owners, tiles * 8, 128)
    rows_wide = jnp.pad(rows, ((0, 0), (0, 2 * width)))
    own_g1, own_g2, own_kv, own_small, all_rows = exchange_grads(
        g1, g2, kv, small_grads, rows_wide.reshape(16 * span_count // 2, -1)
    )
    all_rows = all_rows.reshape(owners * span_count, -1)
    first_grads = first_weight_grads(all_rows, own_kv, at)
    own_small = own_small.reshape(-1)[: 2 * share].reshape(2, share)
    sixth = width // owners
    joined = jnp.stack([jnp.concatenate(first_grads[:3], axis=1), own_g1])
    down = jnp.stack([first_grads[3], own_g2])
    pad = lambda a: jnp.pad(a, ((0, 0), (0, 0), (0, 128 - a.shape[2])))
    small = [
        pad(own_small[:, 4 * sixth : 6 * sixth].reshape(2, 2, sixth)),
        pad(own_small[:, 6 * sixth :].reshape(2, 6, sixth)),
        pad(own_small[:, None, : 4 * sixth]),
        jnp.zeros((2, 7, 128), jnp.float32),
    ]
    small = jnp.concatenate(small, axis=1).reshape(32, 128)
    passed = (head_out.astype(jnp.bfloat16), embeds_grad, skip_grad)
    new_steps, new_moments, passed = adam_update(params, moments, joined, down, small, passed)
    return (*passed, *new_steps, *new_moments)


def solution(mesh):
    return jax.shard_map(
        per_device,
        mesh=mesh,
        in_specs=(
            P(("wide", "narrow"), None),
            P(("wide", "narrow"), None),
            P(("wide", "narrow"), None),
            P(("wide", "narrow")),
            P(None, ("wide", "narrow"), None),
            P(None, ("wide", "narrow"), None),
            P(None, ("wide", "narrow"), None),
            P(None, ("wide", "narrow"), None),
            P(None, ("wide", "narrow")),
            P(None, None, ("wide", "narrow")),
            P(None, None, ("wide", "narrow")),
            P(None, None, ("wide", "narrow"), None),
            P(None, None, ("wide", "narrow"), None),
            P(None, None, ("wide", "narrow"), None),
            P(None, None, ("wide", "narrow"), None),
            P(None, None, ("wide", "narrow")),
            P(None, None, None, ("wide", "narrow")),
            P(None, None, None, ("wide", "narrow")),
        ),
        out_specs=(
            P(("wide", "narrow"), None),
            P(("wide", "narrow"), None),
            P(("wide", "narrow"), None),
            P(None, ("wide", "narrow"), None),
            P(None, ("wide", "narrow"), None),
            P(None, ("wide", "narrow"), None),
            P(None, ("wide", "narrow"), None),
            P(None, ("wide", "narrow")),
            P(None, None, ("wide", "narrow")),
            P(None, None, ("wide", "narrow")),
            P(None, None, ("wide", "narrow"), None),
            P(None, None, ("wide", "narrow"), None),
            P(None, None, ("wide", "narrow"), None),
            P(None, None, ("wide", "narrow"), None),
            P(None, None, ("wide", "narrow")),
            P(None, None, None, ("wide", "narrow")),
            P(None, None, None, ("wide", "narrow")),
        ),
        check_vma=False,
    )
```

```python
import math

import jax
import jax.numpy as jnp
from jax import lax
from jax.experimental import pallas as pl
from jax.experimental.pallas import tpu as pltpu
from jax.sharding import PartitionSpec as P

HEADS = 12
SPAN = 128

norm_epsilon = 1e-12
score_scale = 0.125
masked_score = -1000000000.0
beta_first = 0.9
beta_second = 0.999
adam_epsilon = 1e-08
weight_decay = 0.01
first_fix = 1.0 - 0.9**10
second_fix = 1.0 - 0.999**10


def dot_first(left_side, right_side):
    return lax.dot_general(
        left_side, right_side, (((0,), (0,)), ((), ())), preferred_element_type=jnp.float32
    )


def dot_last(left_side, right_side):
    return lax.dot_general(
        left_side, right_side, (((1,), (1,)), ((), ())), preferred_element_type=jnp.float32
    )


def normalize(values, gain_row, shift_row):
    centred = values - jnp.mean(values, axis=-1, keepdims=True)
    inv_scale = lax.rsqrt(jnp.mean(centred * centred, axis=-1, keepdims=True) + norm_epsilon)
    normed = centred * inv_scale
    return (normed * gain_row + shift_row, normed, inv_scale)


def normalize_back(gradient, normed, inv_scale, gain_row):
    grad_gain = jnp.sum(gradient * normed, axis=0)
    grad_shift = jnp.sum(gradient, axis=0)
    scaled = gradient * gain_row
    grad_in = inv_scale * (
        scaled
        - jnp.mean(scaled, axis=-1, keepdims=True)
        - normed * jnp.mean(scaled * normed, axis=-1, keepdims=True)
    )
    return (grad_in, grad_gain, grad_shift)


def head_view(tensor):
    return tensor.reshape(tensor.shape[0] // SPAN, SPAN, HEADS, tensor.shape[1] // HEADS)


def attend_scores(queries, keys_low, key_valid):
    scores = (
        jnp.einsum(
            "bqhe,bkhe->bhqk",
            head_view(queries),
            head_view(keys_low),
            preferred_element_type=jnp.float32,
        )
        * score_scale
    )
    return jnp.where(key_valid[:, None, None, :], scores, masked_score)


def forward_block(weights, inputs, key_valid):
    qkv_w, out_w, up_w, down_w, up_b, gain_rows, biases = weights
    gains_wide = gain_rows.astype(jnp.float32)
    biases_wide = biases.astype(jnp.float32)
    row_count, model_width = inputs.shape
    mixed_in = jnp.dot(inputs, qkv_w, preferred_element_type=jnp.float32)
    queries = (mixed_in[:, :model_width] + biases_wide[0]).astype(jnp.bfloat16)
    keys_low = mixed_in[:, model_width : 2 * model_width].astype(jnp.bfloat16)
    values_low = (mixed_in[:, 2 * model_width :] + biases_wide[1]).astype(jnp.bfloat16)
    scores = attend_scores(queries, keys_low, key_valid)
    row_max = jnp.max(scores, axis=-1, keepdims=True)
    weights_exp = jnp.exp(scores - row_max)
    row_total = jnp.sum(weights_exp, axis=-1, keepdims=True)
    softmax_out = (weights_exp / row_total).astype(jnp.bfloat16)
    log_total = row_max + jnp.log(row_total)
    context = jnp.einsum(
        "bhqk,bkhe->bqhe", softmax_out, head_view(values_low), preferred_element_type=jnp.float32
    )
    context = context.reshape(row_count, model_width).astype(jnp.bfloat16)
    attended = jnp.dot(context, out_w, preferred_element_type=jnp.float32) + biases_wide[2]
    hidden, normed_one, scale_one = normalize(
        inputs.astype(jnp.float32) + attended, gains_wide[0], biases_wide[3]
    )
    hidden_low = hidden.astype(jnp.bfloat16)
    pre_gelu = jnp.dot(hidden_low, up_w, preferred_element_type=jnp.float32) + up_b.astype(
        jnp.float32
    )
    activated = jax.nn.gelu(pre_gelu, approximate=False).astype(jnp.bfloat16)
    branch_out = jnp.dot(activated, down_w, preferred_element_type=jnp.float32) + biases_wide[4]
    output, normed_two, scale_two = normalize(hidden + branch_out, gains_wide[1], biases_wide[5])
    saved = (
        queries,
        keys_low,
        values_low,
        log_total,
        context,
        normed_one,
        scale_one,
        hidden_low,
        pre_gelu,
        activated,
        normed_two,
        scale_two,
    )
    return (output, saved)


def backward_block(weights, inputs, key_valid, grad_out):
    qkv_w, out_w, up_w, down_w, up_b, gain_rows, biases = weights
    gains_wide = gain_rows.astype(jnp.float32)
    row_count, model_width = inputs.shape
    output, saved = forward_block(weights, inputs, key_valid)
    (
        queries,
        keys_low,
        values_low,
        log_total,
        context,
        normed_one,
        scale_one,
        hidden_low,
        pre_gelu,
        activated,
        normed_two,
        scale_two,
    ) = saved
    grad_pre_two, grad_gain_two, grad_shift_two = normalize_back(
        grad_out, normed_two, scale_two, gains_wide[1]
    )
    grad_branch = grad_pre_two.astype(jnp.bfloat16)
    grad_down_w = dot_first(activated, grad_branch)
    grad_act = dot_last(grad_branch, down_w)
    _, gelu_back = jax.vjp(lambda inner: jax.nn.gelu(inner, approximate=False), pre_gelu)
    grad_pre_gelu = gelu_back(grad_act)[0].astype(jnp.bfloat16)
    grad_up_w = dot_first(hidden_low, grad_pre_gelu)
    grad_hidden = grad_pre_two + dot_last(grad_pre_gelu, up_w)
    grad_pre_one, grad_gain_one, grad_shift_one = normalize_back(
        grad_hidden, normed_one, scale_one, gains_wide[0]
    )
    grad_attended = grad_pre_one.astype(jnp.bfloat16)
    grad_out_w = dot_first(context, grad_attended)
    grad_context = head_view(dot_last(grad_attended, out_w).astype(jnp.bfloat16))
    scores = attend_scores(queries, keys_low, key_valid)
    softmax_full = jnp.exp(scores - log_total)
    grad_probs = jnp.einsum(
        "bqhe,bkhe->bhqk", grad_context, head_view(values_low), preferred_element_type=jnp.float32
    )
    grad_values = jnp.einsum(
        "bhqk,bqhe->bkhe",
        softmax_full.astype(jnp.bfloat16),
        grad_context,
        preferred_element_type=jnp.float32,
    )
    grad_values = grad_values.reshape(row_count, model_width).astype(jnp.bfloat16)
    grad_scores = softmax_full * (
        grad_probs - jnp.sum(softmax_full * grad_probs, axis=-1, keepdims=True)
    )
    grad_scores = grad_scores.astype(jnp.bfloat16)
    grad_queries = (
        jnp.einsum(
            "bhqk,bkhe->bqhe", grad_scores, head_view(keys_low), preferred_element_type=jnp.float32
        )
        * score_scale
    )
    grad_queries = grad_queries.reshape(row_count, model_width).astype(jnp.bfloat16)
    grad_keys = (
        jnp.einsum(
            "bhqk,bqhe->bkhe", grad_scores, head_view(queries), preferred_element_type=jnp.float32
        )
        * score_scale
    )
    grad_keys = grad_keys.reshape(row_count, model_width).astype(jnp.bfloat16)
    grad_mixed = jnp.concatenate([grad_queries, grad_keys, grad_values], axis=1)
    grad_qkv_w = dot_first(inputs, grad_mixed)
    grad_inputs = grad_pre_one + dot_last(grad_mixed, qkv_w)
    grad_gains = jnp.stack([grad_gain_one, grad_gain_two])
    grad_biases = jnp.stack(
        [
            jnp.sum(grad_queries, axis=0, dtype=jnp.float32),
            jnp.sum(grad_values, axis=0, dtype=jnp.float32),
            jnp.sum(grad_attended, axis=0, dtype=jnp.float32),
            grad_shift_one,
            jnp.sum(grad_branch, axis=0, dtype=jnp.float32),
            grad_shift_two,
        ]
    )
    grads = (
        grad_qkv_w,
        grad_out_w,
        grad_up_w,
        grad_down_w,
        jnp.sum(grad_pre_gelu, axis=0, dtype=jnp.float32),
        grad_gains,
        grad_biases,
    )
    return (output, grad_inputs, grads)


MESH = pl.DeviceIdType.MESH


class Refs:
    def __init__(self, **refs):
        for name, ref in refs.items():
            setattr(self, name, ref)


def place():
    wide = lax.axis_index("wide")
    z = lax.axis_index("narrow")
    return wide // 4, (wide // 2) % 2, wide % 2, z


def device(y, x, c, z):
    return ((y * 2 + x) * 2 + c, z)


def flat(y, x, c, z):
    return ((y * 2 + x) * 2 + c) * 4 + z


def near(z, k):
    if k == 0:
        return z
    if k == 1:
        return z + 1 - 2 * (z % 2)
    if k == 2:
        return (z + 2) % 4
    return 3 - z


def greet(wide, z):
    barrier = pltpu.get_barrier_semaphore()
    for k in range(1, 8):
        pl.semaphore_signal(barrier, inc=1, device_id=((wide + k) % 8, z), device_id_type=MESH)

    @pl.when(z < 3)
    def _():
        pl.semaphore_signal(barrier, inc=1, device_id=(wide, z + 1), device_id_type=MESH)

    @pl.when(z > 0)
    def _():
        pl.semaphore_signal(barrier, inc=1, device_id=(wide, z - 1), device_id_type=MESH)

    pl.semaphore_wait(barrier, 8 + ((z + 1) // 2) % 2)


def run_if(pred, action):
    if pred is None:
        action()
    else:
        pl.when(pred)(action)


def send(src, dst, send_sem, recv_sem, there, pred=None):
    run_if(
        pred,
        lambda: pltpu.make_async_remote_copy(
            src_ref=src, dst_ref=dst, send_sem=send_sem, recv_sem=recv_sem, device_id=there, device_id_type=MESH
        ).start(),
    )


def bytes_of(ref, sem):
    me = (lax.axis_index("wide"), lax.axis_index("narrow"))
    return pltpu.make_async_remote_copy(
        src_ref=ref, dst_ref=ref, send_sem=sem, recv_sem=sem, device_id=me, device_id_type=MESH
    )


def await_bytes(ref, sem, pred=None):
    run_if(pred, lambda: bytes_of(ref, sem).wait_recv())


def await_sent(ref, sem, pred=None):
    run_if(pred, lambda: bytes_of(ref, sem).wait_send())


def await_column_sends(many, each, sem, z):
    await_sent(many(each), sem, (z == 0) | (z == 3))
    await_sent(many(5 * each), sem, (z == 1) | (z == 2))


def column_steps(slabs, manys, sem):
    y, x, c, z = place()
    up, down = device(y, x, c, z + 1), device(y, x, c, z - 1)

    def push(i, slab, zz, there, pred):
        send(slab(zz), slab(zz), sem.at[i, 4], sem.at[i, zz], there, pred)

    def own():
        for i, slab in enumerate(slabs):
            push(i, slab, z, up, z < 3)
            push(i, slab, z, down, z > 0)

    def take(dist):
        for i, slab in enumerate(slabs):
            low, high = z - dist, z + dist
            await_bytes(slab(low), sem.at[i, low], z >= dist)
            if dist < 3:
                push(i, slab, low, up, (z >= dist) & (z < 3))
            await_bytes(slab(high), sem.at[i, high], z <= 3 - dist)
            if dist < 3:
                push(i, slab, high, down, (z <= 3 - dist) & (z > 0))

    def drain():
        for i, many in enumerate(manys):
            await_column_sends(many, 1, sem.at[i, 4], z)

    return [own] + [lambda dist=dist: take(dist) for dist in (1, 2, 3)], drain


GATHER_SEMS = 21


def gather_steps(subs, many, sem):
    y, x, c, z = place()
    each = len(subs)
    sib = device(y, x, 1 - c, z)
    xn = device(y, 1 - x, c, z)
    yn = device(1 - y, x, c, z)
    mine = flat(y, x, c, z)

    def unit(sub, far1, far2, zz, core):
        fx, fy = (far1, far2) if sub[2] == "x" else (far2, far1)
        return flat(1 - y if fy else y, 1 - x if fx else x, core, zz)

    def push(sub, at, send_at, role, target, pred=None, src=None):
        send(sub[1](at) if src is None else src, sub[1](at), sem.at[send_at], sem.at[role], target, pred)

    def along(sub, at, up, role, pred, src=None):
        push(sub, at, 17, role, device(y, x, c, z + 1 if up else z - 1), pred, src)

    def first(sub, at, zz, pred=None, src=None):
        push(sub, at, 18, 4 + zz, xn if sub[2] == "x" else yn, pred, src)

    def second(sub, at, far, zz, pred=None, src=None):
        push(sub, at, 19, 8 + 4 * far + zz, yn if sub[2] == "x" else xn, pred, src)

    def sibling(sub, at, pred=None, src=None):
        push(sub, at, 20, 16, sib, pred, src)

    def own():
        for sub in subs:
            along(sub, mine, True, z, z < 3, sub[0])
            along(sub, mine, False, z, z > 0, sub[0])
        for sub in subs:
            first(sub, mine, z, None, sub[0])
            second(sub, mine, 0, z, None, sub[0])
        for sub in subs:
            sibling(sub, mine, None, sub[0])

    def from_z(dist):
        for up in (True, False):
            zz = z - dist if up else z + dist
            have = (z >= dist) if up else (z <= 3 - dist)
            at = flat(y, x, c, zz)

            @pl.when(have)
            def _(up=up, zz=zz, at=at):
                await_bytes(many(each), sem.at[zz])
                for sub in subs:
                    if dist < 3:
                        along(sub, at, up, zz, (z < 3) if up else (z > 0))
                for sub in subs:
                    first(sub, at, zz)
                    second(sub, at, 0, zz)
                    sibling(sub, at)

    def from_first(k):
        zz = near(z, k)
        await_bytes(many(each), sem.at[4 + zz])
        for sub in subs:
            at = unit(sub, True, False, zz, c)
            second(sub, at, 1, zz)
            sibling(sub, at)

    def from_second(far, k):
        zz = near(z, k)
        await_bytes(many(each), sem.at[8 + 4 * far + zz])
        for sub in subs:
            sibling(sub, unit(sub, far == 1, True, zz, c))

    def finish():
        await_bytes(many(16 * each), sem.at[16])

    def drain():
        await_column_sends(many, each, sem.at[17], z)
        await_sent(many(4 * each), sem.at[18])
        await_sent(many(8 * each), sem.at[19])
        await_sent(many(16 * each), sem.at[20])

    steps = [own, lambda: from_z(1), lambda: from_first(0), lambda: from_z(2), lambda: from_first(1)]
    steps += [lambda: from_z(3), lambda: (from_first(2), from_first(3))]
    for far in range(2):
        steps += [lambda far=far, k=k: from_second(far, k) for k in range(4)]
    return steps + [finish], drain


REDUCE_SEMS = 33
TARGETS = (0, 3, 1, 2)


class Reduce:
    def __init__(self, subs, sem):
        self.subs, self.sem, self.each = subs, sem, len(subs)
        self.y, self.x, self.c, self.z = place()
        y, x, c, z = self.y, self.x, self.c, self.z
        self.sib = device(y, x, 1 - c, z)
        self.xn, self.yn = device(y, 1 - x, c, z), device(1 - y, x, c, z)

    def own(self, sub, far1, far2, zz, core):
        fx, fy = (far1, far2) if sub.dim == "x" else (far2, far1)
        cy, cx = (1 - self.y if fy else self.y), (1 - self.x if fx else self.x)
        return sub.own(flat(cy, cx, core, zz)), (cy * 2 + cx) * 4 + zz

    def coord(self, sub, far):
        here = self.x if sub.dim == "x" else self.y
        return 1 - here if far else here

    def take(self, at, buffer, count=1):
        await_bytes(buffer.at[pl.ds(0, count * self.each)], self.sem.at[at])

    def add(self, dst, *parts):
        total = dst[...].astype(jnp.float32)
        for part in parts:
            total = total + part[...].astype(jnp.float32)
        dst[...] = total.astype(dst.dtype)

    def start(self, zz):
        for far1, far2 in ((False, True), (True, True), (True, False), (False, False)):
            at = 6 * zz + (0 if far2 else 1 if far1 else 2)
            for sub in self.subs:
                src, slot = self.own(sub, far1, far2, zz, 1 - self.c)
                send(src, sub.sib.at[slot], self.sem.at[29], self.sem.at[at], self.sib)

    def start_chip(self, chip):
        cy, cx = chip // 2, chip % 2
        for zz in TARGETS:
            for sub in self.subs:
                fy, fx = (cy + self.y) % 2, (cx + self.x) % 2
                far1, far2 = (fx, fy) if sub.dim == "x" else (fy, fx)
                at = 6 * zz + (1 - far2) * (2 - far1)
                src = sub.own(flat(cy, cx, 1 - self.c, zz))
                send(src, sub.sib.at[chip * 4 + zz], self.sem.at[29], self.sem.at[at], self.sib)

    def step_a(self, zz):
        self.take(6 * zz, self.subs[0].sib, 2)
        for far1 in (False, True):
            for sub in self.subs:
                acc, slot = self.own(sub, far1, True, zz, self.c)
                self.add(acc, sub.sib.at[slot])
                slot = self.coord(sub, far1) * 4 + zz
                there = self.yn if sub.dim == "x" else self.xn
                send(acc, sub.second.at[slot], self.sem.at[30], self.sem.at[6 * zz + (3 if far1 else 4)], there)

    def step_b(self, zz):
        self.take(6 * zz + 1, self.subs[0].sib)
        self.take(6 * zz + 3, self.subs[0].second)
        for sub in self.subs:
            acc, slot = self.own(sub, True, False, zz, self.c)
            self.add(acc, sub.sib.at[slot], sub.second.at[self.coord(sub, True) * 4 + zz])
            there = self.xn if sub.dim == "x" else self.yn
            send(acc, sub.first.at[zz], self.sem.at[31], self.sem.at[6 * zz + 5], there)

    def chain(self, sub, acc, zz, up, pred):
        z = self.z
        slot = zz if up else jnp.where(z - 1 == zz, 4, zz)
        there = device(self.y, self.x, self.c, z + 1 if up else z - 1)
        send(acc, sub.chain.at[slot], self.sem.at[32], self.sem.at[24 + slot], there, pred)

    def step_c(self, zz):
        self.take(6 * zz + 2, self.subs[0].sib)
        self.take(6 * zz + 4, self.subs[0].second)
        self.take(6 * zz + 5, self.subs[0].first)
        for sub in self.subs:
            acc, slot = self.own(sub, False, False, zz, self.c)
            self.add(acc, sub.sib.at[slot], sub.second.at[self.coord(sub, False) * 4 + zz], sub.first.at[zz])
            if zz > 0:
                self.chain(sub, acc, zz, True, self.z == 0)
            if zz < 3:
                self.chain(sub, acc, zz, False, self.z == 3)

    def relay(self, zz, at, up):
        @pl.when(self.z == at)
        def _():
            self.take(24 + zz, self.subs[0].chain)
            for sub in self.subs:
                acc, _ = self.own(sub, False, False, zz, self.c)
                self.add(acc, sub.chain.at[zz])
                self.chain(sub, acc, zz, up, None)

    def step_d(self, zz):
        if zz >= 2:
            self.relay(zz, 1, True)
        else:
            self.relay(zz, 2, False)

    def step_e(self, zz):
        if zz == 3:
            self.relay(zz, 2, True)
        if zz == 0:
            self.relay(zz, 1, False)

    def finish(self):
        z = self.z
        for sub in self.subs:
            acc, _ = self.own(sub, False, False, z, self.c)
            sub.out[...] = acc[...].astype(jnp.float32)
        for pred, slot in ((z > 0, z), (z < 3, 4)):

            @pl.when(pred)
            def _(slot=slot):
                self.take(24 + slot, self.subs[0].chain)
                for sub in self.subs:
                    sub.out[...] += sub.chain[slot].astype(jnp.float32)

        for at, count in ((29, 16), (30, 8), (31, 4), (32, 3)):
            await_sent(self.subs[0].all.at[pl.ds(0, count * self.each)], self.sem.at[at])


class Waves:
    def __init__(self, groups, lags):
        self.waves = [(made, zz) for made in groups for zz in TARGETS]
        self.lags = lags
        self.at = 0

    def step(self):
        stages = (Reduce.step_a, Reduce.step_b, Reduce.step_c, Reduce.step_d, Reduce.step_e)
        for lag, stage in zip(self.lags, stages):
            k = self.at - lag
            if 0 <= k < len(self.waves):
                group, zz = self.waves[k]
                for made in group:
                    stage(made, zz)
        k = self.at - self.lags[-1] - 1
        if 0 <= k < len(self.waves) and k % 4 == 3:
            for made in self.waves[k][0]:
                made.finish()
        self.at += 1

    def left(self):
        return len(self.waves) + self.lags[-1] + 1 - self.at


def erf_of(v):
    return lax.erf(v)


def mm(a, b):
    return jnp.dot(a, b, preferred_element_type=jnp.float32)


def mm_nt(a, b):
    return lax.dot_general(a, b, (((1,), (1,)), ((), ())), preferred_element_type=jnp.float32)


def mm_tn(a, b):
    return lax.dot_general(a, b, (((0,), (0,)), ((), ())), preferred_element_type=jnp.float32)


def columns(ref, start, stop):
    block = ref[:, :, start:stop]
    return block.reshape(block.shape[0] * block.shape[1], stop - start)


def rows_of(ref, start, stop):
    block = ref[start:stop]
    return block.reshape(block.shape[0] * block.shape[1], block.shape[2])


def put_columns(ref, start, values):
    owners, share = ref.shape[0], ref.shape[1]
    ref[:, :, start : start + values.shape[1]] = values.astype(ref.dtype).reshape(
        owners, share, values.shape[1]
    )


def norm_rows(values):
    centred = values - jnp.mean(values, axis=-1, keepdims=True)
    inv_scale = lax.rsqrt(jnp.mean(centred * centred, axis=-1, keepdims=True) + norm_epsilon)
    return centred * inv_scale, inv_scale


def norm_rows_back(gradient, normed, inv_scale, gain_row):
    scaled = gradient * gain_row
    return inv_scale * (
        scaled
        - jnp.mean(scaled, axis=-1, keepdims=True)
        - normed * jnp.mean(scaled * normed, axis=-1, keepdims=True)
    )


def column_sum(values):
    return jnp.sum(values.astype(jnp.float32), axis=0, keepdims=True)


def head_forward(s, w1, w2, small, lengths):
    width = s.x.shape[1]
    spans = s.x.shape[0] // SPAN
    x = s.x[...]
    s.q[...] = (mm(x, columns(w1, 0, width)) + small(2)).astype(jnp.bfloat16)
    s.k[...] = mm(x, columns(w1, width, 2 * width)).astype(jnp.bfloat16)
    s.v[...] = (mm(x, columns(w1, 2 * width, 3 * width)) + small(3)).astype(jnp.bfloat16)
    yield
    lane = lax.broadcasted_iota(jnp.int32, (SPAN, 128), 1)
    for span in range(spans):
        keep = lax.broadcasted_iota(jnp.int32, (SPAN, 128), 1) < lengths[span]
        for pair in range(width // 128):
            at = (slice(span * SPAN, (span + 1) * SPAN), slice(pair * 128, (pair + 1) * 128))
            q, k, v = s.q[at], s.k[at], s.v[at]
            parts = []
            for side in range(2):
                here = (lane < 64) if side == 0 else (lane >= 64)
                scores = mm_nt(jnp.where(here, q, jnp.zeros_like(q)), k) * score_scale
                scores = jnp.where(keep, scores, masked_score)
                weight = jnp.exp(scores - jnp.max(scores, axis=-1, keepdims=True))
                probs = weight / jnp.sum(weight, axis=-1, keepdims=True)
                s.p[(span * 6 + pair) * 2 + side] = probs
                parts.append(mm(probs.astype(jnp.bfloat16), v))
            s.ctx[at] = jnp.where(lane < 64, parts[0], parts[1]).astype(jnp.bfloat16)
        yield
    attended = mm(s.ctx[...], columns(w1, 3 * width, 4 * width)) + small(4)
    normed, inv_scale = norm_rows(s.x[...].astype(jnp.float32) + attended)
    s.n1[...] = normed
    s.r1[...] = inv_scale
    hidden = normed * small(0) + small(5)
    s.h[...] = hidden
    s.hl[...] = hidden.astype(jnp.bfloat16)
    yield
    for part in range(4):
        pre = mm(s.hl[...], columns(w1, (4 + part) * width, (5 + part) * width)) + small(8 + part)
        half_erf = 0.5 + 0.5 * erf_of(pre * (0.5**0.5))
        s.g[part] = (pre * half_erf).astype(jnp.bfloat16)
        s.gp[part] = half_erf + pre * (jnp.exp(-0.5 * pre * pre) * (0.5 / math.pi) ** 0.5)
        yield
    branch = small(6)
    share = w2.shape[0] // 4
    for part in range(4):
        branch = branch + mm(s.g[part], rows_of(w2, part * share, (part + 1) * share))
    normed, inv_scale = norm_rows(s.h[...] + branch)
    s.n2[...] = normed
    s.r2[...] = inv_scale
    s.y[...] = (normed * small(1) + small(7)).astype(jnp.bfloat16)
    yield


def head_backward(s, w1, w2, g1, g2, small, sums, grad_in):
    width = s.x.shape[1]
    spans = s.x.shape[0] // SPAN
    grad_out = s.cot[...].astype(jnp.float32)
    sums[1:2] = column_sum(grad_out * s.n2[...])
    sums[7:8] = column_sum(grad_out)
    pre_two = norm_rows_back(grad_out, s.n2[...], s.r2[...], small(1))
    s.h[...] = pre_two
    branch = pre_two.astype(jnp.bfloat16)
    s.dz[...] = branch
    sums[6:7] = column_sum(branch)
    yield
    owners = w2.shape[0]
    share = owners // 4
    for part in range(4):
        own = slice(part * share, (part + 1) * share)
        grad_act = mm_nt(s.dz[...], rows_of(w2, part * share, (part + 1) * share))
        grad_pre = (grad_act * s.gp[part]).astype(jnp.bfloat16)
        g2[own] = (
            mm_tn(s.g[part], s.dz[...]).astype(jnp.bfloat16).reshape(share, g2.shape[1], width)
        )
        s.g[part] = grad_pre
        sums[8 + part : 9 + part] = column_sum(grad_pre)
        yield
    for part in range(4):
        at = (4 + part) * width
        grad_pre = s.g[part]
        s.h[...] += mm_nt(grad_pre, columns(w1, at, at + width))
        put_columns(g1, at, mm_tn(s.hl[...], grad_pre))
        yield
    grad_hidden = s.h[...]
    sums[0:1] = column_sum(grad_hidden * s.n1[...])
    sums[5:6] = column_sum(grad_hidden)
    pre_one = norm_rows_back(grad_hidden, s.n1[...], s.r1[...], small(0))
    s.h[...] = pre_one
    attended = pre_one.astype(jnp.bfloat16)
    s.dz[...] = attended
    sums[4:5] = column_sum(attended)
    yield
    s.hl[...] = mm_nt(attended, columns(w1, 3 * width, 4 * width)).astype(jnp.bfloat16)
    put_columns(g1, 3 * width, mm_tn(s.ctx[...], attended))
    yield
    lane = lax.broadcasted_iota(jnp.int32, (SPAN, 128), 1)
    for span in range(spans):
        for pair in range(width // 128):
            at = (slice(span * SPAN, (span + 1) * SPAN), slice(pair * 128, (pair + 1) * 128))
            q, k, v, dc = s.q[at], s.k[at], s.v[at], s.hl[at]
            dq, dk, dv = [], [], []
            for side in range(2):
                here = (lane < 64) if side == 0 else (lane >= 64)
                probs = s.p[(span * 6 + pair) * 2 + side]
                grad_probs = mm_nt(jnp.where(here, dc, jnp.zeros_like(dc)), v)
                dv.append(mm_tn(probs.astype(jnp.bfloat16), dc))
                grad_scores = probs * (
                    grad_probs - jnp.sum(probs * grad_probs, axis=-1, keepdims=True)
                )
                grad_scores = grad_scores.astype(jnp.bfloat16)
                dq.append(mm(grad_scores, k))
                dk.append(mm_tn(grad_scores, q))
            join = lambda two: jnp.where(lane < 64, two[0], two[1])
            s.q[at] = (join(dq) * score_scale).astype(jnp.bfloat16)
            s.k[at] = (join(dk) * score_scale).astype(jnp.bfloat16)
            s.v[at] = join(dv).astype(jnp.bfloat16)
        yield
    sums[2:3] = column_sum(s.q[...])
    sums[3:4] = column_sum(s.v[...])
    total = s.h[...]
    for k, ref in enumerate((s.q, s.k, s.v)):
        total = total + mm_nt(ref[...], columns(w1, k * width, (k + 1) * width))
    grad_in[...] = total
    yield
    for k, ref in enumerate((s.q, s.k, s.v)):
        put_columns(g1, k * width, mm_tn(s.x[...], ref[...]))
    yield


HIGHEST = lax.Precision.HIGHEST
ROWS = 16


def iota(shape, axis):
    return lax.broadcasted_iota(jnp.int32, shape, axis)


def ones_where(condition, dtype):
    return jnp.where(condition, 1.0, 0.0).astype(dtype)


def exact(a, b, dims):
    return lax.dot_general(
        a, b, (dims, ((), ())), precision=HIGHEST, preferred_element_type=jnp.float32
    )


class Plane:
    def __init__(self, sem):
        self.sem = sem
        self.wide, self.z = lax.axis_index("wide"), lax.axis_index("narrow")
        self.sent = []

    def send(self, index, src, recv):
        for k in range(1, 8):
            peer = (self.wide + k) % 8
            send(src(peer), recv.at[self.wide], self.sem.at[index, 0], self.sem.at[index, 1], (peer, self.z))
        self.sent.append((index, recv))

    def arrive(self, index, recv):
        await_bytes(recv.at[pl.ds(0, 7)], self.sem.at[index, 1])

    def drain(self):
        for index, recv in self.sent:
            await_sent(recv.at[pl.ds(0, 7)], self.sem.at[index, 0])

    def total(self, index, recv):
        self.arrive(index, recv)
        total = recv[0].astype(jnp.float32)
        for k in range(1, 8):
            total = total + recv[k].astype(jnp.float32)
        return total

    def place_rows(self, two):
        row = iota((ROWS, two.shape[1]), 0)
        rows = jnp.where(row % 2 == 0, two[0:1], two[1:2])
        return jnp.where(row // 2 == self.wide, rows, 0.0)

    def pick_rows(self, values, first):
        row = iota(values.shape, 0)
        one = lambda k: jnp.sum(jnp.where(row == first + k, values, 0.0), axis=0, keepdims=True)
        return jnp.concatenate([one(0), one(1)], axis=0)

    def share(self, index, two, src, recv):
        placed = self.place_rows(two).astype(src.dtype)
        src[...] = placed
        recv[self.wide] = placed
        self.send(index, lambda peer: src, recv)

    def collect(self, index, values, src, recv):
        for k in range(2):
            src[k] = values[8 * k : 8 * k + 8]
        recv[self.wide] = jnp.where(self.wide // 4 == 0, values[0:8], values[8:16])
        self.send(index, lambda peer: src.at[peer // 4], recv)

    def collected(self, index, recv):
        return self.pick_rows(self.total(index, recv), 2 * (self.wide % 4))


def backbone_forward(s, plane, small, finish):
    x0, w0 = s.x0, s.w0
    width = x0.shape[1]
    spans = x0.shape[0] // SPAN
    wide = plane.wide
    x = x0[...]
    s.k0[...] = mm(x, columns(w0, width, 2 * width)).astype(jnp.bfloat16)
    s.v0[...] = (mm(x, columns(w0, 2 * width, 3 * width)) + small(3)).astype(jnp.bfloat16)
    first = jnp.concatenate(
        [x0[SPAN * span : SPAN * span + 1].astype(jnp.float32) for span in range(spans)], axis=0
    )
    query = mm(first.astype(jnp.bfloat16), columns(w0, 0, width)) + small(2)
    s.keep[0, 0:spans] = first
    s.keep[1, 0:spans] = query.astype(jnp.bfloat16).astype(jnp.float32)
    yield
    heads = ones_where(iota((width, 128), 0) // (width // HEADS) == iota((width, 128), 1), jnp.bfloat16)
    context = []
    for span in range(spans):
        at = slice(span * SPAN, (span + 1) * SPAN)
        product = s.k0[at].astype(jnp.float32) * s.keep[1, span : span + 1]
        scores = exact(product, heads.astype(jnp.float32), ((1,), (0,))) * score_scale
        scores = jnp.where(iota(scores.shape, 0) < s.lengths[span], scores, masked_score)
        weight = jnp.exp(scores - jnp.max(scores, axis=0, keepdims=True))
        probs = weight / jnp.sum(weight, axis=0, keepdims=True)
        s.p0[span] = probs
        spread = mm_nt(probs.astype(jnp.bfloat16), heads)
        context.append(jnp.sum(spread * s.v0[at].astype(jnp.float32), axis=0, keepdims=True))
    context = jnp.concatenate(context, axis=0).astype(jnp.bfloat16)
    s.keep[2, 0:spans] = context.astype(jnp.float32)
    attended = mm(context, columns(w0, 3 * width, 4 * width)) + small(4)
    normed, inv_scale = norm_rows(s.keep[0, 0:spans] + attended)
    hidden = normed * small(0) + small(5)
    s.keep[3, 0:spans] = normed
    s.keep[4, 0:spans] = jnp.broadcast_to(inv_scale, normed.shape)
    s.keep[5, 0:spans] = hidden
    plane.share(0, hidden, s.e0_src, s.e0)
    yield
    hidden_all = plane.total(0, s.e0).astype(jnp.bfloat16)
    share = width // 8
    pick = ones_where(iota((width, share), 0) == share * wide + iota((width, share), 1), jnp.bfloat16)
    own = mm(hidden_all, pick).astype(jnp.bfloat16)
    upz = s.upz
    part = upz.shape[2] // 8
    for k in range(8):
        s.e1_src[k] = mm(own, columns(upz, k * part, (k + 1) * part))
    s.e1[wide] = s.e1_src[wide]
    plane.send(1, lambda peer: s.e1_src.at[peer], s.e1)
    yield
    bias = jnp.where(wide % 2 == 0, small(8 + wide // 2)[:, :part], small(8 + wide // 2)[:, part:])
    pre = plane.total(1, s.e1) + bias
    half_erf = 0.5 + 0.5 * erf_of(pre * (0.5**0.5))
    s.g0[...] = (pre * half_erf).astype(jnp.bfloat16)
    s.gp0[...] = half_erf + pre * (jnp.exp(-0.5 * pre * pre) * (0.5 / math.pi) ** 0.5)
    plane.collect(2, mm(s.g0[...], rows_of(s.downz, 0, 4)), s.e2_src, s.e2)
    yield
    branch = plane.collected(2, s.e2) + small(6)
    normed, inv_scale = norm_rows(s.keep[5, 0:spans] + branch)
    s.keep[6, 0:spans] = normed
    s.keep[7, 0:spans] = jnp.broadcast_to(inv_scale, normed.shape)
    finish(normed * small(1) + small(7))
    yield


def backbone_backward(s, plane, small, grad_rows):
    x0, w0 = s.x0, s.w0
    width = x0.shape[1]
    spans = x0.shape[0] // SPAN
    wide = plane.wide
    keep = lambda k: s.keep[k, 0:spans]
    acts, sums = s.acts, s.sums0

    def put(item, values):
        for span in range(spans):
            row = span * ROWS + item
            acts[row : row + 1] = values[span : span + 1]

    acts[...] = jnp.zeros_like(acts)
    grad_out = grad_rows()
    sums[1:2] = column_sum(grad_out * keep(6))
    sums[7:8] = column_sum(grad_out)
    pre_two = norm_rows_back(grad_out, keep(6), keep(7), small(1))
    s.keep[8, 0:spans] = pre_two
    low = lambda a: a.astype(jnp.bfloat16).astype(jnp.float32)
    put(11, low(pre_two))
    plane.share(3, pre_two, s.e3_src, s.e3)
    yield
    branch = plane.total(3, s.e3).astype(jnp.bfloat16)
    grad_act = mm_nt(branch, rows_of(s.downz, 0, 4))
    part = s.g0.shape[1]
    s.e4_src[:, :part] = (grad_act * s.gp0[...]).astype(jnp.bfloat16)
    s.e4_src[:, part:] = s.g0[...]
    s.e4[wide] = s.e4_src[...]
    plane.send(4, lambda peer: s.e4_src, s.e4)
    yield
    plane.arrive(4, s.e4)
    total = jnp.zeros((ROWS, width // 8), jnp.float32)
    for k in range(8):
        both = s.e4[k]
        total = total + mm_nt(both[:, :part], columns(s.upz, k * part, (k + 1) * part))
        rows = plane.pick_rows(both.astype(jnp.float32), 2 * wide)
        at = slice((k % 2) * part, (k % 2 + 1) * part)
        for span in range(spans):
            row = span * ROWS + 3 + k // 2
            acts[row : row + 1, at] = rows[span : span + 1, :part]
            acts[row + 4 : row + 5, at] = rows[span : span + 1, part:]
    share = width // 8
    pick = ones_where(iota((width, share), 0) == share * wide + iota((width, share), 1), jnp.float32)
    plane.collect(5, exact(total, pick, ((1,), (1,))), s.e5_src, s.e5)
    yield
    grad_hidden = keep(8) + plane.collected(5, s.e5)
    sums[0:1] = column_sum(grad_hidden * keep(3))
    sums[5:6] = column_sum(grad_hidden)
    pre_one = norm_rows_back(grad_hidden, keep(3), keep(4), small(0))
    attended = pre_one.astype(jnp.bfloat16)
    context = low(mm_nt(attended, columns(w0, 3 * width, 4 * width)))
    heads = ones_where(iota((width, 128), 0) // (width // HEADS) == iota((width, 128), 1), jnp.bfloat16)
    queries = []
    for span in range(spans):
        at = slice(span * SPAN, (span + 1) * SPAN)
        probs = s.p0[span]
        grad_context = context[span : span + 1]
        product = s.v0[at].astype(jnp.float32) * grad_context
        grad_probs = exact(product, heads.astype(jnp.float32), ((1,), (0,)))
        grad_scores = probs * (grad_probs - jnp.sum(probs * grad_probs, axis=0, keepdims=True))
        spread = mm_nt(grad_scores.astype(jnp.bfloat16), heads) * score_scale
        queries.append(jnp.sum(spread * s.k0[at].astype(jnp.float32), axis=0, keepdims=True))
        s.k0[at] = (spread * s.keep[1, span : span + 1]).astype(jnp.bfloat16)
        s.v0[at] = (mm_nt(probs.astype(jnp.bfloat16), heads) * grad_context).astype(jnp.bfloat16)
    queries = jnp.concatenate(queries, axis=0).astype(jnp.bfloat16)
    sums[3:4] = column_sum(s.v0[...])
    put(0, keep(2))
    put(1, attended.astype(jnp.float32))
    put(2, low(keep(5)))
    put(12, keep(0))
    put(13, queries.astype(jnp.float32))
    s.acts_low[...] = acts[...].astype(jnp.bfloat16)
    s.keep[9, 0:spans] = pre_one + mm_nt(queries, columns(w0, 0, width))
    yield
    grad_in = s.embeds_grad
    grad_in[...] = mm_nt(s.k0[...], columns(w0, width, 2 * width))
    grad_in[...] += mm_nt(s.v0[...], columns(w0, 2 * width, 3 * width))
    for span in range(spans):
        grad_in[SPAN * span : SPAN * span + 1] += s.keep[9, span : span + 1]
    put_columns(w0, width, mm_tn(x0[...], s.k0[...]))
    put_columns(w0, 2 * width, mm_tn(x0[...], s.v0[...]))
    yield


def backbone_weight_grads(s, at, o1, o2, small_out):
    width = s.x0.shape[1]
    gathered = s.g[...].reshape(-1, width)
    spans = 64

    def item(k):
        shape = (spans, gathered.shape[0])
        row, column = iota(shape, 0), iota(shape, 1)
        pick = column == (row // 2) * 32 + (row % 2) * ROWS + k
        return mm(ones_where(pick, jnp.bfloat16), gathered)

    share = width // 32
    shape = (width, 128)

    def picker(count, offset, dtype):
        row, column = iota(shape, 0), iota(shape, 1)
        return ones_where((row + offset == count * at + column) & (column < count), dtype)

    narrow = picker(share, 0, jnp.bfloat16)
    own = lambda k: mm(item(k).astype(jnp.bfloat16), narrow).astype(jnp.bfloat16)
    grad_query = item(13)
    o1[0, :, 0:width] = mm_tn(own(12), grad_query.astype(jnp.bfloat16))[:share]
    grad_attended = item(1)
    o1[0, :, 3 * width : 4 * width] = mm_tn(own(0), grad_attended.astype(jnp.bfloat16))[:share]
    branch = item(11)
    hidden = own(2)
    wide_sum = jnp.zeros((1, 128), jnp.float32)
    act = jnp.zeros((spans, 128), jnp.float32)
    for part in range(4):
        grad_pre = item(3 + part)
        o1[0, :, (4 + part) * width : (5 + part) * width] = mm_tn(hidden, grad_pre.astype(jnp.bfloat16))[:share]
        act = act + mm(item(7 + part).astype(jnp.bfloat16), picker(4 * share, part * width, jnp.bfloat16))
        wide_sum = wide_sum + exact(
            column_sum(grad_pre), picker(4 * share, part * width, jnp.float32), ((1,), (0,))
        )
    o2[0] = mm_tn(act.astype(jnp.bfloat16), branch.astype(jnp.bfloat16))[: 4 * share]
    exact_narrow = picker(share, 0, jnp.float32)
    s.late[...] = jnp.zeros_like(s.late)
    for row, values in ((2, grad_query), (4, grad_attended), (6, branch)):
        s.late[row : row + 1] = exact(column_sum(values), exact_narrow, ((1,), (0,)))
    small_out[8:9] = wide_sum


def step_kernel(
    qkv_in, out_in, up_in, down_in, up_bias, gains, biases, x0_in, skip_in, cot_in, lengths, y_out, embeds_out,
    skip_out, o1, o2, small_out, acts_all, *scratch,
):
    s = Refs(lengths=lengths)
    for (name, _, _), ref in zip(step_scratch(x0_in.shape[1]), scratch):
        setattr(s, name, ref)
    x0, skip, skip_grad = s.x0, s.skip, s.skip_grad
    gather_sem, column_sem, reduce_sem, plane_sem, load_sem = scratch[-5:]
    width = x0.shape[1]
    spans = x0.shape[0] // SPAN
    y, x, c, z = place()
    wide = lax.axis_index("wide")
    me = flat(y, x, c, z)
    w0, w1, w2, upz, downz, pars = s.w0, s.w1, s.w2, s.upz, s.downz, s.pars
    loads = [
        pltpu.make_async_copy(src, dst, load_sem.at[k])
        for k, (src, dst) in enumerate(
            (
                (qkv_in, o1.at[:, :, : 3 * width]), (out_in, o1.at[:, :, 3 * width : 4 * width]),
                (up_in, o1.at[:, :, 4 * width :]), (down_in, o2), (x0_in, x0), (skip_in, skip), (cot_in, s.cot),
            )
        )
    ]
    for load in loads:
        load.start()
    greet(wide, z)
    for load in loads[:4]:
        load.wait()
    w0[me] = o1[0, :, : 4 * width].astype(jnp.bfloat16)
    w1[me] = o1[1].astype(jnp.bfloat16)
    w2[me] = o2[1].astype(jnp.bfloat16)
    upz[z] = o1[0, :, 4 * width :].astype(jnp.bfloat16)
    downz[z] = o2[0].astype(jnp.bfloat16)
    s.small_all[me] = jnp.zeros((2 * ROWS, 128), jnp.float32)
    for layer in range(2):
        r, share = ROWS * layer, width // 32
        s.small_all[me, r : r + 2, :share] = gains[layer]
        s.small_all[me, r + 2 : r + 8, :share] = biases[:, layer]
        s.small_all[me, r + 8 : r + 9, : 4 * share] = up_bias[layer : layer + 1]

    half, mid = 2 * width, w2.shape[1] // 2

    def column_pair(ref, start):
        cut = lambda at: (lambda u: ref.at[u, :, at : at + half])
        subs = [(None, cut(start), "x"), (None, cut(start + half), "y")]
        return subs, lambda n: ref.at[pl.ds(0, n), :, start : start + half]

    rows_cut = lambda at: (lambda u: w2.at[u, at : at + mid])
    sets = [
        ([(None, lambda u: s.small_all.at[u], "x")], lambda n: s.small_all.at[pl.ds(0, n)]),
        column_pair(w0, 0),
        column_pair(w1, 0),
        column_pair(w1, 2 * half),
        ([(None, rows_cut(0), "x"), (None, rows_cut(mid), "y")], lambda n: w2.at[pl.ds(0, n), :mid]),
    ]
    events = []
    drains = []
    for k, (subs, many) in enumerate(sets):
        steps, drain = gather_steps(subs, many, gather_sem.at[k])
        drains.append(drain)
        for step, action in enumerate(steps):
            events.append((SET_AT[k][step], action))
    steps, drain = column_steps(
        [lambda zz: upz.at[zz], lambda zz: downz.at[zz]],
        [lambda n: w1.at[pl.ds(0, n), :, : 2 * half], lambda n: w2.at[pl.ds(0, n)]],
        column_sem,
    )
    drains.append(drain)
    events += zip(COLUMN_AT, steps)

    def row_of(layer):
        return lambda k: pars[pl.ds(ROWS * layer + k, 1), :]

    def unpack():
        share = width // 32
        for layer in range(2):
            r = ROWS * layer
            for d in range(32):
                pars[r : r + 8, share * d : share * (d + 1)] = s.small_all[d, r : r + 8, :share]
                at = slice((d % 8) * 4 * share, (d % 8 + 1) * 4 * share)
                pars[r + 8 + d // 8 : r + 9 + d // 8, at] = s.small_all[d, r + 8 : r + 9, : 4 * share]
        pars[...] = pars[...].astype(jnp.bfloat16).astype(jnp.float32)

    def join(rows):
        row = iota(skip.shape, 0)
        joined = skip[...].astype(jnp.float32)
        for span in range(spans):
            joined = jnp.where(row == SPAN * span, rows[span : span + 1], joined)
        s.x[...] = joined.astype(jnp.bfloat16)

    def unload():
        for load in loads[4:]:
            load.wait()

    outs = []

    def put_out(src, dst):
        copy = pltpu.make_async_copy(src, dst, load_sem.at[len(outs)])
        copy.start()
        outs.append(copy)

    events += [(UNPACK_AT, unload)]
    plane = Plane(plane_sem)
    forward0 = backbone_forward(s, plane, row_of(0), join)
    forward1 = head_forward(s, w1, w2, row_of(1), lengths)
    events += [(UNPACK_AT, unpack)]
    events += [(at, lambda: next(forward0)) for at in FORWARD0_AT]
    events += [(at, lambda: next(forward1)) for at in FORWARD1_AT]
    for _, action in sorted(events, key=lambda event: event[0]):
        action()
    for drain in drains:
        drain()
    put_out(s.y, y_out)

    back1 = head_backward(s, w1, w2, w1, w2, row_of(1), s.sums, skip_grad)
    back0 = backbone_backward(
        s, plane, row_of(0),
        lambda: jnp.concatenate([skip_grad[SPAN * k : SPAN * k + 1] for k in range(spans)], axis=0),
    )

    def reduced(whole, own, out, name, dim):
        bufs = [getattr(s, name + kind) for kind in KINDS]
        return Refs(all=whole, own=own, out=out, dim=dim, sib=bufs[0], second=bufs[1], first=bufs[2], chain=bufs[3])

    def pair(ref, start, stop, out, name):
        middle = (start + stop) // 2
        cut = lambda a, b: (ref.at[:, :, a:b], lambda u: ref.at[u, :, a:b], out.at[:, a:b])
        return [
            reduced(*cut(start, middle), name + "a", "x"),
            reduced(*cut(middle, stop), name + "b", "y"),
        ]

    made = iter(range(6))
    group = lambda *subs: Reduce(subs, reduce_sem.at[next(made)])
    cut = lambda a, b: (w2.at[:, a:b], lambda u: w2.at[u, a:b], o2.at[1, a:b])
    downs = [group(reduced(*cut(0, mid), "da", "x"), reduced(*cut(mid, 2 * mid), "db", "y"))]
    ups = [group(*pair(w1, 4 * width, 8 * width, o1.at[1], "u"))]
    lefts = [
        group(*pair(w1, 0, 4 * width, o1.at[1], "q")),
        group(reduced(s.block1, lambda u: s.block1.at[u], small_out.at[ROWS : 2 * ROWS], "s1", "x")),
    ]
    kvs = [
        group(*pair(w0, width, 3 * width, o1.at[0], "k")),
        group(reduced(s.block0, lambda u: s.block0.at[u], small_out.at[0:8], "s0", "y")),
    ]
    waves = Waves([downs, ups, lefts, kvs], LAGS)

    def start(groups):
        for zz in TARGETS:
            for each in groups:
                each.start(zz)

    def fill_blocks(block, sums, wide_too):
        share = width // 32
        block[...] = jnp.zeros_like(block)
        for d in range(32):
            block[d, 0:8, :share] = sums[0:8, share * d : share * (d + 1)]
            if wide_too:
                at = slice((d % 8) * 4 * share, (d % 8 + 1) * 4 * share)
                block[d, 8:9, : 4 * share] = sums[8 + d // 8 : 9 + d // 8, at]

    def step(times):
        for _ in range(times):
            waves.step()

    next(back1)
    for chip in range(4):
        next(back1)
        for each in downs:
            each.start_chip(chip)
    next(back1)
    next(back1)
    step(STEPS[0])
    next(back1)
    next(back1)
    step(STEPS[1])
    next(back1)
    start(ups)
    next(back1)
    step(STEPS[2])
    next(back1)
    step(STEPS[3])
    next(back1)
    step(STEPS[4])
    next(back1)
    next(back0)
    step(STEPS[5])
    next(back1)
    fill_blocks(s.block1, s.sums, True)
    start(lefts)
    next(back0)
    step(STEPS[6])
    next(back0)
    step(STEPS[7])
    next(back0)
    home = lambda u: acts_all.at[u // 8, pl.ds(pl.multiple_of((u % 8) * 32, 32), 32)]
    own_acts = pltpu.make_async_copy(s.acts_low, home(me), load_sem.at[5])
    own_acts.start()
    rows = lambda n: acts_all.at[pl.ds(0, n // 16)] if n >= 16 else acts_all.at[0, pl.ds(0, ROWS * n)]
    part = lambda k: (lambda u: home(u).at[pl.ds(ROWS * k, ROWS)])
    spread, drain = gather_steps(
        [(s.acts_low.at[pl.ds(ROWS * k, ROWS)], part(k), dim) for k, dim in enumerate("xy")], rows, gather_sem.at[5]
    )
    spread[0]()
    next(back0)
    fill_blocks(s.block0, s.sums0, False)
    start(kvs)
    row = iota(skip_grad.shape, 0)
    skip_grad[...] = jnp.where(row % SPAN == 0, 0.0, skip_grad[...])
    put_out(skip_grad, skip_out)
    put_out(s.embeds_grad, embeds_out)
    left = waves.left()
    turns = left - TAIL
    for k in range(left):
        waves.step()
        if k < turns:
            for action in spread[1 + 15 * k // turns : 1 + 15 * (k + 1) // turns]:
                action()
        if k == turns - 1:
            own_acts.wait()
            load = pltpu.make_async_copy(acts_all, s.g, load_sem.at[6])
            load.start()
            load.wait()
            backbone_weight_grads(s, me, o1, o2, small_out)
    small_out[0:8] += s.late[...]
    drain()
    plane.drain()
    for copy in outs:
        copy.wait()


SET_AT = ((0, 1, 2, 3, 4, 5, 6, 7, 8, 9, 10, 11, 12, 13, 14, 15), (0, 1, 2, 3, 4, 5, 6, 7, 8, 9, 10, 11, 12, 13, 14, 15), (1.2, 8, 9, 10, 11, 12, 13, 15, 16, 17, 18, 19, 20, 21, 22, 23), (3.2, 14, 15, 16, 17, 18, 19, 22, 23, 24, 25, 26, 27, 28, 29, 30), (5.2, 20, 21, 22, 23, 24, 25, 28.0, 28.7, 29.4, 30.1, 30.8, 31.5, 32.2, 32.9, 33.6))
UNPACK_AT = 15.05
COLUMN_AT = (2.5, 4.5, 6.5, 8.5)
FORWARD0_AT = (15.3, 16.2, 18, 20, 22)
FORWARD1_AT = (23.1, 23.9, 24.7, 25.34, 30.1, 30.9, 31.7, 32.5, 33.7)
LAGS = (0, 1, 2, 3, 4)
STEPS = (1, 1, 1, 1, 1, 1, 1, 1)
TAIL = 2
KINDS = ("sib", "second", "first", "chain")


def step_scratch(width):
    low, full = jnp.bfloat16, jnp.float32
    share = width // 32
    rows = 2 * SPAN
    found = [
        ("w0", (32, share, 4 * width), low), ("upz", (4, share, 4 * width), low),
        ("downz", (4, 4 * share, width), low), ("w1", (32, share, 8 * width), low),
        ("w2", (32, 4 * share, width), low), ("small_all", (32, 2 * ROWS, 128), full),
        ("pars", (2 * ROWS, width), full), ("sums", (ROWS, width), full), ("sums0", (8, width), full),
        ("keep", (ROWS, 8, width), full), ("p0", (2, SPAN, 128), full),
        ("g0", (ROWS, width // 2), low), ("gp0", (ROWS, width // 2), full),
        ("e0_src", (ROWS, width), low), ("e0", (8, ROWS, width), low),
        ("e1_src", (8, ROWS, width // 2), full), ("e1", (8, ROWS, width // 2), full),
        ("e2_src", (2, 8, width), full), ("e2", (8, 8, width), full),
        ("e3_src", (ROWS, width), low), ("e3", (8, ROWS, width), low),
        ("e4_src", (ROWS, width), low), ("e4", (8, ROWS, width), low),
        ("e5_src", (2, 8, width), full), ("e5", (8, 8, width), full),
        ("acts", (2 * ROWS, width), full), ("acts_low", (2 * ROWS, width), low),
        ("late", (8, 128), full), ("block1", (32, ROWS, 128), full), ("block0", (32, 8, 128), full),
        ("g", (4, rows, width), low), ("gp", (4, rows, width), full),
        ("p", (2 * HEADS, SPAN, SPAN), full), ("r1", (rows, 1), full), ("r2", (rows, 1), full),
    ]
    found += [(name, (rows, width), low) for name in ("x", "q", "k", "v", "ctx", "hl", "dz", "k0", "v0", "x0", "skip", "cot", "y")]
    found += [(name, (rows, width), full) for name in ("n1", "h", "n2", "skip_grad", "embeds_grad")]
    shapes = {
        "d": ((2 * share, width), low), "u": ((share, 2 * width), low), "q": ((share, 2 * width), low),
        "k": ((share, width), low),
    }
    blocks = [(name + side, shape) for name, shape in shapes.items() for side in "ab"]
    blocks += [("s1", ((ROWS, 128), full)), ("s0", ((8, 128), full))]
    for name, (shape, dtype) in blocks:
        for kind, many in zip(KINDS, (16, 8, 4, 5)):
            found.append((name + kind, (many,) + shape, dtype))
    return found


def step_call(params, embeds, skip_tokens, cotangent, lengths):
    vmem, hbm = pl.BlockSpec(memory_space=pltpu.VMEM), pl.BlockSpec(memory_space=pl.ANY)
    rows, width = embeds.shape
    share = width // 32
    scratch = [pltpu.VMEM(shape, dtype) for _, shape, dtype in step_scratch(width)]
    scratch += [
        pltpu.SemaphoreType.DMA((6, GATHER_SEMS)),
        pltpu.SemaphoreType.DMA((2, 5)),
        pltpu.SemaphoreType.DMA((6, REDUCE_SEMS)),
        pltpu.SemaphoreType.DMA((6, 2)),
        pltpu.SemaphoreType.DMA((7,)),
    ]
    shape = jax.ShapeDtypeStruct
    return pl.pallas_call(
        step_kernel,
        out_shape=[
            shape((rows, width), jnp.bfloat16), shape((rows, width), jnp.float32),
            shape((rows, width), jnp.float32), shape((2, share, 8 * width), jnp.float32),
            shape((2, 4 * share, width), jnp.float32), shape((2 * ROWS, 128), jnp.float32),
            shape((4, rows, width), jnp.bfloat16),
        ],
        in_specs=[hbm] * 4 + [vmem] * 3 + [hbm] * 3 + [pl.BlockSpec(memory_space=pltpu.SMEM)],
        out_specs=[hbm] * 3 + [vmem] * 3 + [hbm],
        scratch_shapes=scratch,
        compiler_params=pltpu.CompilerParams(
            collective_id=1, has_side_effects=True, vmem_limit_bytes=64 * 2**20
        ),
    )(*params, embeds, skip_tokens, cotangent, lengths)


def adam_parts(parameter, first, second, gradient, decayed):
    first = beta_first * first + (1.0 - beta_first) * gradient
    second = beta_second * second + (1.0 - beta_second) * gradient * gradient
    update = first / first_fix / (jnp.sqrt(second / second_fix) + adam_epsilon)
    if decayed:
        update = update + weight_decay * parameter
    return update, first, second


def adam_kernel(*refs):
    params, moments = refs[0:7], refs[7:14]
    joined, down, small = refs[14:17]
    passed, steps, news, handed = refs[17:20], refs[20:27], refs[27:34], refs[34:37]

    def update(index, gradient):
        step, first, second = adam_parts(
            params[index][...], moments[index][0], moments[index][1], gradient, index < 4
        )
        steps[index][...] = step
        news[index][0] = first
        news[index][1] = second

    qkv, out = params[0].shape[2], params[1].shape[2]
    update(0, joined[:, :, :qkv])
    update(1, joined[:, :, qkv : qkv + out])
    update(2, joined[:, :, qkv + out :])
    update(3, down[...])

    @pl.when(pl.program_id(1) == 0)
    def _():
        for src, dst in zip(passed, handed):
            dst[...] = src[...]

    @pl.when((pl.program_id(0) == 0) & (pl.program_id(1) == 0))
    def _():
        many = small.shape[0] // 2
        for layer in range(2):
            at = layer * many
            for index, start, stop in ((4, 8, 9), (5, 0, 2), (6, 2, 8)):
                width = params[index].shape[-1]
                here = (slice(layer, layer + 1),) if index == 4 else (layer,)
                here = here if index < 6 else (slice(None), layer)
                step, first, second = adam_parts(
                    params[index][here], moments[index][(0, *here)], moments[index][(1, *here)],
                    small[at + start : at + stop, :width], False,
                )
                steps[index][here] = step
                news[index][(0, *here)] = first
                news[index][(1, *here)] = second


def adam_update(params, moments, joined, down, small, passed):
    cuts = 3 if params[0].shape[1] % 24 == 0 else 1

    def whole(a):
        return pl.BlockSpec(a.shape, lambda l, r, n=a.ndim: (0,) * n)

    def rows(a):
        return pl.BlockSpec((1, a.shape[1] // cuts, a.shape[2]), lambda l, r: (l, r, 0))

    def pairs(a):
        return pl.BlockSpec((2, 1, a.shape[2] // cuts, a.shape[3]), lambda l, r: (0, l, r, 0))

    halves = [pl.BlockSpec((a.shape[0] // 2, a.shape[1]), lambda l, r: (l, 0)) for a in passed]
    param_specs = [rows(a) for a in params[:4]] + [whole(a) for a in params[4:]]
    moment_specs = [pairs(a) for a in moments[:4]] + [whole(a) for a in moments[4:]]
    shape = lambda a: jax.ShapeDtypeStruct(a.shape, a.dtype)
    out = pl.pallas_call(
        adam_kernel,
        grid=(2, cuts),
        out_shape=[shape(a) for a in (*params, *moments, *passed)],
        in_specs=param_specs + moment_specs + [rows(joined), rows(down), whole(small)] + halves,
        out_specs=param_specs + moment_specs + halves,
        compiler_params=pltpu.CompilerParams(vmem_limit_bytes=63 * 2**20),
    )(*params, *moments, joined, down, small, *passed)
    return out[:7], out[7:14], out[14:]


def first_forward(weights, inputs, key_valid):
    qkv_w, out_w, up_w, down_w, up_b, gain_rows, biases = weights
    row_count, width = inputs.shape
    span_count = row_count // SPAN
    first = inputs.reshape(span_count, SPAN, width)[:, 0]
    mixed = jnp.dot(inputs, qkv_w[:, width:], preferred_element_type=jnp.float32)
    keys = mixed[:, :width].astype(jnp.bfloat16).reshape(span_count, SPAN, HEADS, width // HEADS)
    values = (mixed[:, width:] + biases[1]).astype(jnp.bfloat16)
    values = values.reshape(span_count, SPAN, HEADS, width // HEADS)
    queries = jnp.dot(first, qkv_w[:, :width], preferred_element_type=jnp.float32) + biases[0]
    queries = queries.astype(jnp.bfloat16).reshape(span_count, HEADS, width // HEADS)
    scores = (
        jnp.einsum("bhe,bkhe->bhk", queries, keys, preferred_element_type=jnp.float32) * score_scale
    )
    scores = jnp.where(key_valid[:, None, :], scores, masked_score)
    probs = jax.nn.softmax(scores, axis=-1)
    context = jnp.einsum(
        "bhk,bkhe->bhe", probs.astype(jnp.bfloat16), values, preferred_element_type=jnp.float32
    )
    context = context.reshape(span_count, width).astype(jnp.bfloat16)
    attended = jnp.dot(context, out_w, preferred_element_type=jnp.float32) + biases[2]
    hidden, normed_one, scale_one = normalize(
        first.astype(jnp.float32) + attended, gain_rows[0], biases[3]
    )
    hidden_low = hidden.astype(jnp.bfloat16)
    pre_gelu = jnp.dot(hidden_low, up_w, preferred_element_type=jnp.float32) + up_b
    activated = jax.nn.gelu(pre_gelu, approximate=False).astype(jnp.bfloat16)
    branch_out = jnp.dot(activated, down_w, preferred_element_type=jnp.float32) + biases[4]
    output, normed_two, scale_two = normalize(hidden + branch_out, gain_rows[1], biases[5])
    saved = (
        first, queries, keys, values, probs, context, normed_one, scale_one, hidden_low, pre_gelu,
        activated, normed_two, scale_two,
    )
    return output, saved


def first_backward(weights, inputs, saved, grad_out):
    qkv_w, out_w, up_w, down_w, up_b, gain_rows, biases = weights
    (
        first, queries, keys, values, probs, context, normed_one, scale_one, hidden_low, pre_gelu,
        activated, normed_two, scale_two,
    ) = saved
    row_count, width = inputs.shape
    span_count = row_count // SPAN
    grad_pre_two, grad_gain_two, grad_shift_two = normalize_back(
        grad_out, normed_two, scale_two, gain_rows[1]
    )
    grad_branch = grad_pre_two.astype(jnp.bfloat16)
    grad_act = dot_last(grad_branch, down_w)
    _, gelu_back = jax.vjp(lambda inner: jax.nn.gelu(inner, approximate=False), pre_gelu)
    grad_pre_gelu = gelu_back(grad_act)[0].astype(jnp.bfloat16)
    grad_hidden = grad_pre_two + dot_last(grad_pre_gelu, up_w)
    grad_pre_one, grad_gain_one, grad_shift_one = normalize_back(
        grad_hidden, normed_one, scale_one, gain_rows[0]
    )
    grad_attended = grad_pre_one.astype(jnp.bfloat16)
    grad_context = dot_last(grad_attended, out_w).astype(jnp.bfloat16)
    grad_context = grad_context.reshape(span_count, HEADS, width // HEADS)
    grad_probs = jnp.einsum(
        "bhe,bkhe->bhk", grad_context, values, preferred_element_type=jnp.float32
    )
    grad_values = jnp.einsum("bhk,bhe->bkhe", probs.astype(jnp.bfloat16), grad_context)
    grad_values = grad_values.reshape(row_count, width).astype(jnp.bfloat16)
    grad_scores = probs * (grad_probs - jnp.sum(probs * grad_probs, axis=-1, keepdims=True))
    grad_scores = grad_scores.astype(jnp.bfloat16)
    grad_queries = (
        jnp.einsum("bhk,bkhe->bhe", grad_scores, keys, preferred_element_type=jnp.float32)
        * score_scale
    )
    grad_queries = grad_queries.reshape(span_count, width).astype(jnp.bfloat16)
    grad_keys = (
        jnp.einsum("bhk,bhe->bkhe", grad_scores, queries, preferred_element_type=jnp.float32)
        * score_scale
    )
    grad_keys = grad_keys.reshape(row_count, width).astype(jnp.bfloat16)
    grad_kv = jnp.concatenate([grad_keys, grad_values], axis=1)
    grad_kv_w = dot_first(inputs, grad_kv)
    grad_inputs = dot_last(grad_kv, qkv_w[:, width:])
    grad_first = grad_pre_one + dot_last(grad_queries, qkv_w[:, :width])
    placed = jnp.pad(grad_first[:, None], ((0, 0), (0, SPAN - 1), (0, 0))).reshape(row_count, width)
    grad_inputs = grad_inputs + placed
    rows = jnp.concatenate(
        [context, grad_attended, hidden_low, grad_pre_gelu, activated, grad_branch, first, grad_queries],
        axis=1,
    )

    def total(values):
        return jnp.sum(values, axis=0, dtype=jnp.float32)

    small = (
        total(grad_pre_gelu),
        jnp.stack([grad_gain_one, grad_gain_two]),
        jnp.stack(
            [
                total(grad_queries), total(grad_values), total(grad_attended), grad_shift_one,
                total(grad_branch), grad_shift_two,
            ]
        ),
    )
    return grad_inputs, grad_kv_w, rows, small


def first_weight_grads(rows, kv_owned, at):
    width = rows.shape[1] // 16
    wide = 4 * width
    context, grad_attended = rows[:, :width], rows[:, width : 2 * width]
    hidden_low = rows[:, 2 * width : 3 * width]
    grad_pre_gelu = rows[:, 3 * width : 3 * width + wide]
    activated = rows[:, 7 * width : 11 * width]
    grad_branch = rows[:, 11 * width : 12 * width]
    first = rows[:, 12 * width : 13 * width]
    grad_queries = rows[:, 13 * width : 14 * width]
    count = kv_owned.shape[0]
    own = lambda values, many: lax.dynamic_slice_in_dim(values, at * many, many, 1)
    return (
        jnp.concatenate([dot_first(own(first, count), grad_queries), kv_owned], axis=1),
        dot_first(own(context, count), grad_attended),
        dot_first(own(hidden_low, count), grad_pre_gelu),
        dot_first(own(activated, 4 * count), grad_branch),
    )


def pack_small(up_b, gains, biases, owners):
    parts = [up_b.reshape(owners, -1)]
    for tensor in (gains, biases):
        parts.append(tensor.reshape(tensor.shape[0], owners, -1).transpose(1, 0, 2).reshape(owners, -1))
    return jnp.concatenate(parts, axis=1)


def unpack_small(packed, width):
    owners = packed.shape[0]
    share = width // owners
    up_b = packed[:, : 4 * share].reshape(4 * width)
    gains = packed[:, 4 * share : 6 * share].reshape(owners, 2, share).transpose(1, 0, 2)
    biases = packed[:, 6 * share :].reshape(owners, 6, share).transpose(1, 0, 2)
    return up_b, gains.reshape(2, width), biases.reshape(6, width)


def exchange_weights(p1, p2, small):
    both = ("wide", "narrow")
    w1 = lax.all_gather(p1, both, axis=0)
    w2 = lax.all_gather(p2, both, axis=0)
    return (w1[:, 0], w1[:, 1]), (w2[:, 0], w2[:, 1]), lax.all_gather(small, both, axis=0)


def exchange_grads(g1, g2, kv, small, rows):
    both = ("wide", "narrow")
    summed = [
        lax.psum_scatter(a, both, scatter_dimension=0).astype(jnp.float32) for a in (g1, g2, kv, small)
    ]
    return summed + [lax.all_gather(rows, both, axis=0)]


def rows_ahead(group):
    last = group[6]
    return (*group[:6], jnp.swapaxes(last, last.ndim - 3, last.ndim - 2))


def fused_step(embeds, skip_tokens, cotangent, lengths, params, moments):
    params, moments = rows_ahead(params), rows_ahead(moments)
    y, embeds_grad, skip_grad, o1, o2, small, _ = step_call(params, embeds, skip_tokens, cotangent, lengths)
    new_steps, new_moments, passed = adam_update(params, moments, o1, o2, small, (y, embeds_grad, skip_grad))
    return (*passed, *rows_ahead(new_steps), *rows_ahead(new_moments))


def per_device(
    embeds, skip_tokens, cotangent, lengths, qkv_weight, out_weight, up_weight, down_weight, up_bias,
    norm_gains, biases, qkv_moments, out_moments, up_moments, down_moments, up_bias_moments,
    gain_moments, bias_moments,
):
    params = (qkv_weight, out_weight, up_weight, down_weight, up_bias, norm_gains, biases)
    moments = (
        qkv_moments, out_moments, up_moments, down_moments, up_bias_moments, gain_moments, bias_moments,
    )
    wide_size, narrow_size = lax.axis_size("wide"), lax.axis_size("narrow")
    if (wide_size, narrow_size) == (8, 4):
        return fused_step(embeds, skip_tokens, cotangent, lengths, params, moments)
    owners = wide_size * narrow_size
    at = lax.axis_index("wide") * narrow_size + lax.axis_index("narrow")
    span_count = lengths.shape[0]
    row_count, width = embeds.shape
    positions = lax.broadcasted_iota(jnp.int32, (span_count, SPAN), 1)
    key_valid = positions < lengths[:, None]
    row_index = lax.broadcasted_iota(jnp.int32, (1, SPAN, 1), 1)

    p1 = jnp.concatenate([qkv_weight, out_weight, up_weight], axis=2).astype(jnp.bfloat16)
    p2 = down_weight.astype(jnp.bfloat16)
    share = 12 * width // owners
    tiles = -(-2 * share // 1024)
    small_own = jnp.concatenate(
        [up_bias, norm_gains.reshape(2, -1), biases.reshape(2, -1)], axis=1
    ).reshape(-1)
    small_own = jnp.pad(small_own, (0, tiles * 1024 - 2 * share)).reshape(tiles * 8, 128)
    w1, w2, small_all = exchange_weights(p1, p2, small_own)
    small_all = small_all.reshape(owners, -1)[:, : 2 * share].astype(jnp.bfloat16).astype(jnp.float32)

    def layer_weights(layer):
        joined = w1[layer].reshape(width, -1)
        return (
            joined[:, : 3 * width], joined[:, 3 * width : 4 * width], joined[:, 4 * width :],
            w2[layer].reshape(-1, width),
        ) + unpack_small(small_all[:, layer * share : (layer + 1) * share], width)

    backbone, head = layer_weights(0), layer_weights(1)
    backbone_out, saved = first_forward(backbone, embeds, key_valid)
    skip_view = skip_tokens.reshape(span_count, SPAN, width)
    head_in = jnp.where(row_index == 0, backbone_out.astype(jnp.bfloat16)[:, None], skip_view)
    head_in = head_in.reshape(row_count, width)
    head_out, grad_head_in, head_grads = backward_block(
        head, head_in, key_valid, cotangent.astype(jnp.float32)
    )
    grad_view = grad_head_in.reshape(span_count, SPAN, width)
    skip_grad = jnp.where(row_index == 0, 0.0, grad_view).reshape(row_count, width)
    embeds_grad, grad_kv_w, rows, small_first = first_backward(
        backbone, embeds, saved, grad_view[:, 0]
    )
    low = lambda a: a.astype(jnp.bfloat16)
    g1 = jnp.concatenate([low(head_grads[0]), low(head_grads[1]), low(head_grads[2])], axis=1)
    g1 = g1.reshape(owners, width // owners, -1)
    g2 = low(head_grads[3]).reshape(owners, -1, width)
    kv = low(grad_kv_w).reshape(owners, width // owners, -1)
    small_grads = jnp.concatenate(
        [pack_small(*small_first, owners), pack_small(*head_grads[4:], owners)], axis=1
    )
    small_grads = jnp.pad(small_grads, ((0, 0), (0, tiles * 1024 - 2 * share)))
    small_grads = small_grads.reshape(owners, tiles * 8, 128)
    rows_wide = jnp.pad(rows, ((0, 0), (0, 2 * width)))
    own_g1, own_g2, own_kv, own_small, all_rows = exchange_grads(
        g1, g2, kv, small_grads, rows_wide.reshape(16 * span_count // 2, -1)
    )
    all_rows = all_rows.reshape(owners * span_count, -1)
    first_grads = first_weight_grads(all_rows, own_kv, at)
    own_small = own_small.reshape(-1)[: 2 * share].reshape(2, share)
    sixth = width // owners
    joined = jnp.stack([jnp.concatenate(first_grads[:3], axis=1), own_g1])
    down = jnp.stack([first_grads[3], own_g2])
    pad = lambda a: jnp.pad(a, ((0, 0), (0, 0), (0, 128 - a.shape[2])))
    small = [
        pad(own_small[:, 4 * sixth : 6 * sixth].reshape(2, 2, sixth)),
        pad(own_small[:, 6 * sixth :].reshape(2, 6, sixth)),
        pad(own_small[:, None, : 4 * sixth]),
        jnp.zeros((2, 7, 128), jnp.float32),
    ]
    small = jnp.concatenate(small, axis=1).reshape(32, 128)
    passed = (head_out.astype(jnp.bfloat16), embeds_grad, skip_grad)
    new_steps, new_moments, passed = adam_update(
        rows_ahead(params), rows_ahead(moments), joined, down, small, passed
    )
    return (*passed, *rows_ahead(new_steps), *rows_ahead(new_moments))


def solution(mesh):
    return jax.shard_map(
        per_device,
        mesh=mesh,
        in_specs=(
            P(("wide", "narrow"), None),
            P(("wide", "narrow"), None),
            P(("wide", "narrow"), None),
            P(("wide", "narrow")),
            P(None, ("wide", "narrow"), None),
            P(None, ("wide", "narrow"), None),
            P(None, ("wide", "narrow"), None),
            P(None, ("wide", "narrow"), None),
            P(None, ("wide", "narrow")),
            P(None, None, ("wide", "narrow")),
            P(None, None, ("wide", "narrow")),
            P(None, None, ("wide", "narrow"), None),
            P(None, None, ("wide", "narrow"), None),
            P(None, None, ("wide", "narrow"), None),
            P(None, None, ("wide", "narrow"), None),
            P(None, None, ("wide", "narrow")),
            P(None, None, None, ("wide", "narrow")),
            P(None, None, None, ("wide", "narrow")),
        ),
        out_specs=(
            P(("wide", "narrow"), None),
            P(("wide", "narrow"), None),
            P(("wide", "narrow"), None),
            P(None, ("wide", "narrow"), None),
            P(None, ("wide", "narrow"), None),
            P(None, ("wide", "narrow"), None),
            P(None, ("wide", "narrow"), None),
            P(None, ("wide", "narrow")),
            P(None, None, ("wide", "narrow")),
            P(None, None, ("wide", "narrow")),
            P(None, None, ("wide", "narrow"), None),
            P(None, None, ("wide", "narrow"), None),
            P(None, None, ("wide", "narrow"), None),
            P(None, None, ("wide", "narrow"), None),
            P(None, None, ("wide", "narrow")),
            P(None, None, None, ("wide", "narrow")),
            P(None, None, None, ("wide", "narrow")),
        ),
        check_vma=False,
    )
```

```python
import math

import jax
import jax.numpy as jnp
from jax import lax
from jax.experimental import pallas as pl
from jax.experimental.pallas import tpu as pltpu
from jax.sharding import PartitionSpec as P

HEADS = 12
SPAN = 128

norm_epsilon = 1e-12
score_scale = 0.125
masked_score = -1000000000.0
beta_first = 0.9
beta_second = 0.999
adam_epsilon = 1e-08
weight_decay = 0.01
first_fix = 1.0 - 0.9**10
second_fix = 1.0 - 0.999**10


def dot_first(left_side, right_side):
    return lax.dot_general(
        left_side, right_side, (((0,), (0,)), ((), ())), preferred_element_type=jnp.float32
    )


def dot_last(left_side, right_side):
    return lax.dot_general(
        left_side, right_side, (((1,), (1,)), ((), ())), preferred_element_type=jnp.float32
    )


def normalize(values, gain_row, shift_row):
    centred = values - jnp.mean(values, axis=-1, keepdims=True)
    inv_scale = lax.rsqrt(jnp.mean(centred * centred, axis=-1, keepdims=True) + norm_epsilon)
    normed = centred * inv_scale
    return (normed * gain_row + shift_row, normed, inv_scale)


def normalize_back(gradient, normed, inv_scale, gain_row):
    grad_gain = jnp.sum(gradient * normed, axis=0)
    grad_shift = jnp.sum(gradient, axis=0)
    scaled = gradient * gain_row
    grad_in = inv_scale * (
        scaled
        - jnp.mean(scaled, axis=-1, keepdims=True)
        - normed * jnp.mean(scaled * normed, axis=-1, keepdims=True)
    )
    return (grad_in, grad_gain, grad_shift)


def head_view(tensor):
    return tensor.reshape(tensor.shape[0] // SPAN, SPAN, HEADS, tensor.shape[1] // HEADS)


def attend_scores(queries, keys_low, key_valid):
    scores = (
        jnp.einsum(
            "bqhe,bkhe->bhqk",
            head_view(queries),
            head_view(keys_low),
            preferred_element_type=jnp.float32,
        )
        * score_scale
    )
    return jnp.where(key_valid[:, None, None, :], scores, masked_score)


def forward_block(weights, inputs, key_valid):
    qkv_w, out_w, up_w, down_w, up_b, gain_rows, biases = weights
    gains_wide = gain_rows.astype(jnp.float32)
    biases_wide = biases.astype(jnp.float32)
    row_count, model_width = inputs.shape
    mixed_in = jnp.dot(inputs, qkv_w, preferred_element_type=jnp.float32)
    queries = (mixed_in[:, :model_width] + biases_wide[0]).astype(jnp.bfloat16)
    keys_low = mixed_in[:, model_width : 2 * model_width].astype(jnp.bfloat16)
    values_low = (mixed_in[:, 2 * model_width :] + biases_wide[1]).astype(jnp.bfloat16)
    scores = attend_scores(queries, keys_low, key_valid)
    row_max = jnp.max(scores, axis=-1, keepdims=True)
    weights_exp = jnp.exp(scores - row_max)
    row_total = jnp.sum(weights_exp, axis=-1, keepdims=True)
    softmax_out = (weights_exp / row_total).astype(jnp.bfloat16)
    log_total = row_max + jnp.log(row_total)
    context = jnp.einsum(
        "bhqk,bkhe->bqhe", softmax_out, head_view(values_low), preferred_element_type=jnp.float32
    )
    context = context.reshape(row_count, model_width).astype(jnp.bfloat16)
    attended = jnp.dot(context, out_w, preferred_element_type=jnp.float32) + biases_wide[2]
    hidden, normed_one, scale_one = normalize(
        inputs.astype(jnp.float32) + attended, gains_wide[0], biases_wide[3]
    )
    hidden_low = hidden.astype(jnp.bfloat16)
    pre_gelu = jnp.dot(hidden_low, up_w, preferred_element_type=jnp.float32) + up_b.astype(
        jnp.float32
    )
    activated = jax.nn.gelu(pre_gelu, approximate=False).astype(jnp.bfloat16)
    branch_out = jnp.dot(activated, down_w, preferred_element_type=jnp.float32) + biases_wide[4]
    output, normed_two, scale_two = normalize(hidden + branch_out, gains_wide[1], biases_wide[5])
    saved = (
        queries,
        keys_low,
        values_low,
        log_total,
        context,
        normed_one,
        scale_one,
        hidden_low,
        pre_gelu,
        activated,
        normed_two,
        scale_two,
    )
    return (output, saved)


def backward_block(weights, inputs, key_valid, grad_out):
    qkv_w, out_w, up_w, down_w, up_b, gain_rows, biases = weights
    gains_wide = gain_rows.astype(jnp.float32)
    row_count, model_width = inputs.shape
    output, saved = forward_block(weights, inputs, key_valid)
    (
        queries,
        keys_low,
        values_low,
        log_total,
        context,
        normed_one,
        scale_one,
        hidden_low,
        pre_gelu,
        activated,
        normed_two,
        scale_two,
    ) = saved
    grad_pre_two, grad_gain_two, grad_shift_two = normalize_back(
        grad_out, normed_two, scale_two, gains_wide[1]
    )
    grad_branch = grad_pre_two.astype(jnp.bfloat16)
    grad_down_w = dot_first(activated, grad_branch)
    grad_act = dot_last(grad_branch, down_w)
    _, gelu_back = jax.vjp(lambda inner: jax.nn.gelu(inner, approximate=False), pre_gelu)
    grad_pre_gelu = gelu_back(grad_act)[0].astype(jnp.bfloat16)
    grad_up_w = dot_first(hidden_low, grad_pre_gelu)
    grad_hidden = grad_pre_two + dot_last(grad_pre_gelu, up_w)
    grad_pre_one, grad_gain_one, grad_shift_one = normalize_back(
        grad_hidden, normed_one, scale_one, gains_wide[0]
    )
    grad_attended = grad_pre_one.astype(jnp.bfloat16)
    grad_out_w = dot_first(context, grad_attended)
    grad_context = head_view(dot_last(grad_attended, out_w).astype(jnp.bfloat16))
    scores = attend_scores(queries, keys_low, key_valid)
    softmax_full = jnp.exp(scores - log_total)
    grad_probs = jnp.einsum(
        "bqhe,bkhe->bhqk", grad_context, head_view(values_low), preferred_element_type=jnp.float32
    )
    grad_values = jnp.einsum(
        "bhqk,bqhe->bkhe",
        softmax_full.astype(jnp.bfloat16),
        grad_context,
        preferred_element_type=jnp.float32,
    )
    grad_values = grad_values.reshape(row_count, model_width).astype(jnp.bfloat16)
    grad_scores = softmax_full * (
        grad_probs - jnp.sum(softmax_full * grad_probs, axis=-1, keepdims=True)
    )
    grad_scores = grad_scores.astype(jnp.bfloat16)
    grad_queries = (
        jnp.einsum(
            "bhqk,bkhe->bqhe", grad_scores, head_view(keys_low), preferred_element_type=jnp.float32
        )
        * score_scale
    )
    grad_queries = grad_queries.reshape(row_count, model_width).astype(jnp.bfloat16)
    grad_keys = (
        jnp.einsum(
            "bhqk,bqhe->bkhe", grad_scores, head_view(queries), preferred_element_type=jnp.float32
        )
        * score_scale
    )
    grad_keys = grad_keys.reshape(row_count, model_width).astype(jnp.bfloat16)
    grad_mixed = jnp.concatenate([grad_queries, grad_keys, grad_values], axis=1)
    grad_qkv_w = dot_first(inputs, grad_mixed)
    grad_inputs = grad_pre_one + dot_last(grad_mixed, qkv_w)
    grad_gains = jnp.stack([grad_gain_one, grad_gain_two])
    grad_biases = jnp.stack(
        [
            jnp.sum(grad_queries, axis=0, dtype=jnp.float32),
            jnp.sum(grad_values, axis=0, dtype=jnp.float32),
            jnp.sum(grad_attended, axis=0, dtype=jnp.float32),
            grad_shift_one,
            jnp.sum(grad_branch, axis=0, dtype=jnp.float32),
            grad_shift_two,
        ]
    )
    grads = (
        grad_qkv_w,
        grad_out_w,
        grad_up_w,
        grad_down_w,
        jnp.sum(grad_pre_gelu, axis=0, dtype=jnp.float32),
        grad_gains,
        grad_biases,
    )
    return (output, grad_inputs, grads)


MESH = pl.DeviceIdType.MESH


class Refs:
    def __init__(self, **refs):
        for name, ref in refs.items():
            setattr(self, name, ref)


def place():
    wide = lax.axis_index("wide")
    z = lax.axis_index("narrow")
    return wide // 4, (wide // 2) % 2, wide % 2, z


def device(y, x, c, z):
    return ((y * 2 + x) * 2 + c, z)


def flat(y, x, c, z):
    return ((y * 2 + x) * 2 + c) * 4 + z


def near(z, k):
    if k == 0:
        return z
    if k == 1:
        return z + 1 - 2 * (z % 2)
    if k == 2:
        return (z + 2) % 4
    return 3 - z


def greet(wide, z):
    barrier = pltpu.get_barrier_semaphore()
    for k in range(1, 8):
        pl.semaphore_signal(barrier, inc=1, device_id=((wide + k) % 8, z), device_id_type=MESH)

    @pl.when(z < 3)
    def _():
        pl.semaphore_signal(barrier, inc=1, device_id=(wide, z + 1), device_id_type=MESH)

    @pl.when(z > 0)
    def _():
        pl.semaphore_signal(barrier, inc=1, device_id=(wide, z - 1), device_id_type=MESH)

    pl.semaphore_wait(barrier, 8 + ((z + 1) // 2) % 2)


def run_if(pred, action):
    if pred is None:
        action()
    else:
        pl.when(pred)(action)


def send(src, dst, send_sem, recv_sem, there, pred=None):
    run_if(
        pred,
        lambda: pltpu.make_async_remote_copy(
            src_ref=src, dst_ref=dst, send_sem=send_sem, recv_sem=recv_sem, device_id=there, device_id_type=MESH
        ).start(),
    )


def bytes_of(ref, sem):
    me = (lax.axis_index("wide"), lax.axis_index("narrow"))
    return pltpu.make_async_remote_copy(
        src_ref=ref, dst_ref=ref, send_sem=sem, recv_sem=sem, device_id=me, device_id_type=MESH
    )


def await_bytes(ref, sem, pred=None):
    run_if(pred, lambda: bytes_of(ref, sem).wait_recv())


def await_sent(ref, sem, pred=None):
    run_if(pred, lambda: bytes_of(ref, sem).wait_send())


def await_column_sends(many, each, sem, z):
    await_sent(many(each), sem, (z == 0) | (z == 3))
    await_sent(many(5 * each), sem, (z == 1) | (z == 2))


def column_steps(slabs, manys, sem):
    y, x, c, z = place()
    up, down = device(y, x, c, z + 1), device(y, x, c, z - 1)

    def push(i, slab, zz, there, pred):
        send(slab(zz), slab(zz), sem.at[i, 4], sem.at[i, zz], there, pred)

    def own():
        for i, slab in enumerate(slabs):
            push(i, slab, z, up, z < 3)
            push(i, slab, z, down, z > 0)

    def take(dist):
        for i, slab in enumerate(slabs):
            low, high = z - dist, z + dist
            await_bytes(slab(low), sem.at[i, low], z >= dist)
            if dist < 3:
                push(i, slab, low, up, (z >= dist) & (z < 3))
            await_bytes(slab(high), sem.at[i, high], z <= 3 - dist)
            if dist < 3:
                push(i, slab, high, down, (z <= 3 - dist) & (z > 0))

    def drain():
        for i, many in enumerate(manys):
            await_column_sends(many, 1, sem.at[i, 4], z)

    return [own] + [lambda dist=dist: take(dist) for dist in (1, 2, 3)], drain


GATHER_SEMS = 21


def gather_steps(subs, many, sem):
    y, x, c, z = place()
    each = len(subs)
    sib = device(y, x, 1 - c, z)
    xn = device(y, 1 - x, c, z)
    yn = device(1 - y, x, c, z)
    mine = flat(y, x, c, z)

    def unit(sub, far1, far2, zz, core):
        fx, fy = (far1, far2) if sub[2] == "x" else (far2, far1)
        return flat(1 - y if fy else y, 1 - x if fx else x, core, zz)

    def push(sub, at, send_at, role, target, pred=None, src=None):
        send(sub[1](at) if src is None else src, sub[1](at), sem.at[send_at], sem.at[role], target, pred)

    def along(sub, at, up, role, pred, src=None):
        push(sub, at, 17, role, device(y, x, c, z + 1 if up else z - 1), pred, src)

    def first(sub, at, zz, pred=None, src=None):
        push(sub, at, 18, 4 + zz, xn if sub[2] == "x" else yn, pred, src)

    def second(sub, at, far, zz, pred=None, src=None):
        push(sub, at, 19, 8 + 4 * far + zz, yn if sub[2] == "x" else xn, pred, src)

    def sibling(sub, at, pred=None, src=None):
        push(sub, at, 20, 16, sib, pred, src)

    def own():
        for sub in subs:
            along(sub, mine, True, z, z < 3, sub[0])
            along(sub, mine, False, z, z > 0, sub[0])
        for sub in subs:
            first(sub, mine, z, None, sub[0])
            second(sub, mine, 0, z, None, sub[0])
        for sub in subs:
            sibling(sub, mine, None, sub[0])

    def from_z(dist):
        for up in (True, False):
            zz = z - dist if up else z + dist
            have = (z >= dist) if up else (z <= 3 - dist)
            at = flat(y, x, c, zz)

            @pl.when(have)
            def _(up=up, zz=zz, at=at):
                await_bytes(many(each), sem.at[zz])
                for sub in subs:
                    if dist < 3:
                        along(sub, at, up, zz, (z < 3) if up else (z > 0))
                for sub in subs:
                    first(sub, at, zz)
                    second(sub, at, 0, zz)
                    sibling(sub, at)

    def from_first(k):
        zz = near(z, k)
        await_bytes(many(each), sem.at[4 + zz])
        for sub in subs:
            at = unit(sub, True, False, zz, c)
            second(sub, at, 1, zz)
            sibling(sub, at)

    def from_second(far, k):
        zz = near(z, k)
        await_bytes(many(each), sem.at[8 + 4 * far + zz])
        for sub in subs:
            sibling(sub, unit(sub, far == 1, True, zz, c))

    def finish():
        await_bytes(many(16 * each), sem.at[16])

    def drain():
        await_column_sends(many, each, sem.at[17], z)
        await_sent(many(4 * each), sem.at[18])
        await_sent(many(8 * each), sem.at[19])
        await_sent(many(16 * each), sem.at[20])

    steps = [own, lambda: from_z(1), lambda: from_first(0), lambda: from_z(2), lambda: from_first(1)]
    steps += [lambda: from_z(3), lambda: (from_first(2), from_first(3))]
    for far in range(2):
        steps += [lambda far=far, k=k: from_second(far, k) for k in range(4)]
    return steps + [finish], drain


REDUCE_SEMS = 33
TARGETS = (0, 3, 1, 2)


class Reduce:
    def __init__(self, subs, sem):
        self.subs, self.sem, self.each = subs, sem, len(subs)
        self.y, self.x, self.c, self.z = place()
        y, x, c, z = self.y, self.x, self.c, self.z
        self.sib = device(y, x, 1 - c, z)
        self.xn, self.yn = device(y, 1 - x, c, z), device(1 - y, x, c, z)

    def own(self, sub, far1, far2, zz, core):
        fx, fy = (far1, far2) if sub.dim == "x" else (far2, far1)
        cy, cx = (1 - self.y if fy else self.y), (1 - self.x if fx else self.x)
        return sub.own(flat(cy, cx, core, zz)), (cy * 2 + cx) * 4 + zz

    def coord(self, sub, far):
        here = self.x if sub.dim == "x" else self.y
        return 1 - here if far else here

    def take(self, at, buffer, count=1):
        await_bytes(buffer.at[pl.ds(0, count * self.each)], self.sem.at[at])

    def add(self, dst, *parts):
        total = dst[...].astype(jnp.float32)
        for part in parts:
            total = total + part[...].astype(jnp.float32)
        dst[...] = total.astype(dst.dtype)

    def start_role(self, far1, far2):
        return (1 - far2) * (2 - far1)

    second_role = staticmethod(lambda far1: 3 if far1 else 4)

    def start(self, zz):
        for far1, far2 in ((False, True), (True, True), (True, False), (False, False)):
            at = 6 * zz + self.start_role(int(far1), int(far2))
            for sub in self.subs:
                src, slot = self.own(sub, far1, far2, zz, 1 - self.c)
                send(src, sub.sib.at[slot], self.sem.at[29], self.sem.at[at], self.sib)

    def start_chip(self, chip):
        cy, cx = chip // 2, chip % 2
        for zz in TARGETS:
            for sub in self.subs:
                fy, fx = (cy + self.y) % 2, (cx + self.x) % 2
                far1, far2 = (fx, fy) if sub.dim == "x" else (fy, fx)
                at = 6 * zz + self.start_role(far1, far2)
                src = sub.own(flat(cy, cx, 1 - self.c, zz))
                send(src, sub.sib.at[chip * 4 + zz], self.sem.at[29], self.sem.at[at], self.sib)

    def step_a(self, zz):
        self.take(6 * zz, self.subs[0].sib, 2)
        for far1 in (False, True):
            for sub in self.subs:
                acc, slot = self.own(sub, far1, True, zz, self.c)
                self.add(acc, sub.sib.at[slot])
                slot = self.coord(sub, far1) * 4 + zz
                there = self.yn if sub.dim == "x" else self.xn
                send(acc, sub.second.at[slot], self.sem.at[30], self.sem.at[6 * zz + self.second_role(far1)], there)

    def step_b(self, zz):
        self.take(6 * zz + 1, self.subs[0].sib)
        self.take(6 * zz + 3, self.subs[0].second)
        for sub in self.subs:
            acc, slot = self.own(sub, True, False, zz, self.c)
            self.add(acc, sub.sib.at[slot], sub.second.at[self.coord(sub, True) * 4 + zz])
            there = self.xn if sub.dim == "x" else self.yn
            send(acc, sub.first.at[zz], self.sem.at[31], self.sem.at[6 * zz + 5], there)

    def chain(self, sub, acc, zz, up, pred):
        z = self.z
        slot = zz if up else jnp.where(z - 1 == zz, 4, zz)
        there = device(self.y, self.x, self.c, z + 1 if up else z - 1)
        send(acc, sub.chain.at[slot], self.sem.at[32], self.sem.at[24 + slot], there, pred)

    def step_c(self, zz):
        self.take(6 * zz + 2, self.subs[0].sib)
        self.take(6 * zz + 4, self.subs[0].second)
        self.take(6 * zz + 5, self.subs[0].first)
        for sub in self.subs:
            acc, slot = self.own(sub, False, False, zz, self.c)
            self.add(acc, sub.sib.at[slot], sub.second.at[self.coord(sub, False) * 4 + zz], sub.first.at[zz])
            if zz > 0:
                self.chain(sub, acc, zz, True, self.z == 0)
            if zz < 3:
                self.chain(sub, acc, zz, False, self.z == 3)

    def relay(self, zz, at, up):
        @pl.when(self.z == at)
        def _():
            self.take(24 + zz, self.subs[0].chain)
            for sub in self.subs:
                acc, _ = self.own(sub, False, False, zz, self.c)
                self.add(acc, sub.chain.at[zz])
                self.chain(sub, acc, zz, up, None)

    def step_d(self, zz):
        if zz >= 2:
            self.relay(zz, 1, True)
        else:
            self.relay(zz, 2, False)

    def step_e(self, zz):
        if zz == 3:
            self.relay(zz, 2, True)
        if zz == 0:
            self.relay(zz, 1, False)

    def finish(self):
        z = self.z
        for sub in self.subs:
            acc, _ = self.own(sub, False, False, z, self.c)
            sub.out[...] = acc[...].astype(jnp.float32)
        for pred, slot in ((z > 0, z), (z < 3, 4)):

            @pl.when(pred)
            def _(slot=slot):
                self.take(24 + slot, self.subs[0].chain)
                for sub in self.subs:
                    sub.out[...] += sub.chain[slot].astype(jnp.float32)

        self.sent(16, 8, 4, 3)

    def near_finish(self):
        pass

    def sent(self, *counts):
        for k, count in enumerate(counts):
            await_sent(self.subs[0].all.at[pl.ds(0, count * self.each)], self.sem.at[29 + k])


class ReduceLate(Reduce):
    def start_role(self, far1, far2):
        return 1 - far2

    second_role = staticmethod(lambda far1: 3)

    def step_b(self, zz):
        self.take(6 * zz + 1, self.subs[0].sib, 2)
        self.take(6 * zz + 3, self.subs[0].second, 2)
        for far1 in (True, False):
            for sub in self.subs:
                acc, slot = self.own(sub, far1, False, zz, self.c)
                self.add(acc, sub.sib.at[slot], sub.second.at[self.coord(sub, far1) * 4 + zz])
        for up, at in ((True, 0), (False, 3)):
            if zz != at:
                self.pass_on(zz, up, self.z == at)

    def pass_on(self, zz, up, pred):
        z = self.z
        slot = zz if up else jnp.where(z - 1 == zz, 4, zz)
        there = device(self.y, self.x, self.c, z + 1 if up else z - 1)
        for far1 in range(2):
            for sub in self.subs:
                acc, _ = self.own(sub, far1 == 1, False, zz, self.c)
                send(acc, sub.chain.at[2 * slot + far1], self.sem.at[32], self.sem.at[24 + slot], there, pred)

    def join(self, zz, slot):
        self.take(24 + slot, self.subs[0].chain, 2)
        for far1 in range(2):
            for sub in self.subs:
                acc, _ = self.own(sub, far1 == 1, False, zz, self.c)
                self.add(acc, sub.chain.at[2 * slot + far1])

    def relay(self, zz, at, up):
        @pl.when(self.z == at)
        def _():
            self.join(zz, zz)
            self.pass_on(zz, up, None)

    def step_c(self, zz):
        Reduce.step_d(self, zz)

    def step_d(self, zz):
        Reduce.step_e(self, zz)

    def step_e(self, zz):
        pass

    def near_finish(self):
        z = self.z
        for pred, slot in ((z > 0, z), (z < 3, 4)):

            @pl.when(pred)
            def _(slot=slot):
                self.join(z, slot)

        for sub in self.subs:
            acc, _ = self.own(sub, True, False, z, self.c)
            there = self.xn if sub.dim == "x" else self.yn
            send(acc, sub.first.at[0], self.sem.at[31], self.sem.at[5], there)

    def finish(self):
        self.take(5, self.subs[0].first)
        for sub in self.subs:
            acc, _ = self.own(sub, False, False, self.z, self.c)
            sub.out[...] = acc[...].astype(jnp.float32) + sub.first[0].astype(jnp.float32)
        self.sent(16, 8, 1, 6)


class Waves:
    def __init__(self, groups, lags):
        self.waves = [(made, zz) for made in groups for zz in TARGETS]
        self.lags = lags
        self.at = 0

    def step(self):
        stages = ("step_a", "step_b", "step_c", "step_d", "step_e")
        for lag, stage in zip(self.lags, stages):
            k = self.at - lag
            if 0 <= k < len(self.waves):
                group, zz = self.waves[k]
                for made in group:
                    getattr(made, stage)(zz)
        for more, stage in ((1, "near_finish"), (2, "finish")):
            k = self.at - self.lags[-1] - more
            if 0 <= k < len(self.waves) and k % 4 == 3:
                for made in self.waves[k][0]:
                    getattr(made, stage)()
        self.at += 1

    def left(self):
        return len(self.waves) + self.lags[-1] + 2 - self.at


def erf_of(v):
    return lax.erf(v)


def mm(a, b):
    return jnp.dot(a, b, preferred_element_type=jnp.float32)


def mm_nt(a, b):
    return lax.dot_general(a, b, (((1,), (1,)), ((), ())), preferred_element_type=jnp.float32)


def mm_tn(a, b):
    return lax.dot_general(a, b, (((0,), (0,)), ((), ())), preferred_element_type=jnp.float32)


def columns(ref, start, stop):
    block = ref[:, :, start:stop]
    return block.reshape(block.shape[0] * block.shape[1], stop - start)


def rows_of(ref, start, stop):
    block = ref[start:stop]
    return block.reshape(block.shape[0] * block.shape[1], block.shape[2])


def put_columns(ref, start, values):
    owners, share = ref.shape[0], ref.shape[1]
    ref[:, :, start : start + values.shape[1]] = values.astype(ref.dtype).reshape(
        owners, share, values.shape[1]
    )


def norm_rows(values):
    centred = values - jnp.mean(values, axis=-1, keepdims=True)
    inv_scale = lax.rsqrt(jnp.mean(centred * centred, axis=-1, keepdims=True) + norm_epsilon)
    return centred * inv_scale, inv_scale


def norm_rows_back(gradient, normed, inv_scale, gain_row):
    scaled = gradient * gain_row
    return inv_scale * (
        scaled
        - jnp.mean(scaled, axis=-1, keepdims=True)
        - normed * jnp.mean(scaled * normed, axis=-1, keepdims=True)
    )


def column_sum(values):
    return jnp.sum(values.astype(jnp.float32), axis=0, keepdims=True)


def head_forward(s, w1, w2, small, lengths):
    width = s.x.shape[1]
    spans = s.x.shape[0] // SPAN
    x = s.x[...]
    s.q[...] = (mm(x, columns(w1, 0, width)) + small(2)).astype(jnp.bfloat16)
    s.k[...] = mm(x, columns(w1, width, 2 * width)).astype(jnp.bfloat16)
    s.v[...] = (mm(x, columns(w1, 2 * width, 3 * width)) + small(3)).astype(jnp.bfloat16)
    yield
    lane = lax.broadcasted_iota(jnp.int32, (SPAN, 128), 1)
    for span in range(spans):
        keep = lax.broadcasted_iota(jnp.int32, (SPAN, 128), 1) < lengths[span]
        for pair in range(width // 128):
            at = (slice(span * SPAN, (span + 1) * SPAN), slice(pair * 128, (pair + 1) * 128))
            q, k, v = s.q[at], s.k[at], s.v[at]
            parts = []
            for side in range(2):
                here = (lane < 64) if side == 0 else (lane >= 64)
                scores = mm_nt(jnp.where(here, q, jnp.zeros_like(q)), k) * score_scale
                scores = jnp.where(keep, scores, masked_score)
                weight = jnp.exp(scores - jnp.max(scores, axis=-1, keepdims=True))
                probs = weight / jnp.sum(weight, axis=-1, keepdims=True)
                s.p[(span * 6 + pair) * 2 + side] = probs
                parts.append(mm(probs.astype(jnp.bfloat16), v))
            s.ctx[at] = jnp.where(lane < 64, parts[0], parts[1]).astype(jnp.bfloat16)
        yield
    attended = mm(s.ctx[...], columns(w1, 3 * width, 4 * width)) + small(4)
    normed, inv_scale = norm_rows(s.x[...].astype(jnp.float32) + attended)
    s.n1[...] = normed
    s.r1[...] = inv_scale
    hidden = normed * small(0) + small(5)
    s.h[...] = hidden
    s.hl[...] = hidden.astype(jnp.bfloat16)
    yield
    for part in range(4):
        pre = mm(s.hl[...], columns(w1, (4 + part) * width, (5 + part) * width)) + small(8 + part)
        half_erf = 0.5 + 0.5 * erf_of(pre * (0.5**0.5))
        s.g[part] = (pre * half_erf).astype(jnp.bfloat16)
        s.gp[part] = half_erf + pre * (jnp.exp(-0.5 * pre * pre) * (0.5 / math.pi) ** 0.5)
        yield
    branch = small(6)
    share = w2.shape[0] // 4
    for part in range(4):
        branch = branch + mm(s.g[part], rows_of(w2, part * share, (part + 1) * share))
    normed, inv_scale = norm_rows(s.h[...] + branch)
    s.n2[...] = normed
    s.r2[...] = inv_scale
    s.y[...] = (normed * small(1) + small(7)).astype(jnp.bfloat16)
    yield


def head_backward(s, w1, w2, g1, g2, small, sums, grad_in):
    width = s.x.shape[1]
    spans = s.x.shape[0] // SPAN
    grad_out = s.cot[...].astype(jnp.float32)
    sums[1:2] = column_sum(grad_out * s.n2[...])
    sums[7:8] = column_sum(grad_out)
    pre_two = norm_rows_back(grad_out, s.n2[...], s.r2[...], small(1))
    s.h[...] = pre_two
    branch = pre_two.astype(jnp.bfloat16)
    s.dz[...] = branch
    sums[6:7] = column_sum(branch)
    yield
    owners = w2.shape[0]
    share = owners // 4
    for part in range(4):
        own = slice(part * share, (part + 1) * share)
        grad_act = mm_nt(s.dz[...], rows_of(w2, part * share, (part + 1) * share))
        grad_pre = (grad_act * s.gp[part]).astype(jnp.bfloat16)
        g2[own] = (
            mm_tn(s.g[part], s.dz[...]).astype(jnp.bfloat16).reshape(share, g2.shape[1], width)
        )
        s.g[part] = grad_pre
        sums[8 + part : 9 + part] = column_sum(grad_pre)
        yield
    for part in range(4):
        at = (4 + part) * width
        grad_pre = s.g[part]
        s.h[...] += mm_nt(grad_pre, columns(w1, at, at + width))
        put_columns(g1, at, mm_tn(s.hl[...], grad_pre))
        yield
    grad_hidden = s.h[...]
    sums[0:1] = column_sum(grad_hidden * s.n1[...])
    sums[5:6] = column_sum(grad_hidden)
    pre_one = norm_rows_back(grad_hidden, s.n1[...], s.r1[...], small(0))
    s.h[...] = pre_one
    attended = pre_one.astype(jnp.bfloat16)
    s.dz[...] = attended
    sums[4:5] = column_sum(attended)
    yield
    s.hl[...] = mm_nt(attended, columns(w1, 3 * width, 4 * width)).astype(jnp.bfloat16)
    put_columns(g1, 3 * width, mm_tn(s.ctx[...], attended))
    yield
    lane = lax.broadcasted_iota(jnp.int32, (SPAN, 128), 1)
    for span in range(spans):
        for pair in range(width // 128):
            at = (slice(span * SPAN, (span + 1) * SPAN), slice(pair * 128, (pair + 1) * 128))
            q, k, v, dc = s.q[at], s.k[at], s.v[at], s.hl[at]
            dq, dk, dv = [], [], []
            for side in range(2):
                here = (lane < 64) if side == 0 else (lane >= 64)
                probs = s.p[(span * 6 + pair) * 2 + side]
                grad_probs = mm_nt(jnp.where(here, dc, jnp.zeros_like(dc)), v)
                dv.append(mm_tn(probs.astype(jnp.bfloat16), dc))
                grad_scores = probs * (
                    grad_probs - jnp.sum(probs * grad_probs, axis=-1, keepdims=True)
                )
                grad_scores = grad_scores.astype(jnp.bfloat16)
                dq.append(mm(grad_scores, k))
                dk.append(mm_tn(grad_scores, q))
            join = lambda two: jnp.where(lane < 64, two[0], two[1])
            s.q[at] = (join(dq) * score_scale).astype(jnp.bfloat16)
            s.k[at] = (join(dk) * score_scale).astype(jnp.bfloat16)
            s.v[at] = join(dv).astype(jnp.bfloat16)
        yield
    sums[2:3] = column_sum(s.q[...])
    sums[3:4] = column_sum(s.v[...])
    total = s.h[...]
    for k, ref in enumerate((s.q, s.k, s.v)):
        total = total + mm_nt(ref[...], columns(w1, k * width, (k + 1) * width))
    grad_in[...] = total
    yield
    for k, ref in enumerate((s.q, s.k, s.v)):
        put_columns(g1, k * width, mm_tn(s.x[...], ref[...]))
    yield


HIGHEST = lax.Precision.HIGHEST
ROWS = 16


def iota(shape, axis):
    return lax.broadcasted_iota(jnp.int32, shape, axis)


def ones_where(condition, dtype):
    return jnp.where(condition, 1.0, 0.0).astype(dtype)


def exact(a, b, dims):
    return lax.dot_general(
        a, b, (dims, ((), ())), precision=HIGHEST, preferred_element_type=jnp.float32
    )


class Plane:
    def __init__(self, sem):
        self.sem = sem
        self.wide, self.z = lax.axis_index("wide"), lax.axis_index("narrow")
        self.sent = []

    def send(self, index, src, recv):
        for k in range(1, 8):
            peer = (self.wide + k) % 8
            send(src(peer), recv.at[self.wide], self.sem.at[index, 0], self.sem.at[index, 1], (peer, self.z))
        self.sent.append((index, recv))

    def arrive(self, index, recv):
        await_bytes(recv.at[pl.ds(0, 7)], self.sem.at[index, 1])

    def drain(self):
        for index, recv in self.sent:
            await_sent(recv.at[pl.ds(0, 7)], self.sem.at[index, 0])

    def total(self, index, recv):
        self.arrive(index, recv)
        total = recv[0].astype(jnp.float32)
        for k in range(1, 8):
            total = total + recv[k].astype(jnp.float32)
        return total

    def place_rows(self, two):
        row = iota((ROWS, two.shape[1]), 0)
        rows = jnp.where(row % 2 == 0, two[0:1], two[1:2])
        return jnp.where(row // 2 == self.wide, rows, 0.0)

    def pick_rows(self, values, first):
        row = iota(values.shape, 0)
        one = lambda k: jnp.sum(jnp.where(row == first + k, values, 0.0), axis=0, keepdims=True)
        return jnp.concatenate([one(0), one(1)], axis=0)

    def share(self, index, two, src, recv):
        placed = self.place_rows(two).astype(src.dtype)
        src[...] = placed
        recv[self.wide] = placed
        self.send(index, lambda peer: src, recv)

    def collect(self, index, values, src, recv):
        for k in range(2):
            src[k] = values[8 * k : 8 * k + 8]
        recv[self.wide] = jnp.where(self.wide // 4 == 0, values[0:8], values[8:16])
        self.send(index, lambda peer: src.at[peer // 4], recv)

    def collected(self, index, recv):
        return self.pick_rows(self.total(index, recv), 2 * (self.wide % 4))


def backbone_forward(s, plane, small, finish):
    x0, w0 = s.x0, s.w0
    width = x0.shape[1]
    spans = x0.shape[0] // SPAN
    wide = plane.wide
    x = x0[...]
    s.k0[...] = mm(x, columns(w0, width, 2 * width)).astype(jnp.bfloat16)
    s.v0[...] = (mm(x, columns(w0, 2 * width, 3 * width)) + small(3)).astype(jnp.bfloat16)
    first = jnp.concatenate(
        [x0[SPAN * span : SPAN * span + 1].astype(jnp.float32) for span in range(spans)], axis=0
    )
    query = mm(first.astype(jnp.bfloat16), columns(w0, 0, width)) + small(2)
    s.keep[0, 0:spans] = first
    s.keep[1, 0:spans] = query.astype(jnp.bfloat16).astype(jnp.float32)
    yield
    heads = ones_where(iota((width, 128), 0) // (width // HEADS) == iota((width, 128), 1), jnp.bfloat16)
    context = []
    for span in range(spans):
        at = slice(span * SPAN, (span + 1) * SPAN)
        product = s.k0[at].astype(jnp.float32) * s.keep[1, span : span + 1]
        scores = exact(product, heads.astype(jnp.float32), ((1,), (0,))) * score_scale
        scores = jnp.where(iota(scores.shape, 0) < s.lengths[span], scores, masked_score)
        weight = jnp.exp(scores - jnp.max(scores, axis=0, keepdims=True))
        probs = weight / jnp.sum(weight, axis=0, keepdims=True)
        s.p0[span] = probs
        spread = mm_nt(probs.astype(jnp.bfloat16), heads)
        context.append(jnp.sum(spread * s.v0[at].astype(jnp.float32), axis=0, keepdims=True))
    context = jnp.concatenate(context, axis=0).astype(jnp.bfloat16)
    s.keep[2, 0:spans] = context.astype(jnp.float32)
    attended = mm(context, columns(w0, 3 * width, 4 * width)) + small(4)
    normed, inv_scale = norm_rows(s.keep[0, 0:spans] + attended)
    hidden = normed * small(0) + small(5)
    s.keep[3, 0:spans] = normed
    s.keep[4, 0:spans] = jnp.broadcast_to(inv_scale, normed.shape)
    s.keep[5, 0:spans] = hidden
    plane.share(0, hidden, s.e0_src, s.e0)
    yield
    hidden_all = plane.total(0, s.e0).astype(jnp.bfloat16)
    share = width // 8
    pick = ones_where(iota((width, share), 0) == share * wide + iota((width, share), 1), jnp.bfloat16)
    own = mm(hidden_all, pick).astype(jnp.bfloat16)
    upz = s.upz
    part = upz.shape[2] // 8
    for k in range(8):
        s.e1_src[k] = mm(own, columns(upz, k * part, (k + 1) * part))
    s.e1[wide] = s.e1_src[wide]
    plane.send(1, lambda peer: s.e1_src.at[peer], s.e1)
    yield
    bias = jnp.where(wide % 2 == 0, small(8 + wide // 2)[:, :part], small(8 + wide // 2)[:, part:])
    pre = plane.total(1, s.e1) + bias
    half_erf = 0.5 + 0.5 * erf_of(pre * (0.5**0.5))
    s.g0[...] = (pre * half_erf).astype(jnp.bfloat16)
    s.gp0[...] = half_erf + pre * (jnp.exp(-0.5 * pre * pre) * (0.5 / math.pi) ** 0.5)
    plane.collect(2, mm(s.g0[...], rows_of(s.downz, 0, 4)), s.e2_src, s.e2)
    yield
    branch = plane.collected(2, s.e2) + small(6)
    normed, inv_scale = norm_rows(s.keep[5, 0:spans] + branch)
    s.keep[6, 0:spans] = normed
    s.keep[7, 0:spans] = jnp.broadcast_to(inv_scale, normed.shape)
    finish(normed * small(1) + small(7))
    yield


def backbone_backward(s, plane, small, grad_rows):
    x0, w0 = s.x0, s.w0
    width = x0.shape[1]
    spans = x0.shape[0] // SPAN
    wide = plane.wide
    keep = lambda k: s.keep[k, 0:spans]
    acts, sums = s.acts, s.sums0

    def put(item, values):
        for span in range(spans):
            row = span * ROWS + item
            acts[row : row + 1] = values[span : span + 1]

    acts[...] = jnp.zeros_like(acts)
    grad_out = grad_rows()
    sums[1:2] = column_sum(grad_out * keep(6))
    sums[7:8] = column_sum(grad_out)
    pre_two = norm_rows_back(grad_out, keep(6), keep(7), small(1))
    s.keep[8, 0:spans] = pre_two
    low = lambda a: a.astype(jnp.bfloat16).astype(jnp.float32)
    put(11, low(pre_two))
    plane.share(3, pre_two, s.e3_src, s.e3)
    yield
    branch = plane.total(3, s.e3).astype(jnp.bfloat16)
    grad_act = mm_nt(branch, rows_of(s.downz, 0, 4))
    part = s.g0.shape[1]
    s.e4_src[:, :part] = (grad_act * s.gp0[...]).astype(jnp.bfloat16)
    s.e4_src[:, part:] = s.g0[...]
    s.e4[wide] = s.e4_src[...]
    plane.send(4, lambda peer: s.e4_src, s.e4)
    yield
    plane.arrive(4, s.e4)
    total = jnp.zeros((ROWS, width // 8), jnp.float32)
    for k in range(8):
        both = s.e4[k]
        total = total + mm_nt(both[:, :part], columns(s.upz, k * part, (k + 1) * part))
        rows = plane.pick_rows(both.astype(jnp.float32), 2 * wide)
        at = slice((k % 2) * part, (k % 2 + 1) * part)
        for span in range(spans):
            row = span * ROWS + 3 + k // 2
            acts[row : row + 1, at] = rows[span : span + 1, :part]
            acts[row + 4 : row + 5, at] = rows[span : span + 1, part:]
    share = width // 8
    pick = ones_where(iota((width, share), 0) == share * wide + iota((width, share), 1), jnp.float32)
    plane.collect(5, exact(total, pick, ((1,), (1,))), s.e5_src, s.e5)
    yield
    grad_hidden = keep(8) + plane.collected(5, s.e5)
    sums[0:1] = column_sum(grad_hidden * keep(3))
    sums[5:6] = column_sum(grad_hidden)
    pre_one = norm_rows_back(grad_hidden, keep(3), keep(4), small(0))
    attended = pre_one.astype(jnp.bfloat16)
    context = low(mm_nt(attended, columns(w0, 3 * width, 4 * width)))
    heads = ones_where(iota((width, 128), 0) // (width // HEADS) == iota((width, 128), 1), jnp.bfloat16)
    queries = []
    for span in range(spans):
        at = slice(span * SPAN, (span + 1) * SPAN)
        probs = s.p0[span]
        grad_context = context[span : span + 1]
        product = s.v0[at].astype(jnp.float32) * grad_context
        grad_probs = exact(product, heads.astype(jnp.float32), ((1,), (0,)))
        grad_scores = probs * (grad_probs - jnp.sum(probs * grad_probs, axis=0, keepdims=True))
        spread = mm_nt(grad_scores.astype(jnp.bfloat16), heads) * score_scale
        queries.append(jnp.sum(spread * s.k0[at].astype(jnp.float32), axis=0, keepdims=True))
        s.k0[at] = (spread * s.keep[1, span : span + 1]).astype(jnp.bfloat16)
        s.v0[at] = (mm_nt(probs.astype(jnp.bfloat16), heads) * grad_context).astype(jnp.bfloat16)
    queries = jnp.concatenate(queries, axis=0).astype(jnp.bfloat16)
    sums[3:4] = column_sum(s.v0[...])
    put(0, keep(2))
    put(1, attended.astype(jnp.float32))
    put(2, low(keep(5)))
    put(12, keep(0))
    put(13, queries.astype(jnp.float32))
    s.acts_low[...] = acts[...].astype(jnp.bfloat16)
    s.keep[9, 0:spans] = pre_one + mm_nt(queries, columns(w0, 0, width))
    yield
    grad_in = s.embeds_grad
    grad_in[...] = mm_nt(s.k0[...], columns(w0, width, 2 * width))
    grad_in[...] += mm_nt(s.v0[...], columns(w0, 2 * width, 3 * width))
    for span in range(spans):
        grad_in[SPAN * span : SPAN * span + 1] += s.keep[9, span : span + 1]
    put_columns(w0, width, mm_tn(x0[...], s.k0[...]))
    put_columns(w0, 2 * width, mm_tn(x0[...], s.v0[...]))
    yield


def backbone_weight_grads(s, at, o1, o2, small_out):
    width = s.x0.shape[1]
    gathered = s.g[...].reshape(-1, width)
    spans = 64

    def item(k):
        shape = (spans, gathered.shape[0])
        row, column = iota(shape, 0), iota(shape, 1)
        pick = column == (row // 2) * 32 + (row % 2) * ROWS + k
        return mm(ones_where(pick, jnp.bfloat16), gathered)

    share = width // 32
    shape = (width, 128)

    def picker(count, offset, dtype):
        row, column = iota(shape, 0), iota(shape, 1)
        return ones_where((row + offset == count * at + column) & (column < count), dtype)

    narrow = picker(share, 0, jnp.bfloat16)
    own = lambda k: mm(item(k).astype(jnp.bfloat16), narrow).astype(jnp.bfloat16)
    grad_query = item(13)
    o1[0, :, 0:width] = mm_tn(own(12), grad_query.astype(jnp.bfloat16))[:share]
    grad_attended = item(1)
    o1[0, :, 3 * width : 4 * width] = mm_tn(own(0), grad_attended.astype(jnp.bfloat16))[:share]
    branch = item(11)
    hidden = own(2)
    wide_sum = jnp.zeros((1, 128), jnp.float32)
    act = jnp.zeros((spans, 128), jnp.float32)
    for part in range(4):
        grad_pre = item(3 + part)
        o1[0, :, (4 + part) * width : (5 + part) * width] = mm_tn(hidden, grad_pre.astype(jnp.bfloat16))[:share]
        act = act + mm(item(7 + part).astype(jnp.bfloat16), picker(4 * share, part * width, jnp.bfloat16))
        wide_sum = wide_sum + exact(
            column_sum(grad_pre), picker(4 * share, part * width, jnp.float32), ((1,), (0,))
        )
    o2[0] = mm_tn(act.astype(jnp.bfloat16), branch.astype(jnp.bfloat16))[: 4 * share]
    exact_narrow = picker(share, 0, jnp.float32)
    s.late[...] = jnp.zeros_like(s.late)
    for row, values in ((2, grad_query), (4, grad_attended), (6, branch)):
        s.late[row : row + 1] = exact(column_sum(values), exact_narrow, ((1,), (0,)))
    small_out[8:9] = wide_sum


def step_kernel(
    qkv_in, out_in, up_in, down_in, up_bias, gains, biases, x0_in, skip_in, cot_in, lengths, y_out, embeds_out,
    skip_out, o1, o2, small_out, acts_all, *scratch,
):
    s = Refs(lengths=lengths)
    for (name, _, _), ref in zip(step_scratch(x0_in.shape[1]), scratch):
        setattr(s, name, ref)
    x0, skip, skip_grad = s.x0, s.skip, s.skip_grad
    gather_sem, column_sem, reduce_sem, plane_sem, load_sem = scratch[-5:]
    width = x0.shape[1]
    spans = x0.shape[0] // SPAN
    y, x, c, z = place()
    wide = lax.axis_index("wide")
    me = flat(y, x, c, z)
    w0, w1, w2, upz, downz, pars = s.w0, s.w1, s.w2, s.upz, s.downz, s.pars
    loads = [
        pltpu.make_async_copy(src, dst, load_sem.at[k])
        for k, (src, dst) in enumerate(
            (
                (qkv_in, o1.at[:, :, : 3 * width]), (out_in, o1.at[:, :, 3 * width : 4 * width]),
                (up_in, o1.at[:, :, 4 * width :]), (down_in, o2), (x0_in, x0), (skip_in, skip), (cot_in, s.cot),
            )
        )
    ]
    for load in loads:
        load.start()
    greet(wide, z)
    for load in loads[:4]:
        load.wait()
    w0[me] = o1[0, :, : 4 * width].astype(jnp.bfloat16)
    w1[me] = o1[1].astype(jnp.bfloat16)
    w2[me] = o2[1].astype(jnp.bfloat16)
    upz[z] = o1[0, :, 4 * width :].astype(jnp.bfloat16)
    downz[z] = o2[0].astype(jnp.bfloat16)
    s.small_all[me] = jnp.zeros((2 * ROWS, 128), jnp.float32)
    for layer in range(2):
        r, share = ROWS * layer, width // 32
        s.small_all[me, r : r + 2, :share] = gains[layer]
        s.small_all[me, r + 2 : r + 8, :share] = biases[:, layer]
        s.small_all[me, r + 8 : r + 9, : 4 * share] = up_bias[layer : layer + 1]

    half, mid = 2 * width, w2.shape[1] // 2

    def column_pair(ref, start):
        cut = lambda at: (lambda u: ref.at[u, :, at : at + half])
        subs = [(None, cut(start), "x"), (None, cut(start + half), "y")]
        return subs, lambda n: ref.at[pl.ds(0, n), :, start : start + half]

    rows_cut = lambda at: (lambda u: w2.at[u, at : at + mid])
    sets = [
        ([(None, lambda u: s.small_all.at[u], "x")], lambda n: s.small_all.at[pl.ds(0, n)]),
        column_pair(w0, 0),
        column_pair(w1, 0),
        column_pair(w1, 2 * half),
        ([(None, rows_cut(0), "x"), (None, rows_cut(mid), "y")], lambda n: w2.at[pl.ds(0, n), :mid]),
    ]
    events = []
    drains = []
    for k, (subs, many) in enumerate(sets):
        steps, drain = gather_steps(subs, many, gather_sem.at[k])
        drains.append(drain)
        for step, action in enumerate(steps):
            events.append((SET_AT[k][step], action))
    steps, drain = column_steps(
        [lambda zz: upz.at[zz], lambda zz: downz.at[zz]],
        [lambda n: w1.at[pl.ds(0, n), :, : 2 * half], lambda n: w2.at[pl.ds(0, n)]],
        column_sem,
    )
    drains.append(drain)
    events += zip(COLUMN_AT, steps)

    def row_of(layer):
        return lambda k: pars[pl.ds(ROWS * layer + k, 1), :]

    def unpack():
        share = width // 32
        for layer in range(2):
            r = ROWS * layer
            for d in range(32):
                pars[r : r + 8, share * d : share * (d + 1)] = s.small_all[d, r : r + 8, :share]
                at = slice((d % 8) * 4 * share, (d % 8 + 1) * 4 * share)
                pars[r + 8 + d // 8 : r + 9 + d // 8, at] = s.small_all[d, r + 8 : r + 9, : 4 * share]
        pars[...] = pars[...].astype(jnp.bfloat16).astype(jnp.float32)

    def join(rows):
        row = iota(skip.shape, 0)
        joined = skip[...].astype(jnp.float32)
        for span in range(spans):
            joined = jnp.where(row == SPAN * span, rows[span : span + 1], joined)
        s.x[...] = joined.astype(jnp.bfloat16)

    def unload():
        for load in loads[4:]:
            load.wait()

    outs = []

    def put_out(src, dst):
        copy = pltpu.make_async_copy(src, dst, load_sem.at[len(outs)])
        copy.start()
        outs.append(copy)

    events += [(UNPACK_AT, unload)]
    plane = Plane(plane_sem)
    forward0 = backbone_forward(s, plane, row_of(0), join)
    forward1 = head_forward(s, w1, w2, row_of(1), lengths)
    events += [(UNPACK_AT, unpack)]
    events += [(at, lambda: next(forward0)) for at in FORWARD0_AT]
    events += [(at, lambda: next(forward1)) for at in FORWARD1_AT]
    for _, action in sorted(events, key=lambda event: event[0]):
        action()
    for drain in drains:
        drain()
    put_out(s.y, y_out)

    back1 = head_backward(s, w1, w2, w1, w2, row_of(1), s.sums, skip_grad)
    back0 = backbone_backward(
        s, plane, row_of(0),
        lambda: jnp.concatenate([skip_grad[SPAN * k : SPAN * k + 1] for k in range(spans)], axis=0),
    )

    def reduced(whole, own, out, name, dim):
        bufs = [getattr(s, name + kind) for kind in KINDS]
        return Refs(all=whole, own=own, out=out, dim=dim, sib=bufs[0], second=bufs[1], first=bufs[2], chain=bufs[3])

    def pair(ref, start, stop, out, name):
        middle = (start + stop) // 2
        cut = lambda a, b: (ref.at[:, :, a:b], lambda u: ref.at[u, :, a:b], out.at[:, a:b])
        return [
            reduced(*cut(start, middle), name + "a", "x"),
            reduced(*cut(middle, stop), name + "b", "y"),
        ]

    made = iter(range(6))
    group = lambda *subs: Reduce(subs, reduce_sem.at[next(made)])
    group_late = lambda *subs: ReduceLate(subs, reduce_sem.at[next(made)])
    cut = lambda a, b: (w2.at[:, a:b], lambda u: w2.at[u, a:b], o2.at[1, a:b])
    downs = [group_late(reduced(*cut(0, mid), "da", "x"), reduced(*cut(mid, 2 * mid), "db", "y"))]
    ups = [group_late(*pair(w1, 4 * width, 8 * width, o1.at[1], "u"))]
    lefts = [
        group(*pair(w1, 0, 4 * width, o1.at[1], "q")),
        group(reduced(s.block1, lambda u: s.block1.at[u], small_out.at[ROWS : 2 * ROWS], "s1", "x")),
    ]
    kvs = [
        group(*pair(w0, width, 3 * width, o1.at[0], "k")),
        group(reduced(s.block0, lambda u: s.block0.at[u], small_out.at[0:8], "s0", "y")),
    ]
    waves = Waves([downs, ups, lefts, kvs], LAGS)

    def start(groups):
        for zz in TARGETS:
            for each in groups:
                each.start(zz)

    def fill_blocks(block, sums, wide_too):
        share = width // 32
        block[...] = jnp.zeros_like(block)
        for d in range(32):
            block[d, 0:8, :share] = sums[0:8, share * d : share * (d + 1)]
            if wide_too:
                at = slice((d % 8) * 4 * share, (d % 8 + 1) * 4 * share)
                block[d, 8:9, : 4 * share] = sums[8 + d // 8 : 9 + d // 8, at]

    def step(times):
        for _ in range(times):
            waves.step()

    next(back1)
    for chip in range(4):
        next(back1)
        for each in downs:
            each.start_chip(chip)
    next(back1)
    next(back1)
    step(STEPS[0])
    next(back1)
    next(back1)
    step(STEPS[1])
    next(back1)
    start(ups)
    next(back1)
    step(STEPS[2])
    next(back1)
    step(STEPS[3])
    next(back1)
    step(STEPS[4])
    next(back1)
    next(back0)
    step(STEPS[5])
    next(back1)
    fill_blocks(s.block1, s.sums, True)
    start(lefts)
    next(back0)
    step(STEPS[6])
    next(back0)
    step(STEPS[7])
    next(back0)
    home = lambda u: acts_all.at[u // 8, pl.ds(pl.multiple_of((u % 8) * 32, 32), 32)]
    own_acts = pltpu.make_async_copy(s.acts_low, home(me), load_sem.at[5])
    own_acts.start()
    rows = lambda n: acts_all.at[pl.ds(0, n // 16)] if n >= 16 else acts_all.at[0, pl.ds(0, ROWS * n)]
    part = lambda k: (lambda u: home(u).at[pl.ds(ROWS * k, ROWS)])
    spread, drain = gather_steps(
        [(s.acts_low.at[pl.ds(ROWS * k, ROWS)], part(k), dim) for k, dim in enumerate("xy")], rows, gather_sem.at[5]
    )
    spread[0]()
    next(back0)
    fill_blocks(s.block0, s.sums0, False)
    start(kvs)
    row = iota(skip_grad.shape, 0)
    skip_grad[...] = jnp.where(row % SPAN == 0, 0.0, skip_grad[...])
    put_out(skip_grad, skip_out)
    put_out(s.embeds_grad, embeds_out)
    left = waves.left()
    turns = left - TAIL
    for k in range(left):
        waves.step()
        if k < turns:
            for action in spread[1 + 15 * k // turns : 1 + 15 * (k + 1) // turns]:
                action()
        if k == turns - 1:
            own_acts.wait()
            load = pltpu.make_async_copy(acts_all, s.g, load_sem.at[6])
            load.start()
            load.wait()
            backbone_weight_grads(s, me, o1, o2, small_out)
    small_out[0:8] += s.late[...]
    drain()
    plane.drain()
    for copy in outs:
        copy.wait()


SET_AT = ((0, 1, 2, 3, 4, 5, 6, 7, 8, 9, 10, 11, 12, 13, 14, 15), (0, 1, 2, 3, 4, 5, 6, 7, 8, 9, 10, 11, 12, 13, 14, 15), (1.2, 8, 9, 10, 11, 12, 13, 15, 16, 17, 18, 19, 20, 21, 22, 23), (3.2, 14, 15, 16, 17, 18, 19, 22, 23, 24, 25, 26, 27, 28, 29, 30), (5.2, 20, 21, 22, 23, 24, 25, 28.0, 28.7, 29.4, 30.1, 30.8, 31.5, 32.2, 32.9, 33.6))
UNPACK_AT = 15.05
COLUMN_AT = (2.5, 4.5, 6.5, 8.5)
FORWARD0_AT = (15.3, 16.2, 18, 20, 22)
FORWARD1_AT = (23.1, 23.9, 24.7, 25.34, 30.1, 30.9, 31.7, 32.5, 33.7)
LAGS = (0, 2, 4, 6, 8)
STEPS = (2, 2, 1, 1, 1, 1, 2, 2)
TAIL = 2
KINDS = ("sib", "second", "first", "chain")


def step_scratch(width):
    low, full = jnp.bfloat16, jnp.float32
    share = width // 32
    rows = 2 * SPAN
    found = [
        ("w0", (32, share, 4 * width), low), ("upz", (4, share, 4 * width), low),
        ("downz", (4, 4 * share, width), low), ("w1", (32, share, 8 * width), low),
        ("w2", (32, 4 * share, width), low), ("small_all", (32, 2 * ROWS, 128), full),
        ("pars", (2 * ROWS, width), full), ("sums", (ROWS, width), full), ("sums0", (8, width), full),
        ("keep", (ROWS, 8, width), full), ("p0", (2, SPAN, 128), full),
        ("g0", (ROWS, width // 2), low), ("gp0", (ROWS, width // 2), full),
        ("e0_src", (ROWS, width), low), ("e0", (8, ROWS, width), low),
        ("e1_src", (8, ROWS, width // 2), full), ("e1", (8, ROWS, width // 2), full),
        ("e2_src", (2, 8, width), full), ("e2", (8, 8, width), full),
        ("e3_src", (ROWS, width), low), ("e3", (8, ROWS, width), low),
        ("e4_src", (ROWS, width), low), ("e4", (8, ROWS, width), low),
        ("e5_src", (2, 8, width), full), ("e5", (8, 8, width), full),
        ("acts", (2 * ROWS, width), full), ("acts_low", (2 * ROWS, width), low),
        ("late", (8, 128), full), ("block1", (32, ROWS, 128), full), ("block0", (32, 8, 128), full),
        ("g", (4, rows, width), low), ("gp", (4, rows, width), full),
        ("p", (2 * HEADS, SPAN, SPAN), full), ("r1", (rows, 1), full), ("r2", (rows, 1), full),
    ]
    found += [(name, (rows, width), low) for name in ("x", "q", "k", "v", "ctx", "hl", "dz", "k0", "v0", "x0", "skip", "cot", "y")]
    found += [(name, (rows, width), full) for name in ("n1", "h", "n2", "skip_grad", "embeds_grad")]
    shapes = {
        "d": ((2 * share, width), low), "u": ((share, 2 * width), low), "q": ((share, 2 * width), low),
        "k": ((share, width), low),
    }
    blocks = [(name + side, shape) for name, shape in shapes.items() for side in "ab"]
    blocks += [("s1", ((ROWS, 128), full)), ("s0", ((8, 128), full))]
    for name, (shape, dtype) in blocks:
        for kind, many in zip(KINDS, (16, 8, 2, 10) if name[0] in "du" else (16, 8, 4, 5)):
            found.append((name + kind, (many,) + shape, dtype))
    return found


def step_call(params, embeds, skip_tokens, cotangent, lengths):
    vmem, hbm = pl.BlockSpec(memory_space=pltpu.VMEM), pl.BlockSpec(memory_space=pl.ANY)
    rows, width = embeds.shape
    share = width // 32
    scratch = [pltpu.VMEM(shape, dtype) for _, shape, dtype in step_scratch(width)]
    scratch += [
        pltpu.SemaphoreType.DMA((6, GATHER_SEMS)),
        pltpu.SemaphoreType.DMA((2, 5)),
        pltpu.SemaphoreType.DMA((6, REDUCE_SEMS)),
        pltpu.SemaphoreType.DMA((6, 2)),
        pltpu.SemaphoreType.DMA((7,)),
    ]
    shape = jax.ShapeDtypeStruct
    return pl.pallas_call(
        step_kernel,
        out_shape=[
            shape((rows, width), jnp.bfloat16), shape((rows, width), jnp.float32),
            shape((rows, width), jnp.float32), shape((2, share, 8 * width), jnp.float32),
            shape((2, 4 * share, width), jnp.float32), shape((2 * ROWS, 128), jnp.float32),
            shape((4, rows, width), jnp.bfloat16),
        ],
        in_specs=[hbm] * 4 + [vmem] * 3 + [hbm] * 3 + [pl.BlockSpec(memory_space=pltpu.SMEM)],
        out_specs=[hbm] * 3 + [vmem] * 3 + [hbm],
        scratch_shapes=scratch,
        compiler_params=pltpu.CompilerParams(
            collective_id=1, has_side_effects=True, vmem_limit_bytes=64 * 2**20
        ),
    )(*params, embeds, skip_tokens, cotangent, lengths)


def adam_parts(parameter, first, second, gradient, decayed):
    first = beta_first * first + (1.0 - beta_first) * gradient
    second = beta_second * second + (1.0 - beta_second) * gradient * gradient
    update = first / first_fix / (jnp.sqrt(second / second_fix) + adam_epsilon)
    if decayed:
        update = update + weight_decay * parameter
    return update, first, second


def adam_kernel(*refs):
    params, moments = refs[0:7], refs[7:14]
    joined, down, small = refs[14:17]
    passed, steps, news, handed = refs[17:20], refs[20:27], refs[27:34], refs[34:37]

    def update(index, gradient):
        step, first, second = adam_parts(
            params[index][...], moments[index][0], moments[index][1], gradient, index < 4
        )
        steps[index][...] = step
        news[index][0] = first
        news[index][1] = second

    qkv, out = params[0].shape[2], params[1].shape[2]
    update(0, joined[:, :, :qkv])
    update(1, joined[:, :, qkv : qkv + out])
    update(2, joined[:, :, qkv + out :])
    update(3, down[...])

    @pl.when(pl.program_id(1) == 0)
    def _():
        for src, dst in zip(passed, handed):
            dst[...] = src[...]

    @pl.when((pl.program_id(0) == 0) & (pl.program_id(1) == 0))
    def _():
        many = small.shape[0] // 2
        for layer in range(2):
            at = layer * many
            for index, start, stop in ((4, 8, 9), (5, 0, 2), (6, 2, 8)):
                width = params[index].shape[-1]
                here = (slice(layer, layer + 1),) if index == 4 else (layer,)
                here = here if index < 6 else (slice(None), layer)
                step, first, second = adam_parts(
                    params[index][here], moments[index][(0, *here)], moments[index][(1, *here)],
                    small[at + start : at + stop, :width], False,
                )
                steps[index][here] = step
                news[index][(0, *here)] = first
                news[index][(1, *here)] = second


def adam_update(params, moments, joined, down, small, passed):
    cuts = 3 if params[0].shape[1] % 24 == 0 else 1

    def whole(a):
        return pl.BlockSpec(a.shape, lambda l, r, n=a.ndim: (0,) * n)

    def rows(a):
        return pl.BlockSpec((1, a.shape[1] // cuts, a.shape[2]), lambda l, r: (l, r, 0))

    def pairs(a):
        return pl.BlockSpec((2, 1, a.shape[2] // cuts, a.shape[3]), lambda l, r: (0, l, r, 0))

    halves = [pl.BlockSpec((a.shape[0] // 2, a.shape[1]), lambda l, r: (l, 0)) for a in passed]
    param_specs = [rows(a) for a in params[:4]] + [whole(a) for a in params[4:]]
    moment_specs = [pairs(a) for a in moments[:4]] + [whole(a) for a in moments[4:]]
    shape = lambda a: jax.ShapeDtypeStruct(a.shape, a.dtype)
    out = pl.pallas_call(
        adam_kernel,
        grid=(2, cuts),
        out_shape=[shape(a) for a in (*params, *moments, *passed)],
        in_specs=param_specs + moment_specs + [rows(joined), rows(down), whole(small)] + halves,
        out_specs=param_specs + moment_specs + halves,
        compiler_params=pltpu.CompilerParams(vmem_limit_bytes=63 * 2**20),
    )(*params, *moments, joined, down, small, *passed)
    return out[:7], out[7:14], out[14:]


def first_forward(weights, inputs, key_valid):
    qkv_w, out_w, up_w, down_w, up_b, gain_rows, biases = weights
    row_count, width = inputs.shape
    span_count = row_count // SPAN
    first = inputs.reshape(span_count, SPAN, width)[:, 0]
    mixed = jnp.dot(inputs, qkv_w[:, width:], preferred_element_type=jnp.float32)
    keys = mixed[:, :width].astype(jnp.bfloat16).reshape(span_count, SPAN, HEADS, width // HEADS)
    values = (mixed[:, width:] + biases[1]).astype(jnp.bfloat16)
    values = values.reshape(span_count, SPAN, HEADS, width // HEADS)
    queries = jnp.dot(first, qkv_w[:, :width], preferred_element_type=jnp.float32) + biases[0]
    queries = queries.astype(jnp.bfloat16).reshape(span_count, HEADS, width // HEADS)
    scores = (
        jnp.einsum("bhe,bkhe->bhk", queries, keys, preferred_element_type=jnp.float32) * score_scale
    )
    scores = jnp.where(key_valid[:, None, :], scores, masked_score)
    probs = jax.nn.softmax(scores, axis=-1)
    context = jnp.einsum(
        "bhk,bkhe->bhe", probs.astype(jnp.bfloat16), values, preferred_element_type=jnp.float32
    )
    context = context.reshape(span_count, width).astype(jnp.bfloat16)
    attended = jnp.dot(context, out_w, preferred_element_type=jnp.float32) + biases[2]
    hidden, normed_one, scale_one = normalize(
        first.astype(jnp.float32) + attended, gain_rows[0], biases[3]
    )
    hidden_low = hidden.astype(jnp.bfloat16)
    pre_gelu = jnp.dot(hidden_low, up_w, preferred_element_type=jnp.float32) + up_b
    activated = jax.nn.gelu(pre_gelu, approximate=False).astype(jnp.bfloat16)
    branch_out = jnp.dot(activated, down_w, preferred_element_type=jnp.float32) + biases[4]
    output, normed_two, scale_two = normalize(hidden + branch_out, gain_rows[1], biases[5])
    saved = (
        first, queries, keys, values, probs, context, normed_one, scale_one, hidden_low, pre_gelu,
        activated, normed_two, scale_two,
    )
    return output, saved


def first_backward(weights, inputs, saved, grad_out):
    qkv_w, out_w, up_w, down_w, up_b, gain_rows, biases = weights
    (
        first, queries, keys, values, probs, context, normed_one, scale_one, hidden_low, pre_gelu,
        activated, normed_two, scale_two,
    ) = saved
    row_count, width = inputs.shape
    span_count = row_count // SPAN
    grad_pre_two, grad_gain_two, grad_shift_two = normalize_back(
        grad_out, normed_two, scale_two, gain_rows[1]
    )
    grad_branch = grad_pre_two.astype(jnp.bfloat16)
    grad_act = dot_last(grad_branch, down_w)
    _, gelu_back = jax.vjp(lambda inner: jax.nn.gelu(inner, approximate=False), pre_gelu)
    grad_pre_gelu = gelu_back(grad_act)[0].astype(jnp.bfloat16)
    grad_hidden = grad_pre_two + dot_last(grad_pre_gelu, up_w)
    grad_pre_one, grad_gain_one, grad_shift_one = normalize_back(
        grad_hidden, normed_one, scale_one, gain_rows[0]
    )
    grad_attended = grad_pre_one.astype(jnp.bfloat16)
    grad_context = dot_last(grad_attended, out_w).astype(jnp.bfloat16)
    grad_context = grad_context.reshape(span_count, HEADS, width // HEADS)
    grad_probs = jnp.einsum(
        "bhe,bkhe->bhk", grad_context, values, preferred_element_type=jnp.float32
    )
    grad_values = jnp.einsum("bhk,bhe->bkhe", probs.astype(jnp.bfloat16), grad_context)
    grad_values = grad_values.reshape(row_count, width).astype(jnp.bfloat16)
    grad_scores = probs * (grad_probs - jnp.sum(probs * grad_probs, axis=-1, keepdims=True))
    grad_scores = grad_scores.astype(jnp.bfloat16)
    grad_queries = (
        jnp.einsum("bhk,bkhe->bhe", grad_scores, keys, preferred_element_type=jnp.float32)
        * score_scale
    )
    grad_queries = grad_queries.reshape(span_count, width).astype(jnp.bfloat16)
    grad_keys = (
        jnp.einsum("bhk,bhe->bkhe", grad_scores, queries, preferred_element_type=jnp.float32)
        * score_scale
    )
    grad_keys = grad_keys.reshape(row_count, width).astype(jnp.bfloat16)
    grad_kv = jnp.concatenate([grad_keys, grad_values], axis=1)
    grad_kv_w = dot_first(inputs, grad_kv)
    grad_inputs = dot_last(grad_kv, qkv_w[:, width:])
    grad_first = grad_pre_one + dot_last(grad_queries, qkv_w[:, :width])
    placed = jnp.pad(grad_first[:, None], ((0, 0), (0, SPAN - 1), (0, 0))).reshape(row_count, width)
    grad_inputs = grad_inputs + placed
    rows = jnp.concatenate(
        [context, grad_attended, hidden_low, grad_pre_gelu, activated, grad_branch, first, grad_queries],
        axis=1,
    )

    def total(values):
        return jnp.sum(values, axis=0, dtype=jnp.float32)

    small = (
        total(grad_pre_gelu),
        jnp.stack([grad_gain_one, grad_gain_two]),
        jnp.stack(
            [
                total(grad_queries), total(grad_values), total(grad_attended), grad_shift_one,
                total(grad_branch), grad_shift_two,
            ]
        ),
    )
    return grad_inputs, grad_kv_w, rows, small


def first_weight_grads(rows, kv_owned, at):
    width = rows.shape[1] // 16
    wide = 4 * width
    context, grad_attended = rows[:, :width], rows[:, width : 2 * width]
    hidden_low = rows[:, 2 * width : 3 * width]
    grad_pre_gelu = rows[:, 3 * width : 3 * width + wide]
    activated = rows[:, 7 * width : 11 * width]
    grad_branch = rows[:, 11 * width : 12 * width]
    first = rows[:, 12 * width : 13 * width]
    grad_queries = rows[:, 13 * width : 14 * width]
    count = kv_owned.shape[0]
    own = lambda values, many: lax.dynamic_slice_in_dim(values, at * many, many, 1)
    return (
        jnp.concatenate([dot_first(own(first, count), grad_queries), kv_owned], axis=1),
        dot_first(own(context, count), grad_attended),
        dot_first(own(hidden_low, count), grad_pre_gelu),
        dot_first(own(activated, 4 * count), grad_branch),
    )


def pack_small(up_b, gains, biases, owners):
    parts = [up_b.reshape(owners, -1)]
    for tensor in (gains, biases):
        parts.append(tensor.reshape(tensor.shape[0], owners, -1).transpose(1, 0, 2).reshape(owners, -1))
    return jnp.concatenate(parts, axis=1)


def unpack_small(packed, width):
    owners = packed.shape[0]
    share = width // owners
    up_b = packed[:, : 4 * share].reshape(4 * width)
    gains = packed[:, 4 * share : 6 * share].reshape(owners, 2, share).transpose(1, 0, 2)
    biases = packed[:, 6 * share :].reshape(owners, 6, share).transpose(1, 0, 2)
    return up_b, gains.reshape(2, width), biases.reshape(6, width)


def exchange_weights(p1, p2, small):
    both = ("wide", "narrow")
    w1 = lax.all_gather(p1, both, axis=0)
    w2 = lax.all_gather(p2, both, axis=0)
    return (w1[:, 0], w1[:, 1]), (w2[:, 0], w2[:, 1]), lax.all_gather(small, both, axis=0)


def exchange_grads(g1, g2, kv, small, rows):
    both = ("wide", "narrow")
    summed = [
        lax.psum_scatter(a, both, scatter_dimension=0).astype(jnp.float32) for a in (g1, g2, kv, small)
    ]
    return summed + [lax.all_gather(rows, both, axis=0)]


def rows_ahead(group):
    last = group[6]
    return (*group[:6], jnp.swapaxes(last, last.ndim - 3, last.ndim - 2))


def fused_step(embeds, skip_tokens, cotangent, lengths, params, moments):
    params, moments = rows_ahead(params), rows_ahead(moments)
    y, embeds_grad, skip_grad, o1, o2, small, _ = step_call(params, embeds, skip_tokens, cotangent, lengths)
    new_steps, new_moments, passed = adam_update(params, moments, o1, o2, small, (y, embeds_grad, skip_grad))
    return (*passed, *rows_ahead(new_steps), *rows_ahead(new_moments))


def per_device(
    embeds, skip_tokens, cotangent, lengths, qkv_weight, out_weight, up_weight, down_weight, up_bias,
    norm_gains, biases, qkv_moments, out_moments, up_moments, down_moments, up_bias_moments,
    gain_moments, bias_moments,
):
    params = (qkv_weight, out_weight, up_weight, down_weight, up_bias, norm_gains, biases)
    moments = (
        qkv_moments, out_moments, up_moments, down_moments, up_bias_moments, gain_moments, bias_moments,
    )
    wide_size, narrow_size = lax.axis_size("wide"), lax.axis_size("narrow")
    if (wide_size, narrow_size) == (8, 4):
        return fused_step(embeds, skip_tokens, cotangent, lengths, params, moments)
    owners = wide_size * narrow_size
    at = lax.axis_index("wide") * narrow_size + lax.axis_index("narrow")
    span_count = lengths.shape[0]
    row_count, width = embeds.shape
    positions = lax.broadcasted_iota(jnp.int32, (span_count, SPAN), 1)
    key_valid = positions < lengths[:, None]
    row_index = lax.broadcasted_iota(jnp.int32, (1, SPAN, 1), 1)

    p1 = jnp.concatenate([qkv_weight, out_weight, up_weight], axis=2).astype(jnp.bfloat16)
    p2 = down_weight.astype(jnp.bfloat16)
    share = 12 * width // owners
    tiles = -(-2 * share // 1024)
    small_own = jnp.concatenate(
        [up_bias, norm_gains.reshape(2, -1), biases.reshape(2, -1)], axis=1
    ).reshape(-1)
    small_own = jnp.pad(small_own, (0, tiles * 1024 - 2 * share)).reshape(tiles * 8, 128)
    w1, w2, small_all = exchange_weights(p1, p2, small_own)
    small_all = small_all.reshape(owners, -1)[:, : 2 * share].astype(jnp.bfloat16).astype(jnp.float32)

    def layer_weights(layer):
        joined = w1[layer].reshape(width, -1)
        return (
            joined[:, : 3 * width], joined[:, 3 * width : 4 * width], joined[:, 4 * width :],
            w2[layer].reshape(-1, width),
        ) + unpack_small(small_all[:, layer * share : (layer + 1) * share], width)

    backbone, head = layer_weights(0), layer_weights(1)
    backbone_out, saved = first_forward(backbone, embeds, key_valid)
    skip_view = skip_tokens.reshape(span_count, SPAN, width)
    head_in = jnp.where(row_index == 0, backbone_out.astype(jnp.bfloat16)[:, None], skip_view)
    head_in = head_in.reshape(row_count, width)
    head_out, grad_head_in, head_grads = backward_block(
        head, head_in, key_valid, cotangent.astype(jnp.float32)
    )
    grad_view = grad_head_in.reshape(span_count, SPAN, width)
    skip_grad = jnp.where(row_index == 0, 0.0, grad_view).reshape(row_count, width)
    embeds_grad, grad_kv_w, rows, small_first = first_backward(
        backbone, embeds, saved, grad_view[:, 0]
    )
    low = lambda a: a.astype(jnp.bfloat16)
    g1 = jnp.concatenate([low(head_grads[0]), low(head_grads[1]), low(head_grads[2])], axis=1)
    g1 = g1.reshape(owners, width // owners, -1)
    g2 = low(head_grads[3]).reshape(owners, -1, width)
    kv = low(grad_kv_w).reshape(owners, width // owners, -1)
    small_grads = jnp.concatenate(
        [pack_small(*small_first, owners), pack_small(*head_grads[4:], owners)], axis=1
    )
    small_grads = jnp.pad(small_grads, ((0, 0), (0, tiles * 1024 - 2 * share)))
    small_grads = small_grads.reshape(owners, tiles * 8, 128)
    rows_wide = jnp.pad(rows, ((0, 0), (0, 2 * width)))
    own_g1, own_g2, own_kv, own_small, all_rows = exchange_grads(
        g1, g2, kv, small_grads, rows_wide.reshape(16 * span_count // 2, -1)
    )
    all_rows = all_rows.reshape(owners * span_count, -1)
    first_grads = first_weight_grads(all_rows, own_kv, at)
    own_small = own_small.reshape(-1)[: 2 * share].reshape(2, share)
    sixth = width // owners
    joined = jnp.stack([jnp.concatenate(first_grads[:3], axis=1), own_g1])
    down = jnp.stack([first_grads[3], own_g2])
    pad = lambda a: jnp.pad(a, ((0, 0), (0, 0), (0, 128 - a.shape[2])))
    small = [
        pad(own_small[:, 4 * sixth : 6 * sixth].reshape(2, 2, sixth)),
        pad(own_small[:, 6 * sixth :].reshape(2, 6, sixth)),
        pad(own_small[:, None, : 4 * sixth]),
        jnp.zeros((2, 7, 128), jnp.float32),
    ]
    small = jnp.concatenate(small, axis=1).reshape(32, 128)
    passed = (head_out.astype(jnp.bfloat16), embeds_grad, skip_grad)
    new_steps, new_moments, passed = adam_update(
        rows_ahead(params), rows_ahead(moments), joined, down, small, passed
    )
    return (*passed, *rows_ahead(new_steps), *rows_ahead(new_moments))


def solution(mesh):
    return jax.shard_map(
        per_device,
        mesh=mesh,
        in_specs=(
            P(("wide", "narrow"), None),
            P(("wide", "narrow"), None),
            P(("wide", "narrow"), None),
            P(("wide", "narrow")),
            P(None, ("wide", "narrow"), None),
            P(None, ("wide", "narrow"), None),
            P(None, ("wide", "narrow"), None),
            P(None, ("wide", "narrow"), None),
            P(None, ("wide", "narrow")),
            P(None, None, ("wide", "narrow")),
            P(None, None, ("wide", "narrow")),
            P(None, None, ("wide", "narrow"), None),
            P(None, None, ("wide", "narrow"), None),
            P(None, None, ("wide", "narrow"), None),
            P(None, None, ("wide", "narrow"), None),
            P(None, None, ("wide", "narrow")),
            P(None, None, None, ("wide", "narrow")),
            P(None, None, None, ("wide", "narrow")),
        ),
        out_specs=(
            P(("wide", "narrow"), None),
            P(("wide", "narrow"), None),
            P(("wide", "narrow"), None),
            P(None, ("wide", "narrow"), None),
            P(None, ("wide", "narrow"), None),
            P(None, ("wide", "narrow"), None),
            P(None, ("wide", "narrow"), None),
            P(None, ("wide", "narrow")),
            P(None, None, ("wide", "narrow")),
            P(None, None, ("wide", "narrow")),
            P(None, None, ("wide", "narrow"), None),
            P(None, None, ("wide", "narrow"), None),
            P(None, None, ("wide", "narrow"), None),
            P(None, None, ("wide", "narrow"), None),
            P(None, None, ("wide", "narrow")),
            P(None, None, None, ("wide", "narrow")),
            P(None, None, None, ("wide", "narrow")),
        ),
        check_vma=False,
    )
```

```python
import math

import jax
import jax.numpy as jnp
from jax import lax
from jax.experimental import pallas as pl
from jax.experimental.pallas import tpu as pltpu
from jax.sharding import PartitionSpec as P

HEADS = 12
SPAN = 128

norm_epsilon = 1e-12
score_scale = 0.125
masked_score = -1000000000.0
beta_first = 0.9
beta_second = 0.999
adam_epsilon = 1e-08
weight_decay = 0.01
first_fix = 1.0 - 0.9**10
second_fix = 1.0 - 0.999**10


def dot_first(left_side, right_side):
    return lax.dot_general(
        left_side, right_side, (((0,), (0,)), ((), ())), preferred_element_type=jnp.float32
    )


def dot_last(left_side, right_side):
    return lax.dot_general(
        left_side, right_side, (((1,), (1,)), ((), ())), preferred_element_type=jnp.float32
    )


def normalize(values, gain_row, shift_row):
    centred = values - jnp.mean(values, axis=-1, keepdims=True)
    inv_scale = lax.rsqrt(jnp.mean(centred * centred, axis=-1, keepdims=True) + norm_epsilon)
    normed = centred * inv_scale
    return (normed * gain_row + shift_row, normed, inv_scale)


def normalize_back(gradient, normed, inv_scale, gain_row):
    grad_gain = jnp.sum(gradient * normed, axis=0)
    grad_shift = jnp.sum(gradient, axis=0)
    scaled = gradient * gain_row
    grad_in = inv_scale * (
        scaled
        - jnp.mean(scaled, axis=-1, keepdims=True)
        - normed * jnp.mean(scaled * normed, axis=-1, keepdims=True)
    )
    return (grad_in, grad_gain, grad_shift)


def head_view(tensor):
    return tensor.reshape(tensor.shape[0] // SPAN, SPAN, HEADS, tensor.shape[1] // HEADS)


def attend_scores(queries, keys_low, key_valid):
    scores = (
        jnp.einsum(
            "bqhe,bkhe->bhqk",
            head_view(queries),
            head_view(keys_low),
            preferred_element_type=jnp.float32,
        )
        * score_scale
    )
    return jnp.where(key_valid[:, None, None, :], scores, masked_score)


def forward_block(weights, inputs, key_valid):
    qkv_w, out_w, up_w, down_w, up_b, gain_rows, biases = weights
    gains_wide = gain_rows.astype(jnp.float32)
    biases_wide = biases.astype(jnp.float32)
    row_count, model_width = inputs.shape
    mixed_in = jnp.dot(inputs, qkv_w, preferred_element_type=jnp.float32)
    queries = (mixed_in[:, :model_width] + biases_wide[0]).astype(jnp.bfloat16)
    keys_low = mixed_in[:, model_width : 2 * model_width].astype(jnp.bfloat16)
    values_low = (mixed_in[:, 2 * model_width :] + biases_wide[1]).astype(jnp.bfloat16)
    scores = attend_scores(queries, keys_low, key_valid)
    row_max = jnp.max(scores, axis=-1, keepdims=True)
    weights_exp = jnp.exp(scores - row_max)
    row_total = jnp.sum(weights_exp, axis=-1, keepdims=True)
    softmax_out = (weights_exp / row_total).astype(jnp.bfloat16)
    log_total = row_max + jnp.log(row_total)
    context = jnp.einsum(
        "bhqk,bkhe->bqhe", softmax_out, head_view(values_low), preferred_element_type=jnp.float32
    )
    context = context.reshape(row_count, model_width).astype(jnp.bfloat16)
    attended = jnp.dot(context, out_w, preferred_element_type=jnp.float32) + biases_wide[2]
    hidden, normed_one, scale_one = normalize(
        inputs.astype(jnp.float32) + attended, gains_wide[0], biases_wide[3]
    )
    hidden_low = hidden.astype(jnp.bfloat16)
    pre_gelu = jnp.dot(hidden_low, up_w, preferred_element_type=jnp.float32) + up_b.astype(
        jnp.float32
    )
    activated = jax.nn.gelu(pre_gelu, approximate=False).astype(jnp.bfloat16)
    branch_out = jnp.dot(activated, down_w, preferred_element_type=jnp.float32) + biases_wide[4]
    output, normed_two, scale_two = normalize(hidden + branch_out, gains_wide[1], biases_wide[5])
    saved = (
        queries,
        keys_low,
        values_low,
        log_total,
        context,
        normed_one,
        scale_one,
        hidden_low,
        pre_gelu,
        activated,
        normed_two,
        scale_two,
    )
    return (output, saved)


def backward_block(weights, inputs, key_valid, grad_out):
    qkv_w, out_w, up_w, down_w, up_b, gain_rows, biases = weights
    gains_wide = gain_rows.astype(jnp.float32)
    row_count, model_width = inputs.shape
    output, saved = forward_block(weights, inputs, key_valid)
    (
        queries,
        keys_low,
        values_low,
        log_total,
        context,
        normed_one,
        scale_one,
        hidden_low,
        pre_gelu,
        activated,
        normed_two,
        scale_two,
    ) = saved
    grad_pre_two, grad_gain_two, grad_shift_two = normalize_back(
        grad_out, normed_two, scale_two, gains_wide[1]
    )
    grad_branch = grad_pre_two.astype(jnp.bfloat16)
    grad_down_w = dot_first(activated, grad_branch)
    grad_act = dot_last(grad_branch, down_w)
    _, gelu_back = jax.vjp(lambda inner: jax.nn.gelu(inner, approximate=False), pre_gelu)
    grad_pre_gelu = gelu_back(grad_act)[0].astype(jnp.bfloat16)
    grad_up_w = dot_first(hidden_low, grad_pre_gelu)
    grad_hidden = grad_pre_two + dot_last(grad_pre_gelu, up_w)
    grad_pre_one, grad_gain_one, grad_shift_one = normalize_back(
        grad_hidden, normed_one, scale_one, gains_wide[0]
    )
    grad_attended = grad_pre_one.astype(jnp.bfloat16)
    grad_out_w = dot_first(context, grad_attended)
    grad_context = head_view(dot_last(grad_attended, out_w).astype(jnp.bfloat16))
    scores = attend_scores(queries, keys_low, key_valid)
    softmax_full = jnp.exp(scores - log_total)
    grad_probs = jnp.einsum(
        "bqhe,bkhe->bhqk", grad_context, head_view(values_low), preferred_element_type=jnp.float32
    )
    grad_values = jnp.einsum(
        "bhqk,bqhe->bkhe",
        softmax_full.astype(jnp.bfloat16),
        grad_context,
        preferred_element_type=jnp.float32,
    )
    grad_values = grad_values.reshape(row_count, model_width).astype(jnp.bfloat16)
    grad_scores = softmax_full * (
        grad_probs - jnp.sum(softmax_full * grad_probs, axis=-1, keepdims=True)
    )
    grad_scores = grad_scores.astype(jnp.bfloat16)
    grad_queries = (
        jnp.einsum(
            "bhqk,bkhe->bqhe", grad_scores, head_view(keys_low), preferred_element_type=jnp.float32
        )
        * score_scale
    )
    grad_queries = grad_queries.reshape(row_count, model_width).astype(jnp.bfloat16)
    grad_keys = (
        jnp.einsum(
            "bhqk,bqhe->bkhe", grad_scores, head_view(queries), preferred_element_type=jnp.float32
        )
        * score_scale
    )
    grad_keys = grad_keys.reshape(row_count, model_width).astype(jnp.bfloat16)
    grad_mixed = jnp.concatenate([grad_queries, grad_keys, grad_values], axis=1)
    grad_qkv_w = dot_first(inputs, grad_mixed)
    grad_inputs = grad_pre_one + dot_last(grad_mixed, qkv_w)
    grad_gains = jnp.stack([grad_gain_one, grad_gain_two])
    grad_biases = jnp.stack(
        [
            jnp.sum(grad_queries, axis=0, dtype=jnp.float32),
            jnp.sum(grad_values, axis=0, dtype=jnp.float32),
            jnp.sum(grad_attended, axis=0, dtype=jnp.float32),
            grad_shift_one,
            jnp.sum(grad_branch, axis=0, dtype=jnp.float32),
            grad_shift_two,
        ]
    )
    grads = (
        grad_qkv_w,
        grad_out_w,
        grad_up_w,
        grad_down_w,
        jnp.sum(grad_pre_gelu, axis=0, dtype=jnp.float32),
        grad_gains,
        grad_biases,
    )
    return (output, grad_inputs, grads)


MESH = pl.DeviceIdType.MESH


class Refs:
    def __init__(self, **refs):
        for name, ref in refs.items():
            setattr(self, name, ref)


def place():
    wide = lax.axis_index("wide")
    z = lax.axis_index("narrow")
    return wide // 4, (wide // 2) % 2, wide % 2, z


def device(y, x, c, z):
    return ((y * 2 + x) * 2 + c, z)


def flat(y, x, c, z):
    return ((y * 2 + x) * 2 + c) * 4 + z


def near(z, k):
    if k == 0:
        return z
    if k == 1:
        return z + 1 - 2 * (z % 2)
    if k == 2:
        return (z + 2) % 4
    return 3 - z


def greet(wide, z):
    barrier = pltpu.get_barrier_semaphore()
    for k in range(1, 8):
        pl.semaphore_signal(barrier, inc=1, device_id=((wide + k) % 8, z), device_id_type=MESH)

    @pl.when(z < 3)
    def _():
        pl.semaphore_signal(barrier, inc=1, device_id=(wide, z + 1), device_id_type=MESH)

    @pl.when(z > 0)
    def _():
        pl.semaphore_signal(barrier, inc=1, device_id=(wide, z - 1), device_id_type=MESH)

    pl.semaphore_wait(barrier, 8 + ((z + 1) // 2) % 2)


def run_if(pred, action):
    if pred is None:
        action()
    else:
        pl.when(pred)(action)


def send(src, dst, send_sem, recv_sem, there, pred=None):
    run_if(
        pred,
        lambda: pltpu.make_async_remote_copy(
            src_ref=src, dst_ref=dst, send_sem=send_sem, recv_sem=recv_sem, device_id=there, device_id_type=MESH
        ).start(),
    )


def bytes_of(ref, sem):
    me = (lax.axis_index("wide"), lax.axis_index("narrow"))
    return pltpu.make_async_remote_copy(
        src_ref=ref, dst_ref=ref, send_sem=sem, recv_sem=sem, device_id=me, device_id_type=MESH
    )


def await_bytes(ref, sem, pred=None):
    run_if(pred, lambda: bytes_of(ref, sem).wait_recv())


def await_sent(ref, sem, pred=None):
    run_if(pred, lambda: bytes_of(ref, sem).wait_send())


def await_column_sends(many, each, sem, z):
    await_sent(many(each), sem, (z == 0) | (z == 3))
    await_sent(many(5 * each), sem, (z == 1) | (z == 2))


def column_steps(slabs, manys, sem):
    y, x, c, z = place()
    up, down = device(y, x, c, z + 1), device(y, x, c, z - 1)

    def push(i, slab, zz, there, pred):
        send(slab(zz), slab(zz), sem.at[i, 4], sem.at[i, zz], there, pred)

    def own():
        for i, slab in enumerate(slabs):
            push(i, slab, z, up, z < 3)
            push(i, slab, z, down, z > 0)

    def take(dist):
        for i, slab in enumerate(slabs):
            low, high = z - dist, z + dist
            await_bytes(slab(low), sem.at[i, low], z >= dist)
            if dist < 3:
                push(i, slab, low, up, (z >= dist) & (z < 3))
            await_bytes(slab(high), sem.at[i, high], z <= 3 - dist)
            if dist < 3:
                push(i, slab, high, down, (z <= 3 - dist) & (z > 0))

    def drain():
        for i, many in enumerate(manys):
            await_column_sends(many, 1, sem.at[i, 4], z)

    return [own] + [lambda dist=dist: take(dist) for dist in (1, 2, 3)], drain


GATHER_SEMS = 21


def gather_steps(subs, many, sem):
    y, x, c, z = place()
    each = len(subs)
    sib = device(y, x, 1 - c, z)
    xn = device(y, 1 - x, c, z)
    yn = device(1 - y, x, c, z)
    mine = flat(y, x, c, z)

    def unit(sub, far1, far2, zz, core):
        fx, fy = (far1, far2) if sub[2] == "x" else (far2, far1)
        return flat(1 - y if fy else y, 1 - x if fx else x, core, zz)

    def push(sub, at, send_at, role, target, pred=None, src=None):
        send(sub[1](at) if src is None else src, sub[1](at), sem.at[send_at], sem.at[role], target, pred)

    def along(sub, at, up, role, pred, src=None):
        push(sub, at, 17, role, device(y, x, c, z + 1 if up else z - 1), pred, src)

    def first(sub, at, zz, pred=None, src=None):
        push(sub, at, 18, 4 + zz, xn if sub[2] == "x" else yn, pred, src)

    def second(sub, at, far, zz, pred=None, src=None):
        push(sub, at, 19, 8 + 4 * far + zz, yn if sub[2] == "x" else xn, pred, src)

    def sibling(sub, at, pred=None, src=None):
        push(sub, at, 20, 16, sib, pred, src)

    def own():
        for sub in subs:
            along(sub, mine, True, z, z < 3, sub[0])
            along(sub, mine, False, z, z > 0, sub[0])
        for sub in subs:
            first(sub, mine, z, None, sub[0])
            second(sub, mine, 0, z, None, sub[0])
        for sub in subs:
            sibling(sub, mine, None, sub[0])

    def from_z(dist):
        for up in (True, False):
            zz = z - dist if up else z + dist
            have = (z >= dist) if up else (z <= 3 - dist)
            at = flat(y, x, c, zz)

            @pl.when(have)
            def _(up=up, zz=zz, at=at):
                await_bytes(many(each), sem.at[zz])
                for sub in subs:
                    if dist < 3:
                        along(sub, at, up, zz, (z < 3) if up else (z > 0))
                for sub in subs:
                    first(sub, at, zz)
                    second(sub, at, 0, zz)
                    sibling(sub, at)

    def from_first(k):
        zz = near(z, k)
        await_bytes(many(each), sem.at[4 + zz])
        for sub in subs:
            at = unit(sub, True, False, zz, c)
            second(sub, at, 1, zz)
            sibling(sub, at)

    def from_second(far, k):
        zz = near(z, k)
        await_bytes(many(each), sem.at[8 + 4 * far + zz])
        for sub in subs:
            sibling(sub, unit(sub, far == 1, True, zz, c))

    def finish():
        await_bytes(many(16 * each), sem.at[16])

    def drain():
        await_column_sends(many, each, sem.at[17], z)
        await_sent(many(4 * each), sem.at[18])
        await_sent(many(8 * each), sem.at[19])
        await_sent(many(16 * each), sem.at[20])

    steps = [own, lambda: from_z(1), lambda: from_first(0), lambda: from_z(2), lambda: from_first(1)]
    steps += [lambda: from_z(3), lambda: (from_first(2), from_first(3))]
    for far in range(2):
        steps += [lambda far=far, k=k: from_second(far, k) for k in range(4)]
    return steps + [finish], drain


REDUCE_SEMS = 33
TARGETS = (0, 3, 1, 2)


class Reduce:
    def __init__(self, subs, sem):
        self.subs, self.sem, self.each = subs, sem, len(subs)
        self.y, self.x, self.c, self.z = place()
        y, x, c, z = self.y, self.x, self.c, self.z
        self.sib = device(y, x, 1 - c, z)
        self.xn, self.yn = device(y, 1 - x, c, z), device(1 - y, x, c, z)

    def own(self, sub, far1, far2, zz, core):
        fx, fy = (far1, far2) if sub.dim == "x" else (far2, far1)
        cy, cx = (1 - self.y if fy else self.y), (1 - self.x if fx else self.x)
        return sub.own(flat(cy, cx, core, zz)), (cy * 2 + cx) * 4 + zz

    def coord(self, sub, far):
        here = self.x if sub.dim == "x" else self.y
        return 1 - here if far else here

    def take(self, at, buffer, count=1):
        await_bytes(buffer.at[pl.ds(0, count * self.each)], self.sem.at[at])

    def add(self, dst, *parts):
        total = dst[...].astype(jnp.float32)
        for part in parts:
            total = total + part[...].astype(jnp.float32)
        dst[...] = total.astype(dst.dtype)

    def start_role(self, far1, far2):
        return (1 - far2) * (2 - far1)

    second_role = staticmethod(lambda far1: 3 if far1 else 4)

    def start(self, zz):
        for far1, far2 in ((False, True), (True, True), (True, False), (False, False)):
            at = 6 * zz + self.start_role(int(far1), int(far2))
            for sub in self.subs:
                src, slot = self.own(sub, far1, far2, zz, 1 - self.c)
                send(src, sub.sib.at[slot], self.sem.at[29], self.sem.at[at], self.sib)

    def start_chip(self, chip):
        cy, cx = chip // 2, chip % 2
        for zz in TARGETS:
            for sub in self.subs:
                fy, fx = (cy + self.y) % 2, (cx + self.x) % 2
                far1, far2 = (fx, fy) if sub.dim == "x" else (fy, fx)
                at = 6 * zz + self.start_role(far1, far2)
                src = sub.own(flat(cy, cx, 1 - self.c, zz))
                send(src, sub.sib.at[chip * 4 + zz], self.sem.at[29], self.sem.at[at], self.sib)

    def step_a(self, zz):
        self.take(6 * zz, self.subs[0].sib, 2)
        for far1 in (False, True):
            for sub in self.subs:
                acc, slot = self.own(sub, far1, True, zz, self.c)
                self.add(acc, sub.sib.at[slot])
                slot = self.coord(sub, far1) * 4 + zz
                there = self.yn if sub.dim == "x" else self.xn
                send(acc, sub.second.at[slot], self.sem.at[30], self.sem.at[6 * zz + self.second_role(far1)], there)

    def step_b(self, zz):
        self.take(6 * zz + 1, self.subs[0].sib)
        self.take(6 * zz + 3, self.subs[0].second)
        for sub in self.subs:
            acc, slot = self.own(sub, True, False, zz, self.c)
            self.add(acc, sub.sib.at[slot], sub.second.at[self.coord(sub, True) * 4 + zz])
            there = self.xn if sub.dim == "x" else self.yn
            send(acc, sub.first.at[zz], self.sem.at[31], self.sem.at[6 * zz + 5], there)

    def chain(self, sub, acc, zz, up, pred):
        z = self.z
        slot = zz if up else jnp.where(z - 1 == zz, 4, zz)
        there = device(self.y, self.x, self.c, z + 1 if up else z - 1)
        send(acc, sub.chain.at[slot], self.sem.at[32], self.sem.at[24 + slot], there, pred)

    def step_c(self, zz):
        self.take(6 * zz + 2, self.subs[0].sib)
        self.take(6 * zz + 4, self.subs[0].second)
        self.take(6 * zz + 5, self.subs[0].first)
        for sub in self.subs:
            acc, slot = self.own(sub, False, False, zz, self.c)
            self.add(acc, sub.sib.at[slot], sub.second.at[self.coord(sub, False) * 4 + zz], sub.first.at[zz])
            if zz > 0:
                self.chain(sub, acc, zz, True, self.z == 0)
            if zz < 3:
                self.chain(sub, acc, zz, False, self.z == 3)

    def relay(self, zz, at, up):
        @pl.when(self.z == at)
        def _():
            self.take(24 + zz, self.subs[0].chain)
            for sub in self.subs:
                acc, _ = self.own(sub, False, False, zz, self.c)
                self.add(acc, sub.chain.at[zz])
                self.chain(sub, acc, zz, up, None)

    def step_d(self, zz):
        if zz >= 2:
            self.relay(zz, 1, True)
        else:
            self.relay(zz, 2, False)

    def step_e(self, zz):
        if zz == 3:
            self.relay(zz, 2, True)
        if zz == 0:
            self.relay(zz, 1, False)

    def finish(self):
        z = self.z
        for sub in self.subs:
            acc, _ = self.own(sub, False, False, z, self.c)
            sub.out[...] = acc[...].astype(jnp.float32)
        for pred, slot in ((z > 0, z), (z < 3, 4)):

            @pl.when(pred)
            def _(slot=slot):
                self.take(24 + slot, self.subs[0].chain)
                for sub in self.subs:
                    sub.out[...] += sub.chain[slot].astype(jnp.float32)

        self.sent(16, 8, 4, 3)

    def near_finish(self):
        pass

    def sent(self, *counts):
        for k, count in enumerate(counts):
            await_sent(self.subs[0].all.at[pl.ds(0, count * self.each)], self.sem.at[29 + k])


class ReduceLate(Reduce):
    def start_role(self, far1, far2):
        return 1 - far2

    second_role = staticmethod(lambda far1: 3)

    def step_b(self, zz):
        self.take(6 * zz + 1, self.subs[0].sib, 2)
        self.take(6 * zz + 3, self.subs[0].second, 2)
        for far1 in (True, False):
            for sub in self.subs:
                acc, slot = self.own(sub, far1, False, zz, self.c)
                self.add(acc, sub.sib.at[slot], sub.second.at[self.coord(sub, far1) * 4 + zz])
        for up, at in ((True, 0), (False, 3)):
            if zz != at:
                self.pass_on(zz, up, self.z == at)

    def pass_on(self, zz, up, pred):
        z = self.z
        slot = zz if up else jnp.where(z - 1 == zz, 4, zz)
        there = device(self.y, self.x, self.c, z + 1 if up else z - 1)
        for far1 in range(2):
            for sub in self.subs:
                acc, _ = self.own(sub, far1 == 1, False, zz, self.c)
                send(acc, sub.chain.at[2 * slot + far1], self.sem.at[32], self.sem.at[24 + slot], there, pred)

    def join(self, zz, slot):
        self.take(24 + slot, self.subs[0].chain, 2)
        for far1 in range(2):
            for sub in self.subs:
                acc, _ = self.own(sub, far1 == 1, False, zz, self.c)
                self.add(acc, sub.chain.at[2 * slot + far1])

    def relay(self, zz, at, up):
        @pl.when(self.z == at)
        def _():
            self.join(zz, zz)
            self.pass_on(zz, up, None)

    def step_c(self, zz):
        Reduce.step_d(self, zz)

    def step_d(self, zz):
        Reduce.step_e(self, zz)

    def step_e(self, zz):
        pass

    def near_finish(self):
        z = self.z
        for pred, slot in ((z > 0, z), (z < 3, 4)):

            @pl.when(pred)
            def _(slot=slot):
                self.join(z, slot)

        for sub in self.subs:
            acc, _ = self.own(sub, True, False, z, self.c)
            there = self.xn if sub.dim == "x" else self.yn
            send(acc, sub.first.at[0], self.sem.at[31], self.sem.at[5], there)

    def finish(self):
        self.take(5, self.subs[0].first)
        for sub in self.subs:
            acc, _ = self.own(sub, False, False, self.z, self.c)
            sub.out[...] = acc[...].astype(jnp.float32) + sub.first[0].astype(jnp.float32)
        self.sent(16, 8, 1, 6)


class Waves:
    def __init__(self, groups, lags):
        self.waves = [(made, zz) for made in groups for zz in TARGETS]
        self.lags = lags
        self.at = 0

    def step(self):
        stages = ("step_a", "step_b", "step_c", "step_d", "step_e")
        for lag, stage in zip(self.lags, stages):
            k = self.at - lag
            if 0 <= k < len(self.waves):
                group, zz = self.waves[k]
                for made in group:
                    getattr(made, stage)(zz)
        for more, stage in ((1, "near_finish"), (2, "finish")):
            k = self.at - self.lags[-1] - more
            if 0 <= k < len(self.waves) and k % 4 == 3:
                for made in self.waves[k][0]:
                    getattr(made, stage)()
        self.at += 1

    def left(self):
        return len(self.waves) + self.lags[-1] + 2 - self.at


def erf_of(v):
    return lax.erf(v)


def mm(a, b):
    return jnp.dot(a, b, preferred_element_type=jnp.float32)


def mm_nt(a, b):
    return lax.dot_general(a, b, (((1,), (1,)), ((), ())), preferred_element_type=jnp.float32)


def mm_tn(a, b):
    return lax.dot_general(a, b, (((0,), (0,)), ((), ())), preferred_element_type=jnp.float32)


def columns(ref, start, stop):
    block = ref[:, :, start:stop]
    return block.reshape(block.shape[0] * block.shape[1], stop - start)


def rows_of(ref, start, stop):
    block = ref[start:stop]
    return block.reshape(block.shape[0] * block.shape[1], block.shape[2])


def put_columns(ref, start, values):
    owners, share = ref.shape[0], ref.shape[1]
    ref[:, :, start : start + values.shape[1]] = values.astype(ref.dtype).reshape(
        owners, share, values.shape[1]
    )


def norm_rows(values):
    centred = values - jnp.mean(values, axis=-1, keepdims=True)
    inv_scale = lax.rsqrt(jnp.mean(centred * centred, axis=-1, keepdims=True) + norm_epsilon)
    return centred * inv_scale, inv_scale


def norm_rows_back(gradient, normed, inv_scale, gain_row):
    scaled = gradient * gain_row
    return inv_scale * (
        scaled
        - jnp.mean(scaled, axis=-1, keepdims=True)
        - normed * jnp.mean(scaled * normed, axis=-1, keepdims=True)
    )


def column_sum(values):
    return jnp.sum(values.astype(jnp.float32), axis=0, keepdims=True)


def head_forward(s, w1, w2, small, lengths):
    width = s.x.shape[1]
    spans = s.x.shape[0] // SPAN
    x = s.x[...]
    s.q[...] = (mm(x, columns(w1, 0, width)) + small(2)).astype(jnp.bfloat16)
    s.k[...] = mm(x, columns(w1, width, 2 * width)).astype(jnp.bfloat16)
    s.v[...] = (mm(x, columns(w1, 2 * width, 3 * width)) + small(3)).astype(jnp.bfloat16)
    yield
    lane = lax.broadcasted_iota(jnp.int32, (SPAN, 128), 1)
    for span in range(spans):
        keep = lax.broadcasted_iota(jnp.int32, (SPAN, 128), 1) < lengths[span]
        for pair in range(width // 128):
            at = (slice(span * SPAN, (span + 1) * SPAN), slice(pair * 128, (pair + 1) * 128))
            q, k, v = s.q[at], s.k[at], s.v[at]
            parts = []
            for side in range(2):
                here = (lane < 64) if side == 0 else (lane >= 64)
                scores = mm_nt(jnp.where(here, q, jnp.zeros_like(q)), k) * score_scale
                scores = jnp.where(keep, scores, masked_score)
                weight = jnp.exp(scores - jnp.max(scores, axis=-1, keepdims=True))
                probs = weight / jnp.sum(weight, axis=-1, keepdims=True)
                s.p[(span * 6 + pair) * 2 + side] = probs
                parts.append(mm(probs.astype(jnp.bfloat16), v))
            s.ctx[at] = jnp.where(lane < 64, parts[0], parts[1]).astype(jnp.bfloat16)
        yield
    attended = mm(s.ctx[...], columns(w1, 3 * width, 4 * width)) + small(4)
    normed, inv_scale = norm_rows(s.x[...].astype(jnp.float32) + attended)
    s.n1[...] = normed
    s.r1[...] = inv_scale
    hidden = normed * small(0) + small(5)
    s.h[...] = hidden
    s.hl[...] = hidden.astype(jnp.bfloat16)
    yield
    for part in range(4):
        pre = mm(s.hl[...], columns(w1, (4 + part) * width, (5 + part) * width)) + small(8 + part)
        half_erf = 0.5 + 0.5 * erf_of(pre * (0.5**0.5))
        s.g[part] = (pre * half_erf).astype(jnp.bfloat16)
        s.gp[part] = half_erf + pre * (jnp.exp(-0.5 * pre * pre) * (0.5 / math.pi) ** 0.5)
        yield
    branch = small(6)
    share = w2.shape[0] // 4
    for part in range(4):
        branch = branch + mm(s.g[part], rows_of(w2, part * share, (part + 1) * share))
    normed, inv_scale = norm_rows(s.h[...] + branch)
    s.n2[...] = normed
    s.r2[...] = inv_scale
    s.y[...] = (normed * small(1) + small(7)).astype(jnp.bfloat16)
    yield


def head_backward(s, w1, w2, g1, g2, small, sums, grad_in):
    width = s.x.shape[1]
    spans = s.x.shape[0] // SPAN
    grad_out = s.cot[...].astype(jnp.float32)
    sums[1:2] = column_sum(grad_out * s.n2[...])
    sums[7:8] = column_sum(grad_out)
    pre_two = norm_rows_back(grad_out, s.n2[...], s.r2[...], small(1))
    s.h[...] = pre_two
    branch = pre_two.astype(jnp.bfloat16)
    s.dz[...] = branch
    sums[6:7] = column_sum(branch)
    yield
    owners = w2.shape[0]
    share = owners // 4
    for part in range(4):
        own = slice(part * share, (part + 1) * share)
        grad_act = mm_nt(s.dz[...], rows_of(w2, part * share, (part + 1) * share))
        grad_pre = (grad_act * s.gp[part]).astype(jnp.bfloat16)
        g2[own] = (
            mm_tn(s.g[part], s.dz[...]).astype(jnp.bfloat16).reshape(share, g2.shape[1], width)
        )
        s.g[part] = grad_pre
        sums[8 + part : 9 + part] = column_sum(grad_pre)
        yield
    for part in range(4):
        at = (4 + part) * width
        grad_pre = s.g[part]
        s.h[...] += mm_nt(grad_pre, columns(w1, at, at + width))
        put_columns(g1, at, mm_tn(s.hl[...], grad_pre))
        yield
    grad_hidden = s.h[...]
    sums[0:1] = column_sum(grad_hidden * s.n1[...])
    sums[5:6] = column_sum(grad_hidden)
    pre_one = norm_rows_back(grad_hidden, s.n1[...], s.r1[...], small(0))
    s.h[...] = pre_one
    attended = pre_one.astype(jnp.bfloat16)
    s.dz[...] = attended
    sums[4:5] = column_sum(attended)
    yield
    s.hl[...] = mm_nt(attended, columns(w1, 3 * width, 4 * width)).astype(jnp.bfloat16)
    put_columns(g1, 3 * width, mm_tn(s.ctx[...], attended))
    yield
    lane = lax.broadcasted_iota(jnp.int32, (SPAN, 128), 1)
    for span in range(spans):
        for pair in range(width // 128):
            at = (slice(span * SPAN, (span + 1) * SPAN), slice(pair * 128, (pair + 1) * 128))
            q, k, v, dc = s.q[at], s.k[at], s.v[at], s.hl[at]
            dq, dk, dv = [], [], []
            for side in range(2):
                here = (lane < 64) if side == 0 else (lane >= 64)
                probs = s.p[(span * 6 + pair) * 2 + side]
                grad_probs = mm_nt(jnp.where(here, dc, jnp.zeros_like(dc)), v)
                dv.append(mm_tn(probs.astype(jnp.bfloat16), dc))
                grad_scores = probs * (
                    grad_probs - jnp.sum(probs * grad_probs, axis=-1, keepdims=True)
                )
                grad_scores = grad_scores.astype(jnp.bfloat16)
                dq.append(mm(grad_scores, k))
                dk.append(mm_tn(grad_scores, q))
            join = lambda two: jnp.where(lane < 64, two[0], two[1])
            s.q[at] = (join(dq) * score_scale).astype(jnp.bfloat16)
            s.k[at] = (join(dk) * score_scale).astype(jnp.bfloat16)
            s.v[at] = join(dv).astype(jnp.bfloat16)
        yield
    sums[2:3] = column_sum(s.q[...])
    sums[3:4] = column_sum(s.v[...])
    total = s.h[...]
    for k, ref in enumerate((s.q, s.k, s.v)):
        total = total + mm_nt(ref[...], columns(w1, k * width, (k + 1) * width))
    grad_in[...] = total
    yield
    for k, ref in enumerate((s.q, s.k, s.v)):
        put_columns(g1, k * width, mm_tn(s.x[...], ref[...]))
    yield


HIGHEST = lax.Precision.HIGHEST
ROWS = 16


def iota(shape, axis):
    return lax.broadcasted_iota(jnp.int32, shape, axis)


def ones_where(condition, dtype):
    return jnp.where(condition, 1.0, 0.0).astype(dtype)


def exact(a, b, dims):
    return lax.dot_general(
        a, b, (dims, ((), ())), precision=HIGHEST, preferred_element_type=jnp.float32
    )


class Plane:
    def __init__(self, sem):
        self.sem = sem
        self.wide, self.z = lax.axis_index("wide"), lax.axis_index("narrow")
        self.sent = []

    def send(self, index, src, recv):
        for k in range(1, 8):
            peer = (self.wide + k) % 8
            send(src(peer), recv.at[self.wide], self.sem.at[index, 0], self.sem.at[index, 1], (peer, self.z))
        self.sent.append((index, recv))

    def arrive(self, index, recv):
        await_bytes(recv.at[pl.ds(0, 7)], self.sem.at[index, 1])

    def drain(self):
        for index, recv in self.sent:
            await_sent(recv.at[pl.ds(0, 7)], self.sem.at[index, 0])

    def total(self, index, recv):
        self.arrive(index, recv)
        total = recv[0].astype(jnp.float32)
        for k in range(1, 8):
            total = total + recv[k].astype(jnp.float32)
        return total

    def place_rows(self, two):
        row = iota((ROWS, two.shape[1]), 0)
        rows = jnp.where(row % 2 == 0, two[0:1], two[1:2])
        return jnp.where(row // 2 == self.wide, rows, 0.0)

    def pick_rows(self, values, first):
        row = iota(values.shape, 0)
        one = lambda k: jnp.sum(jnp.where(row == first + k, values, 0.0), axis=0, keepdims=True)
        return jnp.concatenate([one(0), one(1)], axis=0)

    def share(self, index, two, src, recv):
        placed = self.place_rows(two).astype(src.dtype)
        src[...] = placed
        recv[self.wide] = placed
        self.send(index, lambda peer: src, recv)

    def collect(self, index, values, src, recv):
        for k in range(2):
            src[k] = values[8 * k : 8 * k + 8]
        recv[self.wide] = jnp.where(self.wide // 4 == 0, values[0:8], values[8:16])
        self.send(index, lambda peer: src.at[peer // 4], recv)

    def collected(self, index, recv):
        return self.pick_rows(self.total(index, recv), 2 * (self.wide % 4))


def backbone_forward(s, plane, small, finish):
    x0, w0 = s.x0, s.w0
    width = x0.shape[1]
    spans = x0.shape[0] // SPAN
    wide = plane.wide
    x = x0[...]
    s.k0[...] = mm(x, columns(w0, width, 2 * width)).astype(jnp.bfloat16)
    s.v0[...] = (mm(x, columns(w0, 2 * width, 3 * width)) + small(3)).astype(jnp.bfloat16)
    first = jnp.concatenate(
        [x0[SPAN * span : SPAN * span + 1].astype(jnp.float32) for span in range(spans)], axis=0
    )
    query = mm(first.astype(jnp.bfloat16), columns(w0, 0, width)) + small(2)
    s.keep[0, 0:spans] = first
    s.keep[1, 0:spans] = query.astype(jnp.bfloat16).astype(jnp.float32)
    yield
    heads = ones_where(iota((width, 128), 0) // (width // HEADS) == iota((width, 128), 1), jnp.bfloat16)
    context = []
    for span in range(spans):
        at = slice(span * SPAN, (span + 1) * SPAN)
        product = s.k0[at].astype(jnp.float32) * s.keep[1, span : span + 1]
        scores = exact(product, heads.astype(jnp.float32), ((1,), (0,))) * score_scale
        scores = jnp.where(iota(scores.shape, 0) < s.lengths[span], scores, masked_score)
        weight = jnp.exp(scores - jnp.max(scores, axis=0, keepdims=True))
        probs = weight / jnp.sum(weight, axis=0, keepdims=True)
        s.p0[span] = probs
        spread = mm_nt(probs.astype(jnp.bfloat16), heads)
        context.append(jnp.sum(spread * s.v0[at].astype(jnp.float32), axis=0, keepdims=True))
    context = jnp.concatenate(context, axis=0).astype(jnp.bfloat16)
    s.keep[2, 0:spans] = context.astype(jnp.float32)
    attended = mm(context, columns(w0, 3 * width, 4 * width)) + small(4)
    normed, inv_scale = norm_rows(s.keep[0, 0:spans] + attended)
    hidden = normed * small(0) + small(5)
    s.keep[3, 0:spans] = normed
    s.keep[4, 0:spans] = jnp.broadcast_to(inv_scale, normed.shape)
    s.keep[5, 0:spans] = hidden
    plane.share(0, hidden, s.e0_src, s.e0)
    yield
    hidden_all = plane.total(0, s.e0).astype(jnp.bfloat16)
    share = width // 8
    pick = ones_where(iota((width, share), 0) == share * wide + iota((width, share), 1), jnp.bfloat16)
    own = mm(hidden_all, pick).astype(jnp.bfloat16)
    upz = s.upz
    part = upz.shape[2] // 8
    for k in range(8):
        s.e1_src[k] = mm(own, columns(upz, k * part, (k + 1) * part))
    s.e1[wide] = s.e1_src[wide]
    plane.send(1, lambda peer: s.e1_src.at[peer], s.e1)
    yield
    bias = jnp.where(wide % 2 == 0, small(8 + wide // 2)[:, :part], small(8 + wide // 2)[:, part:])
    pre = plane.total(1, s.e1) + bias
    half_erf = 0.5 + 0.5 * erf_of(pre * (0.5**0.5))
    s.g0[...] = (pre * half_erf).astype(jnp.bfloat16)
    s.gp0[...] = half_erf + pre * (jnp.exp(-0.5 * pre * pre) * (0.5 / math.pi) ** 0.5)
    plane.collect(2, mm(s.g0[...], rows_of(s.downz, 0, 4)), s.e2_src, s.e2)
    yield
    branch = plane.collected(2, s.e2) + small(6)
    normed, inv_scale = norm_rows(s.keep[5, 0:spans] + branch)
    s.keep[6, 0:spans] = normed
    s.keep[7, 0:spans] = jnp.broadcast_to(inv_scale, normed.shape)
    finish(normed * small(1) + small(7))
    yield


def backbone_backward(s, plane, small, grad_rows):
    x0, w0 = s.x0, s.w0
    width = x0.shape[1]
    spans = x0.shape[0] // SPAN
    wide = plane.wide
    keep = lambda k: s.keep[k, 0:spans]
    acts, sums = s.acts, s.sums0

    def put(item, values):
        for span in range(spans):
            row = span * ROWS + item
            acts[row : row + 1] = values[span : span + 1]

    acts[...] = jnp.zeros_like(acts)
    grad_out = grad_rows()
    sums[1:2] = column_sum(grad_out * keep(6))
    sums[7:8] = column_sum(grad_out)
    pre_two = norm_rows_back(grad_out, keep(6), keep(7), small(1))
    s.keep[8, 0:spans] = pre_two
    low = lambda a: a.astype(jnp.bfloat16).astype(jnp.float32)
    put(11, low(pre_two))
    plane.share(3, pre_two, s.e3_src, s.e3)
    yield
    branch = plane.total(3, s.e3).astype(jnp.bfloat16)
    grad_act = mm_nt(branch, rows_of(s.downz, 0, 4))
    part = s.g0.shape[1]
    s.e4_src[:, :part] = (grad_act * s.gp0[...]).astype(jnp.bfloat16)
    s.e4_src[:, part:] = s.g0[...]
    s.e4[wide] = s.e4_src[...]
    plane.send(4, lambda peer: s.e4_src, s.e4)
    yield
    plane.arrive(4, s.e4)
    total = jnp.zeros((ROWS, width // 8), jnp.float32)
    for k in range(8):
        both = s.e4[k]
        total = total + mm_nt(both[:, :part], columns(s.upz, k * part, (k + 1) * part))
        rows = plane.pick_rows(both.astype(jnp.float32), 2 * wide)
        at = slice((k % 2) * part, (k % 2 + 1) * part)
        for span in range(spans):
            row = span * ROWS + 3 + k // 2
            acts[row : row + 1, at] = rows[span : span + 1, :part]
            acts[row + 4 : row + 5, at] = rows[span : span + 1, part:]
    share = width // 8
    pick = ones_where(iota((width, share), 0) == share * wide + iota((width, share), 1), jnp.float32)
    plane.collect(5, exact(total, pick, ((1,), (1,))), s.e5_src, s.e5)
    yield
    grad_hidden = keep(8) + plane.collected(5, s.e5)
    sums[0:1] = column_sum(grad_hidden * keep(3))
    sums[5:6] = column_sum(grad_hidden)
    pre_one = norm_rows_back(grad_hidden, keep(3), keep(4), small(0))
    attended = pre_one.astype(jnp.bfloat16)
    context = low(mm_nt(attended, columns(w0, 3 * width, 4 * width)))
    heads = ones_where(iota((width, 128), 0) // (width // HEADS) == iota((width, 128), 1), jnp.bfloat16)
    queries = []
    for span in range(spans):
        at = slice(span * SPAN, (span + 1) * SPAN)
        probs = s.p0[span]
        grad_context = context[span : span + 1]
        product = s.v0[at].astype(jnp.float32) * grad_context
        grad_probs = exact(product, heads.astype(jnp.float32), ((1,), (0,)))
        grad_scores = probs * (grad_probs - jnp.sum(probs * grad_probs, axis=0, keepdims=True))
        spread = mm_nt(grad_scores.astype(jnp.bfloat16), heads) * score_scale
        queries.append(jnp.sum(spread * s.k0[at].astype(jnp.float32), axis=0, keepdims=True))
        s.k0[at] = (spread * s.keep[1, span : span + 1]).astype(jnp.bfloat16)
        s.v0[at] = (mm_nt(probs.astype(jnp.bfloat16), heads) * grad_context).astype(jnp.bfloat16)
    queries = jnp.concatenate(queries, axis=0).astype(jnp.bfloat16)
    sums[3:4] = column_sum(s.v0[...])
    put(0, keep(2))
    put(1, attended.astype(jnp.float32))
    put(2, low(keep(5)))
    put(12, keep(0))
    put(13, queries.astype(jnp.float32))
    s.acts_low[...] = acts[...].astype(jnp.bfloat16)
    s.keep[9, 0:spans] = pre_one + mm_nt(queries, columns(w0, 0, width))
    yield
    grad_in = s.embeds_grad
    grad_in[...] = mm_nt(s.k0[...], columns(w0, width, 2 * width))
    grad_in[...] += mm_nt(s.v0[...], columns(w0, 2 * width, 3 * width))
    for span in range(spans):
        grad_in[SPAN * span : SPAN * span + 1] += s.keep[9, span : span + 1]
    put_columns(w0, width, mm_tn(x0[...], s.k0[...]))
    put_columns(w0, 2 * width, mm_tn(x0[...], s.v0[...]))
    yield


def backbone_weight_grads(s, at, o1, o2, small_out):
    width = s.x0.shape[1]
    gathered = s.g[...].reshape(-1, width)
    spans = 64

    def item(k):
        shape = (spans, gathered.shape[0])
        row, column = iota(shape, 0), iota(shape, 1)
        pick = column == (row // 2) * 32 + (row % 2) * ROWS + k
        return mm(ones_where(pick, jnp.bfloat16), gathered)

    share = width // 32
    shape = (width, 128)

    def picker(count, offset, dtype):
        row, column = iota(shape, 0), iota(shape, 1)
        return ones_where((row + offset == count * at + column) & (column < count), dtype)

    narrow = picker(share, 0, jnp.bfloat16)
    own = lambda k: mm(item(k).astype(jnp.bfloat16), narrow).astype(jnp.bfloat16)
    grad_query = item(13)
    o1[0, :, 0:width] = mm_tn(own(12), grad_query.astype(jnp.bfloat16))[:share]
    grad_attended = item(1)
    o1[0, :, 3 * width : 4 * width] = mm_tn(own(0), grad_attended.astype(jnp.bfloat16))[:share]
    branch = item(11)
    hidden = own(2)
    wide_sum = jnp.zeros((1, 128), jnp.float32)
    act = jnp.zeros((spans, 128), jnp.float32)
    for part in range(4):
        grad_pre = item(3 + part)
        o1[0, :, (4 + part) * width : (5 + part) * width] = mm_tn(hidden, grad_pre.astype(jnp.bfloat16))[:share]
        act = act + mm(item(7 + part).astype(jnp.bfloat16), picker(4 * share, part * width, jnp.bfloat16))
        wide_sum = wide_sum + exact(
            column_sum(grad_pre), picker(4 * share, part * width, jnp.float32), ((1,), (0,))
        )
    o2[0] = mm_tn(act.astype(jnp.bfloat16), branch.astype(jnp.bfloat16))[: 4 * share]
    exact_narrow = picker(share, 0, jnp.float32)
    s.late[...] = jnp.zeros_like(s.late)
    for row, values in ((2, grad_query), (4, grad_attended), (6, branch)):
        s.late[row : row + 1] = exact(column_sum(values), exact_narrow, ((1,), (0,)))
    small_out[8:9] = wide_sum


def step_kernel(
    qkv_in, out_in, up_in, down_in, up_bias, gains, biases, x0_in, skip_in, cot_in, lengths, y_out, embeds_out,
    skip_out, o1, o2, small_out, acts_all, *scratch,
):
    s = Refs(lengths=lengths)
    for (name, _, _), ref in zip(step_scratch(x0_in.shape[1]), scratch):
        setattr(s, name, ref)
    x0, skip, skip_grad = s.x0, s.skip, s.skip_grad
    gather_sem, column_sem, reduce_sem, plane_sem, load_sem = scratch[-5:]
    width = x0.shape[1]
    spans = x0.shape[0] // SPAN
    y, x, c, z = place()
    wide = lax.axis_index("wide")
    me = flat(y, x, c, z)
    w0, w1, w2, upz, downz, pars = s.w0, s.w1, s.w2, s.upz, s.downz, s.pars
    loads = [
        pltpu.make_async_copy(src, dst, load_sem.at[k])
        for k, (src, dst) in enumerate(
            (
                (qkv_in, o1.at[:, :, : 3 * width]), (out_in, o1.at[:, :, 3 * width : 4 * width]),
                (up_in, o1.at[:, :, 4 * width :]), (down_in, o2), (x0_in, x0), (skip_in, skip), (cot_in, s.cot),
            )
        )
    ]
    for load in loads:
        load.start()
    greet(wide, z)
    for load in loads[:4]:
        load.wait()
    w0[me] = o1[0, :, : 4 * width].astype(jnp.bfloat16)
    w1[me] = o1[1].astype(jnp.bfloat16)
    w2[me] = o2[1].astype(jnp.bfloat16)
    upz[z] = o1[0, :, 4 * width :].astype(jnp.bfloat16)
    downz[z] = o2[0].astype(jnp.bfloat16)
    s.small_all[me] = jnp.zeros((2 * ROWS, 128), jnp.float32)
    for layer in range(2):
        r, share = ROWS * layer, width // 32
        s.small_all[me, r : r + 2, :share] = gains[layer]
        s.small_all[me, r + 2 : r + 8, :share] = biases[:, layer]
        s.small_all[me, r + 8 : r + 9, : 4 * share] = up_bias[layer : layer + 1]

    half, mid = 2 * width, w2.shape[1] // 2

    def column_pair(ref, start):
        cut = lambda at: (lambda u: ref.at[u, :, at : at + half])
        subs = [(None, cut(start), "x"), (None, cut(start + half), "y")]
        return subs, lambda n: ref.at[pl.ds(0, n), :, start : start + half]

    rows_cut = lambda at: (lambda u: w2.at[u, at : at + mid])
    sets = [
        ([(None, lambda u: s.small_all.at[u], "x")], lambda n: s.small_all.at[pl.ds(0, n)]),
        column_pair(w0, 0),
        column_pair(w1, 0),
        column_pair(w1, 2 * half),
        ([(None, rows_cut(0), "x"), (None, rows_cut(mid), "y")], lambda n: w2.at[pl.ds(0, n), :mid]),
    ]
    events = []
    drains = []
    for k, (subs, many) in enumerate(sets):
        steps, drain = gather_steps(subs, many, gather_sem.at[k])
        drains.append(drain)
        for step, action in enumerate(steps):
            events.append((SET_AT[k][step], action))
    steps, drain = column_steps(
        [lambda zz: upz.at[zz], lambda zz: downz.at[zz]],
        [lambda n: w1.at[pl.ds(0, n), :, : 2 * half], lambda n: w2.at[pl.ds(0, n)]],
        column_sem,
    )
    drains.append(drain)
    events += zip(COLUMN_AT, steps)

    def row_of(layer):
        return lambda k: pars[pl.ds(ROWS * layer + k, 1), :]

    def unpack():
        share = width // 32
        for layer in range(2):
            r = ROWS * layer
            for d in range(32):
                pars[r : r + 8, share * d : share * (d + 1)] = s.small_all[d, r : r + 8, :share]
                at = slice((d % 8) * 4 * share, (d % 8 + 1) * 4 * share)
                pars[r + 8 + d // 8 : r + 9 + d // 8, at] = s.small_all[d, r + 8 : r + 9, : 4 * share]
        pars[...] = pars[...].astype(jnp.bfloat16).astype(jnp.float32)

    def join(rows):
        row = iota(skip.shape, 0)
        joined = skip[...].astype(jnp.float32)
        for span in range(spans):
            joined = jnp.where(row == SPAN * span, rows[span : span + 1], joined)
        s.x[...] = joined.astype(jnp.bfloat16)

    def unload():
        for load in loads[4:]:
            load.wait()

    outs = []

    def put_out(src, dst):
        copy = pltpu.make_async_copy(src, dst, load_sem.at[len(outs)])
        copy.start()
        outs.append(copy)

    events += [(UNPACK_AT, unload)]
    plane = Plane(plane_sem)
    forward0 = backbone_forward(s, plane, row_of(0), join)
    forward1 = head_forward(s, w1, w2, row_of(1), lengths)
    events += [(UNPACK_AT, unpack)]
    events += [(at, lambda: next(forward0)) for at in FORWARD0_AT]
    events += [(at, lambda: next(forward1)) for at in FORWARD1_AT]
    for _, action in sorted(events, key=lambda event: event[0]):
        action()
    for drain in drains:
        drain()
    put_out(s.y, y_out)

    back1 = head_backward(s, w1, w2, w1, w2, row_of(1), s.sums, skip_grad)
    back0 = backbone_backward(
        s, plane, row_of(0),
        lambda: jnp.concatenate([skip_grad[SPAN * k : SPAN * k + 1] for k in range(spans)], axis=0),
    )

    def reduced(whole, own, out, name, dim):
        bufs = [getattr(s, name + kind) for kind in KINDS]
        return Refs(all=whole, own=own, out=out, dim=dim, sib=bufs[0], second=bufs[1], first=bufs[2], chain=bufs[3])

    def pair(ref, start, stop, out, name):
        middle = (start + stop) // 2
        cut = lambda a, b: (ref.at[:, :, a:b], lambda u: ref.at[u, :, a:b], out.at[:, a:b])
        return [
            reduced(*cut(start, middle), name + "a", "x"),
            reduced(*cut(middle, stop), name + "b", "y"),
        ]

    made = iter(range(6))
    group = lambda *subs: Reduce(subs, reduce_sem.at[next(made)])
    group_late = lambda *subs: ReduceLate(subs, reduce_sem.at[next(made)])
    cut = lambda a, b: (w2.at[:, a:b], lambda u: w2.at[u, a:b], o2.at[1, a:b])
    downs = [group_late(reduced(*cut(0, mid), "da", "x"), reduced(*cut(mid, 2 * mid), "db", "y"))]
    ups = [group_late(*pair(w1, 4 * width, 8 * width, o1.at[1], "u"))]
    lefts = [
        group(*pair(w1, 0, 4 * width, o1.at[1], "q")),
        group(reduced(s.block1, lambda u: s.block1.at[u], small_out.at[ROWS : 2 * ROWS], "s1", "x")),
    ]
    kvs = [
        group(*pair(w0, width, 3 * width, o1.at[0], "k")),
        group(reduced(s.block0, lambda u: s.block0.at[u], small_out.at[0:8], "s0", "y")),
    ]
    waves = Waves([downs, ups, lefts, kvs], LAGS)

    def start(groups):
        for zz in TARGETS:
            for each in groups:
                each.start(zz)

    def fill_blocks(block, sums, wide_too):
        share = width // 32
        block[...] = jnp.zeros_like(block)
        for d in range(32):
            block[d, 0:8, :share] = sums[0:8, share * d : share * (d + 1)]
            if wide_too:
                at = slice((d % 8) * 4 * share, (d % 8 + 1) * 4 * share)
                block[d, 8:9, : 4 * share] = sums[8 + d // 8 : 9 + d // 8, at]

    def step(times):
        for _ in range(times):
            waves.step()

    next(back1)
    for chip in range(4):
        next(back1)
        for each in downs:
            each.start_chip(chip)
    next(back1)
    next(back1)
    step(STEPS[0])
    next(back1)
    next(back1)
    step(STEPS[1])
    next(back1)
    start(ups)
    next(back1)
    step(STEPS[2])
    next(back1)
    step(STEPS[3])
    next(back1)
    step(STEPS[4])
    next(back1)
    next(back0)
    step(STEPS[5])
    next(back1)
    fill_blocks(s.block1, s.sums, True)
    start(lefts)
    next(back0)
    step(STEPS[6])
    next(back0)
    step(STEPS[7])
    next(back0)
    home = lambda u: acts_all.at[u // 8, pl.ds(pl.multiple_of((u % 8) * 32, 32), 32)]
    own_acts = pltpu.make_async_copy(s.acts_low, home(me), load_sem.at[5])
    own_acts.start()
    rows = lambda n: acts_all.at[pl.ds(0, n // 16)] if n >= 16 else acts_all.at[0, pl.ds(0, ROWS * n)]
    part = lambda k: (lambda u: home(u).at[pl.ds(ROWS * k, ROWS)])
    spread, drain = gather_steps(
        [(s.acts_low.at[pl.ds(ROWS * k, ROWS)], part(k), dim) for k, dim in enumerate("xy")], rows, gather_sem.at[5]
    )
    spread[0]()
    next(back0)
    fill_blocks(s.block0, s.sums0, False)
    start(kvs)
    row = iota(skip_grad.shape, 0)
    skip_grad[...] = jnp.where(row % SPAN == 0, 0.0, skip_grad[...])
    put_out(skip_grad, skip_out)
    put_out(s.embeds_grad, embeds_out)
    left = waves.left()
    turns = left - TAIL
    for k in range(left):
        waves.step()
        if k < turns:
            for action in spread[1 + 15 * k // turns : 1 + 15 * (k + 1) // turns]:
                action()
        if k == turns - 1:
            own_acts.wait()
            load = pltpu.make_async_copy(acts_all, s.g, load_sem.at[6])
            load.start()
            load.wait()
            backbone_weight_grads(s, me, o1, o2, small_out)
    small_out[0:8] += s.late[...]
    drain()
    plane.drain()
    for copy in outs:
        copy.wait()


def set_at(own, rest, late):
    return (own, *(rest + k for k in range(6)), *(late + 0.5 * k for k in range(9)))


SET_AT = (
    set_at(0, 1, 7), set_at(0, 1, 7), set_at(0.1, 6.2, 12.6), set_at(0.2, 11.2, 17.6), set_at(0.3, 16.2, 22.6)
)
UNPACK_AT = 11.05
COLUMN_AT = (2.5, 4.5, 6.5, 8.5)
FORWARD0_AT = (11.3, 12.2, 14.0, 16.0, 18.0)
FORWARD1_AT = (18.1, 18.9, 19.7, 20.34, 21.7, 22.5, 23.3, 24.1, 26.7)
LAGS = (0, 2, 5, 7, 9)
STEPS = (2, 2, 1, 1, 1, 1, 2, 2)
TAIL = 2
KINDS = ("sib", "second", "first", "chain")


def step_scratch(width):
    low, full = jnp.bfloat16, jnp.float32
    share = width // 32
    rows = 2 * SPAN
    found = [
        ("w0", (32, share, 4 * width), low), ("upz", (4, share, 4 * width), low),
        ("downz", (4, 4 * share, width), low), ("w1", (32, share, 8 * width), low),
        ("w2", (32, 4 * share, width), low), ("small_all", (32, 2 * ROWS, 128), full),
        ("pars", (2 * ROWS, width), full), ("sums", (ROWS, width), full), ("sums0", (8, width), full),
        ("keep", (ROWS, 8, width), full), ("p0", (2, SPAN, 128), full),
        ("g0", (ROWS, width // 2), low), ("gp0", (ROWS, width // 2), full),
        ("e0_src", (ROWS, width), low), ("e0", (8, ROWS, width), low),
        ("e1_src", (8, ROWS, width // 2), full), ("e1", (8, ROWS, width // 2), full),
        ("e2_src", (2, 8, width), full), ("e2", (8, 8, width), full),
        ("e3_src", (ROWS, width), low), ("e3", (8, ROWS, width), low),
        ("e4_src", (ROWS, width), low), ("e4", (8, ROWS, width), low),
        ("e5_src", (2, 8, width), full), ("e5", (8, 8, width), full),
        ("acts", (2 * ROWS, width), full), ("acts_low", (2 * ROWS, width), low),
        ("late", (8, 128), full), ("block1", (32, ROWS, 128), full), ("block0", (32, 8, 128), full),
        ("g", (4, rows, width), low), ("gp", (4, rows, width), full),
        ("p", (2 * HEADS, SPAN, SPAN), full), ("r1", (rows, 1), full), ("r2", (rows, 1), full),
    ]
    found += [(name, (rows, width), low) for name in ("x", "q", "k", "v", "ctx", "hl", "dz", "k0", "v0", "x0", "skip", "cot", "y")]
    found += [(name, (rows, width), full) for name in ("n1", "h", "n2", "skip_grad", "embeds_grad")]
    shapes = {
        "d": ((2 * share, width), low), "u": ((share, 2 * width), low), "q": ((share, 2 * width), low),
        "k": ((share, width), low),
    }
    blocks = [(name + side, shape) for name, shape in shapes.items() for side in "ab"]
    blocks += [("s1", ((ROWS, 128), full)), ("s0", ((8, 128), full))]
    for name, (shape, dtype) in blocks:
        for kind, many in zip(KINDS, (16, 8, 2, 10) if name[0] in "du" else (16, 8, 4, 5)):
            found.append((name + kind, (many,) + shape, dtype))
    return found


def step_call(params, embeds, skip_tokens, cotangent, lengths):
    vmem, hbm = pl.BlockSpec(memory_space=pltpu.VMEM), pl.BlockSpec(memory_space=pl.ANY)
    rows, width = embeds.shape
    share = width // 32
    scratch = [pltpu.VMEM(shape, dtype) for _, shape, dtype in step_scratch(width)]
    scratch += [
        pltpu.SemaphoreType.DMA((6, GATHER_SEMS)),
        pltpu.SemaphoreType.DMA((2, 5)),
        pltpu.SemaphoreType.DMA((6, REDUCE_SEMS)),
        pltpu.SemaphoreType.DMA((6, 2)),
        pltpu.SemaphoreType.DMA((7,)),
    ]
    shape = jax.ShapeDtypeStruct
    return pl.pallas_call(
        step_kernel,
        out_shape=[
            shape((rows, width), jnp.bfloat16), shape((rows, width), jnp.float32),
            shape((rows, width), jnp.float32), shape((2, share, 8 * width), jnp.float32),
            shape((2, 4 * share, width), jnp.float32), shape((2 * ROWS, 128), jnp.float32),
            shape((4, rows, width), jnp.bfloat16),
        ],
        in_specs=[hbm] * 4 + [vmem] * 3 + [hbm] * 3 + [pl.BlockSpec(memory_space=pltpu.SMEM)],
        out_specs=[hbm] * 3 + [vmem] * 3 + [hbm],
        scratch_shapes=scratch,
        compiler_params=pltpu.CompilerParams(
            collective_id=1, has_side_effects=True, vmem_limit_bytes=64 * 2**20
        ),
    )(*params, embeds, skip_tokens, cotangent, lengths)


def adam_parts(parameter, first, second, gradient, decayed):
    first = beta_first * first + (1.0 - beta_first) * gradient
    second = beta_second * second + (1.0 - beta_second) * gradient * gradient
    update = first / first_fix / (jnp.sqrt(second / second_fix) + adam_epsilon)
    if decayed:
        update = update + weight_decay * parameter
    return update, first, second


def adam_kernel(*refs):
    params, moments = refs[0:7], refs[7:14]
    joined, down, small = refs[14:17]
    passed, steps, news, handed = refs[17:20], refs[20:27], refs[27:34], refs[34:37]

    def update(index, gradient):
        step, first, second = adam_parts(
            params[index][...], moments[index][0], moments[index][1], gradient, index < 4
        )
        steps[index][...] = step
        news[index][0] = first
        news[index][1] = second

    qkv, out = params[0].shape[2], params[1].shape[2]
    update(0, joined[:, :, :qkv])
    update(1, joined[:, :, qkv : qkv + out])
    update(2, joined[:, :, qkv + out :])
    update(3, down[...])

    @pl.when(pl.program_id(1) == 0)
    def _():
        for src, dst in zip(passed, handed):
            dst[...] = src[...]

    @pl.when((pl.program_id(0) == 0) & (pl.program_id(1) == 0))
    def _():
        many = small.shape[0] // 2
        for layer in range(2):
            at = layer * many
            for index, start, stop in ((4, 8, 9), (5, 0, 2), (6, 2, 8)):
                width = params[index].shape[-1]
                here = (slice(layer, layer + 1),) if index == 4 else (layer,)
                here = here if index < 6 else (slice(None), layer)
                step, first, second = adam_parts(
                    params[index][here], moments[index][(0, *here)], moments[index][(1, *here)],
                    small[at + start : at + stop, :width], False,
                )
                steps[index][here] = step
                news[index][(0, *here)] = first
                news[index][(1, *here)] = second


def adam_update(params, moments, joined, down, small, passed):
    cuts = 3 if params[0].shape[1] % 24 == 0 else 1

    def whole(a):
        return pl.BlockSpec(a.shape, lambda l, r, n=a.ndim: (0,) * n)

    def rows(a):
        return pl.BlockSpec((1, a.shape[1] // cuts, a.shape[2]), lambda l, r: (l, r, 0))

    def pairs(a):
        return pl.BlockSpec((2, 1, a.shape[2] // cuts, a.shape[3]), lambda l, r: (0, l, r, 0))

    halves = [pl.BlockSpec((a.shape[0] // 2, a.shape[1]), lambda l, r: (l, 0)) for a in passed]
    param_specs = [rows(a) for a in params[:4]] + [whole(a) for a in params[4:]]
    moment_specs = [pairs(a) for a in moments[:4]] + [whole(a) for a in moments[4:]]
    shape = lambda a: jax.ShapeDtypeStruct(a.shape, a.dtype)
    out = pl.pallas_call(
        adam_kernel,
        grid=(2, cuts),
        out_shape=[shape(a) for a in (*params, *moments, *passed)],
        in_specs=param_specs + moment_specs + [rows(joined), rows(down), whole(small)] + halves,
        out_specs=param_specs + moment_specs + halves,
        compiler_params=pltpu.CompilerParams(vmem_limit_bytes=63 * 2**20),
    )(*params, *moments, joined, down, small, *passed)
    return out[:7], out[7:14], out[14:]


def first_forward(weights, inputs, key_valid):
    qkv_w, out_w, up_w, down_w, up_b, gain_rows, biases = weights
    row_count, width = inputs.shape
    span_count = row_count // SPAN
    first = inputs.reshape(span_count, SPAN, width)[:, 0]
    mixed = jnp.dot(inputs, qkv_w[:, width:], preferred_element_type=jnp.float32)
    keys = mixed[:, :width].astype(jnp.bfloat16).reshape(span_count, SPAN, HEADS, width // HEADS)
    values = (mixed[:, width:] + biases[1]).astype(jnp.bfloat16)
    values = values.reshape(span_count, SPAN, HEADS, width // HEADS)
    queries = jnp.dot(first, qkv_w[:, :width], preferred_element_type=jnp.float32) + biases[0]
    queries = queries.astype(jnp.bfloat16).reshape(span_count, HEADS, width // HEADS)
    scores = (
        jnp.einsum("bhe,bkhe->bhk", queries, keys, preferred_element_type=jnp.float32) * score_scale
    )
    scores = jnp.where(key_valid[:, None, :], scores, masked_score)
    probs = jax.nn.softmax(scores, axis=-1)
    context = jnp.einsum(
        "bhk,bkhe->bhe", probs.astype(jnp.bfloat16), values, preferred_element_type=jnp.float32
    )
    context = context.reshape(span_count, width).astype(jnp.bfloat16)
    attended = jnp.dot(context, out_w, preferred_element_type=jnp.float32) + biases[2]
    hidden, normed_one, scale_one = normalize(
        first.astype(jnp.float32) + attended, gain_rows[0], biases[3]
    )
    hidden_low = hidden.astype(jnp.bfloat16)
    pre_gelu = jnp.dot(hidden_low, up_w, preferred_element_type=jnp.float32) + up_b
    activated = jax.nn.gelu(pre_gelu, approximate=False).astype(jnp.bfloat16)
    branch_out = jnp.dot(activated, down_w, preferred_element_type=jnp.float32) + biases[4]
    output, normed_two, scale_two = normalize(hidden + branch_out, gain_rows[1], biases[5])
    saved = (
        first, queries, keys, values, probs, context, normed_one, scale_one, hidden_low, pre_gelu,
        activated, normed_two, scale_two,
    )
    return output, saved


def first_backward(weights, inputs, saved, grad_out):
    qkv_w, out_w, up_w, down_w, up_b, gain_rows, biases = weights
    (
        first, queries, keys, values, probs, context, normed_one, scale_one, hidden_low, pre_gelu,
        activated, normed_two, scale_two,
    ) = saved
    row_count, width = inputs.shape
    span_count = row_count // SPAN
    grad_pre_two, grad_gain_two, grad_shift_two = normalize_back(
        grad_out, normed_two, scale_two, gain_rows[1]
    )
    grad_branch = grad_pre_two.astype(jnp.bfloat16)
    grad_act = dot_last(grad_branch, down_w)
    _, gelu_back = jax.vjp(lambda inner: jax.nn.gelu(inner, approximate=False), pre_gelu)
    grad_pre_gelu = gelu_back(grad_act)[0].astype(jnp.bfloat16)
    grad_hidden = grad_pre_two + dot_last(grad_pre_gelu, up_w)
    grad_pre_one, grad_gain_one, grad_shift_one = normalize_back(
        grad_hidden, normed_one, scale_one, gain_rows[0]
    )
    grad_attended = grad_pre_one.astype(jnp.bfloat16)
    grad_context = dot_last(grad_attended, out_w).astype(jnp.bfloat16)
    grad_context = grad_context.reshape(span_count, HEADS, width // HEADS)
    grad_probs = jnp.einsum(
        "bhe,bkhe->bhk", grad_context, values, preferred_element_type=jnp.float32
    )
    grad_values = jnp.einsum("bhk,bhe->bkhe", probs.astype(jnp.bfloat16), grad_context)
    grad_values = grad_values.reshape(row_count, width).astype(jnp.bfloat16)
    grad_scores = probs * (grad_probs - jnp.sum(probs * grad_probs, axis=-1, keepdims=True))
    grad_scores = grad_scores.astype(jnp.bfloat16)
    grad_queries = (
        jnp.einsum("bhk,bkhe->bhe", grad_scores, keys, preferred_element_type=jnp.float32)
        * score_scale
    )
    grad_queries = grad_queries.reshape(span_count, width).astype(jnp.bfloat16)
    grad_keys = (
        jnp.einsum("bhk,bhe->bkhe", grad_scores, queries, preferred_element_type=jnp.float32)
        * score_scale
    )
    grad_keys = grad_keys.reshape(row_count, width).astype(jnp.bfloat16)
    grad_kv = jnp.concatenate([grad_keys, grad_values], axis=1)
    grad_kv_w = dot_first(inputs, grad_kv)
    grad_inputs = dot_last(grad_kv, qkv_w[:, width:])
    grad_first = grad_pre_one + dot_last(grad_queries, qkv_w[:, :width])
    placed = jnp.pad(grad_first[:, None], ((0, 0), (0, SPAN - 1), (0, 0))).reshape(row_count, width)
    grad_inputs = grad_inputs + placed
    rows = jnp.concatenate(
        [context, grad_attended, hidden_low, grad_pre_gelu, activated, grad_branch, first, grad_queries],
        axis=1,
    )

    def total(values):
        return jnp.sum(values, axis=0, dtype=jnp.float32)

    small = (
        total(grad_pre_gelu),
        jnp.stack([grad_gain_one, grad_gain_two]),
        jnp.stack(
            [
                total(grad_queries), total(grad_values), total(grad_attended), grad_shift_one,
                total(grad_branch), grad_shift_two,
            ]
        ),
    )
    return grad_inputs, grad_kv_w, rows, small


def first_weight_grads(rows, kv_owned, at):
    width = rows.shape[1] // 16
    wide = 4 * width
    context, grad_attended = rows[:, :width], rows[:, width : 2 * width]
    hidden_low = rows[:, 2 * width : 3 * width]
    grad_pre_gelu = rows[:, 3 * width : 3 * width + wide]
    activated = rows[:, 7 * width : 11 * width]
    grad_branch = rows[:, 11 * width : 12 * width]
    first = rows[:, 12 * width : 13 * width]
    grad_queries = rows[:, 13 * width : 14 * width]
    count = kv_owned.shape[0]
    own = lambda values, many: lax.dynamic_slice_in_dim(values, at * many, many, 1)
    return (
        jnp.concatenate([dot_first(own(first, count), grad_queries), kv_owned], axis=1),
        dot_first(own(context, count), grad_attended),
        dot_first(own(hidden_low, count), grad_pre_gelu),
        dot_first(own(activated, 4 * count), grad_branch),
    )


def pack_small(up_b, gains, biases, owners):
    parts = [up_b.reshape(owners, -1)]
    for tensor in (gains, biases):
        parts.append(tensor.reshape(tensor.shape[0], owners, -1).transpose(1, 0, 2).reshape(owners, -1))
    return jnp.concatenate(parts, axis=1)


def unpack_small(packed, width):
    owners = packed.shape[0]
    share = width // owners
    up_b = packed[:, : 4 * share].reshape(4 * width)
    gains = packed[:, 4 * share : 6 * share].reshape(owners, 2, share).transpose(1, 0, 2)
    biases = packed[:, 6 * share :].reshape(owners, 6, share).transpose(1, 0, 2)
    return up_b, gains.reshape(2, width), biases.reshape(6, width)


def exchange_weights(p1, p2, small):
    both = ("wide", "narrow")
    w1 = lax.all_gather(p1, both, axis=0)
    w2 = lax.all_gather(p2, both, axis=0)
    return (w1[:, 0], w1[:, 1]), (w2[:, 0], w2[:, 1]), lax.all_gather(small, both, axis=0)


def exchange_grads(g1, g2, kv, small, rows):
    both = ("wide", "narrow")
    summed = [
        lax.psum_scatter(a, both, scatter_dimension=0).astype(jnp.float32) for a in (g1, g2, kv, small)
    ]
    return summed + [lax.all_gather(rows, both, axis=0)]


def rows_ahead(group):
    last = group[6]
    return (*group[:6], jnp.swapaxes(last, last.ndim - 3, last.ndim - 2))


def fused_step(embeds, skip_tokens, cotangent, lengths, params, moments):
    params, moments = rows_ahead(params), rows_ahead(moments)
    y, embeds_grad, skip_grad, o1, o2, small, _ = step_call(params, embeds, skip_tokens, cotangent, lengths)
    new_steps, new_moments, passed = adam_update(params, moments, o1, o2, small, (y, embeds_grad, skip_grad))
    return (*passed, *rows_ahead(new_steps), *rows_ahead(new_moments))


def per_device(
    embeds, skip_tokens, cotangent, lengths, qkv_weight, out_weight, up_weight, down_weight, up_bias,
    norm_gains, biases, qkv_moments, out_moments, up_moments, down_moments, up_bias_moments,
    gain_moments, bias_moments,
):
    params = (qkv_weight, out_weight, up_weight, down_weight, up_bias, norm_gains, biases)
    moments = (
        qkv_moments, out_moments, up_moments, down_moments, up_bias_moments, gain_moments, bias_moments,
    )
    wide_size, narrow_size = lax.axis_size("wide"), lax.axis_size("narrow")
    if (wide_size, narrow_size) == (8, 4):
        return fused_step(embeds, skip_tokens, cotangent, lengths, params, moments)
    owners = wide_size * narrow_size
    at = lax.axis_index("wide") * narrow_size + lax.axis_index("narrow")
    span_count = lengths.shape[0]
    row_count, width = embeds.shape
    positions = lax.broadcasted_iota(jnp.int32, (span_count, SPAN), 1)
    key_valid = positions < lengths[:, None]
    row_index = lax.broadcasted_iota(jnp.int32, (1, SPAN, 1), 1)

    p1 = jnp.concatenate([qkv_weight, out_weight, up_weight], axis=2).astype(jnp.bfloat16)
    p2 = down_weight.astype(jnp.bfloat16)
    share = 12 * width // owners
    tiles = -(-2 * share // 1024)
    small_own = jnp.concatenate(
        [up_bias, norm_gains.reshape(2, -1), biases.reshape(2, -1)], axis=1
    ).reshape(-1)
    small_own = jnp.pad(small_own, (0, tiles * 1024 - 2 * share)).reshape(tiles * 8, 128)
    w1, w2, small_all = exchange_weights(p1, p2, small_own)
    small_all = small_all.reshape(owners, -1)[:, : 2 * share].astype(jnp.bfloat16).astype(jnp.float32)

    def layer_weights(layer):
        joined = w1[layer].reshape(width, -1)
        return (
            joined[:, : 3 * width], joined[:, 3 * width : 4 * width], joined[:, 4 * width :],
            w2[layer].reshape(-1, width),
        ) + unpack_small(small_all[:, layer * share : (layer + 1) * share], width)

    backbone, head = layer_weights(0), layer_weights(1)
    backbone_out, saved = first_forward(backbone, embeds, key_valid)
    skip_view = skip_tokens.reshape(span_count, SPAN, width)
    head_in = jnp.where(row_index == 0, backbone_out.astype(jnp.bfloat16)[:, None], skip_view)
    head_in = head_in.reshape(row_count, width)
    head_out, grad_head_in, head_grads = backward_block(
        head, head_in, key_valid, cotangent.astype(jnp.float32)
    )
    grad_view = grad_head_in.reshape(span_count, SPAN, width)
    skip_grad = jnp.where(row_index == 0, 0.0, grad_view).reshape(row_count, width)
    embeds_grad, grad_kv_w, rows, small_first = first_backward(
        backbone, embeds, saved, grad_view[:, 0]
    )
    low = lambda a: a.astype(jnp.bfloat16)
    g1 = jnp.concatenate([low(head_grads[0]), low(head_grads[1]), low(head_grads[2])], axis=1)
    g1 = g1.reshape(owners, width // owners, -1)
    g2 = low(head_grads[3]).reshape(owners, -1, width)
    kv = low(grad_kv_w).reshape(owners, width // owners, -1)
    small_grads = jnp.concatenate(
        [pack_small(*small_first, owners), pack_small(*head_grads[4:], owners)], axis=1
    )
    small_grads = jnp.pad(small_grads, ((0, 0), (0, tiles * 1024 - 2 * share)))
    small_grads = small_grads.reshape(owners, tiles * 8, 128)
    rows_wide = jnp.pad(rows, ((0, 0), (0, 2 * width)))
    own_g1, own_g2, own_kv, own_small, all_rows = exchange_grads(
        g1, g2, kv, small_grads, rows_wide.reshape(16 * span_count // 2, -1)
    )
    all_rows = all_rows.reshape(owners * span_count, -1)
    first_grads = first_weight_grads(all_rows, own_kv, at)
    own_small = own_small.reshape(-1)[: 2 * share].reshape(2, share)
    sixth = width // owners
    joined = jnp.stack([jnp.concatenate(first_grads[:3], axis=1), own_g1])
    down = jnp.stack([first_grads[3], own_g2])
    pad = lambda a: jnp.pad(a, ((0, 0), (0, 0), (0, 128 - a.shape[2])))
    small = [
        pad(own_small[:, 4 * sixth : 6 * sixth].reshape(2, 2, sixth)),
        pad(own_small[:, 6 * sixth :].reshape(2, 6, sixth)),
        pad(own_small[:, None, : 4 * sixth]),
        jnp.zeros((2, 7, 128), jnp.float32),
    ]
    small = jnp.concatenate(small, axis=1).reshape(32, 128)
    passed = (head_out.astype(jnp.bfloat16), embeds_grad, skip_grad)
    new_steps, new_moments, passed = adam_update(
        rows_ahead(params), rows_ahead(moments), joined, down, small, passed
    )
    return (*passed, *rows_ahead(new_steps), *rows_ahead(new_moments))


def solution(mesh):
    return jax.shard_map(
        per_device,
        mesh=mesh,
        in_specs=(
            P(("wide", "narrow"), None),
            P(("wide", "narrow"), None),
            P(("wide", "narrow"), None),
            P(("wide", "narrow")),
            P(None, ("wide", "narrow"), None),
            P(None, ("wide", "narrow"), None),
            P(None, ("wide", "narrow"), None),
            P(None, ("wide", "narrow"), None),
            P(None, ("wide", "narrow")),
            P(None, None, ("wide", "narrow")),
            P(None, None, ("wide", "narrow")),
            P(None, None, ("wide", "narrow"), None),
            P(None, None, ("wide", "narrow"), None),
            P(None, None, ("wide", "narrow"), None),
            P(None, None, ("wide", "narrow"), None),
            P(None, None, ("wide", "narrow")),
            P(None, None, None, ("wide", "narrow")),
            P(None, None, None, ("wide", "narrow")),
        ),
        out_specs=(
            P(("wide", "narrow"), None),
            P(("wide", "narrow"), None),
            P(("wide", "narrow"), None),
            P(None, ("wide", "narrow"), None),
            P(None, ("wide", "narrow"), None),
            P(None, ("wide", "narrow"), None),
            P(None, ("wide", "narrow"), None),
            P(None, ("wide", "narrow")),
            P(None, None, ("wide", "narrow")),
            P(None, None, ("wide", "narrow")),
            P(None, None, ("wide", "narrow"), None),
            P(None, None, ("wide", "narrow"), None),
            P(None, None, ("wide", "narrow"), None),
            P(None, None, ("wide", "narrow"), None),
            P(None, None, ("wide", "narrow")),
            P(None, None, None, ("wide", "narrow")),
            P(None, None, None, ("wide", "narrow")),
        ),
        check_vma=False,
    )
```
